32 devices in a mesh: dp: 4 (over y, x), mp: 8 (over z, core).
Axes of the slice: x: 2, y: 2, z: 4, core: 2. Of those that a mesh axis runs over, the one named last changes fastest.
Arguments:
- inputs: bfloat16 [2, 10240, 2048], P(None, ('dp', 'mp')), may hold values from -6 to 6
- cotangent: bfloat16 [2, 10240, 2048], P(None, ('dp', 'mp')), may hold values from -6 to 6
- short_lengths: int32 [4, 4], P('dp'), may hold values from 1 to 1024, 2560 in all within a row
- long_lengths: int32 [4, 2], P('dp'), may hold values from 1 to 2048, 2560 in all within a row
- norm1_gain: float32 [2048], replicated, may hold values from 0.5 to 1.5
- norm1_bias: float32 [2048], replicated, may hold values from -3 to 3
- query_weight: bfloat16 [2048, 512], P(None, 'mp'), may hold values from -0.125 to 0.125
- key_weight: bfloat16 [2048, 512], P(None, 'mp'), may hold values from -0.125 to 0.125
- value_weight: bfloat16 [2048, 512], P(None, 'mp'), may hold values from -0.125 to 0.125
- query_kernel: float32 [3, 512], P(None, 'mp'), may hold values from -3 to 3
- key_kernel: float32 [3, 512], P(None, 'mp'), may hold values from -3 to 3
- value_kernel: float32 [3, 512], P(None, 'mp'), may hold values from -3 to 3
- out_weight: bfloat16 [512, 2048], P('mp'), may hold values from -2 to 2
- norm2_gain: float32 [2048], replicated, may hold values from 0.5 to 1.5
- norm2_bias: float32 [2048], replicated, may hold values from -3 to 3
- up_weight: bfloat16 [2048, 8192], P(None, 'mp'), may hold values from -0.125 to 0.125
- down_weight: bfloat16 [8192, 2048], P('mp'), may hold values from -0.0625 to 0.0625
Outputs:
- output: bfloat16 [2, 10240, 2048], P(None, ('dp', 'mp'))
- input_grad: float32 [2, 10240, 2048], P(None, ('dp', 'mp'))
- norm1_gain_grad: float32 [2048], replicated
- norm1_bias_grad: float32 [2048], replicated
- query_weight_grad: float32 [2048, 512], P(None, 'mp')
- key_weight_grad: float32 [2048, 512], P(None, 'mp')
- value_weight_grad: float32 [2048, 512], P(None, 'mp')
- query_kernel_grad: float32 [3, 512], P(None, 'mp')
- key_kernel_grad: float32 [3, 512], P(None, 'mp')
- value_kernel_grad: float32 [3, 512], P(None, 'mp')
- out_weight_grad: float32 [512, 2048], P('mp')
- norm2_gain_grad: float32 [2048], replicated
- norm2_bias_grad: float32 [2048], replicated
- up_weight_grad: float32 [2048, 8192], P(None, 'mp')
- down_weight_grad: float32 [8192, 2048], P('mp')
The draws below stay inside these ranges and needn't reach their ends.
Inputs may be any that keep to these rules, and one draw needn't show every extreme that they name: `short_lengths`: row g lists, in order, the lengths of the documents packed into data group g's short buffer of 2560 tokens; each row sums to 2560 and its largest entry is 1024. `long_lengths`: row g lists, in order, the lengths of the documents packed into data group g's long buffer of 2560 tokens; each row sums to 2560 and its entries are at most 2048.
All inputs are finite; a program needn't handle non-finite values.
Results may differ from the reference program's by a relative error of at most 0.019.
Values may be sent and summed in bfloat16 or wider, within the bound.
A program may use at most 384 MiB of HBM per device.

```python
import math
from functools import partial
import jax
import jax.numpy as jnp
import numpy as np
from jax import lax

D = 2048
FF = 8192
HD = 64
SHORT_LEN = 1024
LONG_LEN = 2048
HEADS = 8
ATT = 512
GROUP = 2560
ROWS = 10240
SHORT_DOCS = 4
LONG_DOCS = 2
N_DP = 4


def block_levels(rng, dims, pieces, least, largest):
    loudness = 1.0
    for axis_at, shards_of in pieces:
        draws = jax.random.uniform(jax.random.fold_in(jax.random.fold_in(rng, 6), axis_at), (shards_of,), jnp.float32, least / len(pieces), largest / len(pieces))
        loudness = loudness * jnp.repeat(jnp.exp(draws), dims[axis_at] // shards_of).reshape((-1,) + (1,) * (len(dims) - 1 - axis_at))
    return loudness


def split_up(count, total, limit, slope):
    loads = [(1 << 20) // math.isqrt(rank ** slope) + 1 for rank in range(2, count + 1)]
    surplus, counts = total - limit - (count - 1), [1] * (count - 1)
    while surplus > 0:
        candidates = [i for i in range(count - 1) if counts[i] < limit]
        whole, remaining = sum([loads[i] for i in candidates]), surplus
        for i in candidates:
            more = min(limit - counts[i], max(1, remaining * loads[i] // whole), surplus)
            counts[i] = counts[i] + more
            surplus = surplus - more
    return np.array([limit] + counts)


def ragged(stream_key, count, total, most, skew):
    if count == 2:
        one = jax.random.randint(stream_key, (), max(1, total - most), min(most, total - 1) + 1)
        return jnp.stack([one, total - one])
    tallies = jnp.asarray(split_up(count, total, most, skew), jnp.int32)
    pairs = (count - 1) // 2
    giver, taker = tallies[1:1 + 2 * pairs:2], tallies[2:2 + 2 * pairs:2]
    room = jnp.minimum(giver - 1, most - taker)
    moved = jax.random.randint(jax.random.fold_in(stream_key, 1), (pairs,), 0, 1 << 20) % (room + 1)
    tallies = tallies.at[1:1 + 2 * pairs:2].set(giver - moved).at[2:2 + 2 * pairs:2].set(taker + moved)
    return tallies[jax.random.permutation(jax.random.fold_in(stream_key, 2), count)]


def normal_values(stream_key, dims, spread, reach, cuts=(), kind=jnp.bfloat16):
    level = block_levels(stream_key, dims, cuts, -0.22, 0.18) if cuts else 1.0
    values = jax.random.normal(stream_key, dims, jnp.float32) * spread * level
    return jnp.minimum(jnp.maximum(values, -reach), reach).astype(kind)


def setup_inputs(seed: int = 0) -> dict:
    arg_keys = jax.random.split(jax.random.key(seed), 18)
    inputs = normal_values(arg_keys[0], (2, ROWS, D), 1.0, 6.0, ((1, 32),))
    cotangent = normal_values(arg_keys[1], (2, ROWS, D), 1.0, 6.0, ((1, 32),))
    short_lengths = jax.vmap(lambda own: ragged(own, SHORT_DOCS, GROUP, SHORT_LEN, 2))(jax.random.split(arg_keys[2], N_DP)).reshape((N_DP, SHORT_DOCS)).astype(jnp.int32)
    long_lengths = jax.vmap(lambda own: ragged(own, LONG_DOCS, GROUP, LONG_LEN, 2))(jax.random.split(arg_keys[3], N_DP)).reshape((N_DP, LONG_DOCS)).astype(jnp.int32)
    norm1_gain = jnp.clip(1.0 + 0.1 * jax.random.normal(arg_keys[4], (D,), jnp.float32), 0.5, 1.5)
    norm1_bias = normal_values(arg_keys[5], (D,), 0.5, 3.0, (), jnp.float32)
    query_weight = normal_values(arg_keys[6], (D, ATT), D ** -0.5, 0.125, ((1, 8),))
    key_weight = normal_values(arg_keys[7], (D, ATT), D ** -0.5, 0.125, ((1, 8),))
    value_weight = normal_values(arg_keys[8], (D, ATT), D ** -0.5, 0.125, ((1, 8),))
    query_kernel = normal_values(arg_keys[9], (3, ATT), 0.6, 3.0, ((1, 8),), jnp.float32)
    key_kernel = normal_values(arg_keys[10], (3, ATT), 0.6, 3.0, ((1, 8),), jnp.float32)
    value_kernel = normal_values(arg_keys[11], (3, ATT), 0.6, 3.0, ((1, 8),), jnp.float32)
    out_weight = normal_values(arg_keys[12], (ATT, D), (ATT // 64) ** -0.5, 2.0, ((0, 8),))
    norm2_gain = jnp.clip(1.0 + 0.1 * jax.random.normal(arg_keys[13], (D,), jnp.float32), 0.5, 1.5)
    norm2_bias = normal_values(arg_keys[14], (D,), 0.5, 3.0, (), jnp.float32)
    up_weight = normal_values(arg_keys[15], (D, FF), D ** -0.5, 0.125, ((1, 8),))
    down_weight = normal_values(arg_keys[16], (FF, D), FF ** -0.5, 0.0625, ((0, 8),))
    return {"inputs": inputs, "cotangent": cotangent, "short_lengths": short_lengths, "long_lengths": long_lengths, "norm1_gain": norm1_gain, "norm1_bias": norm1_bias, "query_weight": query_weight, "key_weight": key_weight, "value_weight": value_weight, "query_kernel": query_kernel, "key_kernel": key_kernel, "value_kernel": value_kernel, "out_weight": out_weight, "norm2_gain": norm2_gain, "norm2_bias": norm2_bias, "up_weight": up_weight, "down_weight": down_weight}


exact_precision = lax.Precision.HIGHEST

@jax.custom_vjp
def low(v):
    return lax.optimization_barrier(v.astype(jnp.bfloat16)).astype(jnp.float32)

@jax.custom_vjp
def low_back(v):
    return v

def low_keep(v):
    return (low(v), None)

def low_pass(kept, grad):
    return (grad,)

def back_keep(v):
    return (v, None)

def back_low(kept, grad):
    return (low(grad),)
low.defvjp(low_keep, low_pass)
low_back.defvjp(back_keep, back_low)

def layer_norm(rows, gain, shift):
    row_mean = lax.optimization_barrier(jnp.mean(rows, axis=-1, keepdims=True))
    centered = rows - row_mean
    variance = lax.optimization_barrier(jnp.mean(centered * centered, axis=-1, keepdims=True))
    return centered * lax.rsqrt(variance + 1e-05) * gain + shift

def positions(lengths, count):
    ends = jnp.cumsum(lengths).astype(jnp.int32)
    places = jnp.arange(count, dtype=jnp.int32)
    passed = (places[:, None] >= ends[None, :]).astype(jnp.int32)
    doc_ids = lax.optimization_barrier(jnp.sum(passed, axis=1)).astype(jnp.int32)
    starts = lax.optimization_barrier(jnp.sum(passed * lengths[None, :], axis=1)).astype(jnp.int32)
    return (doc_ids, places - starts)

def causal_conv(values, kernel, offsets):
    width = values.shape[1]
    one_back = jnp.concatenate([jnp.zeros((1, width), values.dtype), values[:-1]], axis=0)
    two_back = jnp.concatenate([jnp.zeros((2, width), values.dtype), values[:-2]], axis=0)
    one_back = jnp.where(offsets[:, None] >= 1, one_back, jnp.zeros_like(one_back))
    two_back = jnp.where(offsets[:, None] >= 2, two_back, jnp.zeros_like(two_back))
    return kernel[0] * values + kernel[1] * one_back + kernel[2] * two_back

def head_attention(allowed, triple):
    query, keys, values = triple
    scaled = jnp.dot(query, keys.T, precision=exact_precision) * HD ** (-0.5)
    scores = jnp.where(allowed, low_back(scaled), -1e+30)
    top = lax.optimization_barrier(jnp.max(scores, axis=1, keepdims=True))
    powered = jnp.exp(scores - top)
    probs = powered / lax.optimization_barrier(jnp.sum(powered, axis=1, keepdims=True))
    return low(low_back(jnp.dot(low(probs), values, precision=exact_precision)))

def forward(rows, params, doc_ids, offsets):
    gain_one, shift_one, w_query, w_key, w_value, k_query, k_key, k_value, w_out, gain_two, shift_two, w_up, w_down = params
    normed = low(layer_norm(rows, gain_one, shift_one))
    joined = jnp.concatenate([w_query, w_key, w_value], axis=1)
    kernels = jnp.concatenate([k_query, k_key, k_value], axis=1)
    raw = low_back(jnp.dot(normed, joined, precision=exact_precision))
    mixed = low(causal_conv(raw, kernels, offsets))
    places = jnp.arange(GROUP, dtype=jnp.int32)
    allowed = (doc_ids[:, None] == doc_ids[None, :]) & (places[:, None] >= places[None, :])
    split = mixed.reshape(GROUP, 3, HEADS, HD).transpose(1, 2, 0, 3)
    attended = lax.map(jax.checkpoint(partial(head_attention, allowed)), (split[0], split[1], split[2]))
    merged = attended.transpose(1, 0, 2).reshape(GROUP, ATT)
    middle = rows + low_back(jnp.dot(merged, w_out, precision=exact_precision))
    second = low(layer_norm(middle, gain_two, shift_two))
    pre = low_back(jnp.dot(second, w_up, precision=exact_precision))
    hidden = low(jnp.square(jnp.maximum(pre, 0.0)))
    return middle + jnp.dot(hidden, w_down, precision=exact_precision)

def reference(inputs, cotangent, short_lengths, long_lengths, norm1_gain, norm1_bias, query_weight, key_weight, value_weight, query_kernel, key_kernel, value_kernel, out_weight, norm2_gain, norm2_bias, up_weight, down_weight):
    params = tuple((item.astype(jnp.float32) for item in (norm1_gain, norm1_bias, query_weight, key_weight, value_weight, query_kernel, key_kernel, value_kernel, out_weight, norm2_gain, norm2_bias, up_weight, down_weight)))
    short_layout = jax.vmap(partial(positions, count=GROUP))(short_lengths)
    long_layout = jax.vmap(partial(positions, count=GROUP))(long_lengths)
    doc_ids = jnp.concatenate([short_layout[0], long_layout[0]], axis=0)
    offsets = jnp.concatenate([short_layout[1], long_layout[1]], axis=0)
    rows = inputs.astype(jnp.float32).reshape(2 * N_DP, GROUP, D)
    grads = cotangent.astype(jnp.float32).reshape(2 * N_DP, GROUP, D)

    def one_buffer(totals, item):
        block_rows, block_grads, block_docs, block_offsets = item
        result, pull = jax.vjp(partial(forward, doc_ids=block_docs, offsets=block_offsets), block_rows, params)
        row_grad, param_grads = pull(block_grads)
        totals = jax.tree.map(jnp.add, totals, param_grads)
        return (totals, (result.astype(jnp.bfloat16), row_grad))
    start_totals = jax.tree.map(jnp.zeros_like, params)
    totals, (outputs, row_grads) = lax.scan(one_buffer, start_totals, (rows, grads, doc_ids, offsets))
    return (outputs.reshape(2, N_DP * GROUP, D), row_grads.reshape(2, N_DP * GROUP, D), totals[0], totals[1], totals[2], totals[3], totals[4], totals[5], totals[6], totals[7], totals[8], totals[9], totals[10], totals[11], totals[12])
```

```python
from functools import partial

import jax
import jax.numpy as jnp
from jax import lax
from jax.experimental import pallas as pl
from jax.experimental.pallas import tpu as pltpu
from jax.sharding import PartitionSpec as P

HD = 64
BLOCK = 256
LOW = jnp.bfloat16
F32 = jnp.float32


def dot(left, right):
    return jnp.dot(left, right, preferred_element_type=F32)


def layer_norm(rows, gain, shift):
    row_mean = jnp.mean(rows, axis=-1, keepdims=True)
    centered = rows - row_mean
    variance = jnp.mean(centered * centered, axis=-1, keepdims=True)
    return centered * lax.rsqrt(variance + 1e-05) * gain + shift


def document_starts(lengths, count):
    ends = jnp.cumsum(lengths)
    places = jnp.arange(count, dtype=jnp.int32)
    passed = (places[:, None] >= ends[None, :]).astype(jnp.int32)
    return jnp.sum(passed * lengths[None, :], axis=1)


def allowed_pairs(start_row, key_block, query_block):
    keys = key_block * BLOCK + lax.broadcasted_iota(jnp.int32, (BLOCK, BLOCK), 0)
    queries = query_block * BLOCK + lax.broadcasted_iota(jnp.int32, (BLOCK, BLOCK), 1)
    return (keys <= queries) & (keys >= start_row)


def attend_kernel(first_ref, start_ref, mixed_ref, out_ref, wide_ref, total_ref, values_t):
    step = pl.program_id(0)

    @pl.when(step == 0)
    def _():
        def turn(at, carry):
            rows = pl.ds(pl.multiple_of(at * BLOCK, BLOCK), BLOCK)
            values_t[at] = mixed_ref[rows, 2 * HD : 3 * HD].T
            return carry

        lax.fori_loop(0, values_t.shape[0], turn, 0)

    here = pl.ds(pl.multiple_of(step * BLOCK, BLOCK), BLOCK)
    query_t = (mixed_ref[here, 0:HD] * HD ** (-0.5)).astype(LOW).T
    start_row = start_ref[...]

    def one(at, carry):
        top, summed, acc = carry
        rows = pl.ds(pl.multiple_of(at * BLOCK, BLOCK), BLOCK)
        scores = dot(mixed_ref[rows, HD : 2 * HD], query_t)
        scores = jnp.where(allowed_pairs(start_row, at, step), scores, -1e30)
        new_top = jnp.maximum(top, jnp.max(scores, axis=0, keepdims=True))
        powered = jnp.exp(scores - new_top)
        shrink = jnp.exp(top - new_top)
        summed = summed * shrink + jnp.sum(powered, axis=0, keepdims=True)
        acc = acc * shrink + dot(values_t[at], powered.astype(LOW))
        return new_top, summed, acc

    top, summed, acc = lax.fori_loop(
        first_ref[step],
        step + 1,
        one,
        (
            jnp.full((1, BLOCK), -1e30, F32),
            jnp.zeros((1, BLOCK), F32),
            jnp.zeros((HD, BLOCK), F32),
        ),
    )
    result = acc / summed
    wide_ref[...] = result
    out_ref[...] = result.T.astype(LOW)
    total_ref[...] = top + jnp.log(summed)


def attend(mixed, starts):
    group = mixed.shape[0]
    steps = group // BLOCK
    first = starts[::BLOCK] // BLOCK
    row = pl.BlockSpec((1, BLOCK), lambda i, first: (0, i))
    return pl.pallas_call(
        attend_kernel,
        grid_spec=pltpu.PrefetchScalarGridSpec(
            num_scalar_prefetch=1,
            grid=(steps,),
            in_specs=[row, pl.BlockSpec((group, 3 * HD), lambda i, first: (0, 0))],
            out_specs=[
                pl.BlockSpec((BLOCK, HD), lambda i, first: (i, 0)),
                pl.BlockSpec((HD, BLOCK), lambda i, first: (0, i)),
                row,
            ],
            scratch_shapes=[pltpu.VMEM((steps, HD, BLOCK), LOW)],
        ),
        out_shape=[
            jax.ShapeDtypeStruct((group, HD), LOW),
            jax.ShapeDtypeStruct((HD, group), F32),
            jax.ShapeDtypeStruct((1, group), F32),
        ],
        compiler_params=pltpu.CompilerParams(vmem_limit_bytes=32 * 1024 * 1024),
        cost_estimate=pl.CostEstimate(
            flops=4 * HD * group * group // 4,
            bytes_accessed=group * 2048,
            transcendentals=group * group // 4,
        ),
        name="attend",
    )(first, starts.reshape(1, group), mixed)


def attend_back_kernel(
    first_ref, start_ref, mixed_ref, grad_ref, wide_ref, total_ref, out_ref, keys_t, grad_keys, grad_values
):
    step = pl.program_id(0)

    @pl.when(step == 0)
    def _():
        def turn(at, carry):
            rows = pl.ds(pl.multiple_of(at * BLOCK, BLOCK), BLOCK)
            keys_t[at] = mixed_ref[rows, HD : 2 * HD].T
            return carry

        lax.fori_loop(0, keys_t.shape[0], turn, 0)
        grad_keys[...] = jnp.zeros(grad_keys.shape, F32)
        grad_values[...] = jnp.zeros(grad_values.shape, F32)

    here = pl.ds(pl.multiple_of(step * BLOCK, BLOCK), BLOCK)
    query = (mixed_ref[here, 0:HD] * HD ** (-0.5)).astype(LOW)
    query_t = query.T
    grad = grad_ref[...]
    grad_t = grad.T
    start_row = start_ref[...]
    total = total_ref[...]
    inner = jnp.sum(grad_t.astype(F32) * wide_ref[...], axis=0, keepdims=True)

    def one(at, acc):
        rows = pl.ds(pl.multiple_of(at * BLOCK, BLOCK), BLOCK)
        scores = dot(mixed_ref[rows, HD : 2 * HD], query_t)
        scores = jnp.where(allowed_pairs(start_row, at, step), scores, -1e30)
        probs = jnp.exp(scores - total)
        grad_probs = dot(mixed_ref[rows, 2 * HD : 3 * HD], grad_t)
        grad_scores = (probs * (grad_probs - inner)).astype(LOW)
        grad_values[rows, :] += dot(probs.astype(LOW), grad)
        grad_keys[rows, :] += dot(grad_scores, query)
        return acc + dot(keys_t[at], grad_scores)

    acc = lax.fori_loop(first_ref[step], step + 1, one, jnp.zeros((HD, BLOCK), F32))
    out_ref[here, 0:HD] = (acc * HD ** (-0.5)).T.astype(out_ref.dtype)

    @pl.when(step == pl.num_programs(0) - 1)
    def _():
        out_ref[:, HD : 2 * HD] = grad_keys[...].astype(out_ref.dtype)
        out_ref[:, 2 * HD : 3 * HD] = grad_values[...].astype(out_ref.dtype)


def attend_back(mixed, grad, wide, total, starts):
    group = mixed.shape[0]
    steps = group // BLOCK
    first = starts[::BLOCK] // BLOCK
    row = pl.BlockSpec((1, BLOCK), lambda i, first: (0, i))
    return pl.pallas_call(
        attend_back_kernel,
        grid_spec=pltpu.PrefetchScalarGridSpec(
            num_scalar_prefetch=1,
            grid=(steps,),
            in_specs=[
                row,
                pl.BlockSpec((group, 3 * HD), lambda i, first: (0, 0)),
                pl.BlockSpec((BLOCK, HD), lambda i, first: (i, 0)),
                pl.BlockSpec((HD, BLOCK), lambda i, first: (0, i)),
                row,
            ],
            out_specs=pl.BlockSpec((group, 3 * HD), lambda i, first: (0, 0)),
            scratch_shapes=[
                pltpu.VMEM((steps, HD, BLOCK), LOW),
                pltpu.VMEM((group, HD), F32),
                pltpu.VMEM((group, HD), F32),
            ],
        ),
        out_shape=jax.ShapeDtypeStruct((group, 3 * HD), LOW),
        compiler_params=pltpu.CompilerParams(vmem_limit_bytes=32 * 1024 * 1024),
        cost_estimate=pl.CostEstimate(
            flops=10 * HD * group * group // 4,
            bytes_accessed=group * 2048,
            transcendentals=group * group // 4,
        ),
        name="attend_back",
    )(first, starts.reshape(1, group), mixed, grad, wide, total)


def plane_send(block, mask):
    return lax.ppermute(block, "dp", [(d, d ^ mask) for d in range(lax.axis_size("dp"))])


def plane_gather(block):
    half = block.shape[0] // 2
    one, two = block[:half], block[half:]
    one_x = plane_send(one, 1)
    two_y = plane_send(two, 2)
    one_y = plane_send(one, 2)
    two_x = plane_send(two, 1)
    one_xy = plane_send(one_x, 2)
    two_xy = plane_send(two_y, 1)
    return [one, one_y, one_x, one_xy], [two, two_x, two_y, two_xy]


def plane_scatter(part):
    piece = part.shape[0] // 8

    def at(first, count=1):
        return part[first * piece : (first + count) * piece]

    one = plane_send(at(2, 2), 1)
    two = plane_send(at(6, 2), 2)
    one_sum = (at(0, 2).astype(F32) + one.astype(F32))
    two_sum = (at(4, 2).astype(F32) + two.astype(F32))
    one_last = plane_send(one_sum[piece:].astype(LOW), 2)
    two_last = plane_send(two_sum[piece:].astype(LOW), 1)
    return jnp.concatenate(
        [one_sum[:piece] + one_last.astype(F32), two_sum[:piece] + two_last.astype(F32)], axis=0
    )


def plane_order(first, second, axis):
    me = lax.axis_index("dp")
    blocks = jnp.stack(
        [
            jnp.concatenate([first[0], second[0]], axis=0),
            jnp.concatenate([first[2], second[1]], axis=0),
            jnp.concatenate([first[1], second[2]], axis=0),
            jnp.concatenate([first[3], second[3]], axis=0),
        ],
        axis=0,
    )
    return jnp.concatenate(
        [lax.dynamic_index_in_dim(blocks, me ^ d, 0, keepdims=False) for d in range(4)], axis=axis
    )


def chips():
    return lax.axis_size("mp") // 2


def line_send(block, step, senders):
    count = chips()
    pairs = []
    for z in senders:
        if 0 <= z < count and 0 <= z + step < count:
            pairs += [(2 * z + c, 2 * (z + step) + c) for c in range(2)]
    return lax.ppermute(block, "mp", pairs)


def core_swap(block):
    return lax.ppermute(block, "mp", [(i, i ^ 1) for i in range(lax.axis_size("mp"))])


def line_gather(block):
    count = chips()
    z = lax.axis_index("mp") // 2
    from_below, from_above = [block], [block]
    for step in range(1, count):
        from_below.append(line_send(from_below[-1], 1, range(step - 1, count)))
        from_above.append(line_send(from_above[-1], -1, range(0, count - step + 1)))
    return [block] + [
        jnp.where(z + k < count, from_above[k], from_below[count - k]) for k in range(1, count)
    ]


def line_scatter(parts):
    count = chips()

    def add(left, right):
        return (left.astype(F32) + right.astype(F32)).astype(LOW)

    up, down = parts[count - 1], parts[1]
    for step in range(1, count):
        up_in = line_send(up, 1, range(0, step))
        down_in = line_send(down, -1, range(count - step, count))
        if step < count - 1:
            up = add(up_in, parts[count - step - 1])
            down = add(down_in, parts[step + 1])
    return (parts[0].astype(F32) + up_in.astype(F32) + down_in.astype(F32)).astype(LOW)


def per_device(
    inputs,
    cotangent,
    short_lengths,
    long_lengths,
    norm1_gain,
    norm1_bias,
    query_weight,
    key_weight,
    value_weight,
    query_kernel,
    key_kernel,
    value_kernel,
    out_weight,
    norm2_gain,
    norm2_bias,
    up_weight,
    down_weight,
):
    rows_here = inputs.shape[1]
    width = inputs.shape[2]
    mp = lax.axis_size("mp")
    dp = lax.axis_size("dp")
    me_dp = lax.axis_index("dp")
    me_mp = lax.axis_index("mp")
    group = rows_here * mp
    hidden_here = up_weight.shape[1]
    share = hidden_here // dp

    joined_own = jnp.concatenate([query_weight, key_weight, value_weight], axis=1)
    joined = lax.all_gather(joined_own, "mp", axis=1, tiled=True)
    out_all = lax.all_gather(out_weight, "mp", axis=0, tiled=True)
    kernels = lax.all_gather(
        jnp.concatenate([query_kernel, key_kernel, value_kernel], axis=1), "mp", axis=1, tiled=True
    )
    up_share = lax.dynamic_slice_in_dim(up_weight, me_dp * share, share, 1)
    down_share = lax.dynamic_slice_in_dim(down_weight, me_dp * share, share, 0)
    up_line = jnp.concatenate(line_gather(up_share), axis=1)
    up_all = jnp.concatenate([up_line, core_swap(up_line)], axis=1)
    down_line = jnp.concatenate(line_gather(down_share), axis=0)
    down_all = jnp.concatenate([down_line, core_swap(down_line)], axis=0)

    starts = [document_starts(short_lengths[0], group), document_starts(long_lengths[0], group)]
    places = jnp.arange(group, dtype=jnp.int32)
    halo = 8
    before = lax.ppermute(
        inputs[:, rows_here - halo :], "mp", [(i, i + 1) for i in range(mp - 1)]
    )
    rows = inputs.astype(F32)
    normed_all = layer_norm(
        jnp.concatenate([before, inputs], axis=1).astype(F32), norm1_gain, norm1_bias
    ).astype(LOW)
    normed = normed_all[:, halo:]

    cot_pieces = []
    for index in range(2):
        first, second = plane_gather(cotangent[index])
        cot_pieces.append(jnp.concatenate(first + second, axis=0))

    saved = []
    for index in range(2):
        offsets = lax.dynamic_slice_in_dim(
            jnp.pad(places - starts[index], (0, halo)), me_mp * rows_here, rows_here + halo, 0
        )[:, None]
        raw = dot(normed_all[index], joined)
        here = offsets[:rows_here]
        mixed = (
            kernels[0] * raw[halo:]
            + jnp.where(here >= 1, kernels[1] * raw[halo - 1 : -1], 0.0)
            + jnp.where(here >= 2, kernels[2] * raw[halo - 2 : -2], 0.0)
        ).astype(LOW)
        by_head = mixed.reshape(rows_here, mp, 3 * HD).transpose(1, 0, 2)
        mixed_head = lax.all_to_all(by_head, "mp", 0, 0, tiled=True).reshape(group, 3 * HD)
        attended_head, wide, total = attend(mixed_head, starts[index])
        attended = (
            lax.all_to_all(attended_head.reshape(mp, rows_here, HD), "mp", 0, 0, tiled=True)
            .transpose(1, 0, 2)
            .reshape(rows_here, mp * HD)
        )
        middle = rows[index] + dot(attended, out_all)
        second_norm = layer_norm(middle, norm2_gain, norm2_bias).astype(LOW)
        one, two = plane_gather(second_norm)
        second_all = jnp.concatenate(one + two, axis=0)
        saved.append(
            dict(offsets=offsets, raw=raw, mixed_head=mixed_head, wide=wide, total=total, attended=attended, middle=middle, second_all=second_all)
        )

    results = []
    hiddens, grad_pres = [], []
    for index in range(2):
        keep = saved[index]
        pre = dot(keep["second_all"], up_all)
        hidden = jnp.square(jnp.maximum(pre, 0.0)).astype(LOW)
        grad_hidden = jnp.einsum(
            "gd,fd->gf", cot_pieces[index], down_all, preferred_element_type=F32
        )
        grad_pre = (grad_hidden * 2.0 * jnp.maximum(pre, 0.0)).astype(LOW)
        grad_second = plane_scatter(
            jnp.einsum("gf,df->gd", grad_pre, up_all, preferred_element_type=F32).astype(LOW)
        )
        feed = plane_scatter(dot(hidden, down_all).astype(LOW))
        results.append((keep["middle"] + feed).astype(LOW))
        keep["grad_second"] = grad_second
        hiddens.append(hidden)
        grad_pres.append(grad_pre)

    hidden_both = jnp.concatenate(hiddens, axis=0)
    grad_pre_both = jnp.concatenate(grad_pres, axis=0)
    second_both = jnp.concatenate([saved[0]["second_all"], saved[1]["second_all"]], axis=0)
    cot_both = jnp.concatenate(cot_pieces, axis=0)
    up_part = jnp.einsum("gd,gf->df", second_both, grad_pre_both, preferred_element_type=F32).astype(LOW)
    down_part = jnp.einsum("gf,gd->fd", hidden_both, cot_both, preferred_element_type=F32).astype(LOW)

    def add_low(left, right):
        return (left.astype(F32) + right.astype(F32)).astype(LOW)

    mine = share * (mp // 2)
    up_sum = add_low(up_part[:, :mine], core_swap(up_part[:, mine:]))
    down_sum = add_low(down_part[:mine], core_swap(down_part[mine:]))
    up_mine = line_scatter([up_sum[:, k * share : (k + 1) * share] for k in range(mp // 2)])
    down_mine = line_scatter([down_sum[k * share : (k + 1) * share] for k in range(mp // 2)])
    up_grad = plane_order(*plane_gather(up_mine), axis=1).astype(F32)
    down_grad = plane_order(*plane_gather(down_mine), axis=0).astype(F32)

    out_acc = jnp.zeros((mp * HD, width), F32)
    joined_acc = jnp.zeros(joined.shape, F32)
    kernel_acc = jnp.zeros(kernels.shape, F32)
    norm_acc = [jnp.zeros(norm1_gain.shape, F32) for _ in range(4)]
    input_grads = []
    for index in range(2):
        keep = saved[index]
        unused, pull_two = jax.vjp(layer_norm, keep["middle"], norm2_gain, norm2_bias)
        grad_middle, grad_gain_two, grad_shift_two = pull_two(keep["grad_second"])
        grad_middle = grad_middle + cotangent[index].astype(F32)
        branch = grad_middle.astype(LOW)
        out_acc = out_acc + jnp.einsum(
            "gh,gd->hd", keep["attended"], branch, preferred_element_type=F32
        )
        grad_attended = jnp.einsum(
            "gd,hd->gh", branch, out_all, preferred_element_type=F32
        ).astype(LOW)
        grad_head = lax.all_to_all(
            grad_attended.reshape(rows_here, mp, HD).transpose(1, 0, 2), "mp", 0, 0, tiled=True
        ).reshape(group, HD)
        grad_mixed_head = attend_back(
            keep["mixed_head"], grad_head, keep["wide"], keep["total"], starts[index]
        )
        padded = jnp.pad(grad_mixed_head, ((0, halo), (0, 0)))
        with_halo = jnp.stack(
            [padded[i * rows_here : (i + 1) * rows_here + halo] for i in range(mp)], axis=0
        )
        grad_mixed = (
            lax.all_to_all(with_halo, "mp", 0, 0, tiled=True)
            .transpose(1, 0, 2)
            .reshape(rows_here + halo, mp * 3 * HD)
            .astype(F32)
        )
        offsets, raw = keep["offsets"], keep["raw"]
        here = grad_mixed[:rows_here]
        after_one = jnp.where(offsets[1 : rows_here + 1] >= 1, grad_mixed[1 : rows_here + 1], 0.0)
        after_two = jnp.where(offsets[2 : rows_here + 2] >= 2, grad_mixed[2 : rows_here + 2], 0.0)
        grad_raw = (kernels[0] * here + kernels[1] * after_one + kernels[2] * after_two).astype(LOW)
        own_one = jnp.where(offsets[:rows_here] >= 1, here, 0.0)
        own_two = jnp.where(offsets[:rows_here] >= 2, here, 0.0)
        kernel_acc = kernel_acc + jnp.stack(
            [
                jnp.sum(here * raw[halo:], axis=0),
                jnp.sum(own_one * raw[halo - 1 : -1], axis=0),
                jnp.sum(own_two * raw[halo - 2 : -2], axis=0),
            ],
            axis=0,
        )
        joined_acc = joined_acc + jnp.einsum(
            "gd,gc->dc", normed[index], grad_raw, preferred_element_type=F32
        )
        grad_normed = jnp.einsum("gc,dc->gd", grad_raw, joined, preferred_element_type=F32)
        unused_one, pull_one = jax.vjp(layer_norm, rows[index], norm1_gain, norm1_bias)
        grad_input, grad_gain_one, grad_shift_one = pull_one(grad_normed)
        input_grads.append(grad_middle + grad_input)
        norm_acc = [
            norm_acc[0] + grad_gain_one,
            norm_acc[1] + grad_shift_one,
            norm_acc[2] + grad_gain_two,
            norm_acc[3] + grad_shift_two,
        ]
    joined_grad = lax.psum(
        lax.psum_scatter(joined_acc.astype(LOW), "mp", scatter_dimension=1, tiled=True), "dp"
    ).astype(F32)
    out_grad = lax.psum(
        lax.psum_scatter(out_acc.astype(LOW), "mp", scatter_dimension=0, tiled=True), "dp"
    ).astype(F32)
    kernel_sum, norm_totals = lax.psum((kernel_acc, jnp.stack(norm_acc, axis=0)), ("dp", "mp"))
    kernel_grad = lax.dynamic_slice_in_dim(kernel_sum, me_mp * 3 * HD, 3 * HD, 1)
    return (
        jnp.stack(results, axis=0),
        jnp.stack(input_grads, axis=0),
        norm_totals[0],
        norm_totals[1],
        joined_grad[:, :HD],
        joined_grad[:, HD : 2 * HD],
        joined_grad[:, 2 * HD :],
        kernel_grad[:, :HD],
        kernel_grad[:, HD : 2 * HD],
        kernel_grad[:, 2 * HD :],
        out_grad,
        norm_totals[2],
        norm_totals[3],
        up_grad,
        down_grad,
    )


def solution(mesh):
    return jax.shard_map(
        per_device,
        mesh=mesh,
        in_specs=(
            P(None, ("dp", "mp"), None),
            P(None, ("dp", "mp"), None),
            P("dp", None),
            P("dp", None),
            P(),
            P(),
            P(None, "mp"),
            P(None, "mp"),
            P(None, "mp"),
            P(None, "mp"),
            P(None, "mp"),
            P(None, "mp"),
            P("mp", None),
            P(),
            P(),
            P(None, "mp"),
            P("mp", None),
        ),
        out_specs=(
            P(None, ("dp", "mp"), None),
            P(None, ("dp", "mp"), None),
            P(),
            P(),
            P(None, "mp"),
            P(None, "mp"),
            P(None, "mp"),
            P(None, "mp"),
            P(None, "mp"),
            P(None, "mp"),
            P("mp", None),
            P(),
            P(),
            P(None, "mp"),
            P("mp", None),
        ),
        check_vma=False,
    )
```

```python
from functools import partial

import jax
import jax.numpy as jnp
from jax import lax
from jax.experimental import pallas as pl
from jax.experimental.pallas import tpu as pltpu
from jax.sharding import PartitionSpec as P

HD = 64
BLOCK = 256
CHUNK = 512
VMEM_LIMIT = 62 * 1024 * 1024
MESH = pl.DeviceIdType.MESH
LOW = jnp.bfloat16
F32 = jnp.float32


def dot(left, right):
    return jnp.dot(left, right, preferred_element_type=F32)


def layer_norm(rows, gain, shift):
    row_mean = jnp.mean(rows, axis=-1, keepdims=True)
    centered = rows - row_mean
    variance = jnp.mean(centered * centered, axis=-1, keepdims=True)
    return centered * lax.rsqrt(variance + 1e-05) * gain + shift


def document_starts(lengths, count):
    ends = jnp.cumsum(lengths)
    places = jnp.arange(count, dtype=jnp.int32)
    passed = (places[:, None] >= ends[None, :]).astype(jnp.int32)
    return jnp.sum(passed * lengths[None, :], axis=1)


def allowed_pairs(start_row, key_block, query_block):
    keys = key_block * BLOCK + lax.broadcasted_iota(jnp.int32, (BLOCK, BLOCK), 0)
    queries = query_block * BLOCK + lax.broadcasted_iota(jnp.int32, (BLOCK, BLOCK), 1)
    return (keys <= queries) & (keys >= start_row)


def attend_kernel(
    first_ref, start_ref, qk_ref, v_ref, out_ref, wide_ref, total_ref, values_t
):
    s, step = pl.program_id(0), pl.program_id(1)

    @pl.when(step == 0)
    def _():
        def turn(at, carry):
            rows = pl.ds(pl.multiple_of(at * BLOCK, BLOCK), BLOCK)
            both = v_ref[0, rows, :].T
            values_t[at] = jnp.where(s == 0, both[:HD], both[HD:])
            return carry

        lax.fori_loop(0, values_t.shape[0], turn, 0)

    here = pl.ds(pl.multiple_of(step * BLOCK, BLOCK), BLOCK)
    query_t = (qk_ref[0, here, 0:HD] * HD ** (-0.5)).astype(LOW).T
    start_row = start_ref[0]

    def one(at, carry):
        top, summed, acc = carry
        rows = pl.ds(pl.multiple_of(at * BLOCK, BLOCK), BLOCK)
        scores = dot(qk_ref[0, rows, HD : 2 * HD], query_t)
        scores = jnp.where(allowed_pairs(start_row, at, step), scores, -1e30)
        new_top = jnp.maximum(top, jnp.max(scores, axis=0, keepdims=True))
        powered = jnp.exp(scores - new_top)
        shrink = jnp.exp(top - new_top)
        summed = summed * shrink + jnp.sum(powered, axis=0, keepdims=True)
        acc = acc * shrink + dot(values_t[at], powered.astype(LOW))
        return new_top, summed, acc

    top, summed, acc = lax.fori_loop(
        first_ref[s, step],
        step + 1,
        one,
        (
            jnp.full((1, BLOCK), -1e30, F32),
            jnp.zeros((1, BLOCK), F32),
            jnp.zeros((HD, BLOCK), F32),
        ),
    )
    result = acc / summed
    wide_ref[0] = result
    total_ref[0] = top + jnp.log(summed)
    low = result.T.astype(LOW)

    @pl.when(s == 0)
    def _():
        out_ref[0, here, 0:HD] = low

    @pl.when(s == 1)
    def _():
        out_ref[0, here, HD : 2 * HD] = low


def attend(mixed, starts):
    group = mixed.shape[1]
    steps = group // BLOCK
    row = pl.BlockSpec((1, 1, BLOCK), lambda s, i, first: (s, 0, i))
    return pl.pallas_call(
        attend_kernel,
        grid_spec=pltpu.PrefetchScalarGridSpec(
            num_scalar_prefetch=1,
            grid=(2, steps),
            in_specs=[
                row,
                pl.BlockSpec((1, group, 2 * HD), lambda s, i, first: (s, 0, 0)),
                pl.BlockSpec((1, group, 2 * HD), lambda s, i, first: (2, 0, 0)),
            ],
            out_specs=[
                pl.BlockSpec((1, group, 2 * HD), lambda s, i, first: (0, 0, 0)),
                pl.BlockSpec((1, HD, BLOCK), lambda s, i, first: (s, 0, i)),
                row,
            ],
            scratch_shapes=[pltpu.VMEM((steps, HD, BLOCK), LOW)],
        ),
        out_shape=[
            jax.ShapeDtypeStruct((1, group, 2 * HD), LOW),
            jax.ShapeDtypeStruct((2, HD, group), F32),
            jax.ShapeDtypeStruct((2, 1, group), F32),
        ],
        compiler_params=pltpu.CompilerParams(vmem_limit_bytes=32 * 1024 * 1024),
        cost_estimate=pl.CostEstimate(
            flops=2**34, bytes_accessed=group * 2048, transcendentals=group * group // 4
        ),
        name="attend",
    )(starts[:, ::BLOCK] // BLOCK, starts[:, None, :], mixed, mixed)


def attend_back_kernel(
    first_ref, start_ref, qk_ref, v_ref, grad_ref, wide_ref, total_ref, out_ref,
    keys_t, values, grad_keys, grad_values,
):
    s, step = pl.program_id(0), pl.program_id(1)
    group = qk_ref.shape[1]

    @pl.when(step == 0)
    def _():
        def turn(at, carry):
            rows = pl.ds(pl.multiple_of(at * BLOCK, BLOCK), BLOCK)
            keys_t[at] = qk_ref[0, rows, HD : 2 * HD].T
            both = v_ref[0, rows, :]
            values[rows, :] = jnp.where(s == 0, both[:, :HD], both[:, HD:])
            return carry

        lax.fori_loop(0, keys_t.shape[0], turn, 0)
        grad_keys[...] = jnp.zeros(grad_keys.shape, F32)
        grad_values[...] = jnp.zeros(grad_values.shape, F32)

    here = pl.ds(pl.multiple_of(step * BLOCK, BLOCK), BLOCK)
    query = (qk_ref[0, here, 0:HD] * HD ** (-0.5)).astype(LOW)
    query_t = query.T
    both = grad_ref[0]
    grad = jnp.where(s == 0, both[:, :HD], both[:, HD:])
    grad_t = grad.T
    start_row = start_ref[0]
    total = total_ref[0]
    inner = jnp.sum(grad_t.astype(F32) * wide_ref[0], axis=0, keepdims=True)

    def one(at, acc):
        rows = pl.ds(pl.multiple_of(at * BLOCK, BLOCK), BLOCK)
        scores = dot(qk_ref[0, rows, HD : 2 * HD], query_t)
        scores = jnp.where(allowed_pairs(start_row, at, step), scores, -1e30)
        probs = jnp.exp(scores - total)
        grad_probs = dot(values[rows, :], grad_t)
        grad_scores = (probs * (grad_probs - inner)).astype(LOW)
        grad_values[rows, :] += dot(probs.astype(LOW), grad)
        grad_keys[rows, :] += dot(grad_scores, query)
        return acc + dot(keys_t[at], grad_scores)

    acc = lax.fori_loop(first_ref[s, step], step + 1, one, jnp.zeros((HD, BLOCK), F32))
    out_ref[s, here, 0:HD] = (acc * HD ** (-0.5)).T.astype(out_ref.dtype)

    @pl.when(step == pl.num_programs(1) - 1)
    def _():
        out_ref[s, 0:group, HD : 2 * HD] = grad_keys[...].astype(out_ref.dtype)
        out_ref[s, group:, :] = jnp.zeros((out_ref.shape[1] - group, 2 * HD), out_ref.dtype)

        @pl.when(s == 0)
        def _():
            out_ref[2, 0:group, 0:HD] = grad_values[...].astype(out_ref.dtype)

        @pl.when(s == 1)
        def _():
            out_ref[2, 0:group, HD : 2 * HD] = grad_values[...].astype(out_ref.dtype)
            out_ref[2, group:, :] = jnp.zeros((out_ref.shape[1] - group, 2 * HD), out_ref.dtype)


def attend_back(mixed, grad, wide, total, starts, halo):
    group = mixed.shape[1]
    steps = group // BLOCK
    row = pl.BlockSpec((1, 1, BLOCK), lambda s, i, first: (s, 0, i))
    return pl.pallas_call(
        attend_back_kernel,
        grid_spec=pltpu.PrefetchScalarGridSpec(
            num_scalar_prefetch=1,
            grid=(2, steps),
            in_specs=[
                row,
                pl.BlockSpec((1, group, 2 * HD), lambda s, i, first: (s, 0, 0)),
                pl.BlockSpec((1, group, 2 * HD), lambda s, i, first: (2, 0, 0)),
                pl.BlockSpec((1, BLOCK, 2 * HD), lambda s, i, first: (0, i, 0)),
                pl.BlockSpec((1, HD, BLOCK), lambda s, i, first: (s, 0, i)),
                row,
            ],
            out_specs=pl.BlockSpec((3, group + halo, 2 * HD), lambda s, i, first: (0, 0, 0)),
            scratch_shapes=[
                pltpu.VMEM((steps, HD, BLOCK), LOW),
                pltpu.VMEM((group, HD), LOW),
                pltpu.VMEM((group, HD), F32),
                pltpu.VMEM((group, HD), F32),
            ],
        ),
        out_shape=jax.ShapeDtypeStruct((3, group + halo, 2 * HD), LOW),
        compiler_params=pltpu.CompilerParams(vmem_limit_bytes=32 * 1024 * 1024),
        cost_estimate=pl.CostEstimate(
            flops=2**35, bytes_accessed=group * 2048, transcendentals=group * group // 4
        ),
        name="attend_back",
    )(starts[:, ::BLOCK] // BLOCK, starts[:, None, :], mixed, mixed, grad, wide, total)


def plane_partners():
    me = lax.axis_index("dp")
    return {"dp": me + 1 - 2 * lax.rem(me, 2)}, {"dp": me + 2 - 4 * (me // 2)}


def dot_nt(left, right):
    return lax.dot_general(left, right, (((1,), (1,)), ((), ())), preferred_element_type=F32)


def mesh_place():
    me = lax.axis_index("mp")
    return me // 2, lax.rem(me, 2)


def wire(source, target, send, recv, partner):
    return pltpu.make_async_remote_copy(
        src_ref=source,
        dst_ref=target,
        send_sem=send,
        recv_sem=recv,
        device_id=partner,
        device_id_type=MESH,
    )


def line_partner(z, step):
    _, core = mesh_place()
    return {"mp": 2 * (z + step) + core}


def other_core():
    z, core = mesh_place()
    return {"mp": 2 * z + 1 - core}


def greet(partners):
    barrier = pltpu.get_barrier_semaphore()
    for partner in partners:
        pl.semaphore_signal(barrier, inc=1, device_id=partner, device_id_type=MESH)
    pl.semaphore_wait(barrier, len(partners))


def greet_line(with_plane):
    z, _ = mesh_place()
    count = lax.axis_size("mp") // 2
    barrier = pltpu.get_barrier_semaphore()
    partners = [other_core()]
    if with_plane:
        partners += list(plane_partners())
    for partner in partners:
        pl.semaphore_signal(barrier, inc=1, device_id=partner, device_id_type=MESH)
    for turn in (1, -1):

        @pl.when((z + turn >= 0) & (z + turn < count))
        def _(turn=turn):
            pl.semaphore_signal(barrier, inc=1, device_id=line_partner(z, turn), device_id_type=MESH)

    near = jnp.where(z > 0, 1, 0) + jnp.where(z < count - 1, 1, 0)
    pl.semaphore_wait(barrier, near + len(partners))


class LineGather:
    def __init__(self, place, send, recv, swap_send, swap_recv):
        self.z, self.core = mesh_place()
        self.count = lax.axis_size("mp") // 2
        self.place, self.send, self.recv = place, send, recv
        self.swap_send, self.swap_recv = swap_send, swap_recv

    def copies(self, step):
        z, count = self.z, self.count
        out = []
        for way, turn in enumerate((1, -1)):
            leaves = z - turn * (step - 1)
            lands = z - turn * step
            far = z + turn
            sends = (leaves >= 0) & (leaves < count) & (far >= 0) & (far < count)
            receives = (lands >= 0) & (lands < count)
            at = jnp.clip(leaves, 0, count - 1)
            to = jnp.clip(lands, 0, count - 1)
            sems = (self.send.at[way, step - 1], self.recv.at[way, step - 1], line_partner(z, turn))
            leaving = wire(self.place(at, self.core), self.place(at, self.core), *sems)
            landing = wire(self.place(to, self.core), self.place(to, self.core), *sems)
            out.append((sends, leaving, receives, landing, to))
        return out

    def start(self, step):
        for sends, leaving, _, _, _ in self.copies(step):
            pl.when(sends)(leaving.start)

    def swap(self, at, number):
        sems = (self.swap_send.at[number], self.swap_recv.at[number], other_core())
        leaving = wire(self.place(at, self.core), self.place(at, self.core), *sems)
        landing = wire(self.place(at, 1 - self.core), self.place(at, 1 - self.core), *sems)
        return leaving, landing

    def swap_own(self):
        self.swap(self.z, 0)[0].start()

    def arrive(self, step):
        for way, (_, _, receives, landing, at) in enumerate(self.copies(step)):

            @pl.when(receives)
            def _(landing=landing, at=at, way=way):
                landing.wait_recv()
                self.swap(at, 1 + 2 * (step - 1) + way)[0].start()

    def swapped(self, at, number):
        leaving, landing = self.swap(at, number)
        leaving.wait_send()
        landing.wait_recv()

    def finish(self, steps, own):
        if own:
            self.swapped(self.z, 0)
        for step in steps:
            for way, (sends, leaving, receives, _, at) in enumerate(self.copies(step)):
                pl.when(sends)(leaving.wait_send)
                pl.when(receives)(
                    lambda at=at, way=way, step=step: self.swapped(at, 1 + 2 * (step - 1) + way)
                )


def line_semaphores(count):
    return [
        pltpu.SemaphoreType.DMA((2, count)),
        pltpu.SemaphoreType.DMA((2, count)),
        pltpu.SemaphoreType.DMA((2 * count,)),
        pltpu.SemaphoreType.DMA((2 * count,)),
    ]


def early_steps(count):
    return range(1, count // 2 + 1)


def prepare_kernel(
    inputs_ref, gain_ref, shift_ref, qk_ref, v_ref, out_ref, taps_ref, up_ref,
    all_qk_ref, all_v_ref, all_out_ref, all_taps_ref, normed_ref, halo_ref, up_all_ref,
    rows, normed, local, *sems,
):
    mp = lax.axis_size("mp")
    dp = lax.axis_index("dp")
    me = lax.axis_index("mp")
    z, core = mesh_place()
    count = mp // 2
    rows_here, depth = rows.shape[1:]
    to_x, to_y = plane_partners()
    share = up_ref.shape[0]
    owned = (qk_ref, v_ref, out_ref)
    whole = (all_qk_ref, all_v_ref, all_out_ref)
    (plane_send_sem, plane_recv_sem, plane_swap_send, plane_swap_recv) = sems[:4]
    taps_send, taps_recv, halo_send, halo_recv = sems[4:8]
    line_sems = [sems[8 + 4 * part : 12 + 4 * part] for part in range(4)]

    def up_place(at, at_core):
        start = pl.multiple_of((at_core * count + at) * share, 16)
        return up_all_ref.at[pl.ds(start, share), :]

    loads = [
        pltpu.make_async_copy(inputs_ref, rows, local.at[0]),
        pltpu.make_async_copy(taps_ref, all_taps_ref.at[me], local.at[1]),
        pltpu.make_async_copy(up_ref, up_place(z, core), local.at[2]),
    ] + [
        pltpu.make_async_copy(
            owned[part].at[dp], whole[part].at[z, core, dp], local.at[3 + part]
        )
        for part in range(3)
    ]
    for copy in loads:
        copy.start()

    barrier = pltpu.get_barrier_semaphore()
    for step in range(1, mp):
        pl.semaphore_signal(
            barrier, inc=1, device_id={"mp": lax.rem(me + step, mp)}, device_id_type=MESH
        )
    for partner in (to_x, to_y):
        pl.semaphore_signal(barrier, inc=1, device_id=partner, device_id_type=MESH)
    pl.semaphore_wait(barrier, mp + 1)
    for copy in loads[1:]:
        copy.wait()

    lines = [
        LineGather(lambda at, at_core, part=part: whole[part].at[at, at_core, dp], *line_sems[part])
        for part in range(3)
    ]
    up_line = LineGather(up_place, *line_sems[3])
    for line in lines:
        line.start(1)
    tap_copies = [
        (
            wire(
                taps_ref, all_taps_ref.at[me], taps_send.at[step], taps_recv.at[step],
                {"mp": lax.rem(me + step, mp)},
            ),
            wire(
                taps_ref, all_taps_ref.at[lax.rem(me + mp - step, mp)], taps_send.at[step],
                taps_recv.at[step], {"mp": lax.rem(me + step, mp)},
            ),
        )
        for step in range(1, mp)
    ]
    for copy, _ in tap_copies:
        copy.start()
    for line in lines:
        line.swap_own()

    loads[0].wait()
    tall = 16

    def norm(s):
        def some(at, carry):
            here = pl.ds(pl.multiple_of(at * tall, tall), tall)
            values = rows[s, here, :].astype(F32)
            centered = values - jnp.mean(values, axis=1, keepdims=True)
            variance = jnp.mean(centered * centered, axis=1, keepdims=True)
            normed[s, here, :] = (
                centered * lax.rsqrt(variance + 1e-05) * gain_ref[...] + shift_ref[...]
            ).astype(LOW)
            return carry

        lax.fori_loop(0, rows_here // tall, some, 0)

    norm(0)
    for step in range(1, count):
        for line in lines:
            line.arrive(step)
        if step + 1 < count:
            for line in lines:
                line.start(step + 1)

    half = depth // 2
    lanes = (pl.ds(0, half), pl.ds(half, half))
    dp_x = dp + 1 - 2 * lax.rem(dp, 2)
    dp_y = dp + 2 - 4 * (dp // 2)
    dp_xy = dp_x + 2 - 4 * (dp_x // 2)
    legs = ((0, to_x), (1, to_y), (0, to_y), (1, to_x), (0, to_y), (1, to_x))

    def plane(number, quarter):
        side, partner = legs[number]
        out = []
        for part in range(3):
            block = whole[part].at[:, core, quarter, :, lanes[side]]
            out.append(
                wire(
                    block, block, plane_send_sem.at[part, number], plane_recv_sem.at[part, number], partner
                )
            )
        return out

    leaving = [plane(number, quarter) for number, quarter in enumerate((dp, dp, dp, dp, dp_x, dp_y))]
    landing = [
        plane(number, quarter) for number, quarter in enumerate((dp_x, dp_y, dp_y, dp_x, dp_xy, dp_xy))
    ]

    def pass_on(number, at_core):
        quarter = (dp_x, dp_y, dp_xy)[number]
        out = []
        for part in range(3):
            block = whole[part].at[:, at_core, quarter]
            out.append(
                wire(
                    block, block, plane_swap_send.at[part, number], plane_swap_recv.at[part, number],
                    other_core(),
                )
            )
        return out

    def each(copies, what):
        for copy in copies:
            getattr(copy, what)()

    for number in range(4):
        each(leaving[number], "start")
    up_line.start(1)
    up_line.swap_own()
    norm(1)
    save = pltpu.make_async_copy(normed, normed_ref, local.at[0])
    save.start()
    halo = halo_ref.shape[1]
    halo_copy = wire(
        normed.at[:, pl.ds(rows_here - halo, halo), :], halo_ref, halo_send, halo_recv,
        {"mp": lax.rem(me + 1, mp)},
    )
    halo_copy.start()
    each(landing[0], "wait_recv")
    each(leaving[4], "start")
    each(landing[1], "wait_recv")
    each(leaving[5], "start")
    early = early_steps(count)
    up_line.arrive(1)
    up_line.start(2)
    each(landing[3], "wait_recv")
    each(pass_on(0, core), "start")
    each(landing[2], "wait_recv")
    each(pass_on(1, core), "start")
    each(landing[4], "wait_recv")
    each(landing[5], "wait_recv")
    each(pass_on(2, core), "start")
    for step in early[1:]:
        up_line.arrive(step)
        if step != early[-1]:
            up_line.start(step + 1)
    for line in lines:
        line.finish(range(1, count), True)
    up_line.finish(early, True)
    for number in range(6):
        each(leaving[number], "wait_send")
    for number in range(3):
        each(pass_on(number, core), "wait_send")
        each(pass_on(number, 1 - core), "wait_recv")
    for copy, landed in tap_copies:
        copy.wait_send()
        landed.wait_recv()
    halo_copy.wait()
    save.wait()


HALO = 16


def prepare(inputs, gain, shift, qk, v, out, taps, up):
    mp = lax.axis_size("mp")
    count = mp // 2
    rows_here, depth = inputs.shape[1:]
    anywhere = pl.BlockSpec(memory_space=pl.ANY)
    vmem = pl.BlockSpec(memory_space=pltpu.VMEM)
    dma = pltpu.SemaphoreType.DMA
    return pl.pallas_call(
        prepare_kernel,
        in_specs=[anywhere, vmem, vmem] + [anywhere] * 5,
        out_specs=[anywhere] * 7,
        out_shape=[
            jax.ShapeDtypeStruct((count, 2) + qk.shape, LOW),
            jax.ShapeDtypeStruct((count, 2) + v.shape, LOW),
            jax.ShapeDtypeStruct((count, 2) + out.shape, LOW),
            jax.ShapeDtypeStruct((mp,) + taps.shape, F32),
            jax.ShapeDtypeStruct(inputs.shape, LOW),
            jax.ShapeDtypeStruct((2, HALO, depth), LOW),
            jax.ShapeDtypeStruct((mp * up.shape[0], depth), LOW),
        ],
        scratch_shapes=[
            pltpu.VMEM(inputs.shape, LOW),
            pltpu.VMEM(inputs.shape, LOW),
            dma((6,)),
            dma((3, 6)),
            dma((3, 6)),
            dma((3, 3)),
            dma((3, 3)),
            dma((mp,)),
            dma((mp,)),
            dma,
            dma,
        ]
        + line_semaphores(count) * 4,
        compiler_params=pltpu.CompilerParams(
            collective_id=3, has_side_effects=True, vmem_limit_bytes=32 * 2**20
        ),
        cost_estimate=pl.CostEstimate(flops=2**36, bytes_accessed=2**26, transcendentals=0),
        name="prepare",
    )(inputs, gain.reshape(1, depth), shift.reshape(1, depth), qk, v, out, taps, up)


def exchange_kernel(halo, x_ref, o_ref, local, send, recv):
    mp = lax.axis_size("mp")
    me = lax.axis_index("mp")
    if halo is None:

        def source(at):
            return x_ref.at[:, :, pl.ds(pl.multiple_of(at * 128, 128), 128)]

        def target(at):
            return o_ref.at[:, at]
    else:
        tall = o_ref.shape[1]

        def source(at):
            return x_ref.at[:, pl.ds(pl.multiple_of(at * (tall - halo), 16), tall), :]

        def target(at):
            return o_ref.at[:, :, pl.ds(pl.multiple_of(at * 128, 128), 128)]

    barrier = pltpu.get_barrier_semaphore()
    for step in range(1, mp):
        pl.semaphore_signal(
            barrier, inc=1, device_id={"mp": lax.rem(me + step, mp)}, device_id_type=MESH
        )
    own = pltpu.make_async_copy(source(me), target(me), local)
    own.start()
    pl.semaphore_wait(barrier, mp - 1)
    copies = []
    for step in range(1, mp):
        to = lax.rem(me + step, mp)
        sems = (send.at[step], recv.at[step], {"mp": to})
        leaving = wire(source(to), target(me), *sems)
        landing = wire(source(to), target(lax.rem(me + mp - step, mp)), *sems)
        leaving.start()
        copies.append((leaving, landing))
    own.wait()
    for leaving, landing in copies:
        leaving.wait_send()
        landing.wait_recv()


def exchange(x, shape, halo, number, name):
    mp = lax.axis_size("mp")
    anywhere = pl.BlockSpec(memory_space=pl.ANY)
    return pl.pallas_call(
        partial(exchange_kernel, halo),
        in_specs=[anywhere],
        out_specs=anywhere,
        out_shape=jax.ShapeDtypeStruct(shape, x.dtype),
        scratch_shapes=[
            pltpu.SemaphoreType.DMA,
            pltpu.SemaphoreType.DMA((mp,)),
            pltpu.SemaphoreType.DMA((mp,)),
        ],
        compiler_params=pltpu.CompilerParams(collective_id=number, has_side_effects=True),
        cost_estimate=pl.CostEstimate(flops=2**34, bytes_accessed=2**24, transcendentals=0),
        name=name,
    )(x)


def heads_out(x, number, name):
    parts, rows_here, width = x.shape
    mp = lax.axis_size("mp")
    out = exchange(x, (parts, mp, rows_here, 128), None, number, name)
    return out.reshape(parts, mp * rows_here, 128)


def heads_back(x, rows_here, halo, number, name):
    mp = lax.axis_size("mp")
    return exchange(x, (x.shape[0], rows_here + halo, mp * 128), halo, number, name)


def feed_in_kernel(
    second_ref, up_ref, down_ref, all_ref, relu_ref, hidden_ref, down_all_ref, up_all_ref,
    rows, up, relu, hidden, local, outs, send, recv, *line_sems,
):
    depth = rows.shape[3]
    units = up.shape[0]
    share = down_ref.shape[0]
    count = lax.axis_size("mp") // 2
    z, core = mesh_place()
    lanes = (pl.ds(0, depth // 2), pl.ds(depth // 2, depth // 2))
    to_x, to_y = plane_partners()

    def line_place(ref):
        return lambda at, at_core: ref.at[
            pl.ds(pl.multiple_of((at_core * count + at) * share, 16), share), :
        ]

    own = [pltpu.make_async_copy(second_ref.at[s], rows.at[s, 0], local.at[s]) for s in range(2)]
    own.append(pltpu.make_async_copy(up_ref, up, local.at[2]))
    own.append(pltpu.make_async_copy(down_ref, line_place(down_all_ref)(z, core), local.at[4]))
    for copy in own:
        copy.start()
    for copy in own:
        copy.wait()
    greet_line(True)
    up_line = LineGather(line_place(up), *line_sems[:4])
    down_line = LineGather(line_place(down_all_ref), *line_sems[4:])

    def remote(s, source, target, half, partner, number):
        return wire(
            rows.at[s, source, :, lanes[half]], rows.at[s, target, :, lanes[half]],
            send.at[s, number], recv.at[s, number], partner,
        )

    copies = [
        [
            remote(s, 0, 1, 0, to_x, 0),
            remote(s, 0, 2, 1, to_y, 1),
            remote(s, 0, 2, 0, to_y, 2),
            remote(s, 0, 1, 1, to_x, 3),
            remote(s, 1, 3, 0, to_y, 4),
            remote(s, 2, 3, 1, to_x, 5),
        ]
        for s in range(2)
    ]
    pending = [None, None]
    done = [0]

    def tile(s, m):
        slot = done[0] % 2
        done[0] += 1
        if pending[slot] is not None:
            for copy in pending[slot]:
                copy.wait()

        def one(at, carry):
            columns = pl.ds(pl.multiple_of(at * CHUNK, CHUNK), CHUNK)
            kept = jnp.maximum(dot_nt(rows[s, m], up[columns, :]), 0.0)
            relu[slot, :, columns] = kept
            hidden[slot, :, columns] = (kept * kept).astype(LOW)
            return carry

        lax.fori_loop(0, units // CHUNK, one, 0)
        pending[slot] = [
            pltpu.make_async_copy(relu.at[slot], relu_ref.at[s, m], outs.at[slot, 0]),
            pltpu.make_async_copy(hidden.at[slot], hidden_ref.at[s, m], outs.at[slot, 1]),
        ]
        for copy in pending[slot]:
            copy.start()

    for number in range(4):
        copies[0][number].start()
    late = range(early_steps(count)[-1] + 1, count)
    for step in late:
        up_line.start(step)
        if step != late[-1]:
            up_line.arrive(step)
    copies[0][0].wait_recv()
    copies[0][4].start()
    copies[0][1].wait_recv()
    copies[0][5].start()
    copies[1][0].start()
    copies[1][1].start()
    up_line.arrive(late[-1])
    down_line.start(1)
    down_line.swap_own()
    up_line.finish(late, False)
    whole_up = pltpu.make_async_copy(up, up_all_ref, local.at[0])
    whole_up.start()
    tile(0, 0)
    tile(1, 0)
    copies[0][3].wait_recv()
    tile(0, 1)
    copies[0][2].wait_recv()
    copies[1][2].start()
    copies[1][3].start()
    tile(0, 2)
    down_line.arrive(1)
    down_line.start(2)
    copies[1][0].wait_recv()
    copies[1][4].start()
    copies[1][1].wait_recv()
    copies[1][5].start()
    copies[0][4].wait_recv()
    copies[0][5].wait_recv()
    tile(0, 3)
    down_line.arrive(2)
    for step in range(3, count):
        down_line.start(step)
        if step != count - 1:
            down_line.arrive(step)
    copies[1][3].wait_recv()
    tile(1, 1)
    copies[1][2].wait_recv()
    tile(1, 2)
    copies[1][4].wait_recv()
    copies[1][5].wait_recv()
    gathered = pltpu.make_async_copy(rows, all_ref, local.at[3])
    gathered.start()
    tile(1, 3)
    down_line.arrive(count - 1)
    down_line.finish(range(1, count), True)
    for slot in pending:
        for copy in slot:
            copy.wait()
    for s in range(2):
        for copy in copies[s]:
            copy.wait_send()
    gathered.wait()
    whole_up.wait()


def feed_in(second, up_all, down):
    rows_here, depth = second.shape[1:]
    units = up_all.shape[0]
    count = lax.axis_size("mp") // 2
    anywhere = pl.BlockSpec(memory_space=pl.ANY)
    return pl.pallas_call(
        feed_in_kernel,
        in_specs=[anywhere] * 3,
        out_specs=[anywhere] * 5,
        out_shape=[
            jax.ShapeDtypeStruct((2, 4, rows_here, depth), LOW),
            jax.ShapeDtypeStruct((2, 4, rows_here, units), F32),
            jax.ShapeDtypeStruct((2, 4, rows_here, units), LOW),
            jax.ShapeDtypeStruct((units, depth), LOW),
            jax.ShapeDtypeStruct((units, depth), LOW),
        ],
        scratch_shapes=[
            pltpu.VMEM((2, 4, rows_here, depth), LOW),
            pltpu.VMEM((units, depth), LOW),
            pltpu.VMEM((2, rows_here, units), F32),
            pltpu.VMEM((2, rows_here, units), LOW),
            pltpu.SemaphoreType.DMA((5,)),
            pltpu.SemaphoreType.DMA((2, 2)),
            pltpu.SemaphoreType.DMA((2, 6)),
            pltpu.SemaphoreType.DMA((2, 6)),
        ]
        + line_semaphores(count) * 2,
        compiler_params=pltpu.CompilerParams(
            collective_id=1, has_side_effects=True, vmem_limit_bytes=VMEM_LIMIT
        ),
        cost_estimate=pl.CostEstimate(
            flops=2 * 8 * rows_here * depth * units * 3,
            bytes_accessed=60 * 2**20,
            transcendentals=0,
        ),
        name="feed_in",
    )(second, up_all, down)


def feed_out_kernel(
    cot_ref, relu_ref, hidden_ref, up_ref, down_ref, grad_ref, feed_ref, back_ref,
    up, down, cot, relu, grad, part, arrived, feed, result, local, loads, outs, send, recv,
):
    units, depth = up.shape
    half = depth // 2
    lanes = (pl.ds(0, half), pl.ds(half, half))
    to_x, to_y = plane_partners()
    weights = [
        pltpu.make_async_copy(down_ref, down, local.at[0]),
        pltpu.make_async_copy(up_ref, up, local.at[1]),
    ]
    order = [(s, m) for s in range(2) for m in (3, 1, 2, 0)]

    def load(at):
        s, m = order[at]
        slot = at % 2
        return [
            pltpu.make_async_copy(cot_ref.at[s, m], cot.at[slot], loads.at[slot, 0]),
            pltpu.make_async_copy(relu_ref.at[s, m], relu.at[slot], loads.at[slot, 1]),
        ]

    for copy in load(0) + weights:
        copy.start()
    greet([to_x, to_y])
    for copy in weights:
        copy.wait()

    def remote(s, source, number, side, partner):
        return pltpu.make_async_remote_copy(
            src_ref=part.at[s, source, :, lanes[side]],
            dst_ref=arrived.at[s, number],
            send_sem=send.at[s, number],
            recv_sem=recv.at[s, number],
            device_id=partner,
            device_id_type=MESH,
        )

    copies = [
        [
            remote(s, 1, 0, 0, to_x),
            remote(s, 3, 1, 0, to_x),
            remote(s, 2, 2, 1, to_y),
            remote(s, 3, 3, 1, to_y),
            remote(s, 2, 4, 0, to_y),
            remote(s, 1, 5, 1, to_x),
        ]
        for s in range(2)
    ]
    saving = [None, None]

    def tile(at):
        s, m = order[at]
        slot = at % 2
        for copy in load(at):
            copy.wait()
        if at + 1 < len(order):
            for copy in load(at + 1):
                copy.start()
        if saving[slot] is not None:
            saving[slot].wait()

        def back(step, carry):
            columns = pl.ds(pl.multiple_of(step * CHUNK, CHUNK), CHUNK)
            product = dot_nt(cot[slot], down[columns, :])
            grad[slot, :, columns] = (product * 2.0 * relu[slot, :, columns]).astype(LOW)
            return carry

        lax.fori_loop(0, units // CHUNK, back, 0)
        saving[slot] = pltpu.make_async_copy(grad.at[slot], grad_ref.at[s, m], outs.at[slot])
        saving[slot].start()

        def through(step, carry):
            columns = pl.ds(pl.multiple_of(step * CHUNK, CHUNK), CHUNK)
            part[s, m, :, columns] = dot(grad[slot], up[:, columns]).astype(LOW)
            return carry

        lax.fori_loop(0, depth // CHUNK, through, 0)

    def second_leg(s):
        copies[s][1].wait_recv()
        part[s, 2, :, lanes[0]] = (
            part[s, 2, :, lanes[0]].astype(F32) + arrived[s, 1].astype(F32)
        ).astype(LOW)
        copies[s][4].start()
        copies[s][3].wait_recv()
        part[s, 1, :, lanes[1]] = (
            part[s, 1, :, lanes[1]].astype(F32) + arrived[s, 3].astype(F32)
        ).astype(LOW)
        copies[s][5].start()

    def finish(s):
        for side, near, last in ((0, 0, 4), (1, 2, 5)):
            copies[s][near].wait_recv()
            copies[s][last].wait_recv()
            result[:, lanes[side]] = (
                part[s, 0, :, lanes[side]].astype(F32)
                + arrived[s, near].astype(F32)
                + arrived[s, last].astype(F32)
            )
        done = pltpu.make_async_copy(result, back_ref.at[s], local.at[2])
        done.start()
        return done

    def send_after(at):
        s, m = order[at]
        for number in {3: (1, 3), 1: (0,), 2: (2,), 0: ()}[m]:
            copies[s][number].start()

    for at in range(5):
        tile(at)
        send_after(at)
    second_leg(0)
    for at in range(5, 8):
        tile(at)
        send_after(at)
    done = finish(0)

    feeding = [None, None]

    def feed_load(at):
        s, m = order[at]
        return pltpu.make_async_copy(hidden_ref.at[s, m], cot.at[at % 2], loads.at[at % 2, 0])

    def feed_tile(at):
        s, m = order[at]
        slot = at % 2
        feed_load(at).wait()
        if at + 1 < len(order):
            feed_load(at + 1).start()
        if feeding[slot] is not None:
            feeding[slot].wait()

        def one(step, carry):
            columns = pl.ds(pl.multiple_of(step * CHUNK, CHUNK), CHUNK)
            feed[slot, :, columns] = dot(cot[slot], down[:, columns]).astype(LOW)
            return carry

        lax.fori_loop(0, depth // CHUNK, one, 0)
        feeding[slot] = pltpu.make_async_copy(feed.at[slot], feed_ref.at[s, m], outs.at[2 + slot])
        feeding[slot].start()

    feed_load(0).start()
    for at in range(2):
        feed_tile(at)
    second_leg(1)
    for at in range(2, 8):
        feed_tile(at)
    done.wait()
    finish(1).wait()
    for slot in range(2):
        saving[slot].wait()
        feeding[slot].wait()
    for s in range(2):
        for number in range(6):
            copies[s][number].wait_send()


def feed_out(cot_all, relu, hidden, up_all, down_all):
    rows_here, depth = cot_all.shape[2:]
    units = up_all.shape[0]
    anywhere = pl.BlockSpec(memory_space=pl.ANY)
    return pl.pallas_call(
        feed_out_kernel,
        in_specs=[anywhere] * 5,
        out_specs=[anywhere] * 3,
        out_shape=[
            jax.ShapeDtypeStruct((2, 4, rows_here, units), LOW),
            jax.ShapeDtypeStruct((2, 4, rows_here, depth), LOW),
            jax.ShapeDtypeStruct((2, rows_here, depth), F32),
        ],
        scratch_shapes=[
            pltpu.VMEM((units, depth), LOW),
            pltpu.VMEM((units, depth), LOW),
            pltpu.VMEM((2, rows_here, depth), LOW),
            pltpu.VMEM((2, rows_here, units), F32),
            pltpu.VMEM((2, rows_here, units), LOW),
            pltpu.VMEM((2, 4, rows_here, depth), LOW),
            pltpu.VMEM((2, 6, rows_here, depth // 2), LOW),
            pltpu.VMEM((2, rows_here, depth), LOW),
            pltpu.VMEM((rows_here, depth), F32),
            pltpu.SemaphoreType.DMA((3,)),
            pltpu.SemaphoreType.DMA((2, 2)),
            pltpu.SemaphoreType.DMA((4,)),
            pltpu.SemaphoreType.DMA((2, 6)),
            pltpu.SemaphoreType.DMA((2, 6)),
        ],
        compiler_params=pltpu.CompilerParams(
            collective_id=2, has_side_effects=True, vmem_limit_bytes=VMEM_LIMIT
        ),
        cost_estimate=pl.CostEstimate(
            flops=2 * 8 * rows_here * depth * units * 4,
            bytes_accessed=60 * 2**20,
            transcendentals=0,
        ),
        name="feed_out",
    )(cot_all, relu, hidden, up_all, down_all)


def plane_send(block, mask):
    return lax.ppermute(block, "dp", [(d, d ^ mask) for d in range(lax.axis_size("dp"))])


def plane_gather(block):
    half = block.shape[1] // 2
    one, two = block[:, :half], block[:, half:]
    one_x = plane_send(one, 1)
    two_y = plane_send(two, 2)
    one_y = plane_send(one, 2)
    two_x = plane_send(two, 1)
    one_xy = plane_send(one_x, 2)
    two_xy = plane_send(two_y, 1)
    return [
        block,
        jnp.concatenate([one_x, two_x], axis=1),
        jnp.concatenate([one_y, two_y], axis=1),
        jnp.concatenate([one_xy, two_xy], axis=1),
    ]


def plane_scatter(part):
    half = part.shape[2] // 2
    wide = lambda block: block.astype(F32)
    one, two = part[:, :, :half], part[:, :, half:]
    one_in = plane_send(one[1::2], 1)
    two_in = plane_send(two[2:], 2)
    one_sum = (wide(one[2]) + wide(one_in[1])).astype(LOW)
    two_sum = (wide(two[1]) + wide(two_in[1])).astype(LOW)
    one_last = plane_send(one_sum, 2)
    two_last = plane_send(two_sum, 1)
    return jnp.concatenate(
        [
            wide(one[0]) + wide(one_in[0]) + wide(one_last),
            wide(two[0]) + wide(two_in[0]) + wide(two_last),
        ],
        axis=1,
    )


def plane_order(blocks, axis):
    me = lax.axis_index("dp")
    stacked = jnp.stack(blocks, axis=0)
    return jnp.concatenate(
        [lax.dynamic_index_in_dim(stacked, me ^ d, 0, keepdims=False) for d in range(4)], axis=axis
    )


def chips():
    return lax.axis_size("mp") // 2


def line_send(block, step, senders):
    count = chips()
    pairs = []
    for z in senders:
        if 0 <= z < count and 0 <= z + step < count:
            pairs += [(2 * z + c, 2 * (z + step) + c) for c in range(2)]
    return lax.ppermute(block, "mp", pairs)


def core_swap(block):
    return lax.ppermute(block, "mp", [(i, i ^ 1) for i in range(lax.axis_size("mp"))])


def line_scatter(parts):
    count = chips()

    def add(left, right):
        return (left.astype(F32) + right.astype(F32)).astype(LOW)

    up, down = parts[count - 1], parts[1]
    for step in range(1, count):
        up_in = line_send(up, 1, range(0, step))
        down_in = line_send(down, -1, range(count - step, count))
        if step < count - 1:
            up = add(up_in, parts[count - step - 1])
            down = add(down_in, parts[step + 1])
    return (parts[0].astype(F32) + up_in.astype(F32) + down_in.astype(F32)).astype(LOW)


def per_device(
    inputs,
    cotangent,
    short_lengths,
    long_lengths,
    norm1_gain,
    norm1_bias,
    query_weight,
    key_weight,
    value_weight,
    query_kernel,
    key_kernel,
    value_kernel,
    out_weight,
    norm2_gain,
    norm2_bias,
    up_weight,
    down_weight,
):
    rows_here = inputs.shape[1]
    width = inputs.shape[2]
    mp = lax.axis_size("mp")
    dp = lax.axis_size("dp")
    me_dp = lax.axis_index("dp")
    me_mp = lax.axis_index("mp")
    group = rows_here * mp
    hidden_here = up_weight.shape[1]
    share = hidden_here // dp

    starts = jnp.stack(
        [document_starts(short_lengths[0], group), document_starts(long_lengths[0], group)]
    )
    rows = inputs.astype(F32)

    def quarters(weight):
        return weight.reshape(4, weight.shape[0] // 4, width)

    qk_own = jnp.concatenate([query_weight, key_weight], axis=1).T
    up_own = lax.dynamic_slice_in_dim(up_weight, me_dp * share, share, 1).T
    down_own = lax.dynamic_slice_in_dim(down_weight, me_dp * share, share, 0)
    taps_own = jnp.pad(
        jnp.concatenate([query_kernel, key_kernel, value_kernel], axis=1), ((0, 5), (0, HD))
    )
    qk_all, v_all, out_all, taps_all, normed, halo_rows, up_early = prepare(
        inputs, norm1_gain, norm1_bias, quarters(qk_own), quarters(value_weight.T), quarters(out_weight), taps_own, up_own,
    )
    qk_all = qk_all.reshape(mp * 2 * HD, width)
    v_all = v_all.reshape(mp * HD, width)
    out_all = out_all.reshape(mp * HD, width)
    taps = taps_all[:, :3].transpose(1, 0, 2)
    qk_taps = taps[:, :, : 2 * HD].reshape(3, mp * 2 * HD)
    v_taps = taps[:, :, 2 * HD : 3 * HD].reshape(3, mp * HD)

    cot_all = jnp.stack([jnp.stack(plane_gather(cotangent[index])) for index in range(2)])

    normed_ext = jnp.concatenate([halo_rows, normed], axis=1)
    raw_qk = jnp.einsum("srd,cd->src", normed_ext, qk_all, preferred_element_type=F32)
    raw_v = jnp.einsum("srd,cd->src", normed_ext, v_all, preferred_element_type=F32)
    places = jnp.arange(group, dtype=jnp.int32)
    offsets = lax.dynamic_slice_in_dim(
        jnp.pad(places[None, :] - starts, ((0, 0), (0, HALO))), me_mp * rows_here, rows_here + HALO, 1
    )[:, :, None]
    here = offsets[:, :rows_here]

    def conv(raw, tap):
        return (
            tap[0] * raw[:, HALO:]
            + jnp.where(here >= 1, tap[1] * raw[:, HALO - 1 : -1], 0.0)
            + jnp.where(here >= 2, tap[2] * raw[:, HALO - 2 : -2], 0.0)
        ).astype(LOW)

    mixed_qk = conv(raw_qk, qk_taps)
    mixed_v = conv(raw_v, v_taps)

    def side_by_side(pair):
        split = pair.reshape(2, rows_here, mp, HD)
        return split.transpose(1, 2, 0, 3).reshape(1, rows_here, mp * 2 * HD)

    def apart(joint):
        split = joint.reshape(joint.shape[1], mp, 2, HD)
        return split.transpose(2, 0, 1, 3).reshape(2, joint.shape[1], mp * HD)

    mixed = heads_out(jnp.concatenate([mixed_qk, side_by_side(mixed_v)], axis=0), 4, "mixed_out")
    attended_head, wide, total = attend(mixed, starts)
    attended = apart(heads_back(attended_head, rows_here, 0, 5, "attended_back"))
    middle = rows + dot(attended, out_all)
    second = layer_norm(middle, norm2_gain, norm2_bias).astype(LOW)

    second_all, relu, hidden, down_all, up_all = feed_in(second, up_early, down_own)
    grad_pre, feed_part, grad_second = feed_out(cot_all, relu, hidden, up_all, down_all)
    down_part = jnp.einsum(
        "gf,gd->fd",
        hidden.reshape(-1, hidden.shape[3]),
        cot_all.reshape(-1, width),
        preferred_element_type=F32,
    ).astype(LOW)
    up_part = jnp.einsum(
        "gf,gd->fd",
        grad_pre.reshape(-1, hidden.shape[3]),
        second_all.reshape(-1, width),
        preferred_element_type=F32,
    ).astype(LOW)
    results = jnp.stack(
        [(middle[index] + plane_scatter(feed_part[index])).astype(LOW) for index in range(2)]
    )

    def add_low(left, right):
        return (left.astype(F32) + right.astype(F32)).astype(LOW)

    core = me_mp % 2
    mine = share * (mp // 2)

    def reduce_units(part):
        own = lax.dynamic_slice_in_dim(part, core * mine, mine, 0)
        other = lax.dynamic_slice_in_dim(part, (1 - core) * mine, mine, 0)
        total = add_low(own, core_swap(other)).reshape(mp // 2, share, width)
        z = me_mp // 2
        return line_scatter(
            [
                lax.dynamic_index_in_dim(total, (z + k) % (mp // 2), 0, keepdims=False)
                for k in range(mp // 2)
            ]
        )

    up_mine = reduce_units(up_part).T
    down_mine = reduce_units(down_part)
    up_grad = plane_order(plane_gather(up_mine), axis=1).astype(F32)
    down_grad = plane_order(plane_gather(down_mine), axis=0).astype(F32)

    def norm_back(values, gain, grad):
        flat = values.reshape(-1, width)
        unused, pull = jax.vjp(layer_norm, flat, gain, norm1_bias)
        grad_rows, grad_gain, grad_shift = pull(grad.reshape(-1, width))
        return grad_rows.reshape(values.shape), grad_gain, grad_shift

    grad_middle, gain_two, shift_two = norm_back(middle, norm2_gain, grad_second)
    grad_middle = grad_middle + cotangent.astype(F32)
    branch = grad_middle.astype(LOW)
    out_part = jnp.einsum("srh,srd->hd", attended, branch, preferred_element_type=F32).astype(LOW)
    grad_attended = jnp.einsum("srd,hd->srh", branch, out_all, preferred_element_type=F32).astype(LOW)
    grad_head = heads_out(side_by_side(grad_attended), 6, "attended_grad_out")
    grad_mixed_head = attend_back(mixed, grad_head, wide, total, starts, HALO)
    grad_mixed = heads_back(grad_mixed_head, rows_here, HALO, 7, "mixed_grad_back")
    grad_qk = grad_mixed[:2].astype(F32)
    grad_v = apart(grad_mixed[2:]).astype(F32)

    def conv_back(grad, raw, tap):
        after_one = jnp.where(offsets[:, 1 : rows_here + 1] >= 1, grad[:, 1 : rows_here + 1], 0.0)
        after_two = jnp.where(offsets[:, 2 : rows_here + 2] >= 2, grad[:, 2 : rows_here + 2], 0.0)
        own = grad[:, :rows_here]
        grad_raw = (tap[0] * own + tap[1] * after_one + tap[2] * after_two).astype(LOW)
        grad_tap = jnp.stack(
            [
                jnp.sum(own * raw[:, HALO:], axis=(0, 1)),
                jnp.sum(jnp.where(here >= 1, own, 0.0) * raw[:, HALO - 1 : -1], axis=(0, 1)),
                jnp.sum(jnp.where(here >= 2, own, 0.0) * raw[:, HALO - 2 : -2], axis=(0, 1)),
            ]
        )
        return grad_raw, grad_tap

    grad_raw_qk, grad_tap_qk = conv_back(grad_qk, raw_qk, qk_taps)
    grad_raw_v, grad_tap_v = conv_back(grad_v, raw_v, v_taps)
    qk_part = jnp.einsum("src,srd->cd", grad_raw_qk, normed, preferred_element_type=F32).astype(LOW)
    v_part = jnp.einsum("src,srd->cd", grad_raw_v, normed, preferred_element_type=F32).astype(LOW)
    grad_normed = dot(grad_raw_qk, qk_all) + dot(grad_raw_v, v_all)
    grad_input, gain_one, shift_one = norm_back(rows, norm1_gain, grad_normed)
    input_grads = grad_middle + grad_input

    joint = jnp.concatenate(
        [
            qk_part.reshape(mp, 2 * HD, width),
            v_part.reshape(mp, HD, width),
            out_part.reshape(mp, HD, width),
        ],
        axis=1,
    ).reshape(mp * 4 * HD, width)
    joint_grad = lax.psum(
        lax.psum_scatter(joint, "mp", scatter_dimension=0, tiled=True), "dp"
    ).astype(F32)
    small_sum, tap_sum = lax.psum(
        (
            jnp.stack([gain_one, shift_one, gain_two, shift_two]),
            jnp.concatenate([grad_tap_qk, grad_tap_v], axis=1),
        ),
        ("dp", "mp"),
    )
    qk_tap_grad = lax.dynamic_slice_in_dim(tap_sum, me_mp * 2 * HD, 2 * HD, 1)
    v_tap_grad = lax.dynamic_slice_in_dim(tap_sum, mp * 2 * HD + me_mp * HD, HD, 1)
    return (
        results,
        input_grads,
        small_sum[0],
        small_sum[1],
        joint_grad[:HD].T,
        joint_grad[HD : 2 * HD].T,
        joint_grad[2 * HD : 3 * HD].T,
        qk_tap_grad[:, :HD],
        qk_tap_grad[:, HD:],
        v_tap_grad,
        joint_grad[3 * HD :],
        small_sum[2],
        small_sum[3],
        up_grad,
        down_grad,
    )


def solution(mesh):
    return jax.shard_map(
        per_device,
        mesh=mesh,
        in_specs=(
            P(None, ("dp", "mp"), None),
            P(None, ("dp", "mp"), None),
            P("dp", None),
            P("dp", None),
            P(),
            P(),
            P(None, "mp"),
            P(None, "mp"),
            P(None, "mp"),
            P(None, "mp"),
            P(None, "mp"),
            P(None, "mp"),
            P("mp", None),
            P(),
            P(),
            P(None, "mp"),
            P("mp", None),
        ),
        out_specs=(
            P(None, ("dp", "mp"), None),
            P(None, ("dp", "mp"), None),
            P(),
            P(),
            P(None, "mp"),
            P(None, "mp"),
            P(None, "mp"),
            P(None, "mp"),
            P(None, "mp"),
            P(None, "mp"),
            P("mp", None),
            P(),
            P(),
            P(None, "mp"),
            P("mp", None),
        ),
        check_vma=False,
    )
```

```python
from functools import partial

import jax
import jax.numpy as jnp
from jax import lax
from jax.experimental import pallas as pl
from jax.experimental.pallas import tpu as pltpu
from jax.sharding import PartitionSpec as P

HD = 64
BLOCK = 256
CHUNK = 512
VMEM_LIMIT = 62 * 1024 * 1024
MESH = pl.DeviceIdType.MESH
LOW = jnp.bfloat16
F32 = jnp.float32


def dot(left, right):
    return jnp.dot(left, right, preferred_element_type=F32)


def layer_norm(rows, gain, shift):
    row_mean = jnp.mean(rows, axis=-1, keepdims=True)
    centered = rows - row_mean
    variance = jnp.mean(centered * centered, axis=-1, keepdims=True)
    return centered * lax.rsqrt(variance + 1e-05) * gain + shift


def document_starts(lengths, count):
    ends = jnp.cumsum(lengths)
    places = jnp.arange(count, dtype=jnp.int32)
    passed = (places[:, None] >= ends[None, :]).astype(jnp.int32)
    return jnp.sum(passed * lengths[None, :], axis=1)


def allowed_pairs(start_row, key_block, query_block):
    keys = key_block * BLOCK + lax.broadcasted_iota(jnp.int32, (BLOCK, BLOCK), 0)
    queries = query_block * BLOCK + lax.broadcasted_iota(jnp.int32, (BLOCK, BLOCK), 1)
    return (keys <= queries) & (keys >= start_row)


def attend_kernel(
    first_ref, start_ref, qk_ref, v_ref, out_ref, wide_ref, total_ref, values_t
):
    s, step = pl.program_id(0), pl.program_id(1)

    @pl.when(step == 0)
    def _():
        def turn(at, carry):
            rows = pl.ds(pl.multiple_of(at * BLOCK, BLOCK), BLOCK)
            both = v_ref[0, rows, :].T
            values_t[at] = jnp.where(s == 0, both[:HD], both[HD:])
            return carry

        lax.fori_loop(0, values_t.shape[0], turn, 0)

    here = pl.ds(pl.multiple_of(step * BLOCK, BLOCK), BLOCK)
    query_t = (qk_ref[0, here, 0:HD] * HD ** (-0.5)).astype(LOW).T
    start_row = start_ref[0]

    def one(at, carry):
        top, summed, acc = carry
        rows = pl.ds(pl.multiple_of(at * BLOCK, BLOCK), BLOCK)
        scores = dot(qk_ref[0, rows, HD : 2 * HD], query_t)
        scores = jnp.where(allowed_pairs(start_row, at, step), scores, -1e30)
        new_top = jnp.maximum(top, jnp.max(scores, axis=0, keepdims=True))
        powered = jnp.exp(scores - new_top)
        shrink = jnp.exp(top - new_top)
        summed = summed * shrink + jnp.sum(powered, axis=0, keepdims=True)
        acc = acc * shrink + dot(values_t[at], powered.astype(LOW))
        return new_top, summed, acc

    top, summed, acc = lax.fori_loop(
        first_ref[s, step],
        step + 1,
        one,
        (
            jnp.full((1, BLOCK), -1e30, F32),
            jnp.zeros((1, BLOCK), F32),
            jnp.zeros((HD, BLOCK), F32),
        ),
    )
    result = acc / summed
    wide_ref[0] = result
    total_ref[0] = top + jnp.log(summed)
    low = result.T.astype(LOW)

    @pl.when(s == 0)
    def _():
        out_ref[0, here, 0:HD] = low

    @pl.when(s == 1)
    def _():
        out_ref[0, here, HD : 2 * HD] = low


def attend(mixed, starts):
    group = mixed.shape[1]
    steps = group // BLOCK
    row = pl.BlockSpec((1, 1, BLOCK), lambda s, i, first: (s, 0, i))
    return pl.pallas_call(
        attend_kernel,
        grid_spec=pltpu.PrefetchScalarGridSpec(
            num_scalar_prefetch=1,
            grid=(2, steps),
            in_specs=[
                row,
                pl.BlockSpec((1, group, 2 * HD), lambda s, i, first: (s, 0, 0)),
                pl.BlockSpec((1, group, 2 * HD), lambda s, i, first: (2, 0, 0)),
            ],
            out_specs=[
                pl.BlockSpec((1, group, 2 * HD), lambda s, i, first: (0, 0, 0)),
                pl.BlockSpec((1, HD, BLOCK), lambda s, i, first: (s, 0, i)),
                row,
            ],
            scratch_shapes=[pltpu.VMEM((steps, HD, BLOCK), LOW)],
        ),
        out_shape=[
            jax.ShapeDtypeStruct((1, group, 2 * HD), LOW),
            jax.ShapeDtypeStruct((2, HD, group), F32),
            jax.ShapeDtypeStruct((2, 1, group), F32),
        ],
        compiler_params=pltpu.CompilerParams(vmem_limit_bytes=32 * 1024 * 1024),
        cost_estimate=pl.CostEstimate(
            flops=2**34, bytes_accessed=group * 2048, transcendentals=group * group // 4
        ),
        name="attend",
    )(starts[:, ::BLOCK] // BLOCK, starts[:, None, :], mixed, mixed)


def attend_back_kernel(
    first_ref, start_ref, qk_ref, v_ref, grad_ref, wide_ref, total_ref, out_ref,
    keys_t, values, grad_keys, grad_values,
):
    s, step = pl.program_id(0), pl.program_id(1)
    group = qk_ref.shape[1]

    @pl.when(step == 0)
    def _():
        def turn(at, carry):
            rows = pl.ds(pl.multiple_of(at * BLOCK, BLOCK), BLOCK)
            keys_t[at] = qk_ref[0, rows, HD : 2 * HD].T
            both = v_ref[0, rows, :]
            values[rows, :] = jnp.where(s == 0, both[:, :HD], both[:, HD:])
            return carry

        lax.fori_loop(0, keys_t.shape[0], turn, 0)
        grad_keys[...] = jnp.zeros(grad_keys.shape, F32)
        grad_values[...] = jnp.zeros(grad_values.shape, F32)

    here = pl.ds(pl.multiple_of(step * BLOCK, BLOCK), BLOCK)
    query = (qk_ref[0, here, 0:HD] * HD ** (-0.5)).astype(LOW)
    query_t = query.T
    both = grad_ref[0]
    grad = jnp.where(s == 0, both[:, :HD], both[:, HD:])
    grad_t = grad.T
    start_row = start_ref[0]
    total = total_ref[0]
    inner = jnp.sum(grad_t.astype(F32) * wide_ref[0], axis=0, keepdims=True)

    def one(at, acc):
        rows = pl.ds(pl.multiple_of(at * BLOCK, BLOCK), BLOCK)
        scores = dot(qk_ref[0, rows, HD : 2 * HD], query_t)
        scores = jnp.where(allowed_pairs(start_row, at, step), scores, -1e30)
        probs = jnp.exp(scores - total)
        grad_probs = dot(values[rows, :], grad_t)
        grad_scores = (probs * (grad_probs - inner)).astype(LOW)
        grad_values[rows, :] += dot(probs.astype(LOW), grad)
        grad_keys[rows, :] += dot(grad_scores, query)
        return acc + dot(keys_t[at], grad_scores)

    acc = lax.fori_loop(first_ref[s, step], step + 1, one, jnp.zeros((HD, BLOCK), F32))
    out_ref[s, here, 0:HD] = (acc * HD ** (-0.5)).T.astype(out_ref.dtype)

    @pl.when(step == pl.num_programs(1) - 1)
    def _():
        out_ref[s, 0:group, HD : 2 * HD] = grad_keys[...].astype(out_ref.dtype)
        out_ref[s, group:, :] = jnp.zeros((out_ref.shape[1] - group, 2 * HD), out_ref.dtype)

        @pl.when(s == 0)
        def _():
            out_ref[2, 0:group, 0:HD] = grad_values[...].astype(out_ref.dtype)

        @pl.when(s == 1)
        def _():
            out_ref[2, 0:group, HD : 2 * HD] = grad_values[...].astype(out_ref.dtype)
            out_ref[2, group:, :] = jnp.zeros((out_ref.shape[1] - group, 2 * HD), out_ref.dtype)


def attend_back(mixed, grad, wide, total, starts, halo):
    group = mixed.shape[1]
    steps = group // BLOCK
    row = pl.BlockSpec((1, 1, BLOCK), lambda s, i, first: (s, 0, i))
    return pl.pallas_call(
        attend_back_kernel,
        grid_spec=pltpu.PrefetchScalarGridSpec(
            num_scalar_prefetch=1,
            grid=(2, steps),
            in_specs=[
                row,
                pl.BlockSpec((1, group, 2 * HD), lambda s, i, first: (s, 0, 0)),
                pl.BlockSpec((1, group, 2 * HD), lambda s, i, first: (2, 0, 0)),
                pl.BlockSpec((1, BLOCK, 2 * HD), lambda s, i, first: (0, i, 0)),
                pl.BlockSpec((1, HD, BLOCK), lambda s, i, first: (s, 0, i)),
                row,
            ],
            out_specs=pl.BlockSpec((3, group + halo, 2 * HD), lambda s, i, first: (0, 0, 0)),
            scratch_shapes=[
                pltpu.VMEM((steps, HD, BLOCK), LOW),
                pltpu.VMEM((group, HD), LOW),
                pltpu.VMEM((group, HD), F32),
                pltpu.VMEM((group, HD), F32),
            ],
        ),
        out_shape=jax.ShapeDtypeStruct((3, group + halo, 2 * HD), LOW),
        compiler_params=pltpu.CompilerParams(vmem_limit_bytes=32 * 1024 * 1024),
        cost_estimate=pl.CostEstimate(
            flops=2**35, bytes_accessed=group * 2048, transcendentals=group * group // 4
        ),
        name="attend_back",
    )(starts[:, ::BLOCK] // BLOCK, starts[:, None, :], mixed, mixed, grad, wide, total)


def plane_partners():
    me = lax.axis_index("dp")
    return {"dp": me + 1 - 2 * lax.rem(me, 2)}, {"dp": me + 2 - 4 * (me // 2)}


def dot_nt(left, right):
    return lax.dot_general(left, right, (((1,), (1,)), ((), ())), preferred_element_type=F32)


def mesh_place():
    me = lax.axis_index("mp")
    return me // 2, lax.rem(me, 2)


def wire(source, target, send, recv, partner):
    return pltpu.make_async_remote_copy(
        src_ref=source,
        dst_ref=target,
        send_sem=send,
        recv_sem=recv,
        device_id=partner,
        device_id_type=MESH,
    )


def line_partner(z, step):
    _, core = mesh_place()
    return {"mp": 2 * (z + step) + core}


def other_core():
    z, core = mesh_place()
    return {"mp": 2 * z + 1 - core}


def greet(partners):
    barrier = pltpu.get_barrier_semaphore()
    for partner in partners:
        pl.semaphore_signal(barrier, inc=1, device_id=partner, device_id_type=MESH)
    pl.semaphore_wait(barrier, len(partners))


def greet_line(with_plane):
    z, _ = mesh_place()
    count = lax.axis_size("mp") // 2
    barrier = pltpu.get_barrier_semaphore()
    partners = [other_core()]
    if with_plane:
        partners += list(plane_partners())
    for partner in partners:
        pl.semaphore_signal(barrier, inc=1, device_id=partner, device_id_type=MESH)
    for turn in (1, -1):

        @pl.when((z + turn >= 0) & (z + turn < count))
        def _(turn=turn):
            pl.semaphore_signal(barrier, inc=1, device_id=line_partner(z, turn), device_id_type=MESH)

    near = jnp.where(z > 0, 1, 0) + jnp.where(z < count - 1, 1, 0)
    pl.semaphore_wait(barrier, near + len(partners))


class LineGather:
    def __init__(self, place, send, recv, swap_send, swap_recv):
        self.z, self.core = mesh_place()
        self.count = lax.axis_size("mp") // 2
        self.place, self.send, self.recv = place, send, recv
        self.swap_send, self.swap_recv = swap_send, swap_recv

    def copies(self, step):
        z, count = self.z, self.count
        out = []
        for way, turn in enumerate((1, -1)):
            leaves = z - turn * (step - 1)
            lands = z - turn * step
            far = z + turn
            sends = (leaves >= 0) & (leaves < count) & (far >= 0) & (far < count)
            receives = (lands >= 0) & (lands < count)
            at = jnp.clip(leaves, 0, count - 1)
            to = jnp.clip(lands, 0, count - 1)
            sems = (self.send.at[way, step - 1], self.recv.at[way, step - 1], line_partner(z, turn))
            leaving = wire(self.place(at, self.core), self.place(at, self.core), *sems)
            landing = wire(self.place(to, self.core), self.place(to, self.core), *sems)
            out.append((sends, leaving, receives, landing, to))
        return out

    def start(self, step):
        for sends, leaving, _, _, _ in self.copies(step):
            pl.when(sends)(leaving.start)

    def swap(self, at, number):
        sems = (self.swap_send.at[number], self.swap_recv.at[number], other_core())
        leaving = wire(self.place(at, self.core), self.place(at, self.core), *sems)
        landing = wire(self.place(at, 1 - self.core), self.place(at, 1 - self.core), *sems)
        return leaving, landing

    def swap_own(self):
        self.swap(self.z, 0)[0].start()

    def arrive(self, step):
        for way, (_, _, receives, landing, at) in enumerate(self.copies(step)):

            @pl.when(receives)
            def _(landing=landing, at=at, way=way):
                landing.wait_recv()
                self.swap(at, 1 + 2 * (step - 1) + way)[0].start()

    def swapped(self, at, number):
        leaving, landing = self.swap(at, number)
        leaving.wait_send()
        landing.wait_recv()

    def finish(self, steps, own):
        if own:
            self.swapped(self.z, 0)
        for step in steps:
            for way, (sends, leaving, receives, _, at) in enumerate(self.copies(step)):
                pl.when(sends)(leaving.wait_send)
                pl.when(receives)(
                    lambda at=at, way=way, step=step: self.swapped(at, 1 + 2 * (step - 1) + way)
                )


def line_semaphores(count):
    return [
        pltpu.SemaphoreType.DMA((2, count)),
        pltpu.SemaphoreType.DMA((2, count)),
        pltpu.SemaphoreType.DMA((2 * count,)),
        pltpu.SemaphoreType.DMA((2 * count,)),
    ]


def early_steps(count):
    return range(1, count // 2 + 1)


def prepare_kernel(
    inputs_ref, gain_ref, shift_ref, qk_ref, v_ref, out_ref, taps_ref, up_ref,
    all_qk_ref, all_v_ref, all_out_ref, all_taps_ref, normed_ref, halo_ref, up_all_ref,
    rows, normed, all_qk, all_v, all_out, up_all, local, *sems,
):
    mp = lax.axis_size("mp")
    dp = lax.axis_index("dp")
    me = lax.axis_index("mp")
    z, core = mesh_place()
    count = mp // 2
    rows_here, depth = rows.shape[1:]
    to_x, to_y = plane_partners()
    share = up_ref.shape[0]
    owned = (qk_ref, v_ref, out_ref)
    whole = (all_qk, all_v, all_out)
    (plane_send_sem, plane_recv_sem, plane_swap_send, plane_swap_recv) = sems[:4]
    taps_send, taps_recv, halo_send, halo_recv = sems[4:8]
    line_sems = [sems[8 + 4 * part : 12 + 4 * part] for part in range(4)]

    def up_place(at, at_core):
        start = pl.multiple_of((2 * at + at_core) * share, 16)
        return up_all.at[pl.ds(start, share), :]

    loads = [
        pltpu.make_async_copy(inputs_ref, rows, local.at[0]),
        pltpu.make_async_copy(taps_ref, all_taps_ref.at[me], local.at[1]),
        pltpu.make_async_copy(up_ref, up_place(z, core), local.at[2]),
    ] + [
        pltpu.make_async_copy(
            owned[part].at[dp], whole[part].at[z, core, dp], local.at[3 + part]
        )
        for part in range(3)
    ]
    for copy in loads:
        copy.start()

    barrier = pltpu.get_barrier_semaphore()
    for step in range(1, mp):
        pl.semaphore_signal(
            barrier, inc=1, device_id={"mp": lax.rem(me + step, mp)}, device_id_type=MESH
        )
    for partner in (to_x, to_y):
        pl.semaphore_signal(barrier, inc=1, device_id=partner, device_id_type=MESH)
    pl.semaphore_wait(barrier, mp + 1)
    for copy in loads[1:]:
        copy.wait()

    lines = [
        LineGather(lambda at, at_core, part=part: whole[part].at[at, at_core, dp], *line_sems[part])
        for part in range(3)
    ]
    up_line = LineGather(up_place, *line_sems[3])
    for line in lines:
        line.start(1)
    tap_copies = [
        (
            wire(
                taps_ref, all_taps_ref.at[me], taps_send.at[step], taps_recv.at[step],
                {"mp": lax.rem(me + step, mp)},
            ),
            wire(
                taps_ref, all_taps_ref.at[lax.rem(me + mp - step, mp)], taps_send.at[step],
                taps_recv.at[step], {"mp": lax.rem(me + step, mp)},
            ),
        )
        for step in range(1, mp)
    ]
    for copy, _ in tap_copies:
        copy.start()
    for line in lines:
        line.swap_own()

    loads[0].wait()
    tall = 16

    def norm(s):
        def some(at, carry):
            here = pl.ds(pl.multiple_of(at * tall, tall), tall)
            values = rows[s, here, :].astype(F32)
            centered = values - jnp.mean(values, axis=1, keepdims=True)
            variance = jnp.mean(centered * centered, axis=1, keepdims=True)
            normed[s, here, :] = (
                centered * lax.rsqrt(variance + 1e-05) * gain_ref[...] + shift_ref[...]
            ).astype(LOW)
            return carry

        lax.fori_loop(0, rows_here // tall, some, 0)

    norm(0)
    for step in range(1, count):
        for line in lines:
            line.arrive(step)
        if step + 1 < count:
            for line in lines:
                line.start(step + 1)

    half = depth // 2
    lanes = (pl.ds(0, half), pl.ds(half, half))
    dp_x = dp + 1 - 2 * lax.rem(dp, 2)
    dp_y = dp + 2 - 4 * (dp // 2)
    dp_xy = dp_x + 2 - 4 * (dp_x // 2)
    legs = ((0, to_x), (1, to_y), (0, to_y), (1, to_x), (0, to_y), (1, to_x))

    def plane(number, quarter):
        side, partner = legs[number]
        out = []
        for part in range(3):
            block = whole[part].at[:, core, quarter, :, lanes[side]]
            out.append(
                wire(
                    block, block, plane_send_sem.at[part, number], plane_recv_sem.at[part, number], partner
                )
            )
        return out

    leaving = [plane(number, quarter) for number, quarter in enumerate((dp, dp, dp, dp, dp_x, dp_y))]
    landing = [
        plane(number, quarter) for number, quarter in enumerate((dp_x, dp_y, dp_y, dp_x, dp_xy, dp_xy))
    ]

    def pass_on(number, at_core):
        quarter = (dp_x, dp_y, dp_xy)[number]
        out = []
        for part in range(3):
            block = whole[part].at[:, at_core, quarter]
            out.append(
                wire(
                    block, block, plane_swap_send.at[part, number], plane_swap_recv.at[part, number],
                    other_core(),
                )
            )
        return out

    def each(copies, what):
        for copy in copies:
            getattr(copy, what)()

    for number in range(4):
        each(leaving[number], "start")
    up_line.start(1)
    up_line.swap_own()
    norm(1)
    save = pltpu.make_async_copy(normed, normed_ref, local.at[0])
    save.start()
    halo = halo_ref.shape[1]
    halo_copy = wire(
        normed.at[:, pl.ds(rows_here - halo, halo), :], halo_ref, halo_send, halo_recv,
        {"mp": lax.rem(me + 1, mp)},
    )
    halo_copy.start()
    each(landing[0], "wait_recv")
    each(leaving[4], "start")
    each(landing[1], "wait_recv")
    each(leaving[5], "start")
    early = early_steps(count)
    up_line.arrive(1)
    up_line.start(2)
    each(landing[3], "wait_recv")
    each(pass_on(0, core), "start")
    each(landing[2], "wait_recv")
    each(pass_on(1, core), "start")
    each(landing[4], "wait_recv")
    each(landing[5], "wait_recv")
    each(pass_on(2, core), "start")
    for step in early[1:]:
        up_line.arrive(step)
        if step != early[-1]:
            up_line.start(step + 1)
    for line in lines:
        line.finish(range(1, count), True)
    up_line.finish(early, True)
    for number in range(6):
        each(leaving[number], "wait_send")
    for number in range(3):
        each(pass_on(number, core), "wait_send")
        each(pass_on(number, 1 - core), "wait_recv")
    for copy, landed in tap_copies:
        copy.wait_send()
        landed.wait_recv()
    halo_copy.wait()
    save.wait()
    saves = [
        pltpu.make_async_copy(here, there, local.at[2 + at])
        for at, (here, there) in enumerate(
            ((all_qk, all_qk_ref), (all_v, all_v_ref), (all_out, all_out_ref), (up_all, up_all_ref))
        )
    ]
    for copy in saves:
        copy.start()
    for copy in saves:
        copy.wait()


HALO = 16


def prepare(inputs, gain, shift, qk, v, out, taps, up):
    mp = lax.axis_size("mp")
    count = mp // 2
    rows_here, depth = inputs.shape[1:]
    anywhere = pl.BlockSpec(memory_space=pl.ANY)
    vmem = pl.BlockSpec(memory_space=pltpu.VMEM)
    dma = pltpu.SemaphoreType.DMA
    return pl.pallas_call(
        prepare_kernel,
        in_specs=[anywhere, vmem, vmem] + [anywhere] * 5,
        out_specs=[anywhere] * 7,
        out_shape=[
            jax.ShapeDtypeStruct((count, 2) + qk.shape, LOW),
            jax.ShapeDtypeStruct((count, 2) + v.shape, LOW),
            jax.ShapeDtypeStruct((count, 2) + out.shape, LOW),
            jax.ShapeDtypeStruct((mp,) + taps.shape, F32),
            jax.ShapeDtypeStruct(inputs.shape, LOW),
            jax.ShapeDtypeStruct((2, HALO, depth), LOW),
            jax.ShapeDtypeStruct((mp * up.shape[0], depth), LOW),
        ],
        scratch_shapes=[
            pltpu.VMEM(inputs.shape, LOW),
            pltpu.VMEM(inputs.shape, LOW),
            pltpu.VMEM((count, 2) + qk.shape, LOW),
            pltpu.VMEM((count, 2) + v.shape, LOW),
            pltpu.VMEM((count, 2) + out.shape, LOW),
            pltpu.VMEM((mp * up.shape[0], depth), LOW),
            dma((6,)),
            dma((3, 6)),
            dma((3, 6)),
            dma((3, 3)),
            dma((3, 3)),
            dma((mp,)),
            dma((mp,)),
            dma,
            dma,
        ]
        + line_semaphores(count) * 4,
        compiler_params=pltpu.CompilerParams(
            collective_id=3, has_side_effects=True, vmem_limit_bytes=VMEM_LIMIT
        ),
        cost_estimate=pl.CostEstimate(flops=2**36, bytes_accessed=2**26, transcendentals=0),
        name="prepare",
    )(inputs, gain.reshape(1, depth), shift.reshape(1, depth), qk, v, out, taps, up)


def weight_grad(left_ref, pieces, whole, tiles, outs, out_ref, load, tile_sem, out_sem):
    wide = tiles.shape[2]
    steps = left_ref.shape[1] // wide
    if len(pieces) == 1:
        loading = [pltpu.make_async_copy(pieces[0], whole, load.at[0])]
    else:
        tall = whole.shape[0] // 8
        loading = []
        for s in range(2):
            for m in range(4):
                target = whole.at[pl.ds((4 * s + m) * tall, tall), :]
                loading += piece_copies(pieces, s, m, target, load.at[s, m])

    def tile(at, slot):
        columns = pl.ds(pl.multiple_of(at * wide, wide), wide)
        return pltpu.make_async_copy(left_ref.at[:, columns], tiles.at[slot], tile_sem.at[slot])

    def out(at, slot):
        rows = pl.ds(pl.multiple_of(at * wide, wide), wide)
        return pltpu.make_async_copy(outs.at[slot], out_ref.at[rows, :], out_sem.at[slot])

    for copy in loading:
        copy.start()
    tile(0, 0).start()
    for copy in loading:
        copy.wait()

    def one(at, carry):
        slot = lax.rem(at, 2)
        tile(at, slot).wait()

        @pl.when(at + 1 < steps)
        def _():
            tile(at + 1, 1 - slot).start()

        @pl.when(at >= 2)
        def _():
            out(at - 2, slot).wait()

        outs[slot] = lax.dot_general(
            tiles[slot], whole[...], (((0,), (0,)), ((), ())), preferred_element_type=F32
        ).astype(LOW)
        out(at, slot).start()
        return carry

    lax.fori_loop(0, steps, one, 0)
    out(steps - 2, lax.rem(steps - 2, 2)).wait()
    out(steps - 1, lax.rem(steps - 1, 2)).wait()


def weight_grad_scratch(rows, depth, pieces):
    dma = pltpu.SemaphoreType.DMA
    return [
        pltpu.VMEM((rows, depth), LOW),
        pltpu.VMEM((2, rows, 256), LOW),
        pltpu.VMEM((2, 256, depth), LOW),
        dma((1,)) if pieces == 1 else dma((2, 4, 2)),
        dma((2,)),
        dma((2,)),
    ]


def whole_weight_grad(left, right):
    rows, units = left.shape
    depth = right[0].shape[-1]
    anywhere = pl.BlockSpec(memory_space=pl.ANY)

    def kernel(left_ref, *refs):
        pieces, out_ref, scratch = refs[: len(right)], refs[len(right)], refs[len(right) + 1 :]
        weight_grad(left_ref, pieces, *scratch[:3], out_ref, *scratch[3:])

    return pl.pallas_call(
        kernel,
        in_specs=[anywhere] * (1 + len(right)),
        out_specs=anywhere,
        out_shape=jax.ShapeDtypeStruct((units, depth), LOW),
        scratch_shapes=weight_grad_scratch(rows, depth, len(right)),
        compiler_params=pltpu.CompilerParams(vmem_limit_bytes=48 * 2**20),
        cost_estimate=pl.CostEstimate(
            flops=2 * rows * units * depth, bytes_accessed=2**25, transcendentals=0
        ),
        name="weight_grad",
    )(left, *right)


def carry_copies(carried, targets, send, recv):
    partners = plane_partners()
    return [
        wire(ref, target, send.at[at], recv.at[at], partners[way])
        for at, ((way, ref), target) in enumerate(zip(carried, targets))
    ]


def exchange_kernel(halo, pieces, ways, x_ref, *refs):
    count = 1 + pieces if pieces else 0
    left_ref, right_refs = (refs[0], refs[1:count]) if pieces else (None, ())
    carried = list(zip(ways, refs[count : count + len(ways)]))
    refs = refs[count + len(ways) :]
    o_ref, refs = refs[0], refs[1:]
    if pieces:
        grad_ref, refs = refs[0], refs[1:]
    targets, refs = refs[: len(ways)], refs[len(ways) :]
    landed, local, send, recv = refs[:4]
    refs = refs[4:]
    mp = lax.axis_size("mp")
    me = lax.axis_index("mp")
    if halo is None:

        def source(at):
            return x_ref.at[:, :, pl.ds(pl.multiple_of(at * 128, 128), 128)]

        def target(at):
            return landed.at[:, at]
    else:
        tall = o_ref.shape[1]

        def source(at):
            return x_ref.at[:, pl.ds(pl.multiple_of(at * (tall - halo), 16), tall), :]

        def target(at):
            return landed.at[:, :, pl.ds(pl.multiple_of(at * 128, 128), 128)]

    barrier = pltpu.get_barrier_semaphore()
    for step in range(1, mp):
        pl.semaphore_signal(
            barrier, inc=1, device_id={"mp": lax.rem(me + step, mp)}, device_id_type=MESH
        )
    partners = plane_partners() if ways else ()
    for partner in partners:
        pl.semaphore_signal(barrier, inc=1, device_id=partner, device_id_type=MESH)
    own = pltpu.make_async_copy(source(me), target(me), local.at[0])
    own.start()
    pl.semaphore_wait(barrier, mp - 1 + len(partners))
    copies = []
    for step in range(1, mp):
        to = lax.rem(me + step, mp)
        sems = (send.at[step], recv.at[step], {"mp": to})
        leaving = wire(source(to), target(me), *sems)
        landing = wire(source(to), target(lax.rem(me + mp - step, mp)), *sems)
        leaving.start()
        copies.append((leaving, landing))
    carries = []
    if ways:
        carries = carry_copies(carried, targets, refs[0], refs[1])
        refs = refs[2:]
    for copy in carries:
        copy.start()
    if pieces:
        weight_grad(left_ref, right_refs, *refs[:3], grad_ref, *refs[3:])
    own.wait()
    for leaving, landing in copies:
        landing.wait_recv()
    save = pltpu.make_async_copy(landed, o_ref, local.at[1])
    save.start()
    for leaving, landing in copies:
        leaving.wait_send()
    for copy in carries:
        copy.wait()
    save.wait()


def exchange(x, shape, halo, number, name, left=None, right=(), carried=()):
    mp = lax.axis_size("mp")
    anywhere = pl.BlockSpec(memory_space=pl.ANY)
    dma = pltpu.SemaphoreType.DMA
    scratch = [pltpu.VMEM(shape, x.dtype), dma((2,)), dma((mp,)), dma((mp,))]
    if carried:
        scratch += [dma((len(carried),)), dma((len(carried),))]
    outs = [jax.ShapeDtypeStruct(shape, x.dtype)]
    extra = ()
    if left is not None:
        rows, units = left.shape
        depth = right[0].shape[-1]
        outs.append(jax.ShapeDtypeStruct((units, depth), LOW))
        scratch += weight_grad_scratch(rows, depth, len(right))
        extra = (left,) + tuple(right)
    ways = tuple(way for way, _ in carried)
    extra += tuple(block for _, block in carried)
    outs += [jax.ShapeDtypeStruct(block.shape, block.dtype) for _, block in carried]
    return pl.pallas_call(
        partial(exchange_kernel, halo, len(right), ways),
        in_specs=[pl.BlockSpec(memory_space=pltpu.VMEM)] + [anywhere] * len(extra),
        out_specs=[anywhere] * len(outs),
        out_shape=outs,
        scratch_shapes=scratch,
        compiler_params=pltpu.CompilerParams(
            collective_id=number, has_side_effects=True, vmem_limit_bytes=48 * 2**20
        ),
        cost_estimate=pl.CostEstimate(flops=2**35, bytes_accessed=2**24, transcendentals=0),
        name=name,
    )(x, *extra)


def heads_out(x, number, name, left=None, right=(), carried=()):
    parts, rows_here, width = x.shape
    mp = lax.axis_size("mp")
    shape = (parts, mp, rows_here, 128)
    out, *more = exchange(x, shape, None, number, name, left, right, carried)
    return [out.reshape(parts, mp * rows_here, 128)] + more


def heads_back(x, rows_here, halo, number, name, left=None, right=(), carried=()):
    mp = lax.axis_size("mp")
    shape = (x.shape[0], rows_here + halo, mp * 128)
    return exchange(x, shape, halo, number, name, left, right, carried)


def line_blocks(place, sources, local, send, recv):
    z, core = mesh_place()
    count = lax.axis_size("mp") // 2
    out = []
    for number, (step, way, ref) in enumerate(sources):
        at = z - way * step
        there = (at >= 0) & (at < count)
        at = jnp.clip(at, 0, count - 1)
        sems = (send.at[number], recv.at[number], other_core())
        out.append(
            (
                there,
                pltpu.make_async_copy(ref, place(at, core), local.at[number]),
                wire(ref, place(at, core), *sems),
                wire(ref, place(at, 1 - core), *sems),
            )
        )
    return out


def blocks_start(blocks):
    for there, here, leaving, _ in blocks:

        @pl.when(there)
        def _(here=here, leaving=leaving):
            here.start()
            leaving.start()


def blocks_wait(blocks, local=True):
    for there, here, leaving, landing in blocks:

        @pl.when(there)
        def _(here=here, leaving=leaving, landing=landing):
            if local:
                here.wait()
            leaving.wait_send()
            landing.wait_recv()


def feed_in_kernel(up_steps, down_steps, *refs):
    second_ref, up_ref = refs[:2]
    up_sources = [(step, way, ref) for (step, way), ref in zip(up_steps, refs[2:])]
    refs = refs[2 + len(up_steps) :]
    down_sources = [(step, way, ref) for (step, way), ref in zip(down_steps, refs)]
    (
        all_ref, relu_ref, hidden_ref, down_all_ref, up_all_ref,
        rows, up, relu, hidden, down, local, outs, send, recv,
        up_local, up_send, up_recv, down_local, down_send, down_recv, *line_sems,
    ) = refs[len(down_steps) :]
    count = lax.axis_size("mp") // 2
    depth = rows.shape[3]
    units = up.shape[0]
    share = units // lax.axis_size("mp")
    lanes = (pl.ds(0, depth // 2), pl.ds(depth // 2, depth // 2))
    to_x, to_y = plane_partners()

    def line_place(ref):
        return lambda at, at_core: ref.at[
            pl.ds(pl.multiple_of((2 * at + at_core) * share, 16), share), :
        ]

    own = [pltpu.make_async_copy(second_ref.at[s], rows.at[s, 0], local.at[s]) for s in range(2)]
    weights = pltpu.make_async_copy(up_ref, up, local.at[2])
    for copy in own + [weights]:
        copy.start()
    for copy in own + [weights]:
        copy.wait()
    greet_line(True)
    up_blocks = line_blocks(line_place(up), up_sources, up_local, up_send, up_recv)
    down_blocks = line_blocks(line_place(down), down_sources, down_local, down_send, down_recv)
    down_line = LineGather(line_place(down), *line_sems)

    def remote(s, source, target, half, partner, number):
        return wire(
            rows.at[s, source, :, lanes[half]], rows.at[s, target, :, lanes[half]],
            send.at[s, number], recv.at[s, number], partner,
        )

    copies = [
        [
            remote(s, 0, 1, 0, to_x, 0),
            remote(s, 0, 2, 1, to_y, 1),
            remote(s, 0, 2, 0, to_y, 2),
            remote(s, 0, 1, 1, to_x, 3),
            remote(s, 1, 3, 0, to_y, 4),
            remote(s, 2, 3, 1, to_x, 5),
        ]
        for s in range(2)
    ]
    pending = [None, None]
    done = [0]

    def tile(s, m):
        slot = done[0] % 2
        done[0] += 1
        if pending[slot] is not None:
            for copy in pending[slot]:
                copy.wait()

        def one(at, carry):
            columns = pl.ds(pl.multiple_of(at * CHUNK, CHUNK), CHUNK)
            kept = jnp.maximum(dot_nt(rows[s, m], up[columns, :]), 0.0)
            relu[slot, :, columns] = kept
            hidden[slot, :, columns] = (kept * kept).astype(LOW)
            return carry

        lax.fori_loop(0, units // CHUNK, one, 0)
        pending[slot] = [
            pltpu.make_async_copy(relu.at[slot], relu_ref.at[s, m], outs.at[slot, 0]),
            pltpu.make_async_copy(hidden.at[slot], hidden_ref.at[s, m], outs.at[slot, 1]),
        ]
        for copy in pending[slot]:
            copy.start()

    for number in range(4):
        copies[0][number].start()
    blocks_start(up_blocks)
    blocks_start(down_blocks)
    blocks_wait(up_blocks)
    for there, here, _, _ in down_blocks:
        pl.when(there)(here.wait)
    down_line.start(1)
    whole_up = pltpu.make_async_copy(up, up_all_ref, local.at[2])
    whole_up.start()
    tile(0, 0)
    copies[0][0].wait_recv()
    copies[0][4].start()
    copies[0][1].wait_recv()
    copies[0][5].start()
    copies[1][0].start()
    copies[1][1].start()
    tile(1, 0)
    copies[0][3].wait_recv()
    tile(0, 1)
    copies[0][2].wait_recv()
    copies[1][2].start()
    copies[1][3].start()
    tile(0, 2)
    down_line.arrive(1)
    if count > 2:
        down_line.start(2)
    copies[1][0].wait_recv()
    copies[1][4].start()
    copies[1][1].wait_recv()
    copies[1][5].start()
    copies[0][4].wait_recv()
    copies[0][5].wait_recv()
    tile(0, 3)
    blocks_wait(down_blocks, local=False)
    for step in range(3, count):
        down_line.arrive(step - 1)
        down_line.start(step)
    copies[1][3].wait_recv()
    tile(1, 1)
    copies[1][2].wait_recv()
    tile(1, 2)
    copies[1][4].wait_recv()
    copies[1][5].wait_recv()
    gathered = pltpu.make_async_copy(rows, all_ref, local.at[3])
    gathered.start()
    tile(1, 3)
    if count > 2:
        down_line.arrive(count - 1)
    down_line.finish(range(1, count), False)
    whole_down = pltpu.make_async_copy(down, down_all_ref, local.at[0])
    whole_down.start()
    for slot in pending:
        for copy in slot:
            copy.wait()
    for s in range(2):
        for copy in copies[s]:
            copy.wait_send()
    gathered.wait()
    whole_up.wait()
    whole_down.wait()


def feed_in(second, up_early, up_late, down_blocks):
    rows_here, depth = second.shape[1:]
    units = up_early.shape[0]
    anywhere = pl.BlockSpec(memory_space=pl.ANY)
    dma = pltpu.SemaphoreType.DMA
    return pl.pallas_call(
        partial(feed_in_kernel, tuple(up_late), tuple(down_blocks)),
        in_specs=[anywhere] * (2 + len(up_late) + len(down_blocks)),
        out_specs=[anywhere] * 5,
        out_shape=[
            jax.ShapeDtypeStruct((2, 4, rows_here, depth), LOW),
            jax.ShapeDtypeStruct((2, 4, rows_here, units), F32),
            jax.ShapeDtypeStruct((2, 4, rows_here, units), LOW),
            jax.ShapeDtypeStruct((units, depth), LOW),
            jax.ShapeDtypeStruct((units, depth), LOW),
        ],
        scratch_shapes=[
            pltpu.VMEM((2, 4, rows_here, depth), LOW),
            pltpu.VMEM((units, depth), LOW),
            pltpu.VMEM((2, rows_here, units), F32),
            pltpu.VMEM((2, rows_here, units), LOW),
            pltpu.VMEM((units, depth), LOW),
            dma((4,)),
            dma((2, 2)),
            dma((2, 6)),
            dma((2, 6)),
        ]
        + [dma((len(up_late),))] * 3
        + [dma((len(down_blocks),))] * 3
        + line_semaphores(lax.axis_size("mp") // 2),
        compiler_params=pltpu.CompilerParams(
            collective_id=1, has_side_effects=True, vmem_limit_bytes=VMEM_LIMIT
        ),
        cost_estimate=pl.CostEstimate(
            flops=2 * 8 * rows_here * depth * units * 3,
            bytes_accessed=60 * 2**20,
            transcendentals=0,
        ),
        name="feed_in",
    )(second, up_early, *up_late.values(), *down_blocks.values())


def piece_copies(pieces, s, m, target, sems):
    half = target.shape[-1] // 2
    if m == 0:
        return [pltpu.make_async_copy(pieces[0].at[s], target, sems.at[0])]
    return [
        pltpu.make_async_copy(
            pieces[2 * m - 1 + side].at[s], target.at[:, pl.ds(side * half, half)], sems.at[side]
        )
        for side in range(2)
    ]


def feed_out_kernel(
    cot_0, cot_1, cot_2, cot_3, cot_4, cot_5, cot_6, relu_ref, hidden_ref, up_ref, down_ref,
    grad_ref, feed_x0_ref, feed_x1_ref, feed_y0_ref, feed_y1_ref, keep_a_ref, keep_b_ref, back_ref,
    up, down, cot, relu, grad, part, arrived, feed, result, local, loads, outs, send, recv,
):
    units, depth = up.shape
    half = depth // 2
    lanes = (pl.ds(0, half), pl.ds(half, half))
    to_x, to_y = plane_partners()
    weights = [
        pltpu.make_async_copy(down_ref, down, local.at[0]),
        pltpu.make_async_copy(up_ref, up, local.at[1]),
    ]
    order = [(s, m) for s in range(2) for m in (3, 1, 2, 0)]
    feed_x_refs, feed_y_refs = (feed_x0_ref, feed_x1_ref), (feed_y0_ref, feed_y1_ref)
    pieces = (cot_0, cot_1, cot_2, cot_3, cot_4, cot_5, cot_6)

    def load(at):
        s, m = order[at]
        slot = at % 2
        return piece_copies(pieces, s, m, cot.at[slot], loads.at[slot]) + [
            pltpu.make_async_copy(relu_ref.at[s, m], relu.at[slot], loads.at[slot, 2]),
        ]

    for copy in load(0) + weights:
        copy.start()
    greet([to_x, to_y])
    for copy in weights:
        copy.wait()

    def remote(s, source, number, side, partner):
        return pltpu.make_async_remote_copy(
            src_ref=part.at[s, source, :, lanes[side]],
            dst_ref=arrived.at[s, number],
            send_sem=send.at[s, number],
            recv_sem=recv.at[s, number],
            device_id=partner,
            device_id_type=MESH,
        )

    copies = [
        [
            remote(s, 1, 0, 0, to_x),
            remote(s, 3, 1, 0, to_x),
            remote(s, 2, 2, 1, to_y),
            remote(s, 3, 3, 1, to_y),
            remote(s, 2, 4, 0, to_y),
            remote(s, 1, 5, 1, to_x),
        ]
        for s in range(2)
    ]
    saving = [None, None]

    def tile(at):
        s, m = order[at]
        slot = at % 2
        for copy in load(at):
            copy.wait()
        if at + 1 < len(order):
            for copy in load(at + 1):
                copy.start()
        if saving[slot] is not None:
            saving[slot].wait()

        def back(step, carry):
            columns = pl.ds(pl.multiple_of(step * CHUNK, CHUNK), CHUNK)
            product = dot_nt(cot[slot], down[columns, :])
            grad[slot, :, columns] = (product * 2.0 * relu[slot, :, columns]).astype(LOW)
            return carry

        lax.fori_loop(0, units // CHUNK, back, 0)
        saving[slot] = pltpu.make_async_copy(grad.at[slot], grad_ref.at[s, m], outs.at[slot])
        saving[slot].start()

        def through(step, carry):
            columns = pl.ds(pl.multiple_of(step * CHUNK, CHUNK), CHUNK)
            part[s, m, :, columns] = dot(grad[slot], up[:, columns]).astype(LOW)
            return carry

        lax.fori_loop(0, depth // CHUNK, through, 0)

    def second_leg(s):
        copies[s][1].wait_recv()
        part[s, 2, :, lanes[0]] = (
            part[s, 2, :, lanes[0]].astype(F32) + arrived[s, 1].astype(F32)
        ).astype(LOW)
        copies[s][4].start()
        copies[s][3].wait_recv()
        part[s, 1, :, lanes[1]] = (
            part[s, 1, :, lanes[1]].astype(F32) + arrived[s, 3].astype(F32)
        ).astype(LOW)
        copies[s][5].start()

    def finish(s):
        for side, near, last in ((0, 0, 4), (1, 2, 5)):
            copies[s][near].wait_recv()
            copies[s][last].wait_recv()
            result[:, lanes[side]] = (
                part[s, 0, :, lanes[side]].astype(F32)
                + arrived[s, near].astype(F32)
                + arrived[s, last].astype(F32)
            )
        done = pltpu.make_async_copy(result, back_ref.at[s], local.at[2])
        done.start()
        return done

    def send_after(at):
        s, m = order[at]
        for number in {3: (1, 3), 1: (0,), 2: (2,), 0: ()}[m]:
            copies[s][number].start()

    for at in range(5):
        tile(at)
        send_after(at)
    second_leg(0)
    for at in range(5, 8):
        tile(at)
        send_after(at)
    done = finish(0)

    feeding = [None, None]

    def feed_load(at):
        s, m = order[at]
        return pltpu.make_async_copy(hidden_ref.at[s, m], cot.at[at % 2], loads.at[at % 2, 0])

    def feed_tile(at):
        s, m = order[at]
        slot = at % 2
        feed_load(at).wait()
        if at + 1 < len(order):
            feed_load(at + 1).start()
        if feeding[slot] is not None:
            for copy in feeding[slot]:
                copy.wait()

        def one(step, carry):
            columns = pl.ds(pl.multiple_of(step * CHUNK, CHUNK), CHUNK)
            feed[slot, :, columns] = dot(cot[slot], down[:, columns]).astype(LOW)
            return carry

        lax.fori_loop(0, depth // CHUNK, one, 0)
        targets = (
            (keep_a_ref.at[s, 0], feed_x_refs[s].at[0], keep_a_ref.at[s, 1], feed_x_refs[s].at[1])[m],
            (keep_b_ref.at[s, 0], keep_b_ref.at[s, 1], feed_y_refs[s].at[0], feed_y_refs[s].at[1])[m],
        )
        feeding[slot] = [
            pltpu.make_async_copy(feed.at[slot, :, lanes[side]], target, outs.at[2 + 2 * slot + side])
            for side, target in enumerate(targets)
        ]
        for copy in feeding[slot]:
            copy.start()

    feed_load(0).start()
    for at in range(2):
        feed_tile(at)
    second_leg(1)
    for at in range(2, 8):
        feed_tile(at)
    done.wait()
    finish(1).wait()
    for slot in range(2):
        saving[slot].wait()
        for copy in feeding[slot]:
            copy.wait()
    for s in range(2):
        for number in range(6):
            copies[s][number].wait_send()


def feed_out(cot_pieces, relu, hidden, up_all, down_all):
    rows_here, units = relu.shape[2:]
    depth = up_all.shape[1]
    anywhere = pl.BlockSpec(memory_space=pl.ANY)
    return pl.pallas_call(
        feed_out_kernel,
        in_specs=[anywhere] * 11,
        out_specs=[anywhere] * 8,
        out_shape=[
            jax.ShapeDtypeStruct((2, 4, rows_here, units), LOW),
        ]
        + [jax.ShapeDtypeStruct((2, rows_here, depth // 2), LOW)] * 4
        + [jax.ShapeDtypeStruct((2, 2, rows_here, depth // 2), LOW)] * 2
        + [
            jax.ShapeDtypeStruct((2, rows_here, depth), F32),
        ],
        scratch_shapes=[
            pltpu.VMEM((units, depth), LOW),
            pltpu.VMEM((units, depth), LOW),
            pltpu.VMEM((2, rows_here, depth), LOW),
            pltpu.VMEM((2, rows_here, units), F32),
            pltpu.VMEM((2, rows_here, units), LOW),
            pltpu.VMEM((2, 4, rows_here, depth), LOW),
            pltpu.VMEM((2, 6, rows_here, depth // 2), LOW),
            pltpu.VMEM((2, rows_here, depth), LOW),
            pltpu.VMEM((rows_here, depth), F32),
            pltpu.SemaphoreType.DMA((3,)),
            pltpu.SemaphoreType.DMA((2, 3)),
            pltpu.SemaphoreType.DMA((6,)),
            pltpu.SemaphoreType.DMA((2, 6)),
            pltpu.SemaphoreType.DMA((2, 6)),
        ],
        compiler_params=pltpu.CompilerParams(
            collective_id=2, has_side_effects=True, vmem_limit_bytes=VMEM_LIMIT
        ),
        cost_estimate=pl.CostEstimate(
            flops=2 * 8 * rows_here * depth * units * 4,
            bytes_accessed=60 * 2**20,
            transcendentals=0,
        ),
        name="feed_out",
    )(*cot_pieces, relu, hidden, up_all, down_all)


def finish_kernel(
    ways, qk_ref, v_ref, out_ref, norms_ref, taps_ref, *refs
):
    carried, refs = list(zip(ways, refs[: len(ways)])), refs[len(ways) :]
    joint_ref, norms_sum_ref, taps_sum_ref = refs[:3]
    targets, refs = refs[3 : 3 + len(ways)], refs[3 + len(ways) :]
    (
    acc, got, plane_in, line_in, gathered, norms_all, taps_all, norms_dp, taps_dp,
    local, swap_send, swap_recv, plane_send_sem, plane_recv_sem, line_send_sem, line_recv_sem,
    gather_send, gather_recv, small_send, small_recv, carry_send, carry_recv,
    ) = refs
    mp = lax.axis_size("mp")
    dp = lax.axis_index("dp")
    me = lax.axis_index("mp")
    z, core = mesh_place()
    count = mp // 2
    depth = acc.shape[3]
    half = depth // 2
    lanes = (pl.ds(0, half), pl.ds(half, half))
    to_x, to_y = plane_partners()
    dp_x = dp + 1 - 2 * lax.rem(dp, 2)
    dp_y = dp + 2 - 4 * (dp // 2)
    dp_xy = dp_x + 2 - 4 * (dp_x // 2)
    parts = (qk_ref, v_ref, out_ref)
    spans = (pl.ds(0, HD // 2), pl.ds(HD // 2, HD // 4), pl.ds(3 * HD // 4, HD // 4))
    loads = [
        pltpu.make_async_copy(part.at[:, core], acc.at[:, :, span, :], local.at[at])
        for at, (part, span) in enumerate(zip(parts, spans))
    ]
    for copy in loads:
        copy.start()

    barrier = pltpu.get_barrier_semaphore()
    for step in range(1, mp):
        pl.semaphore_signal(
            barrier, inc=1, device_id={"mp": lax.rem(me + step, mp)}, device_id_type=MESH
        )
    for step in range(1, 4):
        pl.semaphore_signal(
            barrier, inc=1, device_id={"dp": lax.rem(dp + step, 4)}, device_id_type=MESH
        )
    pl.semaphore_wait(barrier, mp + 2)

    swaps = [
        [
            wire(
                part.at[:, 1 - core, quarter], got.at[:, quarter, span, :],
                swap_send.at[at, number], swap_recv.at[at, number], other_core(),
            )
            for at, (part, span) in enumerate(zip(parts, spans))
        ]
        for number, quarter in enumerate((dp_xy, dp_x, dp_y, dp))
    ]
    for group in swaps:
        for copy in group:
            copy.start()

    def small(axis, at, others, source, target, number, first):
        out = []
        for step in range(1, others):
            to = lax.rem(at + step, others)
            frm = lax.rem(at + others - step, others)
            sems = (small_send.at[number, step], small_recv.at[number, step], {axis: to})
            out.append((wire(source(to), target.at[at], *sems), wire(source(to), target.at[frm], *sems)))
        return out

    own_small = [
        pltpu.make_async_copy(norms_ref, norms_all.at[me], local.at[3]),
        pltpu.make_async_copy(taps_ref.at[me], taps_all.at[me], local.at[4]),
    ]
    for copy in own_small:
        copy.start()
    over_mp = small("mp", me, mp, lambda to: norms_ref, norms_all, 0, None) + small(
        "mp", me, mp, lambda to: taps_ref.at[to], taps_all, 1, None
    )
    for leaving, _ in over_mp:
        leaving.start()

    def add(quarter, side, number):
        acc[:, quarter, :, lanes[side]] = (
            acc[:, quarter, :, lanes[side]].astype(F32) + plane_in[number].astype(F32)
        ).astype(LOW)

    def add_core(number, quarter):
        for copy in swaps[number]:
            copy.wait_recv()
        acc[:, quarter] = (acc[:, quarter].astype(F32) + got[:, quarter].astype(F32)).astype(LOW)

    def plane(quarter, side, partner, number):
        return wire(
            acc.at[:, quarter, :, lanes[side]], plane_in.at[number],
            plane_send_sem.at[number], plane_recv_sem.at[number], partner,
        )

    sends = [
        plane(dp_x, 0, to_x, 0),
        plane(dp_xy, 0, to_x, 1),
        plane(dp_y, 1, to_y, 2),
        plane(dp_xy, 1, to_y, 3),
        plane(dp_y, 0, to_y, 4),
        plane(dp_x, 1, to_x, 5),
    ]
    for copy in loads:
        copy.wait()
    add_core(0, dp_xy)
    sends[1].start()
    sends[3].start()
    add_core(1, dp_x)
    sends[0].start()
    add_core(2, dp_y)
    sends[2].start()
    add_core(3, dp)
    for _, landing in over_mp:
        landing.wait_recv()
    for copy in own_small:
        copy.wait()
    norms_dp[dp] = jnp.sum(norms_all[...], axis=0)
    taps_dp[dp] = jnp.sum(taps_all[...], axis=0)
    over_dp = small("dp", dp, 4, lambda to: norms_dp.at[dp], norms_dp, 2, None) + small(
        "dp", dp, 4, lambda to: taps_dp.at[dp], taps_dp, 3, None
    )
    for leaving, _ in over_dp:
        leaving.start()
    sends[1].wait_recv()
    add(dp_y, 0, 1)
    sends[4].start()
    sends[3].wait_recv()
    add(dp_x, 1, 3)
    sends[5].start()
    sends[0].wait_recv()
    add(dp, 0, 0)
    sends[2].wait_recv()
    add(dp, 1, 2)
    sends[4].wait_recv()
    add(dp, 0, 4)
    sends[5].wait_recv()
    add(dp, 1, 5)

    carries = carry_copies(carried, targets, carry_send, carry_recv)
    for copy in carries:
        copy.start()

    def line(step):
        out = []
        for way, turn in enumerate((1, -1)):
            target = z + turn * (count - step)
            far = z + turn
            lands = far - 2 * turn + turn * (count - step)
            sends = (target >= 0) & (target < count)
            receives = (lands >= 0) & (lands < count) & (z - turn >= 0) & (z - turn < count)
            at = jnp.clip(target, 0, count - 1)
            to = jnp.clip(lands, 0, count - 1)
            copy = wire(
                acc.at[at, dp], line_in.at[way, step - 1],
                line_send_sem.at[way, step - 1], line_recv_sem.at[way, step - 1],
                line_partner(z, turn),
            )
            out.append((sends, receives, to, copy))
        return out

    for step in range(1, count):
        legs = line(step)
        for sends_now, _, _, copy in legs:
            pl.when(sends_now)(copy.start)
        for way, (_, receives, to, copy) in enumerate(legs):

            @pl.when(receives)
            def _(to=to, copy=copy, way=way):
                copy.wait_recv()
                acc[to, dp] = (
                    acc[to, dp].astype(F32) + line_in[way, step - 1].astype(F32)
                ).astype(LOW)

    gathered[dp] = acc[z, dp]

    def gather(quarter, side, partner, number):
        block = gathered.at[quarter, :, lanes[side]]
        return wire(block, block, gather_send.at[number], gather_recv.at[number], partner)

    leaving = [
        gather(dp, 0, to_x, 0), gather(dp, 1, to_y, 1), gather(dp, 0, to_y, 2), gather(dp, 1, to_x, 3),
        gather(dp_x, 0, to_y, 4), gather(dp_y, 1, to_x, 5),
    ]
    landing = [
        gather(dp_x, 0, to_x, 0), gather(dp_y, 1, to_y, 1), gather(dp_y, 0, to_y, 2), gather(dp_x, 1, to_x, 3),
        gather(dp_xy, 0, to_y, 4), gather(dp_xy, 1, to_x, 5),
    ]
    for number in range(4):
        leaving[number].start()
    for _, landed in over_dp:
        landed.wait_recv()
    norms_sum_ref[...] = jnp.sum(norms_dp[...], axis=0)
    taps_sum_ref[...] = jnp.sum(taps_dp[...], axis=0)
    landing[0].wait_recv()
    leaving[4].start()
    landing[1].wait_recv()
    leaving[5].start()
    for number in range(2, 6):
        landing[number].wait_recv()
    save = pltpu.make_async_copy(gathered, joint_ref, local.at[5])
    save.start()
    for group in swaps:
        for copy in group:
            copy.wait_send()
    for copy in sends:
        copy.wait_send()
    for step in range(1, count):
        for sends_now, _, _, copy in line(step):
            pl.when(sends_now)(copy.wait_send)
    for copy in leaving:
        copy.wait_send()
    for copy, _ in over_mp + over_dp:
        copy.wait_send()
    for copy in carries:
        copy.wait()
    save.wait()


def finish(qk, v, out, norms, taps, carried):
    mp = lax.axis_size("mp")
    count = mp // 2
    depth = qk.shape[-1]
    anywhere = pl.BlockSpec(memory_space=pl.ANY)
    vmem = pl.BlockSpec(memory_space=pltpu.VMEM)
    dma = pltpu.SemaphoreType.DMA
    return pl.pallas_call(
        partial(finish_kernel, tuple(way for way, _ in carried)),
        in_specs=[anywhere] * 3 + [vmem] * 2 + [anywhere] * len(carried),
        out_specs=[anywhere, vmem, vmem] + [anywhere] * len(carried),
        out_shape=[
            jax.ShapeDtypeStruct((4, HD, depth), LOW),
            jax.ShapeDtypeStruct(norms.shape, F32),
            jax.ShapeDtypeStruct(taps.shape[1:], F32),
        ]
        + [jax.ShapeDtypeStruct(block.shape, block.dtype) for _, block in carried],
        scratch_shapes=[
            pltpu.VMEM((count, 4, HD, depth), LOW),
            pltpu.VMEM((count, 4, HD, depth), LOW),
            pltpu.VMEM((6, count, HD, depth // 2), LOW),
            pltpu.VMEM((2, count, HD, depth), LOW),
            pltpu.VMEM((4, HD, depth), LOW),
            pltpu.VMEM((mp,) + norms.shape, F32),
            pltpu.VMEM(taps.shape, F32),
            pltpu.VMEM((4,) + norms.shape, F32),
            pltpu.VMEM((4,) + taps.shape[1:], F32),
            dma((6,)),
            dma((3, 4)),
            dma((3, 4)),
            dma((6,)),
            dma((6,)),
            dma((2, count)),
            dma((2, count)),
            dma((6,)),
            dma((6,)),
            dma((4, mp)),
            dma((4, mp)),
            dma((len(carried),)),
            dma((len(carried),)),
        ],
        compiler_params=pltpu.CompilerParams(
            collective_id=8, has_side_effects=True, vmem_limit_bytes=VMEM_LIMIT
        ),
        cost_estimate=pl.CostEstimate(flops=2**36, bytes_accessed=2**26, transcendentals=0),
        name="finish",
    )(qk, v, out, norms, taps, *(block for _, block in carried))


def plane_send(block, mask):
    return lax.ppermute(block, "dp", [(d, d ^ mask) for d in range(lax.axis_size("dp"))])


def plane_gather_begin(block):
    half = block.shape[-1] // 2
    one, two = block[..., :half], block[..., half:]
    return plane_send(one, 1), plane_send(two, 2), plane_send(one, 2), plane_send(two, 1)


def plane_gather_end(block, legs):
    one_x, two_y, one_y, two_x = legs
    return plane_send(one_x, 2), plane_send(two_y, 1)


def plane_blocks(block, legs, last):
    one_x, two_y, one_y, two_x = legs
    return [
        block,
        jnp.concatenate([one_x, two_x], axis=-1),
        jnp.concatenate([one_y, two_y], axis=-1),
        jnp.concatenate(last, axis=-1),
    ]


def plane_order(blocks, axis):
    me = lax.axis_index("dp")
    stacked = jnp.stack(blocks, axis=0)
    return jnp.concatenate(
        [lax.dynamic_index_in_dim(stacked, me ^ d, 0, keepdims=False) for d in range(4)], axis=axis
    )


def line_step(blocks, step):
    count = lax.axis_size("mp") // 2
    up = [(2 * z + c, 2 * z + 2 + c) for z in range(step - 1, count - 1) for c in range(2)]
    down = [(2 * z + c, 2 * z - 2 + c) for z in range(1, count - step + 1) for c in range(2)]
    return lax.ppermute(blocks[0], "mp", up), lax.ppermute(blocks[1], "mp", down)


def per_device(
    inputs,
    cotangent,
    short_lengths,
    long_lengths,
    norm1_gain,
    norm1_bias,
    query_weight,
    key_weight,
    value_weight,
    query_kernel,
    key_kernel,
    value_kernel,
    out_weight,
    norm2_gain,
    norm2_bias,
    up_weight,
    down_weight,
):
    rows_here = inputs.shape[1]
    width = inputs.shape[2]
    mp = lax.axis_size("mp")
    dp = lax.axis_size("dp")
    me_dp = lax.axis_index("dp")
    me_mp = lax.axis_index("mp")
    group = rows_here * mp
    hidden_here = up_weight.shape[1]
    share = hidden_here // dp

    starts = jnp.stack(
        [document_starts(short_lengths[0], group), document_starts(long_lengths[0], group)]
    )
    rows = inputs.astype(F32)

    def quarters(weight):
        return weight.reshape(4, weight.shape[0] // 4, width)

    qk_own = jnp.concatenate([query_weight, key_weight], axis=1).T
    up_own = lax.dynamic_slice_in_dim(up_weight, me_dp * share, share, 1).T
    down_own = lax.dynamic_slice_in_dim(down_weight, me_dp * share, share, 0)
    taps_own = jnp.pad(
        jnp.concatenate([query_kernel, key_kernel, value_kernel], axis=1), ((0, 5), (0, HD))
    )
    qk_all, v_all, out_all, taps_all, normed, halo_rows, up_early = prepare(
        inputs, norm1_gain, norm1_bias, quarters(qk_own), quarters(value_weight.T), quarters(out_weight), taps_own, up_own,
    )
    qk_all = qk_all.reshape(mp * 2 * HD, width)
    v_all = v_all.reshape(mp * HD, width)
    out_all = out_all.reshape(mp * HD, width)
    taps = taps_all[:, :3].transpose(1, 0, 2)
    qk_taps = taps[:, :, : 2 * HD].reshape(3, mp * 2 * HD)
    v_taps = taps[:, :, 2 * HD : 3 * HD].reshape(3, mp * HD)

    cot, qk_all, up_early, down_own = lax.optimization_barrier(
        (cotangent, qk_all, up_early, down_own)
    )
    cot_legs = plane_gather_begin(cot)
    chips = mp // 2
    late = list(range(early_steps(chips)[-1] + 1, chips))
    z = me_mp // 2

    def early_block(at):
        start = (2 * jnp.clip(at, 0, chips - 1) + me_mp % 2) * share
        return lax.dynamic_slice_in_dim(up_early, start, share, 0)

    up_late = {}
    blocks = (early_block(z - late[0] + 1), early_block(z + late[0] - 1))
    for step in late:
        blocks = line_step(blocks, step)
        up_late[step, 1], up_late[step, -1] = blocks
    normed_ext = jnp.concatenate([halo_rows, normed], axis=1)
    raw_qk = jnp.einsum("srd,cd->src", normed_ext, qk_all, preferred_element_type=F32)
    raw_v = jnp.einsum("srd,cd->src", normed_ext, v_all, preferred_element_type=F32)
    places = jnp.arange(group, dtype=jnp.int32)
    offsets = lax.dynamic_slice_in_dim(
        jnp.pad(places[None, :] - starts, ((0, 0), (0, HALO))), me_mp * rows_here, rows_here + HALO, 1
    )[:, :, None]
    here = offsets[:, :rows_here]

    def conv(raw, tap):
        return (
            tap[0] * raw[:, HALO:]
            + jnp.where(here >= 1, tap[1] * raw[:, HALO - 1 : -1], 0.0)
            + jnp.where(here >= 2, tap[2] * raw[:, HALO - 2 : -2], 0.0)
        ).astype(LOW)

    mixed_qk = conv(raw_qk, qk_taps)
    mixed_v = conv(raw_v, v_taps)

    def side_by_side(pair):
        split = pair.reshape(2, rows_here, mp, HD)
        return split.transpose(1, 2, 0, 3).reshape(1, rows_here, mp * 2 * HD)

    def apart(joint):
        split = joint.reshape(joint.shape[1], mp, 2, HD)
        return split.transpose(2, 0, 1, 3).reshape(2, joint.shape[1], mp * HD)

    mixed_qk, up_late = lax.optimization_barrier((mixed_qk, up_late))
    (mixed,) = heads_out(jnp.concatenate([mixed_qk, side_by_side(mixed_v)], axis=0), 4, "mixed_out")
    mixed, cot_legs = lax.optimization_barrier((mixed, cot_legs))
    cot_last = plane_gather_end(cot, cot_legs)
    down_blocks = {(0, 1): down_own}
    attended_head, wide, total = attend(mixed, starts)
    attended_head, cot_last = lax.optimization_barrier((attended_head, cot_last))
    one_x, two_y, one_y, two_x = cot_legs
    cot_pieces = (cot, one_x, two_x, one_y, two_y) + tuple(cot_last)
    (attended,) = heads_back(attended_head, rows_here, 0, 5, "attended_back")
    attended = apart(attended)
    middle = rows + dot(attended, out_all)
    second = layer_norm(middle, norm2_gain, norm2_bias).astype(LOW)

    second_all, relu, hidden, down_all, up_all = feed_in(second, up_early, up_late, down_blocks)
    down_part = whole_weight_grad(hidden.reshape(-1, hidden.shape[3]), cot_pieces)
    down_mine = lax.psum_scatter(down_part, "mp", scatter_dimension=0, tiled=True)
    down_part, relu = lax.optimization_barrier((down_part, relu))
    grad_pre, feed_x0, feed_x1, feed_y0, feed_y1, keep_a, keep_b, grad_second = feed_out(
        cot_pieces, relu, hidden, up_all, down_all
    )
    def norm_back(values, gain, grad):
        flat = values.reshape(-1, width)
        unused, pull = jax.vjp(layer_norm, flat, gain, norm1_bias)
        grad_rows, grad_gain, grad_shift = pull(grad.reshape(-1, width))
        return grad_rows.reshape(values.shape), grad_gain, grad_shift

    grad_middle, gain_two, shift_two = norm_back(middle, norm2_gain, grad_second)
    grad_middle = grad_middle + cotangent.astype(F32)
    branch = grad_middle.astype(LOW)
    out_part = jnp.einsum("srh,srd->hd", attended, branch, preferred_element_type=F32).astype(LOW)
    grad_attended = jnp.einsum("srd,hd->srh", branch, out_all, preferred_element_type=F32).astype(LOW)
    grad_head, up_part, x_first, y_first = heads_out(
        side_by_side(grad_attended), 6, "attended_grad_out", grad_pre.reshape(-1, hidden.shape[3]),
        (second_all.reshape(-1, width),), ((0, feed_x0), (1, feed_y0)),
    )
    up_mine = lax.psum_scatter(up_part, "mp", scatter_dimension=0, tiled=True)
    grad_head, down_mine = lax.optimization_barrier((grad_head, down_mine))
    down_legs = plane_gather_begin(down_mine)
    grad_mixed_head = attend_back(mixed, grad_head, wide, total, starts, HALO)
    grad_mixed_head, down_legs = lax.optimization_barrier((grad_mixed_head, down_legs))
    down_last = plane_gather_end(down_mine, down_legs)
    grad_mixed, x_second, y_second = heads_back(
        grad_mixed_head, rows_here, HALO, 7, "mixed_grad_back",
        carried=((0, feed_x1), (1, feed_y1)),
    )
    grad_mixed, down_last = lax.optimization_barrier((grad_mixed, down_last))
    down_grad = plane_order(plane_blocks(down_mine, down_legs, down_last), axis=0).astype(F32)
    x_in, y_in = jnp.stack([x_first, x_second]), jnp.stack([y_first, y_second])

    def add(left, right):
        return left.astype(F32) + right.astype(F32)

    feed_a = add(keep_a[:, 1], x_in[:, 1]).astype(LOW)
    feed_b = add(keep_b[:, 1], y_in[:, 1]).astype(LOW)
    grad_qk = grad_mixed[:2].astype(F32)
    grad_v = apart(grad_mixed[2:]).astype(F32)

    def conv_back(grad, raw, tap):
        after_one = jnp.where(offsets[:, 1 : rows_here + 1] >= 1, grad[:, 1 : rows_here + 1], 0.0)
        after_two = jnp.where(offsets[:, 2 : rows_here + 2] >= 2, grad[:, 2 : rows_here + 2], 0.0)
        own = grad[:, :rows_here]
        grad_raw = (tap[0] * own + tap[1] * after_one + tap[2] * after_two).astype(LOW)
        grad_tap = jnp.stack(
            [
                jnp.sum(own * raw[:, HALO:], axis=(0, 1)),
                jnp.sum(jnp.where(here >= 1, own, 0.0) * raw[:, HALO - 1 : -1], axis=(0, 1)),
                jnp.sum(jnp.where(here >= 2, own, 0.0) * raw[:, HALO - 2 : -2], axis=(0, 1)),
            ]
        )
        return grad_raw, grad_tap

    grad_raw_qk, grad_tap_qk = conv_back(grad_qk, raw_qk, qk_taps)
    grad_raw_v, grad_tap_v = conv_back(grad_v, raw_v, v_taps)
    grad_raw_qk, up_mine = lax.optimization_barrier((grad_raw_qk, up_mine))
    up_legs = plane_gather_begin(up_mine)
    qk_part = jnp.einsum("src,srd->cd", grad_raw_qk, normed, preferred_element_type=F32).astype(LOW)
    v_part = jnp.einsum("src,srd->cd", grad_raw_v, normed, preferred_element_type=F32).astype(LOW)
    grad_normed = dot(grad_raw_qk, qk_all) + dot(grad_raw_v, v_all)
    grad_input, gain_one, shift_one = norm_back(rows, norm1_gain, grad_normed)
    input_grads = grad_middle + grad_input

    def split_parts(part):
        return part.reshape(mp // 2, 2, 4, part.shape[0] // (4 * mp), width)

    norms = jnp.stack([gain_one, shift_one, gain_two, shift_two]).reshape(8, width // 2)
    taps_part = jnp.concatenate(
        [grad_tap_qk.reshape(3, mp, 2 * HD), grad_tap_v.reshape(3, mp, HD)], axis=2
    ).transpose(1, 0, 2)
    taps_part = jnp.pad(taps_part, ((0, 0), (0, 5), (0, HD)))
    norms, up_legs = lax.optimization_barrier((norms, up_legs))
    up_last = plane_gather_end(up_mine, up_legs)
    joint_grad, norms_sum, taps_sum, feed_a, feed_b = finish(
        split_parts(qk_part), split_parts(v_part), split_parts(out_part), norms, taps_part,
        ((1, feed_a), (0, feed_b)),
    )
    results = (
        middle
        + jnp.concatenate(
            [
                add(keep_a[:, 0], x_in[:, 0]) + feed_a.astype(F32),
                add(keep_b[:, 0], y_in[:, 0]) + feed_b.astype(F32),
            ],
            axis=2,
        )
    ).astype(LOW)
    joint_grad, up_last = lax.optimization_barrier((joint_grad, up_last))
    up_grad = plane_order(plane_blocks(up_mine, up_legs, up_last), axis=0).T.astype(F32)
    joint_grad = joint_grad.astype(F32)
    small_sum = norms_sum.reshape(4, width)
    qk_grad = joint_grad[:, : HD // 2].reshape(2 * HD, width).T
    v_grad = joint_grad[:, HD // 2 : 3 * HD // 4].reshape(HD, width).T
    out_grad = joint_grad[:, 3 * HD // 4 :].reshape(HD, width)
    taps_sum = taps_sum[:3]
    return (
        results,
        input_grads,
        small_sum[0],
        small_sum[1],
        qk_grad[:, :HD],
        qk_grad[:, HD:],
        v_grad,
        taps_sum[:, :HD],
        taps_sum[:, HD : 2 * HD],
        taps_sum[:, 2 * HD : 3 * HD],
        out_grad,
        small_sum[2],
        small_sum[3],
        up_grad,
        down_grad,
    )


def solution(mesh):
    return jax.shard_map(
        per_device,
        mesh=mesh,
        in_specs=(
            P(None, ("dp", "mp"), None),
            P(None, ("dp", "mp"), None),
            P("dp", None),
            P("dp", None),
            P(),
            P(),
            P(None, "mp"),
            P(None, "mp"),
            P(None, "mp"),
            P(None, "mp"),
            P(None, "mp"),
            P(None, "mp"),
            P("mp", None),
            P(),
            P(),
            P(None, "mp"),
            P("mp", None),
        ),
        out_specs=(
            P(None, ("dp", "mp"), None),
            P(None, ("dp", "mp"), None),
            P(),
            P(),
            P(None, "mp"),
            P(None, "mp"),
            P(None, "mp"),
            P(None, "mp"),
            P(None, "mp"),
            P(None, "mp"),
            P("mp", None),
            P(),
            P(),
            P(None, "mp"),
            P("mp", None),
        ),
        check_vma=False,
    )
```

```python
from functools import partial

import jax
import jax.numpy as jnp
from jax import lax
from jax.experimental import pallas as pl
from jax.experimental.pallas import tpu as pltpu
from jax.sharding import PartitionSpec as P

HD = 64
QUERIES, KEYS = 512, 512
WIDE = 256
CHUNK = 512
VMEM_LIMIT = 62 * 1024 * 1024
MESH = pl.DeviceIdType.MESH
LOW = jnp.bfloat16
F32 = jnp.float32


def dot(left, right):
    return jnp.dot(left, right, preferred_element_type=F32)


def layer_norm(rows, gain, shift):
    row_mean = jnp.mean(rows, axis=-1, keepdims=True)
    centered = rows - row_mean
    variance = jnp.mean(centered * centered, axis=-1, keepdims=True)
    return centered * lax.rsqrt(variance + 1e-05) * gain + shift


def document_starts(lengths, count):
    ends = jnp.cumsum(lengths)
    places = jnp.arange(count, dtype=jnp.int32)
    passed = (places[:, None] >= ends[None, :]).astype(jnp.int32)
    return jnp.sum(passed * lengths[None, :], axis=1)


def allowed_pairs(start_row, key_block, query_block):
    shape = (KEYS, QUERIES)
    keys = key_block * KEYS + lax.broadcasted_iota(jnp.int32, shape, 0)
    queries = query_block * QUERIES + lax.broadcasted_iota(jnp.int32, (1, QUERIES), 1)
    return (keys <= queries) & (keys >= start_row)


def key_blocks(first_ref, s, step):
    return first_ref[s, step], ((step + 1) * QUERIES + KEYS - 1) // KEYS


def attend_kernel(
    first_ref, start_ref, qk_ref, v_ref, out_ref, wide_ref, total_ref, values_t
):
    s, step = pl.program_id(0), pl.program_id(1)

    @pl.when(step == 0)
    def _():
        def turn(at, carry):
            rows = pl.ds(pl.multiple_of(at * KEYS, KEYS), KEYS)
            both = v_ref[0, rows, :].T
            values_t[at] = jnp.where(s == 0, both[:HD], both[HD:])
            return carry

        lax.fori_loop(0, values_t.shape[0], turn, 0)

    here = pl.ds(pl.multiple_of(step * QUERIES, QUERIES), QUERIES)
    query_t = (qk_ref[0, here, 0:HD] * HD ** (-0.5)).astype(LOW).T
    start_row = start_ref[0]

    def one(at, carry):
        top, summed, acc = carry
        rows = pl.ds(pl.multiple_of(at * KEYS, KEYS), KEYS)
        scores = dot(qk_ref[0, rows, HD : 2 * HD], query_t)
        scores = jnp.where(allowed_pairs(start_row, at, step), scores, -1e30)
        new_top = jnp.maximum(top, jnp.max(scores, axis=0, keepdims=True))
        powered = jnp.exp(scores - new_top)
        shrink = jnp.exp(top - new_top)
        summed = summed * shrink + jnp.sum(powered, axis=0, keepdims=True)
        acc = acc * shrink + dot(values_t[at], powered.astype(LOW))
        return new_top, summed, acc

    top, summed, acc = lax.fori_loop(
        *key_blocks(first_ref, s, step),
        one,
        (
            jnp.full((1, QUERIES), -1e30, F32),
            jnp.zeros((1, QUERIES), F32),
            jnp.zeros((HD, QUERIES), F32),
        ),
    )
    result = acc / summed
    wide_ref[0] = result
    total_ref[0] = top + jnp.log(summed)
    low = result.T.astype(LOW)

    @pl.when(s == 0)
    def _():
        out_ref[0, here, 0:HD] = low

    @pl.when(s == 1)
    def _():
        out_ref[0, here, HD : 2 * HD] = low


def attend(mixed, starts):
    group = mixed.shape[1]
    steps = group // QUERIES
    row = pl.BlockSpec((1, 1, QUERIES), lambda s, i, first: (s, 0, i))
    return pl.pallas_call(
        attend_kernel,
        grid_spec=pltpu.PrefetchScalarGridSpec(
            num_scalar_prefetch=1,
            grid=(2, steps),
            in_specs=[
                row,
                pl.BlockSpec((1, group, 2 * HD), lambda s, i, first: (s, 0, 0)),
                pl.BlockSpec((1, group, 2 * HD), lambda s, i, first: (2, 0, 0)),
            ],
            out_specs=[
                pl.BlockSpec((1, group, 2 * HD), lambda s, i, first: (0, 0, 0)),
                pl.BlockSpec((1, HD, QUERIES), lambda s, i, first: (s, 0, i)),
                row,
            ],
            scratch_shapes=[pltpu.VMEM((group // KEYS, HD, KEYS), LOW)],
        ),
        out_shape=[
            jax.ShapeDtypeStruct((1, group, 2 * HD), LOW),
            jax.ShapeDtypeStruct((2, HD, group), F32),
            jax.ShapeDtypeStruct((2, 1, group), F32),
        ],
        compiler_params=pltpu.CompilerParams(vmem_limit_bytes=32 * 1024 * 1024),
        cost_estimate=pl.CostEstimate(
            flops=2**34, bytes_accessed=group * 2048, transcendentals=group * group // 4
        ),
        name="attend",
    )(starts[:, ::QUERIES] // KEYS, starts[:, None, :], mixed, mixed)


def attend_back_kernel(
    first_ref, start_ref, qk_ref, v_ref, grad_ref, wide_ref, total_ref, out_ref,
    keys_t, values, grad_keys, grad_values,
):
    s, step = pl.program_id(0), pl.program_id(1)
    group = qk_ref.shape[1]

    @pl.when(step == 0)
    def _():
        def turn(at, carry):
            rows = pl.ds(pl.multiple_of(at * KEYS, KEYS), KEYS)
            keys_t[at] = qk_ref[0, rows, HD : 2 * HD].T
            both = v_ref[0, rows, :]
            values[rows, :] = jnp.where(s == 0, both[:, :HD], both[:, HD:])
            return carry

        lax.fori_loop(0, keys_t.shape[0], turn, 0)
        grad_keys[...] = jnp.zeros(grad_keys.shape, F32)
        grad_values[...] = jnp.zeros(grad_values.shape, F32)

    here = pl.ds(pl.multiple_of(step * QUERIES, QUERIES), QUERIES)
    query = (qk_ref[0, here, 0:HD] * HD ** (-0.5)).astype(LOW)
    query_t = query.T
    both = grad_ref[0]
    grad = jnp.where(s == 0, both[:, :HD], both[:, HD:])
    grad_t = grad.T
    start_row = start_ref[0]
    total = total_ref[0]
    inner = jnp.sum(grad_t.astype(F32) * wide_ref[0], axis=0, keepdims=True)

    def one(at, acc):
        rows = pl.ds(pl.multiple_of(at * KEYS, KEYS), KEYS)
        scores = dot(qk_ref[0, rows, HD : 2 * HD], query_t)
        scores = jnp.where(allowed_pairs(start_row, at, step), scores, -1e30)
        probs = jnp.exp(scores - total)
        grad_probs = dot(values[rows, :], grad_t)
        grad_scores = (probs * (grad_probs - inner)).astype(LOW)
        grad_values[rows, :] += dot(probs.astype(LOW), grad)
        grad_keys[rows, :] += dot(grad_scores, query)
        return acc + dot(keys_t[at], grad_scores)

    acc = lax.fori_loop(
        *key_blocks(first_ref, s, step), one, jnp.zeros((HD, QUERIES), F32)
    )
    out_ref[s, here, 0:HD] = (acc * HD ** (-0.5)).T.astype(out_ref.dtype)

    @pl.when(step == pl.num_programs(1) - 1)
    def _():
        out_ref[s, 0:group, HD : 2 * HD] = grad_keys[...].astype(out_ref.dtype)
        out_ref[s, group:, :] = jnp.zeros((out_ref.shape[1] - group, 2 * HD), out_ref.dtype)

        @pl.when(s == 0)
        def _():
            out_ref[2, 0:group, 0:HD] = grad_values[...].astype(out_ref.dtype)

        @pl.when(s == 1)
        def _():
            out_ref[2, 0:group, HD : 2 * HD] = grad_values[...].astype(out_ref.dtype)
            out_ref[2, group:, :] = jnp.zeros((out_ref.shape[1] - group, 2 * HD), out_ref.dtype)


def attend_back(mixed, grad, wide, total, starts, halo):
    group = mixed.shape[1]
    steps = group // QUERIES
    row = pl.BlockSpec((1, 1, QUERIES), lambda s, i, first: (s, 0, i))
    return pl.pallas_call(
        attend_back_kernel,
        grid_spec=pltpu.PrefetchScalarGridSpec(
            num_scalar_prefetch=1,
            grid=(2, steps),
            in_specs=[
                row,
                pl.BlockSpec((1, group, 2 * HD), lambda s, i, first: (s, 0, 0)),
                pl.BlockSpec((1, group, 2 * HD), lambda s, i, first: (2, 0, 0)),
                pl.BlockSpec((1, QUERIES, 2 * HD), lambda s, i, first: (0, i, 0)),
                pl.BlockSpec((1, HD, QUERIES), lambda s, i, first: (s, 0, i)),
                row,
            ],
            out_specs=pl.BlockSpec((3, group + halo, 2 * HD), lambda s, i, first: (0, 0, 0)),
            scratch_shapes=[
                pltpu.VMEM((group // KEYS, HD, KEYS), LOW),
                pltpu.VMEM((group, HD), LOW),
                pltpu.VMEM((group, HD), F32),
                pltpu.VMEM((group, HD), F32),
            ],
        ),
        out_shape=jax.ShapeDtypeStruct((3, group + halo, 2 * HD), LOW),
        compiler_params=pltpu.CompilerParams(vmem_limit_bytes=32 * 1024 * 1024),
        cost_estimate=pl.CostEstimate(
            flops=2**35, bytes_accessed=group * 2048, transcendentals=group * group // 4
        ),
        name="attend_back",
    )(starts[:, ::QUERIES] // KEYS, starts[:, None, :], mixed, mixed, grad, wide, total)


def plane_partners():
    me = lax.axis_index("dp")
    return {"dp": me + 1 - 2 * lax.rem(me, 2)}, {"dp": me + 2 - 4 * (me // 2)}


def dot_nt(left, right):
    return lax.dot_general(left, right, (((1,), (1,)), ((), ())), preferred_element_type=F32)


def mesh_place():
    me = lax.axis_index("mp")
    return me // 2, lax.rem(me, 2)


def wire(source, target, send, recv, partner):
    return pltpu.make_async_remote_copy(
        src_ref=source,
        dst_ref=target,
        send_sem=send,
        recv_sem=recv,
        device_id=partner,
        device_id_type=MESH,
    )


def line_partner(z, step):
    _, core = mesh_place()
    return {"mp": 2 * (z + step) + core}


def other_core():
    z, core = mesh_place()
    return {"mp": 2 * z + 1 - core}


def greet(partners):
    barrier = pltpu.get_barrier_semaphore()
    for partner in partners:
        pl.semaphore_signal(barrier, inc=1, device_id=partner, device_id_type=MESH)
    pl.semaphore_wait(barrier, len(partners))


def greet_line(with_plane):
    z, _ = mesh_place()
    count = lax.axis_size("mp") // 2
    barrier = pltpu.get_barrier_semaphore()
    partners = [other_core()]
    if with_plane:
        partners += list(plane_partners())
    for partner in partners:
        pl.semaphore_signal(barrier, inc=1, device_id=partner, device_id_type=MESH)
    for turn in (1, -1):

        @pl.when((z + turn >= 0) & (z + turn < count))
        def _(turn=turn):
            pl.semaphore_signal(barrier, inc=1, device_id=line_partner(z, turn), device_id_type=MESH)

    near = jnp.where(z > 0, 1, 0) + jnp.where(z < count - 1, 1, 0)
    pl.semaphore_wait(barrier, near + len(partners))


class LineGather:
    def __init__(self, place, send, recv, swap_send, swap_recv):
        self.z, self.core = mesh_place()
        self.count = lax.axis_size("mp") // 2
        self.place, self.send, self.recv = place, send, recv
        self.swap_send, self.swap_recv = swap_send, swap_recv

    def copies(self, step):
        z, count = self.z, self.count
        out = []
        for way, turn in enumerate((1, -1)):
            leaves = z - turn * (step - 1)
            lands = z - turn * step
            far = z + turn
            sends = (leaves >= 0) & (leaves < count) & (far >= 0) & (far < count)
            receives = (lands >= 0) & (lands < count)
            at = jnp.clip(leaves, 0, count - 1)
            to = jnp.clip(lands, 0, count - 1)
            sems = (self.send.at[way, step - 1], self.recv.at[way, step - 1], line_partner(z, turn))
            leaving = wire(self.place(at, self.core), self.place(at, self.core), *sems)
            landing = wire(self.place(to, self.core), self.place(to, self.core), *sems)
            out.append((sends, leaving, receives, landing, to))
        return out

    def start(self, step):
        for sends, leaving, _, _, _ in self.copies(step):
            pl.when(sends)(leaving.start)

    def swap(self, at, number):
        sems = (self.swap_send.at[number], self.swap_recv.at[number], other_core())
        leaving = wire(self.place(at, self.core), self.place(at, self.core), *sems)
        landing = wire(self.place(at, 1 - self.core), self.place(at, 1 - self.core), *sems)
        return leaving, landing

    def swap_own(self):
        self.swap(self.z, 0)[0].start()

    def arrive(self, step):
        for way, (_, _, receives, landing, at) in enumerate(self.copies(step)):

            @pl.when(receives)
            def _(landing=landing, at=at, way=way):
                landing.wait_recv()
                self.swap(at, 1 + 2 * (step - 1) + way)[0].start()

    def swapped(self, at, number):
        leaving, landing = self.swap(at, number)
        leaving.wait_send()
        landing.wait_recv()

    def finish(self, steps, own):
        if own:
            self.swapped(self.z, 0)
        for step in steps:
            for way, (sends, leaving, receives, _, at) in enumerate(self.copies(step)):
                pl.when(sends)(leaving.wait_send)
                pl.when(receives)(
                    lambda at=at, way=way, step=step: self.swapped(at, 1 + 2 * (step - 1) + way)
                )


def line_semaphores(count):
    return [
        pltpu.SemaphoreType.DMA((2, count)),
        pltpu.SemaphoreType.DMA((2, count)),
        pltpu.SemaphoreType.DMA((2 * count,)),
        pltpu.SemaphoreType.DMA((2 * count,)),
    ]


def early_steps(count):
    return range(1, count // 2 + 1)


HALO = 16


def weight_grad(left_ref, pieces, whole, tiles, outs, out_ref, load, tile_sem, out_sem):
    wide = tiles.shape[2]
    steps = left_ref.shape[1] // wide
    if len(pieces) == 1:
        loading = [pltpu.make_async_copy(pieces[0], whole, load.at[0])]
    else:
        tall = whole.shape[0] // 8
        loading = []
        for s in range(2):
            for m in range(4):
                target = whole.at[pl.ds((4 * s + m) * tall, tall), :]
                loading += piece_copies(pieces, s, m, target, load.at[s, m])

    def tile(at, slot):
        columns = pl.ds(pl.multiple_of(at * wide, wide), wide)
        return pltpu.make_async_copy(left_ref.at[:, columns], tiles.at[slot], tile_sem.at[slot])

    def out(at, slot):
        rows = pl.ds(pl.multiple_of(at * wide, wide), wide)
        return pltpu.make_async_copy(outs.at[slot], out_ref.at[rows, :], out_sem.at[slot])

    for copy in loading:
        copy.start()
    tile(0, 0).start()
    for copy in loading:
        copy.wait()

    def one(at, carry):
        slot = lax.rem(at, 2)
        tile(at, slot).wait()

        @pl.when(at + 1 < steps)
        def _():
            tile(at + 1, 1 - slot).start()

        @pl.when(at >= 2)
        def _():
            out(at - 2, slot).wait()

        outs[slot] = lax.dot_general(
            tiles[slot], whole[...], (((0,), (0,)), ((), ())), preferred_element_type=F32
        ).astype(LOW)
        out(at, slot).start()
        return carry

    lax.fori_loop(0, steps, one, 0)
    out(steps - 2, lax.rem(steps - 2, 2)).wait()
    out(steps - 1, lax.rem(steps - 1, 2)).wait()


def weight_grad_scratch(rows, depth, pieces):
    dma = pltpu.SemaphoreType.DMA
    return [
        pltpu.VMEM((rows, depth), LOW),
        pltpu.VMEM((2, rows, 256), LOW),
        pltpu.VMEM((2, 256, depth), LOW),
        dma((1,)) if pieces == 1 else dma((2, 4, 2)),
        dma((2,)),
        dma((2,)),
    ]


def carry_copies(carried, targets, send, recv):
    partners = plane_partners()
    return [
        wire(ref, target, send.at[at], recv.at[at], partners[way])
        for at, ((way, ref), target) in enumerate(zip(carried, targets))
    ]


def greet_members(ways):
    mp = lax.axis_size("mp")
    me = lax.axis_index("mp")
    barrier = pltpu.get_barrier_semaphore()
    for step in range(1, mp):
        pl.semaphore_signal(
            barrier, inc=1, device_id={"mp": lax.rem(me + step, mp)}, device_id_type=MESH
        )
    partners = plane_partners() if ways else ()
    for partner in partners:
        pl.semaphore_signal(barrier, inc=1, device_id=partner, device_id_type=MESH)
    pl.semaphore_wait(barrier, mp - 1 + len(partners))


def member_copies(source, target, send, recv):
    mp = lax.axis_size("mp")
    me = lax.axis_index("mp")
    copies = []
    for step in range(1, mp):
        to = lax.rem(me + step, mp)
        sems = (send.at[step], recv.at[step], {"mp": to})
        copies.append(
            (
                wire(source(to), target(me), *sems),
                wire(source(to), target(lax.rem(me + mp - step, mp)), *sems),
            )
        )
    return copies


def head_lanes(at):
    return pl.ds(pl.multiple_of(at * 128, 128), 128)


def exchange_kernel(halo, pieces, ways, x_ref, *refs):
    count = 1 + pieces if pieces else 0
    left_ref, right_refs = (refs[0], refs[1:count]) if pieces else (None, ())
    carried = list(zip(ways, refs[count : count + len(ways)]))
    refs = refs[count + len(ways) :]
    o_ref, refs = refs[0], refs[1:]
    if pieces:
        grad_ref, refs = refs[0], refs[1:]
    targets, refs = refs[: len(ways)], refs[len(ways) :]
    landed, local, send, recv = refs[:4]
    refs = refs[4:]
    me = lax.axis_index("mp")
    if halo is None:

        def source(at):
            return x_ref.at[:, :, head_lanes(at)]

        def target(at):
            return landed.at[:, at]
    else:
        tall = o_ref.shape[1]

        def source(at):
            return x_ref.at[:, pl.ds(pl.multiple_of(at * (tall - halo), 16), tall), :]

        def target(at):
            return landed.at[:, :, head_lanes(at)]

    own = pltpu.make_async_copy(source(me), target(me), local.at[0])
    own.start()
    greet_members(ways)
    copies = member_copies(source, target, send, recv)
    for leaving, _ in copies:
        leaving.start()
    carries = []
    if ways:
        carries = carry_copies(carried, targets, refs[0], refs[1])
        refs = refs[2:]
    for copy in carries:
        copy.start()
    if pieces:
        weight_grad(left_ref, right_refs, *refs[:3], grad_ref, *refs[3:])
    own.wait()
    for leaving, landing in copies:
        landing.wait_recv()
    save = pltpu.make_async_copy(landed, o_ref, local.at[1])
    save.start()
    for leaving, landing in copies:
        leaving.wait_send()
    for copy in carries:
        copy.wait()
    save.wait()


def front_kernel(
    inputs_ref, gain_ref, shift_ref, qk_ref, v_ref, out_ref, taps_ref, up_ref, masks_ref, cot_ref,
    all_qk_ref, all_v_ref, all_out_ref, all_taps_ref, normed_ref, up_all_ref, raw_ref, o_ref, cot_x_ref, cot_y_ref,
    inputs, rows, all_qk, all_v, all_out, all_taps, up_all, raw, mixed, landed, local, *sems,
):
    mp = lax.axis_size("mp")
    dp = lax.axis_index("dp")
    me = lax.axis_index("mp")
    z, core = mesh_place()
    count = mp // 2
    rows_here, depth = inputs.shape[1:]
    halo = rows.shape[1] - rows_here
    to_x, to_y = plane_partners()
    share = up_ref.shape[0]
    owned = (qk_ref, v_ref, out_ref)
    whole = (all_qk, all_v, all_out)
    (plane_send_sem, plane_recv_sem, plane_swap_send, plane_swap_recv) = sems[:4]
    taps_send, taps_recv, halo_send, halo_recv, carry_send, carry_recv, head_send, head_recv = sems[4:12]
    line_sems = [sems[12 + 4 * part : 16 + 4 * part] for part in range(4)]

    def up_place(at, at_core):
        start = pl.multiple_of((2 * at + at_core) * share, 16)
        return up_all.at[pl.ds(start, share), :]

    def taps_place(at):
        return all_taps.at[:, :, head_lanes(at)]

    loads = [
        pltpu.make_async_copy(inputs_ref, inputs, local.at[0]),
        pltpu.make_async_copy(taps_ref, taps_place(me), local.at[1]),
        pltpu.make_async_copy(up_ref, up_place(z, core), local.at[2]),
    ] + [
        pltpu.make_async_copy(
            owned[part].at[dp], whole[part].at[z, core, dp], local.at[3 + part]
        )
        for part in range(3)
    ]
    for copy in loads:
        copy.start()
    greet_members((0, 1))
    for copy in loads[1:]:
        copy.wait()

    lines = [
        LineGather(lambda at, at_core, part=part: whole[part].at[at, at_core, dp], *line_sems[part])
        for part in range(3)
    ]
    up_line = LineGather(up_place, *line_sems[3])
    for line in lines:
        line.start(1)
    tap_copies = member_copies(lambda to: taps_ref, taps_place, taps_send, taps_recv)
    for copy, _ in tap_copies:
        copy.start()
    for line in lines:
        line.swap_own()

    loads[0].wait()
    tall = 16

    def norm(s):
        def some(at, carry):
            here = pl.ds(pl.multiple_of(at * tall, tall), tall)
            there = pl.ds(pl.multiple_of(halo + at * tall, tall), tall)
            values = inputs[s, here, :].astype(F32)
            centered = values - jnp.mean(values, axis=1, keepdims=True)
            variance = jnp.mean(centered * centered, axis=1, keepdims=True)
            rows[s, there, :] = (
                centered * lax.rsqrt(variance + 1e-05) * gain_ref[...] + shift_ref[...]
            ).astype(LOW)
            return carry

        lax.fori_loop(0, rows_here // tall, some, 0)

    norm(0)
    for step in range(1, count):
        for line in lines:
            line.arrive(step)
        if step + 1 < count:
            for line in lines:
                line.start(step + 1)

    half = depth // 2
    lanes = (pl.ds(0, half), pl.ds(half, half))
    dp_x = dp + 1 - 2 * lax.rem(dp, 2)
    dp_y = dp + 2 - 4 * (dp // 2)
    dp_xy = dp_x + 2 - 4 * (dp_x // 2)
    legs = ((0, to_x), (1, to_y), (0, to_y), (1, to_x), (0, to_y), (1, to_x))

    def plane(number, quarter):
        side, partner = legs[number]
        out = []
        for part in range(3):
            block = whole[part].at[:, core, quarter, :, lanes[side]]
            out.append(
                wire(
                    block, block, plane_send_sem.at[part, number], plane_recv_sem.at[part, number], partner
                )
            )
        return out

    leaving = [plane(number, quarter) for number, quarter in enumerate((dp, dp, dp, dp, dp_x, dp_y))]
    landing = [
        plane(number, quarter) for number, quarter in enumerate((dp_x, dp_y, dp_y, dp_x, dp_xy, dp_xy))
    ]

    def pass_on(number, at_core):
        quarter = (dp_x, dp_y, dp_xy)[number]
        out = []
        for part in range(3):
            block = whole[part].at[:, at_core, quarter]
            out.append(
                wire(
                    block, block, plane_swap_send.at[part, number], plane_swap_recv.at[part, number],
                    other_core(),
                )
            )
        return out

    def each(copies, what):
        for copy in copies:
            getattr(copy, what)()

    for number in range(4):
        each(leaving[number], "start")
    early = early_steps(count)
    up_line.start(1)
    up_line.swap_own()
    norm(1)
    own_rows = rows.at[:, pl.ds(halo, rows_here), :]
    save = pltpu.make_async_copy(own_rows, normed_ref, local.at[0])
    save.start()
    halo_copy = wire(
        rows.at[:, pl.ds(rows_here, halo), :], rows.at[:, pl.ds(0, halo), :], halo_send, halo_recv,
        {"mp": lax.rem(me + 1, mp)},
    )
    halo_copy.start()
    each(landing[0], "wait_recv")
    each(leaving[4], "start")
    each(landing[1], "wait_recv")
    each(leaving[5], "start")
    each(landing[3], "wait_recv")
    each(pass_on(0, core), "start")
    each(landing[2], "wait_recv")
    each(pass_on(1, core), "start")
    up_line.arrive(1)
    up_line.start(2)
    each(landing[4], "wait_recv")
    each(landing[5], "wait_recv")
    each(pass_on(2, core), "start")
    for step in early[1:-1]:
        up_line.arrive(step)
        up_line.start(step + 1)
    carries = [
        wire(cot_ref.at[:, :, lanes[0]], cot_x_ref, carry_send.at[0], carry_recv.at[0], to_x),
        wire(cot_ref.at[:, :, lanes[1]], cot_y_ref, carry_send.at[1], carry_recv.at[1], to_y),
    ]
    for copy in carries:
        copy.start()
    for line in lines:
        line.finish(range(1, count), True)
    for number in range(3):
        each(pass_on(number, 1 - core), "wait_recv")
    for _, landed_taps in tap_copies:
        landed_taps.wait_recv()
    halo_copy.wait_recv()
    saves = [
        pltpu.make_async_copy(here, there, local.at[2 + at])
        for at, (here, there) in enumerate(
            ((all_qk, all_qk_ref), (all_v, all_v_ref), (all_out, all_out_ref), (all_taps, all_taps_ref))
        )
    ]
    for copy in saves:
        copy.start()

    def chip(at, carry):
        weights = all_qk[at].reshape(4 * HD, depth)
        columns = pl.ds(pl.multiple_of(at * 4 * HD, 4 * HD), 4 * HD)
        for s in range(2):
            raw[s, :, columns] = dot_nt(rows[s], weights)
        return carry

    lax.fori_loop(0, count, chip, 0)
    lane = lax.broadcasted_iota(jnp.int32, (rows.shape[1], 128), 1)

    def two_heads(at, carry):
        weights = all_v[at].reshape(2 * HD, depth)
        zero, one = dot_nt(rows[0], weights), dot_nt(rows[1], weights)
        raw[2, :, head_lanes(2 * at)] = jnp.where(lane < HD, zero, pltpu.roll(one, HD, 1))
        raw[2, :, head_lanes(2 * at + 1)] = jnp.where(lane < HD, pltpu.roll(zero, HD, 1), one)
        return carry

    lax.fori_loop(0, count, two_heads, 0)
    save_raw = pltpu.make_async_copy(raw, raw_ref, local.at[6])
    save_raw.start()
    for plane_at in range(3):
        tap = all_taps.at[plane_at]

        def conv(at, carry, plane_at=plane_at, tap=tap):
            lanes_at = head_lanes(at)
            values = raw[plane_at, :, lanes_at]
            one = pltpu.roll(values, 1, 0)[halo:]
            two = pltpu.roll(values, 2, 0)[halo:]
            mixed[plane_at, :, lanes_at] = (
                tap[0:1, lanes_at] * values[halo:]
                + jnp.where(masks_ref[plane_at, 0] > 0.5, tap[1:2, lanes_at] * one, 0.0)
                + jnp.where(masks_ref[plane_at, 1] > 0.5, tap[2:3, lanes_at] * two, 0.0)
            ).astype(LOW)
            return carry

        lax.fori_loop(0, mp, conv, 0)

    def source(at):
        return mixed.at[:, :, head_lanes(at)]

    def target(at):
        return landed.at[:, at]

    own = pltpu.make_async_copy(source(me), target(me), local.at[7])
    own.start()
    copies = member_copies(source, target, head_send, head_recv)
    for copy, _ in copies:
        copy.start()
    up_line.arrive(early[-1])
    up_line.finish(early, True)
    save_up = pltpu.make_async_copy(up_all, up_all_ref, local.at[8])
    save_up.start()
    own.wait()
    for _, copy in copies:
        copy.wait_recv()
    save_heads = pltpu.make_async_copy(landed, o_ref, local.at[9])
    save_heads.start()
    for number in range(6):
        each(leaving[number], "wait_send")
    for number in range(3):
        each(pass_on(number, core), "wait_send")
    for copy, _ in tap_copies + copies:
        copy.wait_send()
    halo_copy.wait_send()
    for copy in carries:
        copy.wait()
    save.wait()
    for copy in saves:
        copy.wait()
    save_raw.wait()
    save_up.wait()
    save_heads.wait()


def front(inputs, gain, shift, qk, v, out, taps, up, masks, cot):
    mp = lax.axis_size("mp")
    count = mp // 2
    rows_here, depth = inputs.shape[1:]
    tall = rows_here + HALO
    anywhere = pl.BlockSpec(memory_space=pl.ANY)
    vmem = pl.BlockSpec(memory_space=pltpu.VMEM)
    dma = pltpu.SemaphoreType.DMA
    whole = [((count, 2) + part.shape, LOW) for part in (qk, v, out)]
    whole.append(((3, 8, mp * 128), F32))
    kept = [
        ((2, rows_here, depth), LOW),
        ((mp * up.shape[0], depth), LOW),
        ((3, tall, mp * 128), F32),
        ((3, mp, rows_here, 128), LOW),
        ((2, rows_here, depth // 2), LOW),
        ((2, rows_here, depth // 2), LOW),
    ]
    return pl.pallas_call(
        front_kernel,
        in_specs=[anywhere, vmem, vmem] + [anywhere] * 5 + [vmem, anywhere],
        out_specs=[anywhere] * 10,
        out_shape=[jax.ShapeDtypeStruct(*shape) for shape in whole + kept],
        scratch_shapes=[
            pltpu.VMEM(inputs.shape, LOW),
            pltpu.VMEM((2, tall, depth), LOW),
        ]
        + [pltpu.VMEM(*shape) for shape in whole]
        + [
            pltpu.VMEM(*kept[1]),
            pltpu.VMEM(*kept[2]),
            pltpu.VMEM((3, rows_here, mp * 128), LOW),
            pltpu.VMEM(*kept[3]),
            dma((10,)),
            dma((3, 6)),
            dma((3, 6)),
            dma((3, 3)),
            dma((3, 3)),
            dma((mp,)),
            dma((mp,)),
            dma,
            dma,
            dma((2,)),
            dma((2,)),
            dma((mp,)),
            dma((mp,)),
        ]
        + line_semaphores(count) * 4,
        compiler_params=pltpu.CompilerParams(
            collective_id=3, has_side_effects=True, vmem_limit_bytes=VMEM_LIMIT
        ),
        cost_estimate=pl.CostEstimate(flops=2**36, bytes_accessed=2**26, transcendentals=0),
        name="front",
    )(inputs, gain.reshape(1, depth), shift.reshape(1, depth), qk, v, out, taps, up, masks, cot)


def project_back_kernel(
    ways, x_ref, raw_ref, taps_ref, masks_ref, *refs
):
    carried, refs = list(zip(ways, refs[: len(ways)])), refs[len(ways) :]
    grad_ref, sums_ref = refs[:2]
    targets, refs = refs[2 : 2 + len(ways)], refs[2 + len(ways) :]
    landed, raw, local, send, recv, carry_send, carry_recv = refs
    me = lax.axis_index("mp")
    tall = landed.shape[1]
    rows_here = grad_ref.shape[1]
    halo = tall - rows_here
    heads = landed.shape[2] // 128

    def source(at):
        return x_ref.at[:, pl.ds(pl.multiple_of(at * rows_here, 16), tall), :]

    def target(at):
        return landed.at[:, :, head_lanes(at)]

    own = pltpu.make_async_copy(source(me), target(me), local.at[0])
    own.start()
    load = pltpu.make_async_copy(raw_ref, raw, local.at[1])
    load.start()
    greet_members(ways)
    copies = member_copies(source, target, send, recv)
    for leaving, _ in copies:
        leaving.start()
    carries = carry_copies(carried, targets, carry_send, carry_recv)
    for copy in carries:
        copy.start()
    own.wait()
    load.wait()
    for _, landing in copies:
        landing.wait_recv()
    for plane in range(3):
        tap = taps_ref.at[plane]

        def back(at, carry, plane=plane, tap=tap):
            lanes = head_lanes(at)
            grad = landed[plane, :, lanes].astype(F32)
            one = pltpu.roll(grad, tall - 1, 0)[:rows_here]
            two = pltpu.roll(grad, tall - 2, 0)[:rows_here]
            here = grad[:rows_here]
            grad_ref[plane, :, lanes] = (
                tap[0:1, lanes] * here
                + jnp.where(masks_ref[plane, 2] > 0.5, tap[1:2, lanes] * one, 0.0)
                + jnp.where(masks_ref[plane, 3] > 0.5, tap[2:3, lanes] * two, 0.0)
            ).astype(LOW)
            values = raw[plane, :, lanes]
            before = pltpu.roll(values, 1, 0)[halo:]
            before_two = pltpu.roll(values, 2, 0)[halo:]
            products = (
                here * values[halo:],
                jnp.where(masks_ref[plane, 0] > 0.5, here * before, 0.0),
                jnp.where(masks_ref[plane, 1] > 0.5, here * before_two, 0.0),
            )
            for row, product in enumerate(products):
                sums_ref[plane, row : row + 1, lanes] = jnp.sum(product, axis=0, keepdims=True)
            sums_ref[plane, 3:8, lanes] = jnp.zeros((5, 128), F32)
            return carry

        lax.fori_loop(0, heads, back, 0)
    for leaving, _ in copies:
        leaving.wait_send()
    for copy in carries:
        copy.wait()


def project_back(x, raw, taps, masks, carried):
    mp = lax.axis_size("mp")
    rows_here = masks.shape[2]
    tall = raw.shape[1]
    anywhere = pl.BlockSpec(memory_space=pl.ANY)
    dma = pltpu.SemaphoreType.DMA
    vmem = pl.BlockSpec(memory_space=pltpu.VMEM)
    return pl.pallas_call(
        partial(project_back_kernel, tuple(way for way, _ in carried)),
        in_specs=[vmem, anywhere, vmem, vmem] + [anywhere] * len(carried),
        out_specs=[vmem] * 2 + [anywhere] * len(carried),
        out_shape=[
            jax.ShapeDtypeStruct((3, rows_here, mp * 128), LOW),
            jax.ShapeDtypeStruct((3, 8, mp * 128), F32),
        ]
        + [jax.ShapeDtypeStruct(block.shape, block.dtype) for _, block in carried],
        scratch_shapes=[
            pltpu.VMEM((3, tall, mp * 128), LOW),
            pltpu.VMEM((3, tall, mp * 128), F32),
            dma((2,)),
            dma((mp,)),
            dma((mp,)),
            dma((len(carried),)),
            dma((len(carried),)),
        ],
        compiler_params=pltpu.CompilerParams(
            collective_id=7, has_side_effects=True, vmem_limit_bytes=VMEM_LIMIT
        ),
        cost_estimate=pl.CostEstimate(flops=2**35, bytes_accessed=2**24, transcendentals=0),
        name="project_back",
    )(x, raw, taps, masks, *(block for _, block in carried))


def exchange(x, shape, halo, number, name, left=None, right=(), carried=()):
    mp = lax.axis_size("mp")
    anywhere = pl.BlockSpec(memory_space=pl.ANY)
    dma = pltpu.SemaphoreType.DMA
    scratch = [pltpu.VMEM(shape, x.dtype), dma((2,)), dma((mp,)), dma((mp,))]
    if carried:
        scratch += [dma((len(carried),)), dma((len(carried),))]
    outs = [jax.ShapeDtypeStruct(shape, x.dtype)]
    extra = ()
    if left is not None:
        rows, units = left.shape
        depth = right[0].shape[-1]
        outs.append(jax.ShapeDtypeStruct((units, depth), LOW))
        scratch += weight_grad_scratch(rows, depth, len(right))
        extra = (left,) + tuple(right)
    ways = tuple(way for way, _ in carried)
    extra += tuple(block for _, block in carried)
    outs += [jax.ShapeDtypeStruct(block.shape, block.dtype) for _, block in carried]
    return pl.pallas_call(
        partial(exchange_kernel, halo, len(right), ways),
        in_specs=[pl.BlockSpec(memory_space=pltpu.VMEM)] + [anywhere] * len(extra),
        out_specs=[anywhere] * len(outs),
        out_shape=outs,
        scratch_shapes=scratch,
        compiler_params=pltpu.CompilerParams(
            collective_id=number, has_side_effects=True, vmem_limit_bytes=48 * 2**20
        ),
        cost_estimate=pl.CostEstimate(flops=2**35, bytes_accessed=2**24, transcendentals=0),
        name=name,
    )(x, *extra)


def heads_out(x, number, name, left=None, right=(), carried=()):
    parts, rows_here, width = x.shape
    mp = lax.axis_size("mp")
    shape = (parts, mp, rows_here, 128)
    out, *more = exchange(x, shape, None, number, name, left, right, carried)
    return [out.reshape(parts, mp * rows_here, 128)] + more


def heads_back(x, rows_here, halo, number, name, left=None, right=(), carried=()):
    mp = lax.axis_size("mp")
    shape = (x.shape[0], rows_here + halo, mp * 128)
    return exchange(x, shape, halo, number, name, left, right, carried)


def feed_in_kernel(
    second_ref, up_ref, down_ref, cot_0, cot_1, cot_2, cot_3, cot_4, cot_5, cot_6,
    all_ref, relu_ref, hidden_ref, down_all_ref, up_all_ref, first_ref,
    rows, up, relu, hidden, down, cot, tiles, sums, local, outs, send, recv, cot_sem, tile_sem, sum_sem, *line_sems,
):
    count = lax.axis_size("mp") // 2
    depth = rows.shape[3]
    units = up.shape[0]
    share = down_ref.shape[0]
    z, core = mesh_place()
    lanes = (pl.ds(0, depth // 2), pl.ds(depth // 2, depth // 2))
    to_x, to_y = plane_partners()
    pieces = (cot_0, cot_1, cot_2, cot_3, cot_4, cot_5, cot_6)

    def line_place(ref):
        return lambda at, at_core: ref.at[
            pl.ds(pl.multiple_of((2 * at + at_core) * share, 16), share), :
        ]

    own = [pltpu.make_async_copy(second_ref.at[s], rows.at[s, 0], local.at[s]) for s in range(2)]
    own.append(pltpu.make_async_copy(up_ref, up, local.at[2]))
    own.append(pltpu.make_async_copy(down_ref, line_place(down)(z, core), local.at[3]))
    for copy in own:
        copy.start()
    for copy in own:
        copy.wait()
    greet_line(True)
    up_line = LineGather(line_place(up), *line_sems[:4])
    down_line = LineGather(line_place(down), *line_sems[4:])

    def remote(s, source, target, half, partner, number):
        return wire(
            rows.at[s, source, :, lanes[half]], rows.at[s, target, :, lanes[half]],
            send.at[s, number], recv.at[s, number], partner,
        )

    copies = [
        [
            remote(s, 0, 1, 0, to_x, 0),
            remote(s, 0, 2, 1, to_y, 1),
            remote(s, 0, 2, 0, to_y, 2),
            remote(s, 0, 1, 1, to_x, 3),
            remote(s, 1, 3, 0, to_y, 4),
            remote(s, 2, 3, 1, to_x, 5),
        ]
        for s in range(2)
    ]
    pending = [None, None]
    done = [0]

    def settle(slot):
        if pending[slot] is not None:
            for copy in pending[slot]:
                copy.wait()
        pending[slot] = None

    def tile(s, m):
        slot = done[0] % 2
        done[0] += 1
        settle(slot)

        def one(at, carry):
            columns = pl.ds(pl.multiple_of(at * CHUNK, CHUNK), CHUNK)
            kept = jnp.maximum(dot_nt(rows[s, m], up[columns, :]), 0.0)
            relu[slot, :, columns] = kept
            hidden[slot, :, columns] = (kept * kept).astype(LOW)
            return carry

        lax.fori_loop(0, units // CHUNK, one, 0)
        pending[slot] = [
            pltpu.make_async_copy(relu.at[slot], relu_ref.at[s, m], outs.at[slot, 0]),
            pltpu.make_async_copy(hidden.at[slot], hidden_ref.at[s, m], outs.at[slot, 1]),
        ]
        for copy in pending[slot]:
            copy.start()

    for number in range(4):
        copies[0][number].start()
    late = range(early_steps(count)[-1] + 1, count)
    for step in late:
        up_line.start(step)
        if step != late[-1]:
            up_line.arrive(step)
    cot_loads = []
    for m in range(4):
        cot_loads += piece_copies(pieces, 0, m, cot.at[m], cot_sem.at[m])
    for copy in cot_loads:
        copy.start()
    copies[0][0].wait_recv()
    copies[0][4].start()
    copies[0][1].wait_recv()
    copies[0][5].start()
    copies[1][0].start()
    copies[1][1].start()
    up_line.arrive(late[-1])
    down_line.start(1)
    down_line.swap_own()
    up_line.finish(late, False)
    whole_up = pltpu.make_async_copy(up, up_all_ref, local.at[2])
    whole_up.start()
    tile(0, 0)
    copies[0][3].wait_recv()
    tile(0, 1)
    copies[0][2].wait_recv()
    copies[1][2].start()
    copies[1][3].start()
    tile(0, 2)
    down_line.arrive(1)
    if count > 2:
        down_line.start(2)
    copies[1][0].wait_recv()
    copies[1][4].start()
    copies[1][1].wait_recv()
    copies[1][5].start()
    copies[0][4].wait_recv()
    copies[0][5].wait_recv()
    tile(0, 3)
    tile(1, 0)
    settle(0)
    settle(1)
    for copy in cot_loads:
        copy.wait()

    def first_half():
        gradient_tiles(hidden_ref.at[0], cot, tiles, sums, first_ref, tile_sem, sum_sem)

    first_half()
    for step in range(3, count):
        down_line.arrive(step - 1)
        down_line.start(step)
    copies[1][3].wait_recv()
    tile(1, 1)
    copies[1][2].wait_recv()
    tile(1, 2)
    copies[1][4].wait_recv()
    copies[1][5].wait_recv()
    gathered = pltpu.make_async_copy(rows, all_ref, local.at[0])
    gathered.start()
    tile(1, 3)
    if count > 2:
        down_line.arrive(count - 1)
    down_line.finish(range(1, count), True)
    whole_down = pltpu.make_async_copy(down, down_all_ref, local.at[1])
    whole_down.start()
    settle(0)
    settle(1)
    for s in range(2):
        for copy in copies[s]:
            copy.wait_send()
    gathered.wait()
    whole_up.wait()
    whole_down.wait()


def gradient_tiles(left_ref, right, tiles, sums, out_ref, tile_sem, sum_sem, before=None):
    wide = tiles.shape[3]
    steps = left_ref.shape[2] // wide

    def load(at, slot):
        columns = pl.ds(pl.multiple_of(at * wide, wide), wide)
        return pltpu.make_async_copy(left_ref.at[:, :, columns], tiles.at[slot], tile_sem.at[slot])

    def rows_of(at):
        return pl.ds(pl.multiple_of(at * wide, wide), wide)

    def save(at, slot):
        return pltpu.make_async_copy(sums.at[slot], out_ref.at[rows_of(at), :], sum_sem.at[slot])

    def load_before(at, slot):
        before_ref, buffer, sem = before
        return pltpu.make_async_copy(before_ref.at[rows_of(at), :], buffer.at[slot], sem.at[slot])

    load(0, 0).start()
    if before is not None:
        load_before(0, 0).start()

    def one(at, carry):
        slot = lax.rem(at, 2)
        load(at, slot).wait()
        if before is not None:
            load_before(at, slot).wait()

        @pl.when(at + 1 < steps)
        def _():
            load(at + 1, 1 - slot).start()
            if before is not None:
                load_before(at + 1, 1 - slot).start()

        @pl.when(at >= 2)
        def _():
            save(at - 2, slot).wait()

        blocks, tall = right.shape[:2]
        result = lax.dot_general(
            tiles[slot].reshape(blocks * tall, wide),
            right[...].reshape(blocks * tall, right.shape[2]),
            (((0,), (0,)), ((), ())),
            preferred_element_type=F32,
        )
        if before is not None:
            result = result + before[1][slot].astype(F32)
        sums[slot] = result.astype(LOW)
        save(at, slot).start()
        return carry

    lax.fori_loop(0, steps, one, 0)
    save(steps - 2, (steps - 2) % 2).wait()
    save(steps - 1, (steps - 1) % 2).wait()


def down_grad_rest(hidden, cot_pieces, first):
    rows_here, units = hidden.shape[2:]
    depth = first.shape[1]
    anywhere = pl.BlockSpec(memory_space=pl.ANY)
    dma = pltpu.SemaphoreType.DMA

    def kernel(hidden_ref, first_ref, *refs):
        pieces, out_ref = refs[:7], refs[7]
        cot, tiles, sums, buffer, cot_sem, tile_sem, sum_sem, first_sem = refs[8:]
        loads = []
        for m in range(4):
            loads += piece_copies(pieces, 1, m, cot.at[m], cot_sem.at[m])
        for copy in loads:
            copy.start()
        for copy in loads:
            copy.wait()
        gradient_tiles(
            hidden_ref.at[1], cot, tiles, sums, out_ref, tile_sem, sum_sem, (first_ref, buffer, first_sem)
        )

    return pl.pallas_call(
        kernel,
        in_specs=[anywhere] * 9,
        out_specs=anywhere,
        out_shape=jax.ShapeDtypeStruct((units, depth), LOW),
        scratch_shapes=[
            pltpu.VMEM((4, rows_here, depth), LOW),
            pltpu.VMEM((2, 4, rows_here, WIDE), LOW),
            pltpu.VMEM((2, WIDE, depth), LOW),
            pltpu.VMEM((2, WIDE, depth), LOW),
            dma((4, 2)),
            dma((2,)),
            dma((2,)),
            dma((2,)),
        ],
        compiler_params=pltpu.CompilerParams(vmem_limit_bytes=48 * 2**20),
        cost_estimate=pl.CostEstimate(
            flops=2 * 4 * rows_here * units * depth, bytes_accessed=2**25, transcendentals=0
        ),
        name="down_grad_rest",
    )(hidden, first, *cot_pieces)


def feed_in(second, up_early, down, cot_pieces):
    rows_here, depth = second.shape[1:]
    units = up_early.shape[0]
    count = lax.axis_size("mp") // 2
    anywhere = pl.BlockSpec(memory_space=pl.ANY)
    dma = pltpu.SemaphoreType.DMA
    return pl.pallas_call(
        feed_in_kernel,
        in_specs=[anywhere] * 10,
        out_specs=[anywhere] * 6,
        out_shape=[
            jax.ShapeDtypeStruct((2, 4, rows_here, depth), LOW),
            jax.ShapeDtypeStruct((2, 4, rows_here, units), F32),
            jax.ShapeDtypeStruct((2, 4, rows_here, units), LOW),
            jax.ShapeDtypeStruct((units, depth), LOW),
            jax.ShapeDtypeStruct((units, depth), LOW),
            jax.ShapeDtypeStruct((units, depth), LOW),
        ],
        scratch_shapes=[
            pltpu.VMEM((2, 4, rows_here, depth), LOW),
            pltpu.VMEM((units, depth), LOW),
            pltpu.VMEM((2, rows_here, units), F32),
            pltpu.VMEM((2, rows_here, units), LOW),
            pltpu.VMEM((units, depth), LOW),
            pltpu.VMEM((4, rows_here, depth), LOW),
            pltpu.VMEM((2, 4, rows_here, WIDE), LOW),
            pltpu.VMEM((2, WIDE, depth), LOW),
            dma((4,)),
            dma((2, 2)),
            dma((2, 6)),
            dma((2, 6)),
            dma((4, 2)),
            dma((2,)),
            dma((2,)),
        ]
        + line_semaphores(count) * 2,
        compiler_params=pltpu.CompilerParams(
            collective_id=1, has_side_effects=True, vmem_limit_bytes=VMEM_LIMIT
        ),
        cost_estimate=pl.CostEstimate(
            flops=2 * 8 * rows_here * depth * units * 3,
            bytes_accessed=60 * 2**20,
            transcendentals=0,
        ),
        name="feed_in",
    )(second, up_early, down, *cot_pieces)


def piece_copies(pieces, s, m, target, sems):
    half = target.shape[-1] // 2
    if m == 0:
        return [pltpu.make_async_copy(pieces[0].at[s], target, sems.at[0])]
    return [
        pltpu.make_async_copy(
            pieces[2 * m - 1 + side].at[s], target.at[:, pl.ds(side * half, half)], sems.at[side]
        )
        for side in range(2)
    ]


def feed_out_kernel(
    cot_0, cot_1, cot_2, cot_3, cot_4, cot_5, cot_6, relu_ref, hidden_ref, up_ref, down_ref,
    grad_ref, feed_x0_ref, feed_x1_ref, feed_y0_ref, feed_y1_ref, keep_a_ref, keep_b_ref, back_ref,
    up, down, cot, relu, grad, part, arrived, feed, result, local, loads, outs, send, recv,
):
    units, depth = up.shape
    half = depth // 2
    lanes = (pl.ds(0, half), pl.ds(half, half))
    to_x, to_y = plane_partners()
    weights = [
        pltpu.make_async_copy(down_ref, down, local.at[0]),
        pltpu.make_async_copy(up_ref, up, local.at[1]),
    ]
    order = [(s, m) for s in range(2) for m in (3, 1, 2, 0)]
    feed_x_refs, feed_y_refs = (feed_x0_ref, feed_x1_ref), (feed_y0_ref, feed_y1_ref)
    pieces = (cot_0, cot_1, cot_2, cot_3, cot_4, cot_5, cot_6)

    def load(at):
        s, m = order[at]
        slot = at % 2
        return piece_copies(pieces, s, m, cot.at[slot], loads.at[slot]) + [
            pltpu.make_async_copy(relu_ref.at[s, m], relu.at[slot], loads.at[slot, 2]),
        ]

    for copy in load(0) + weights:
        copy.start()
    greet([to_x, to_y])
    for copy in weights:
        copy.wait()

    def remote(s, source, number, side, partner):
        return pltpu.make_async_remote_copy(
            src_ref=part.at[s, source, :, lanes[side]],
            dst_ref=arrived.at[s, number],
            send_sem=send.at[s, number],
            recv_sem=recv.at[s, number],
            device_id=partner,
            device_id_type=MESH,
        )

    copies = [
        [
            remote(s, 1, 0, 0, to_x),
            remote(s, 3, 1, 0, to_x),
            remote(s, 2, 2, 1, to_y),
            remote(s, 3, 3, 1, to_y),
            remote(s, 2, 4, 0, to_y),
            remote(s, 1, 5, 1, to_x),
        ]
        for s in range(2)
    ]
    saving = [None, None]

    def tile(at):
        s, m = order[at]
        slot = at % 2
        for copy in load(at):
            copy.wait()
        if at + 1 < len(order):
            for copy in load(at + 1):
                copy.start()
        if saving[slot] is not None:
            saving[slot].wait()

        def back(step, carry):
            columns = pl.ds(pl.multiple_of(step * CHUNK, CHUNK), CHUNK)
            product = dot_nt(cot[slot], down[columns, :])
            grad[slot, :, columns] = (product * 2.0 * relu[slot, :, columns]).astype(LOW)
            return carry

        lax.fori_loop(0, units // CHUNK, back, 0)
        saving[slot] = pltpu.make_async_copy(grad.at[slot], grad_ref.at[s, m], outs.at[slot])
        saving[slot].start()

        def through(step, carry):
            columns = pl.ds(pl.multiple_of(step * CHUNK, CHUNK), CHUNK)
            part[s, m, :, columns] = dot(grad[slot], up[:, columns]).astype(LOW)
            return carry

        lax.fori_loop(0, depth // CHUNK, through, 0)

    def second_leg(s):
        copies[s][1].wait_recv()
        part[s, 2, :, lanes[0]] = (
            part[s, 2, :, lanes[0]].astype(F32) + arrived[s, 1].astype(F32)
        ).astype(LOW)
        copies[s][4].start()
        copies[s][3].wait_recv()
        part[s, 1, :, lanes[1]] = (
            part[s, 1, :, lanes[1]].astype(F32) + arrived[s, 3].astype(F32)
        ).astype(LOW)
        copies[s][5].start()

    def finish(s):
        for side, near, last in ((0, 0, 4), (1, 2, 5)):
            copies[s][near].wait_recv()
            copies[s][last].wait_recv()
            result[:, lanes[side]] = (
                part[s, 0, :, lanes[side]].astype(F32)
                + arrived[s, near].astype(F32)
                + arrived[s, last].astype(F32)
            )
        done = pltpu.make_async_copy(result, back_ref.at[s], local.at[2])
        done.start()
        return done

    def send_after(at):
        s, m = order[at]
        for number in {3: (1, 3), 1: (0,), 2: (2,), 0: ()}[m]:
            copies[s][number].start()

    for at in range(5):
        tile(at)
        send_after(at)
    second_leg(0)
    for at in range(5, 8):
        tile(at)
        send_after(at)
    done = finish(0)

    feeding = [None, None]

    def feed_load(at):
        s, m = order[at]
        return pltpu.make_async_copy(hidden_ref.at[s, m], cot.at[at % 2], loads.at[at % 2, 0])

    def feed_tile(at):
        s, m = order[at]
        slot = at % 2
        feed_load(at).wait()
        if at + 1 < len(order):
            feed_load(at + 1).start()
        if feeding[slot] is not None:
            for copy in feeding[slot]:
                copy.wait()

        def one(step, carry):
            columns = pl.ds(pl.multiple_of(step * CHUNK, CHUNK), CHUNK)
            feed[slot, :, columns] = dot(cot[slot], down[:, columns]).astype(LOW)
            return carry

        lax.fori_loop(0, depth // CHUNK, one, 0)
        targets = (
            (keep_a_ref.at[s, 0], feed_x_refs[s].at[0], keep_a_ref.at[s, 1], feed_x_refs[s].at[1])[m],
            (keep_b_ref.at[s, 0], keep_b_ref.at[s, 1], feed_y_refs[s].at[0], feed_y_refs[s].at[1])[m],
        )
        feeding[slot] = [
            pltpu.make_async_copy(feed.at[slot, :, lanes[side]], target, outs.at[2 + 2 * slot + side])
            for side, target in enumerate(targets)
        ]
        for copy in feeding[slot]:
            copy.start()

    feed_load(0).start()
    for at in range(2):
        feed_tile(at)
    second_leg(1)
    for at in range(2, 8):
        feed_tile(at)
    done.wait()
    finish(1).wait()
    for slot in range(2):
        saving[slot].wait()
        for copy in feeding[slot]:
            copy.wait()
    for s in range(2):
        for number in range(6):
            copies[s][number].wait_send()


def feed_out(cot_pieces, relu, hidden, up_all, down_all):
    rows_here, units = relu.shape[2:]
    depth = up_all.shape[1]
    anywhere = pl.BlockSpec(memory_space=pl.ANY)
    return pl.pallas_call(
        feed_out_kernel,
        in_specs=[anywhere] * 11,
        out_specs=[anywhere] * 8,
        out_shape=[
            jax.ShapeDtypeStruct((2, 4, rows_here, units), LOW),
        ]
        + [jax.ShapeDtypeStruct((2, rows_here, depth // 2), LOW)] * 4
        + [jax.ShapeDtypeStruct((2, 2, rows_here, depth // 2), LOW)] * 2
        + [
            jax.ShapeDtypeStruct((2, rows_here, depth), F32),
        ],
        scratch_shapes=[
            pltpu.VMEM((units, depth), LOW),
            pltpu.VMEM((units, depth), LOW),
            pltpu.VMEM((2, rows_here, depth), LOW),
            pltpu.VMEM((2, rows_here, units), F32),
            pltpu.VMEM((2, rows_here, units), LOW),
            pltpu.VMEM((2, 4, rows_here, depth), LOW),
            pltpu.VMEM((2, 6, rows_here, depth // 2), LOW),
            pltpu.VMEM((2, rows_here, depth), LOW),
            pltpu.VMEM((rows_here, depth), F32),
            pltpu.SemaphoreType.DMA((3,)),
            pltpu.SemaphoreType.DMA((2, 3)),
            pltpu.SemaphoreType.DMA((6,)),
            pltpu.SemaphoreType.DMA((2, 6)),
            pltpu.SemaphoreType.DMA((2, 6)),
        ],
        compiler_params=pltpu.CompilerParams(
            collective_id=2, has_side_effects=True, vmem_limit_bytes=VMEM_LIMIT
        ),
        cost_estimate=pl.CostEstimate(
            flops=2 * 8 * rows_here * depth * units * 4,
            bytes_accessed=60 * 2**20,
            transcendentals=0,
        ),
        name="feed_out",
    )(*cot_pieces, relu, hidden, up_all, down_all)


def finish_kernel(
    ways, qk_ref, v_ref, out_ref, norms_ref, taps_ref, *refs
):
    carried, refs = list(zip(ways, refs[: len(ways)])), refs[len(ways) :]
    joint_ref, norms_sum_ref, taps_sum_ref = refs[:3]
    targets, refs = refs[3 : 3 + len(ways)], refs[3 + len(ways) :]
    (
    acc, got, plane_in, line_in, gathered, norms_all, taps_all, norms_dp, taps_dp,
    local, swap_send, swap_recv, plane_send_sem, plane_recv_sem, line_send_sem, line_recv_sem,
    gather_send, gather_recv, small_send, small_recv, carry_send, carry_recv,
    ) = refs
    mp = lax.axis_size("mp")
    dp = lax.axis_index("dp")
    me = lax.axis_index("mp")
    z, core = mesh_place()
    count = mp // 2
    depth = acc.shape[3]
    half = depth // 2
    lanes = (pl.ds(0, half), pl.ds(half, half))
    to_x, to_y = plane_partners()
    dp_x = dp + 1 - 2 * lax.rem(dp, 2)
    dp_y = dp + 2 - 4 * (dp // 2)
    dp_xy = dp_x + 2 - 4 * (dp_x // 2)
    parts = (qk_ref, v_ref, out_ref)
    spans = (pl.ds(0, HD // 2), pl.ds(HD // 2, HD // 4), pl.ds(3 * HD // 4, HD // 4))
    loads = [
        pltpu.make_async_copy(part.at[:, core], acc.at[:, :, span, :], local.at[at])
        for at, (part, span) in enumerate(zip(parts, spans))
    ]
    for copy in loads:
        copy.start()

    barrier = pltpu.get_barrier_semaphore()
    for step in range(1, mp):
        pl.semaphore_signal(
            barrier, inc=1, device_id={"mp": lax.rem(me + step, mp)}, device_id_type=MESH
        )
    for step in range(1, 4):
        pl.semaphore_signal(
            barrier, inc=1, device_id={"dp": lax.rem(dp + step, 4)}, device_id_type=MESH
        )
    pl.semaphore_wait(barrier, mp + 2)

    swaps = [
        [
            wire(
                part.at[:, 1 - core, quarter], got.at[:, quarter, span, :],
                swap_send.at[at, number], swap_recv.at[at, number], other_core(),
            )
            for at, (part, span) in enumerate(zip(parts, spans))
        ]
        for number, quarter in enumerate((dp_xy, dp_x, dp_y, dp))
    ]
    for group in swaps:
        for copy in group:
            copy.start()

    def small(axis, at, others, source, target, number, first):
        out = []
        for step in range(1, others):
            to = lax.rem(at + step, others)
            frm = lax.rem(at + others - step, others)
            sems = (small_send.at[number, step], small_recv.at[number, step], {axis: to})
            out.append((wire(source(to), target.at[at], *sems), wire(source(to), target.at[frm], *sems)))
        return out

    own_small = [
        pltpu.make_async_copy(norms_ref, norms_all.at[me], local.at[3]),
        pltpu.make_async_copy(taps_ref.at[me], taps_all.at[me], local.at[4]),
    ]
    for copy in own_small:
        copy.start()
    over_mp = small("mp", me, mp, lambda to: norms_ref, norms_all, 0, None) + small(
        "mp", me, mp, lambda to: taps_ref.at[to], taps_all, 1, None
    )
    for leaving, _ in over_mp:
        leaving.start()

    def add(quarter, side, number):
        acc[:, quarter, :, lanes[side]] = (
            acc[:, quarter, :, lanes[side]].astype(F32) + plane_in[number].astype(F32)
        ).astype(LOW)

    def add_core(number, quarter):
        for copy in swaps[number]:
            copy.wait_recv()
        acc[:, quarter] = (acc[:, quarter].astype(F32) + got[:, quarter].astype(F32)).astype(LOW)

    def plane(quarter, side, partner, number):
        return wire(
            acc.at[:, quarter, :, lanes[side]], plane_in.at[number],
            plane_send_sem.at[number], plane_recv_sem.at[number], partner,
        )

    sends = [
        plane(dp_x, 0, to_x, 0),
        plane(dp_xy, 0, to_x, 1),
        plane(dp_y, 1, to_y, 2),
        plane(dp_xy, 1, to_y, 3),
        plane(dp_y, 0, to_y, 4),
        plane(dp_x, 1, to_x, 5),
    ]
    for copy in loads:
        copy.wait()
    add_core(0, dp_xy)
    sends[1].start()
    sends[3].start()
    add_core(1, dp_x)
    sends[0].start()
    add_core(2, dp_y)
    sends[2].start()
    add_core(3, dp)
    for _, landing in over_mp:
        landing.wait_recv()
    for copy in own_small:
        copy.wait()
    norms_dp[dp] = jnp.sum(norms_all[...], axis=0)
    taps_dp[dp] = jnp.sum(taps_all[...], axis=0)
    over_dp = small("dp", dp, 4, lambda to: norms_dp.at[dp], norms_dp, 2, None) + small(
        "dp", dp, 4, lambda to: taps_dp.at[dp], taps_dp, 3, None
    )
    for leaving, _ in over_dp:
        leaving.start()
    sends[1].wait_recv()
    add(dp_y, 0, 1)
    sends[4].start()
    sends[3].wait_recv()
    add(dp_x, 1, 3)
    sends[5].start()
    sends[0].wait_recv()
    add(dp, 0, 0)
    sends[2].wait_recv()
    add(dp, 1, 2)
    sends[4].wait_recv()
    add(dp, 0, 4)
    sends[5].wait_recv()
    add(dp, 1, 5)

    carries = carry_copies(carried, targets, carry_send, carry_recv)
    for copy in carries:
        copy.start()

    def line(step):
        out = []
        for way, turn in enumerate((1, -1)):
            target = z + turn * (count - step)
            far = z + turn
            lands = far - 2 * turn + turn * (count - step)
            sends = (target >= 0) & (target < count)
            receives = (lands >= 0) & (lands < count) & (z - turn >= 0) & (z - turn < count)
            at = jnp.clip(target, 0, count - 1)
            to = jnp.clip(lands, 0, count - 1)
            copy = wire(
                acc.at[at, dp], line_in.at[way, step - 1],
                line_send_sem.at[way, step - 1], line_recv_sem.at[way, step - 1],
                line_partner(z, turn),
            )
            out.append((sends, receives, to, copy))
        return out

    for step in range(1, count):
        legs = line(step)
        for sends_now, _, _, copy in legs:
            pl.when(sends_now)(copy.start)
        for way, (_, receives, to, copy) in enumerate(legs):

            @pl.when(receives)
            def _(to=to, copy=copy, way=way):
                copy.wait_recv()
                acc[to, dp] = (
                    acc[to, dp].astype(F32) + line_in[way, step - 1].astype(F32)
                ).astype(LOW)

    gathered[dp] = acc[z, dp]

    def gather(quarter, side, partner, number):
        block = gathered.at[quarter, :, lanes[side]]
        return wire(block, block, gather_send.at[number], gather_recv.at[number], partner)

    leaving = [
        gather(dp, 0, to_x, 0), gather(dp, 1, to_y, 1), gather(dp, 0, to_y, 2), gather(dp, 1, to_x, 3),
        gather(dp_x, 0, to_y, 4), gather(dp_y, 1, to_x, 5),
    ]
    landing = [
        gather(dp_x, 0, to_x, 0), gather(dp_y, 1, to_y, 1), gather(dp_y, 0, to_y, 2), gather(dp_x, 1, to_x, 3),
        gather(dp_xy, 0, to_y, 4), gather(dp_xy, 1, to_x, 5),
    ]
    for number in range(4):
        leaving[number].start()
    for _, landed in over_dp:
        landed.wait_recv()
    norms_sum_ref[...] = jnp.sum(norms_dp[...], axis=0)
    taps_sum_ref[...] = jnp.sum(taps_dp[...], axis=0)
    landing[0].wait_recv()
    leaving[4].start()
    landing[1].wait_recv()
    leaving[5].start()
    for number in range(2, 6):
        landing[number].wait_recv()
    save = pltpu.make_async_copy(gathered, joint_ref, local.at[5])
    save.start()
    for group in swaps:
        for copy in group:
            copy.wait_send()
    for copy in sends:
        copy.wait_send()
    for step in range(1, count):
        for sends_now, _, _, copy in line(step):
            pl.when(sends_now)(copy.wait_send)
    for copy in leaving:
        copy.wait_send()
    for copy, _ in over_mp + over_dp:
        copy.wait_send()
    for copy in carries:
        copy.wait()
    save.wait()


def finish(qk, v, out, norms, taps, carried):
    mp = lax.axis_size("mp")
    count = mp // 2
    depth = qk.shape[-1]
    anywhere = pl.BlockSpec(memory_space=pl.ANY)
    vmem = pl.BlockSpec(memory_space=pltpu.VMEM)
    dma = pltpu.SemaphoreType.DMA
    return pl.pallas_call(
        partial(finish_kernel, tuple(way for way, _ in carried)),
        in_specs=[anywhere] * 3 + [vmem] * 2 + [anywhere] * len(carried),
        out_specs=[anywhere, vmem, vmem] + [anywhere] * len(carried),
        out_shape=[
            jax.ShapeDtypeStruct((4, HD, depth), LOW),
            jax.ShapeDtypeStruct(norms.shape, F32),
            jax.ShapeDtypeStruct(taps.shape[1:], F32),
        ]
        + [jax.ShapeDtypeStruct(block.shape, block.dtype) for _, block in carried],
        scratch_shapes=[
            pltpu.VMEM((count, 4, HD, depth), LOW),
            pltpu.VMEM((count, 4, HD, depth), LOW),
            pltpu.VMEM((6, count, HD, depth // 2), LOW),
            pltpu.VMEM((2, count, HD, depth), LOW),
            pltpu.VMEM((4, HD, depth), LOW),
            pltpu.VMEM((mp,) + norms.shape, F32),
            pltpu.VMEM(taps.shape, F32),
            pltpu.VMEM((4,) + norms.shape, F32),
            pltpu.VMEM((4,) + taps.shape[1:], F32),
            dma((6,)),
            dma((3, 4)),
            dma((3, 4)),
            dma((6,)),
            dma((6,)),
            dma((2, count)),
            dma((2, count)),
            dma((6,)),
            dma((6,)),
            dma((4, mp)),
            dma((4, mp)),
            dma((len(carried),)),
            dma((len(carried),)),
        ],
        compiler_params=pltpu.CompilerParams(
            collective_id=8, has_side_effects=True, vmem_limit_bytes=VMEM_LIMIT
        ),
        cost_estimate=pl.CostEstimate(flops=2**36, bytes_accessed=2**26, transcendentals=0),
        name="finish",
    )(qk, v, out, norms, taps, *(block for _, block in carried))


def plane_send(block, mask):
    return lax.ppermute(block, "dp", [(d, d ^ mask) for d in range(lax.axis_size("dp"))])


def plane_gather_begin(block, axis=-1):
    half = block.shape[axis] // 2
    one, two = jnp.split(block, [half], axis=axis)
    return plane_send(one, 1), plane_send(two, 2), plane_send(one, 2), plane_send(two, 1)


def plane_gather_end(legs):
    one_x, two_y, one_y, two_x = legs
    return plane_send(one_x, 2), plane_send(two_y, 1)


def plane_blocks(block, legs, last, axis=-1):
    one_x, two_y, one_y, two_x = legs
    return [
        block,
        jnp.concatenate([one_x, two_x], axis=axis),
        jnp.concatenate([one_y, two_y], axis=axis),
        jnp.concatenate(last, axis=axis),
    ]


def plane_order(blocks, axis):
    me = lax.axis_index("dp")
    stacked = jnp.stack(blocks, axis=0)
    return jnp.concatenate(
        [lax.dynamic_index_in_dim(stacked, me ^ d, 0, keepdims=False) for d in range(4)], axis=axis
    )


def per_device(
    inputs,
    cotangent,
    short_lengths,
    long_lengths,
    norm1_gain,
    norm1_bias,
    query_weight,
    key_weight,
    value_weight,
    query_kernel,
    key_kernel,
    value_kernel,
    out_weight,
    norm2_gain,
    norm2_bias,
    up_weight,
    down_weight,
):
    rows_here = inputs.shape[1]
    width = inputs.shape[2]
    mp = lax.axis_size("mp")
    dp = lax.axis_size("dp")
    me_dp = lax.axis_index("dp")
    me_mp = lax.axis_index("mp")
    group = rows_here * mp
    hidden_here = up_weight.shape[1]
    share = hidden_here // dp

    starts = jnp.stack(
        [document_starts(short_lengths[0], group), document_starts(long_lengths[0], group)]
    )
    rows = inputs.astype(F32)

    def quarters(weight):
        return weight.reshape(4, weight.shape[0] // 4, width)

    qk_own = jnp.concatenate([query_weight, key_weight], axis=1).T
    up_own = lax.dynamic_slice_in_dim(up_weight, me_dp * share, share, 1).T
    down_own = lax.dynamic_slice_in_dim(down_weight, me_dp * share, share, 0)
    qk_taps = jnp.concatenate([query_kernel, key_kernel], axis=1)
    v_taps = jnp.concatenate([value_kernel, value_kernel], axis=1)
    taps_own = jnp.pad(jnp.stack([qk_taps, qk_taps, v_taps]), ((0, 0), (0, 5), (0, 0)))
    places = jnp.arange(group, dtype=jnp.int32)
    offsets = lax.dynamic_slice_in_dim(
        jnp.pad(places[None, :] - starts, ((0, 0), (0, HALO))), me_mp * rows_here, rows_here + HALO, 1
    )
    masks = jnp.stack(
        [
            offsets[:, :rows_here] >= 1,
            offsets[:, :rows_here] >= 2,
            offsets[:, 1 : rows_here + 1] >= 1,
            offsets[:, 2 : rows_here + 2] >= 2,
        ],
        axis=1,
    ).astype(F32)[..., None]
    wide_masks = jnp.broadcast_to(masks, masks.shape[:3] + (HD,))
    masks = jnp.stack(
        [
            jnp.concatenate([wide_masks[left], wide_masks[right]], axis=2)
            for left, right in ((0, 0), (1, 1), (0, 1))
        ]
    )

    qk_all, v_all, out_all, taps, normed, up_early, raw, mixed, one_x, two_y = front(
        inputs, norm1_gain, norm1_bias, quarters(qk_own), quarters(value_weight.T), quarters(out_weight), taps_own, up_own,
        masks, cotangent,
    )
    qk_all = qk_all.reshape(mp * 2 * HD, width)
    v_all = v_all.reshape(mp * HD, width)
    out_all = out_all.reshape(mp * HD, width)
    mixed = mixed.reshape(3, group, 128)
    cot, mixed = lax.optimization_barrier((cotangent, mixed))
    one_y, two_x = plane_send(cot[:, :, : width // 2], 2), plane_send(cot[:, :, width // 2 :], 1)
    one_xy, two_xy = plane_send(one_x, 2), plane_send(two_y, 1)

    def side_by_side(pair):
        split = pair.reshape(2, rows_here, mp, HD)
        return split.transpose(1, 2, 0, 3).reshape(1, rows_here, mp * 2 * HD)

    def apart(joint):
        split = joint.reshape(joint.shape[1], mp, 2, HD)
        return split.transpose(2, 0, 1, 3).reshape(2, joint.shape[1], mp * HD)

    attended_head, wide, total = attend(mixed, starts)
    (attended,) = heads_back(attended_head, rows_here, 0, 5, "attended_back")
    attended = apart(attended)
    middle = rows + dot(attended, out_all)
    second = layer_norm(middle, norm2_gain, norm2_bias).astype(LOW)

    second, one_y, two_x, one_xy, two_xy = lax.optimization_barrier(
        (second, one_y, two_x, one_xy, two_xy)
    )
    cot_pieces = (cot, one_x, two_x, one_y, two_y, one_xy, two_xy)
    second_all, relu, hidden, down_all, up_all, down_first = feed_in(
        second, up_early, down_own, cot_pieces
    )
    down_part = down_grad_rest(hidden, cot_pieces, down_first)
    down_mine = lax.psum_scatter(down_part, "mp", scatter_dimension=0, tiled=True)
    down_part, relu = lax.optimization_barrier((down_part, relu))
    grad_pre, feed_x0, feed_x1, feed_y0, feed_y1, keep_a, keep_b, grad_second = feed_out(
        cot_pieces, relu, hidden, up_all, down_all
    )
    def norm_back(values, gain, grad):
        flat = values.reshape(-1, width)
        unused, pull = jax.vjp(layer_norm, flat, gain, norm1_bias)
        grad_rows, grad_gain, grad_shift = pull(grad.reshape(-1, width))
        return grad_rows.reshape(values.shape), grad_gain, grad_shift

    grad_middle, gain_two, shift_two = norm_back(middle, norm2_gain, grad_second)
    grad_middle = grad_middle + cotangent.astype(F32)
    branch = grad_middle.astype(LOW)
    out_part = jnp.einsum("srh,srd->hd", attended, branch, preferred_element_type=F32).astype(LOW)
    grad_attended = jnp.einsum("srd,hd->srh", branch, out_all, preferred_element_type=F32).astype(LOW)
    grad_head, up_part, x_first, y_first = heads_out(
        side_by_side(grad_attended), 6, "attended_grad_out", grad_pre.reshape(-1, hidden.shape[3]),
        (second_all.reshape(-1, width),), ((0, feed_x0), (1, feed_y0)),
    )
    up_mine = lax.psum_scatter(up_part, "mp", scatter_dimension=0, tiled=True)
    grad_head, down_mine = lax.optimization_barrier((grad_head, down_mine))
    down_legs = plane_gather_begin(down_mine)
    grad_mixed_head = attend_back(mixed, grad_head, wide, total, starts, HALO)
    grad_mixed_head, down_legs = lax.optimization_barrier((grad_mixed_head, down_legs))
    down_last = plane_gather_end(down_legs)
    grad_raw, tap_sums, x_second, y_second = project_back(
        grad_mixed_head, raw, taps, masks, ((0, feed_x1), (1, feed_y1))
    )
    grad_raw, down_last = lax.optimization_barrier((grad_raw, down_last))
    down_grad = plane_order(plane_blocks(down_mine, down_legs, down_last), axis=0).astype(F32)
    x_in, y_in = jnp.stack([x_first, x_second]), jnp.stack([y_first, y_second])

    def add(left, right):
        return left.astype(F32) + right.astype(F32)

    feed_a = add(keep_a[:, 1], x_in[:, 1]).astype(LOW)
    feed_b = add(keep_b[:, 1], y_in[:, 1]).astype(LOW)
    grad_raw_qk, grad_raw_v = grad_raw[:2], apart(grad_raw[2:])
    grad_raw_qk, up_mine = lax.optimization_barrier((grad_raw_qk, up_mine))
    up_mine = up_mine.T
    up_legs = plane_gather_begin(up_mine, 0)
    qk_part = jnp.einsum("src,srd->cd", grad_raw_qk, normed, preferred_element_type=F32).astype(LOW)
    v_part = jnp.einsum("src,srd->cd", grad_raw_v, normed, preferred_element_type=F32).astype(LOW)
    grad_normed = dot(grad_raw_qk, qk_all) + dot(grad_raw_v, v_all)
    grad_input, gain_one, shift_one = norm_back(rows, norm1_gain, grad_normed)
    input_grads = grad_middle + grad_input

    def split_parts(part):
        return part.reshape(mp // 2, 2, 4, part.shape[0] // (4 * mp), width)

    norms = jnp.stack([gain_one, shift_one, gain_two, shift_two]).reshape(8, width // 2)
    qk_sums = (tap_sums[0] + tap_sums[1]).reshape(8, mp, 2 * HD)
    v_sums = tap_sums[2].reshape(8, mp, 2, HD).sum(axis=2)
    taps_part = jnp.concatenate([qk_sums, v_sums, jnp.zeros_like(v_sums)], axis=2)
    taps_part = taps_part.transpose(1, 0, 2)
    norms, up_legs = lax.optimization_barrier((norms, up_legs))
    up_last = plane_gather_end(up_legs)
    joint_grad, norms_sum, taps_sum, feed_a, feed_b = finish(
        split_parts(qk_part), split_parts(v_part), split_parts(out_part), norms, taps_part,
        ((1, feed_a), (0, feed_b)),
    )
    results = (
        middle
        + jnp.concatenate(
            [
                add(keep_a[:, 0], x_in[:, 0]) + feed_a.astype(F32),
                add(keep_b[:, 0], y_in[:, 0]) + feed_b.astype(F32),
            ],
            axis=2,
        )
    ).astype(LOW)
    joint_grad, up_last = lax.optimization_barrier((joint_grad, up_last))
    up_grad = plane_order(plane_blocks(up_mine, up_legs, up_last, 0), axis=1).astype(F32)
    joint_grad = joint_grad.astype(F32)
    small_sum = norms_sum.reshape(4, width)
    qk_grad = joint_grad[:, : HD // 2].reshape(2 * HD, width).T
    v_grad = joint_grad[:, HD // 2 : 3 * HD // 4].reshape(HD, width).T
    out_grad = joint_grad[:, 3 * HD // 4 :].reshape(HD, width)
    taps_sum = taps_sum[:3]
    return (
        results,
        input_grads,
        small_sum[0],
        small_sum[1],
        qk_grad[:, :HD],
        qk_grad[:, HD:],
        v_grad,
        taps_sum[:, :HD],
        taps_sum[:, HD : 2 * HD],
        taps_sum[:, 2 * HD : 3 * HD],
        out_grad,
        small_sum[2],
        small_sum[3],
        up_grad,
        down_grad,
    )


def solution(mesh):
    return jax.shard_map(
        per_device,
        mesh=mesh,
        in_specs=(
            P(None, ("dp", "mp"), None),
            P(None, ("dp", "mp"), None),
            P("dp", None),
            P("dp", None),
            P(),
            P(),
            P(None, "mp"),
            P(None, "mp"),
            P(None, "mp"),
            P(None, "mp"),
            P(None, "mp"),
            P(None, "mp"),
            P("mp", None),
            P(),
            P(),
            P(None, "mp"),
            P("mp", None),
        ),
        out_specs=(
            P(None, ("dp", "mp"), None),
            P(None, ("dp", "mp"), None),
            P(),
            P(),
            P(None, "mp"),
            P(None, "mp"),
            P(None, "mp"),
            P(None, "mp"),
            P(None, "mp"),
            P(None, "mp"),
            P("mp", None),
            P(),
            P(),
            P(None, "mp"),
            P("mp", None),
        ),
        check_vma=False,
    )
```

```python
import math
from functools import partial

import jax
import jax.numpy as jnp
from jax import lax
from jax.experimental import pallas as pl
from jax.experimental.pallas import tpu as pltpu
from jax.sharding import PartitionSpec as P

HD = 64
QUERIES, KEYS = 512, 512
WIDE = 256
CHUNK = 512
VMEM_LIMIT = 63 * 1024 * 1024
MESH = pl.DeviceIdType.MESH
LOW = jnp.bfloat16
F32 = jnp.float32


def dot(left, right):
    return jnp.dot(left, right, preferred_element_type=F32)


def layer_norm(rows, gain, shift):
    row_mean = jnp.mean(rows, axis=-1, keepdims=True)
    centered = rows - row_mean
    variance = jnp.mean(centered * centered, axis=-1, keepdims=True)
    return centered * lax.rsqrt(variance + 1e-05) * gain + shift


def document_starts(lengths, count):
    ends = jnp.cumsum(lengths)
    places = jnp.arange(count, dtype=jnp.int32)
    passed = (places[:, None] >= ends[None, :]).astype(jnp.int32)
    return jnp.sum(passed * lengths[None, :], axis=1)


def allowed_pairs(start_row, key_block, query_block):
    shape = (KEYS, QUERIES)
    keys = key_block * KEYS + lax.broadcasted_iota(jnp.int32, shape, 0)
    queries = query_block * QUERIES + lax.broadcasted_iota(jnp.int32, (1, QUERIES), 1)
    return (keys <= queries) & (keys >= start_row)


def key_blocks(first_ref, s, step):
    return first_ref[s, step], ((step + 1) * QUERIES + KEYS - 1) // KEYS


def attend_kernel(
    first_ref, start_ref, qk_ref, v_ref, out_ref, wide_ref, total_ref, values_t
):
    s, step = pl.program_id(0), pl.program_id(1)

    @pl.when(step == 0)
    def _():
        def turn(at, carry):
            rows = pl.ds(pl.multiple_of(at * KEYS, KEYS), KEYS)
            both = v_ref[0, rows, :].T
            values_t[at] = jnp.where(s == 0, both[:HD], both[HD:])
            return carry

        lax.fori_loop(0, values_t.shape[0], turn, 0)

    here = pl.ds(pl.multiple_of(step * QUERIES, QUERIES), QUERIES)
    query_t = (qk_ref[0, here, 0:HD] * HD ** (-0.5)).astype(LOW).T
    start_row = start_ref[0]

    def one(at, carry):
        top, summed, acc = carry
        rows = pl.ds(pl.multiple_of(at * KEYS, KEYS), KEYS)
        scores = dot(qk_ref[0, rows, HD : 2 * HD], query_t)
        scores = jnp.where(allowed_pairs(start_row, at, step), scores, -1e30)
        new_top = jnp.maximum(top, jnp.max(scores, axis=0, keepdims=True))
        powered = jnp.exp(scores - new_top)
        shrink = jnp.exp(top - new_top)
        summed = summed * shrink + jnp.sum(powered, axis=0, keepdims=True)
        acc = acc * shrink + dot(values_t[at], powered.astype(LOW))
        return new_top, summed, acc

    top, summed, acc = lax.fori_loop(
        *key_blocks(first_ref, s, step),
        one,
        (
            jnp.full((1, QUERIES), -1e30, F32),
            jnp.zeros((1, QUERIES), F32),
            jnp.zeros((HD, QUERIES), F32),
        ),
    )
    result = acc / summed
    wide_ref[0] = result
    total_ref[0] = top + jnp.log(summed)
    low = result.T.astype(LOW)

    @pl.when(s == 0)
    def _():
        out_ref[0, here, 0:HD] = low

    @pl.when(s == 1)
    def _():
        out_ref[0, here, HD : 2 * HD] = low


def attend(mixed, starts):
    group = mixed.shape[1]
    steps = group // QUERIES
    row = pl.BlockSpec((1, 1, QUERIES), lambda s, i, first: (s, 0, i))
    return pl.pallas_call(
        attend_kernel,
        grid_spec=pltpu.PrefetchScalarGridSpec(
            num_scalar_prefetch=1,
            grid=(2, steps),
            in_specs=[
                row,
                pl.BlockSpec((1, group, 2 * HD), lambda s, i, first: (s, 0, 0)),
                pl.BlockSpec((1, group, 2 * HD), lambda s, i, first: (2, 0, 0)),
            ],
            out_specs=[
                pl.BlockSpec((1, group, 2 * HD), lambda s, i, first: (0, 0, 0)),
                pl.BlockSpec((1, HD, QUERIES), lambda s, i, first: (s, 0, i)),
                row,
            ],
            scratch_shapes=[pltpu.VMEM((group // KEYS, HD, KEYS), LOW)],
        ),
        out_shape=[
            jax.ShapeDtypeStruct((1, group, 2 * HD), LOW),
            jax.ShapeDtypeStruct((2, HD, group), F32),
            jax.ShapeDtypeStruct((2, 1, group), F32),
        ],
        compiler_params=pltpu.CompilerParams(vmem_limit_bytes=32 * 1024 * 1024),
        cost_estimate=pl.CostEstimate(
            flops=2**34, bytes_accessed=group * 2048, transcendentals=group * group // 4
        ),
        name="attend",
    )(starts[:, ::QUERIES] // KEYS, starts[:, None, :], mixed, mixed)


def attend_back_kernel(
    first_ref, start_ref, qk_ref, v_ref, grad_ref, wide_ref, total_ref, out_ref,
    keys_t, values, grad_keys, grad_values,
):
    s, step = pl.program_id(0), pl.program_id(1)
    group = qk_ref.shape[1]

    @pl.when(step == 0)
    def _():
        def turn(at, carry):
            rows = pl.ds(pl.multiple_of(at * KEYS, KEYS), KEYS)
            keys_t[at] = qk_ref[0, rows, HD : 2 * HD].T
            both = v_ref[0, rows, :]
            values[rows, :] = jnp.where(s == 0, both[:, :HD], both[:, HD:])
            return carry

        lax.fori_loop(0, keys_t.shape[0], turn, 0)
        grad_keys[...] = jnp.zeros(grad_keys.shape, F32)
        grad_values[...] = jnp.zeros(grad_values.shape, F32)

    here = pl.ds(pl.multiple_of(step * QUERIES, QUERIES), QUERIES)
    query = (qk_ref[0, here, 0:HD] * HD ** (-0.5)).astype(LOW)
    query_t = query.T
    both = grad_ref[0]
    grad = jnp.where(s == 0, both[:, :HD], both[:, HD:])
    grad_t = grad.T
    start_row = start_ref[0]
    total = total_ref[0]
    inner = jnp.sum(grad_t.astype(F32) * wide_ref[0], axis=0, keepdims=True)

    def one(at, acc):
        rows = pl.ds(pl.multiple_of(at * KEYS, KEYS), KEYS)
        scores = dot(qk_ref[0, rows, HD : 2 * HD], query_t)
        scores = jnp.where(allowed_pairs(start_row, at, step), scores, -1e30)
        probs = jnp.exp(scores - total)
        grad_probs = dot(values[rows, :], grad_t)
        grad_scores = (probs * (grad_probs - inner)).astype(LOW)
        grad_values[rows, :] += dot(probs.astype(LOW), grad)
        grad_keys[rows, :] += dot(grad_scores, query)
        return acc + dot(keys_t[at], grad_scores)

    acc = lax.fori_loop(
        *key_blocks(first_ref, s, step), one, jnp.zeros((HD, QUERIES), F32)
    )
    out_ref[s, here, 0:HD] = (acc * HD ** (-0.5)).T.astype(out_ref.dtype)

    @pl.when(step == pl.num_programs(1) - 1)
    def _():
        out_ref[s, 0:group, HD : 2 * HD] = grad_keys[...].astype(out_ref.dtype)
        out_ref[s, group:, :] = jnp.zeros((out_ref.shape[1] - group, 2 * HD), out_ref.dtype)

        @pl.when(s == 0)
        def _():
            out_ref[2, 0:group, 0:HD] = grad_values[...].astype(out_ref.dtype)

        @pl.when(s == 1)
        def _():
            out_ref[2, 0:group, HD : 2 * HD] = grad_values[...].astype(out_ref.dtype)
            out_ref[2, group:, :] = jnp.zeros((out_ref.shape[1] - group, 2 * HD), out_ref.dtype)


def attend_back(mixed, grad, wide, total, starts, halo):
    group = mixed.shape[1]
    steps = group // QUERIES
    row = pl.BlockSpec((1, 1, QUERIES), lambda s, i, first: (s, 0, i))
    return pl.pallas_call(
        attend_back_kernel,
        grid_spec=pltpu.PrefetchScalarGridSpec(
            num_scalar_prefetch=1,
            grid=(2, steps),
            in_specs=[
                row,
                pl.BlockSpec((1, group, 2 * HD), lambda s, i, first: (s, 0, 0)),
                pl.BlockSpec((1, group, 2 * HD), lambda s, i, first: (2, 0, 0)),
                pl.BlockSpec((1, QUERIES, 2 * HD), lambda s, i, first: (0, i, 0)),
                pl.BlockSpec((1, HD, QUERIES), lambda s, i, first: (s, 0, i)),
                row,
            ],
            out_specs=pl.BlockSpec((3, group + halo, 2 * HD), lambda s, i, first: (0, 0, 0)),
            scratch_shapes=[
                pltpu.VMEM((group // KEYS, HD, KEYS), LOW),
                pltpu.VMEM((group, HD), LOW),
                pltpu.VMEM((group, HD), F32),
                pltpu.VMEM((group, HD), F32),
            ],
        ),
        out_shape=jax.ShapeDtypeStruct((3, group + halo, 2 * HD), LOW),
        compiler_params=pltpu.CompilerParams(vmem_limit_bytes=32 * 1024 * 1024),
        cost_estimate=pl.CostEstimate(
            flops=2**35, bytes_accessed=group * 2048, transcendentals=group * group // 4
        ),
        name="attend_back",
    )(starts[:, ::QUERIES] // KEYS, starts[:, None, :], mixed, mixed, grad, wide, total)


def plane_partners():
    me = lax.axis_index("dp")
    return {"dp": me + 1 - 2 * lax.rem(me, 2)}, {"dp": me + 2 - 4 * (me // 2)}


def dot_nt(left, right):
    return lax.dot_general(left, right, (((1,), (1,)), ((), ())), preferred_element_type=F32)


def mesh_place():
    me = lax.axis_index("mp")
    return me // 2, lax.rem(me, 2)


def wire(source, target, send, recv, partner):
    return pltpu.make_async_remote_copy(
        src_ref=source,
        dst_ref=target,
        send_sem=send,
        recv_sem=recv,
        device_id=partner,
        device_id_type=MESH,
    )


def line_partner(z, step):
    _, core = mesh_place()
    return {"mp": 2 * (z + step) + core}


def other_core():
    z, core = mesh_place()
    return {"mp": 2 * z + 1 - core}


def greet(partners):
    barrier = pltpu.get_barrier_semaphore()
    for partner in partners:
        pl.semaphore_signal(barrier, inc=1, device_id=partner, device_id_type=MESH)
    pl.semaphore_wait(barrier, len(partners))


def greet_line(with_plane):
    z, _ = mesh_place()
    count = lax.axis_size("mp") // 2
    barrier = pltpu.get_barrier_semaphore()
    partners = [other_core()]
    if with_plane:
        partners += list(plane_partners())
    for partner in partners:
        pl.semaphore_signal(barrier, inc=1, device_id=partner, device_id_type=MESH)
    for turn in (1, -1):

        @pl.when((z + turn >= 0) & (z + turn < count))
        def _(turn=turn):
            pl.semaphore_signal(barrier, inc=1, device_id=line_partner(z, turn), device_id_type=MESH)

    near = jnp.where(z > 0, 1, 0) + jnp.where(z < count - 1, 1, 0)
    pl.semaphore_wait(barrier, near + len(partners))


class LineGather:
    def __init__(self, place, send, recv, swap_send, swap_recv):
        self.z, self.core = mesh_place()
        self.count = lax.axis_size("mp") // 2
        self.place, self.send, self.recv = place, send, recv
        self.swap_send, self.swap_recv = swap_send, swap_recv

    def copies(self, step):
        z, count = self.z, self.count
        out = []
        for way, turn in enumerate((1, -1)):
            leaves = z - turn * (step - 1)
            lands = z - turn * step
            far = z + turn
            sends = (leaves >= 0) & (leaves < count) & (far >= 0) & (far < count)
            receives = (lands >= 0) & (lands < count)
            at = jnp.clip(leaves, 0, count - 1)
            to = jnp.clip(lands, 0, count - 1)
            sems = (self.send.at[way, step - 1], self.recv.at[way, step - 1], line_partner(z, turn))
            leaving = wire(self.place(at, self.core), self.place(at, self.core), *sems)
            landing = wire(self.place(to, self.core), self.place(to, self.core), *sems)
            out.append((sends, leaving, receives, landing, to))
        return out

    def start(self, step):
        for sends, leaving, _, _, _ in self.copies(step):
            pl.when(sends)(leaving.start)

    def swap(self, at, number):
        sems = (self.swap_send.at[number], self.swap_recv.at[number], other_core())
        leaving = wire(self.place(at, self.core), self.place(at, self.core), *sems)
        landing = wire(self.place(at, 1 - self.core), self.place(at, 1 - self.core), *sems)
        return leaving, landing

    def swap_own(self):
        self.swap(self.z, 0)[0].start()

    def arrive(self, step):
        for way, (_, _, receives, landing, at) in enumerate(self.copies(step)):

            @pl.when(receives)
            def _(landing=landing, at=at, way=way):
                landing.wait_recv()
                self.swap(at, 1 + 2 * (step - 1) + way)[0].start()

    def swapped(self, at, number):
        leaving, landing = self.swap(at, number)
        leaving.wait_send()
        landing.wait_recv()

    def finish(self, steps, own):
        if own:
            self.swapped(self.z, 0)
        for step in steps:
            for way, (sends, leaving, receives, _, at) in enumerate(self.copies(step)):
                pl.when(sends)(leaving.wait_send)
                pl.when(receives)(
                    lambda at=at, way=way, step=step: self.swapped(at, 1 + 2 * (step - 1) + way)
                )


def line_semaphores(count):
    return [
        pltpu.SemaphoreType.DMA((2, count)),
        pltpu.SemaphoreType.DMA((2, count)),
        pltpu.SemaphoreType.DMA((2 * count,)),
        pltpu.SemaphoreType.DMA((2 * count,)),
    ]


def early_steps(count):
    return range(1, count // 2 + 1)


HALO = 16


def carry_copies(carried, targets, send, recv):
    partners = plane_partners()
    return [
        wire(ref, target, send.at[at], recv.at[at], partners[way])
        for at, ((way, ref), target) in enumerate(zip(carried, targets))
    ]


def greet_members(ways):
    mp = lax.axis_size("mp")
    me = lax.axis_index("mp")
    barrier = pltpu.get_barrier_semaphore()
    for step in range(1, mp):
        pl.semaphore_signal(
            barrier, inc=1, device_id={"mp": lax.rem(me + step, mp)}, device_id_type=MESH
        )
    partners = plane_partners() if ways else ()
    for partner in partners:
        pl.semaphore_signal(barrier, inc=1, device_id=partner, device_id_type=MESH)
    pl.semaphore_wait(barrier, mp - 1 + len(partners))


def member_copies(source, target, send, recv):
    mp = lax.axis_size("mp")
    me = lax.axis_index("mp")
    copies = []
    for step in range(1, mp):
        to = lax.rem(me + step, mp)
        sems = (send.at[step], recv.at[step], {"mp": to})
        copies.append(
            (
                wire(source(to), target(me), *sems),
                wire(source(to), target(lax.rem(me + mp - step, mp)), *sems),
            )
        )
    return copies


def head_lanes(at):
    return pl.ds(pl.multiple_of(at * 128, 128), 128)


def front_kernel(
    inputs_ref, gain_ref, shift_ref, qk_ref, v_ref, out_ref, taps_ref, up_ref, masks_ref, cot_ref,
    all_qk_ref, all_v_ref, all_out_ref, all_taps_ref, normed_ref, up_all_ref, raw_ref, o_ref, cot_x_ref, cot_y_ref,
    inputs, rows, all_qk, all_v, all_out, all_taps, up_all, raw, mixed, landed, local, *sems,
):
    mp = lax.axis_size("mp")
    dp = lax.axis_index("dp")
    me = lax.axis_index("mp")
    z, core = mesh_place()
    count = mp // 2
    rows_here, depth = inputs.shape[1:]
    halo = rows.shape[1] - rows_here
    to_x, to_y = plane_partners()
    share = up_ref.shape[0]
    owned = (qk_ref, v_ref, out_ref)
    whole = (all_qk, all_v, all_out)
    (plane_send_sem, plane_recv_sem, plane_swap_send, plane_swap_recv) = sems[:4]
    taps_send, taps_recv, halo_send, halo_recv, carry_send, carry_recv, head_send, head_recv = sems[4:12]
    line_sems = [sems[12 + 4 * part : 16 + 4 * part] for part in range(4)]

    def up_place(at, at_core):
        start = pl.multiple_of((2 * at + at_core) * share, 16)
        return up_all.at[pl.ds(start, share), :]

    def taps_place(at):
        return all_taps.at[:, :, head_lanes(at)]

    loads = [
        pltpu.make_async_copy(inputs_ref, inputs, local.at[0]),
        pltpu.make_async_copy(taps_ref, taps_place(me), local.at[1]),
        pltpu.make_async_copy(up_ref, up_place(z, core), local.at[2]),
    ] + [
        pltpu.make_async_copy(
            owned[part].at[dp], whole[part].at[z, core, dp], local.at[3 + part]
        )
        for part in range(3)
    ]
    for copy in loads:
        copy.start()
    greet_members((0, 1))
    for copy in loads[1:]:
        copy.wait()

    lines = [
        LineGather(lambda at, at_core, part=part: whole[part].at[at, at_core, dp], *line_sems[part])
        for part in range(3)
    ]
    up_line = LineGather(up_place, *line_sems[3])
    for line in lines:
        line.start(1)
    tap_copies = member_copies(lambda to: taps_ref, taps_place, taps_send, taps_recv)
    for copy, _ in tap_copies:
        copy.start()
    for line in lines:
        line.swap_own()

    loads[0].wait()
    tall = 16

    def norm(s):
        def some(at, carry):
            here = pl.ds(pl.multiple_of(at * tall, tall), tall)
            there = pl.ds(pl.multiple_of(halo + at * tall, tall), tall)
            values = inputs[s, here, :].astype(F32)
            centered = values - jnp.mean(values, axis=1, keepdims=True)
            variance = jnp.mean(centered * centered, axis=1, keepdims=True)
            rows[s, there, :] = (
                centered * lax.rsqrt(variance + 1e-05) * gain_ref[...] + shift_ref[...]
            ).astype(LOW)
            return carry

        lax.fori_loop(0, rows_here // tall, some, 0)

    norm(0)
    for step in range(1, count):
        for line in lines:
            line.arrive(step)
        if step + 1 < count:
            for line in lines:
                line.start(step + 1)

    half = depth // 2
    lanes = (pl.ds(0, half), pl.ds(half, half))
    dp_x = dp + 1 - 2 * lax.rem(dp, 2)
    dp_y = dp + 2 - 4 * (dp // 2)
    dp_xy = dp_x + 2 - 4 * (dp_x // 2)
    legs = ((0, to_x), (1, to_y), (0, to_y), (1, to_x), (0, to_y), (1, to_x))

    def plane(number, quarter):
        side, partner = legs[number]
        out = []
        for part in range(3):
            block = whole[part].at[:, core, quarter, :, lanes[side]]
            out.append(
                wire(
                    block, block, plane_send_sem.at[part, number], plane_recv_sem.at[part, number], partner
                )
            )
        return out

    leaving = [plane(number, quarter) for number, quarter in enumerate((dp, dp, dp, dp, dp_x, dp_y))]
    landing = [
        plane(number, quarter) for number, quarter in enumerate((dp_x, dp_y, dp_y, dp_x, dp_xy, dp_xy))
    ]

    def pass_on(number, at_core):
        quarter = (dp_x, dp_y, dp_xy)[number]
        out = []
        for part in range(3):
            block = whole[part].at[:, at_core, quarter]
            out.append(
                wire(
                    block, block, plane_swap_send.at[part, number], plane_swap_recv.at[part, number],
                    other_core(),
                )
            )
        return out

    def each(copies, what):
        for copy in copies:
            getattr(copy, what)()

    for number in range(4):
        each(leaving[number], "start")
    early = early_steps(count)
    up_line.start(1)
    up_line.swap_own()
    norm(1)
    own_rows = rows.at[:, pl.ds(halo, rows_here), :]
    save = pltpu.make_async_copy(own_rows, normed_ref, local.at[0])
    save.start()
    halo_copy = wire(
        rows.at[:, pl.ds(rows_here, halo), :], rows.at[:, pl.ds(0, halo), :], halo_send, halo_recv,
        {"mp": lax.rem(me + 1, mp)},
    )
    halo_copy.start()
    each(landing[0], "wait_recv")
    each(leaving[4], "start")
    each(landing[1], "wait_recv")
    each(leaving[5], "start")
    each(landing[3], "wait_recv")
    each(pass_on(0, core), "start")
    each(landing[2], "wait_recv")
    each(pass_on(1, core), "start")
    up_line.arrive(1)
    up_line.start(2)
    each(landing[4], "wait_recv")
    each(landing[5], "wait_recv")
    each(pass_on(2, core), "start")
    for step in early[1:-1]:
        up_line.arrive(step)
        up_line.start(step + 1)
    carries = [
        wire(cot_ref.at[:, :, lanes[0]], cot_x_ref, carry_send.at[0], carry_recv.at[0], to_x),
        wire(cot_ref.at[:, :, lanes[1]], cot_y_ref, carry_send.at[1], carry_recv.at[1], to_y),
    ]
    for copy in carries:
        copy.start()
    for line in lines:
        line.finish(range(1, count), True)
    for number in range(3):
        each(pass_on(number, 1 - core), "wait_recv")
    for _, landed_taps in tap_copies:
        landed_taps.wait_recv()
    halo_copy.wait_recv()
    saves = [
        pltpu.make_async_copy(here, there, local.at[2 + at])
        for at, (here, there) in enumerate(
            ((all_qk, all_qk_ref), (all_v, all_v_ref), (all_out, all_out_ref), (all_taps, all_taps_ref))
        )
    ]
    for copy in saves:
        copy.start()

    def chip(at, carry):
        weights = all_qk[at].reshape(4 * HD, depth)
        columns = pl.ds(pl.multiple_of(at * 4 * HD, 4 * HD), 4 * HD)
        for s in range(2):
            raw[s, :, columns] = dot_nt(rows[s], weights)
        return carry

    lax.fori_loop(0, count, chip, 0)
    lane = lax.broadcasted_iota(jnp.int32, (rows.shape[1], 128), 1)

    def two_heads(at, carry):
        weights = all_v[at].reshape(2 * HD, depth)
        zero, one = dot_nt(rows[0], weights), dot_nt(rows[1], weights)
        raw[2, :, head_lanes(2 * at)] = jnp.where(lane < HD, zero, pltpu.roll(one, HD, 1))
        raw[2, :, head_lanes(2 * at + 1)] = jnp.where(lane < HD, pltpu.roll(zero, HD, 1), one)
        return carry

    lax.fori_loop(0, count, two_heads, 0)
    save_raw = pltpu.make_async_copy(raw, raw_ref, local.at[6])
    save_raw.start()
    for plane_at in range(3):
        tap = all_taps.at[plane_at]

        def conv(at, carry, plane_at=plane_at, tap=tap):
            lanes_at = head_lanes(at)
            values = raw[plane_at, :, lanes_at]
            one = pltpu.roll(values, 1, 0)[halo:]
            two = pltpu.roll(values, 2, 0)[halo:]
            mixed[plane_at, :, lanes_at] = (
                tap[0:1, lanes_at] * values[halo:]
                + jnp.where(masks_ref[plane_at, 0] > 0.5, tap[1:2, lanes_at] * one, 0.0)
                + jnp.where(masks_ref[plane_at, 1] > 0.5, tap[2:3, lanes_at] * two, 0.0)
            ).astype(LOW)
            return carry

        lax.fori_loop(0, mp, conv, 0)

    def source(at):
        return mixed.at[:, :, head_lanes(at)]

    def target(at):
        return landed.at[:, at]

    own = pltpu.make_async_copy(source(me), target(me), local.at[7])
    own.start()
    copies = member_copies(source, target, head_send, head_recv)
    for copy, _ in copies:
        copy.start()
    up_line.arrive(early[-1])
    up_line.finish(early, True)
    save_up = pltpu.make_async_copy(up_all, up_all_ref, local.at[8])
    save_up.start()
    own.wait()
    for _, copy in copies:
        copy.wait_recv()
    save_heads = pltpu.make_async_copy(landed, o_ref, local.at[9])
    save_heads.start()
    for number in range(6):
        each(leaving[number], "wait_send")
    for number in range(3):
        each(pass_on(number, core), "wait_send")
    for copy, _ in tap_copies + copies:
        copy.wait_send()
    halo_copy.wait_send()
    for copy in carries:
        copy.wait()
    save.wait()
    for copy in saves:
        copy.wait()
    save_raw.wait()
    save_up.wait()
    save_heads.wait()


def front(inputs, gain, shift, qk, v, out, taps, up, masks, cot):
    mp = lax.axis_size("mp")
    count = mp // 2
    rows_here, depth = inputs.shape[1:]
    tall = rows_here + HALO
    anywhere = pl.BlockSpec(memory_space=pl.ANY)
    vmem = pl.BlockSpec(memory_space=pltpu.VMEM)
    dma = pltpu.SemaphoreType.DMA
    whole = [((count, 2) + part.shape, LOW) for part in (qk, v, out)]
    whole.append(((3, 8, mp * 128), F32))
    kept = [
        ((2, rows_here, depth), LOW),
        ((mp * up.shape[0], depth), LOW),
        ((3, tall, mp * 128), F32),
        ((3, mp, rows_here, 128), LOW),
        ((2, rows_here, depth // 2), LOW),
        ((2, rows_here, depth // 2), LOW),
    ]
    return pl.pallas_call(
        front_kernel,
        in_specs=[anywhere, vmem, vmem] + [anywhere] * 5 + [vmem, anywhere],
        out_specs=[anywhere] * 10,
        out_shape=[jax.ShapeDtypeStruct(*shape) for shape in whole + kept],
        scratch_shapes=[
            pltpu.VMEM(inputs.shape, LOW),
            pltpu.VMEM((2, tall, depth), LOW),
        ]
        + [pltpu.VMEM(*shape) for shape in whole]
        + [
            pltpu.VMEM(*kept[1]),
            pltpu.VMEM(*kept[2]),
            pltpu.VMEM((3, rows_here, mp * 128), LOW),
            pltpu.VMEM(*kept[3]),
            dma((10,)),
            dma((3, 6)),
            dma((3, 6)),
            dma((3, 3)),
            dma((3, 3)),
            dma((mp,)),
            dma((mp,)),
            dma,
            dma,
            dma((2,)),
            dma((2,)),
            dma((mp,)),
            dma((mp,)),
        ]
        + line_semaphores(count) * 4,
        compiler_params=pltpu.CompilerParams(
            collective_id=3, has_side_effects=True, vmem_limit_bytes=VMEM_LIMIT
        ),
        cost_estimate=pl.CostEstimate(flops=2**36, bytes_accessed=2**26, transcendentals=0),
        name="front",
    )(inputs, gain.reshape(1, depth), shift.reshape(1, depth), qk, v, out, taps, up, masks, cot)


def left_t_right(left, right):
    return lax.dot_general(left, right, (((0,), (0,)), ((), ())), preferred_element_type=F32)


def stream_out(steps, compute, buffer, ref, sem):
    def save(at, slot):
        return pltpu.make_async_copy(buffer.at[slot], ref.at[at], sem.at[slot])

    def one(at, carry):
        slot = lax.rem(at, 2)

        @pl.when(at >= 2)
        def _():
            save(at - 2, slot).wait()

        buffer[slot] = compute(at)
        save(at, slot).start()
        return carry

    lax.fori_loop(0, steps, one, 0)
    save(steps - 2, (steps - 2) % 2).wait()
    save(steps - 1, (steps - 1) % 2).wait()


def project_back_kernel(
    ways, x_ref, raw_ref, taps_ref, masks_ref, normed_ref, attended_ref, branch_ref, *refs
):
    carried, refs = list(zip(ways, refs[: len(ways)])), refs[len(ways) :]
    grad_ref, sums_ref, qk_part_ref, v_part_ref, out_part_ref = refs[:5]
    targets, refs = refs[5 : 5 + len(ways)], refs[5 + len(ways) :]
    landed, raw, wide, narrow, part_sem, local, send, recv, carry_send, carry_recv = refs
    me = lax.axis_index("mp")
    tall = landed.shape[1]
    rows_here = grad_ref.shape[1]
    halo = tall - rows_here
    heads = landed.shape[2] // 128

    def source(at):
        return x_ref.at[:, pl.ds(pl.multiple_of(at * rows_here, 16), tall), :]

    def target(at):
        return landed.at[:, :, head_lanes(at)]

    own = pltpu.make_async_copy(source(me), target(me), local.at[0])
    own.start()
    load = pltpu.make_async_copy(raw_ref, raw, local.at[1])
    load.start()
    greet_members(ways)
    copies = member_copies(source, target, send, recv)
    for leaving, _ in copies:
        leaving.start()
    carries = carry_copies(carried, targets, carry_send, carry_recv)
    for copy in carries:
        copy.start()

    def out_part(at):
        lanes = head_lanes(at)
        return (
            left_t_right(attended_ref[0, :, lanes], branch_ref[0])
            + left_t_right(attended_ref[1, :, lanes], branch_ref[1])
        ).astype(LOW)

    stream_out(heads // 2, out_part, narrow, out_part_ref, part_sem)
    own.wait()
    load.wait()
    for _, landing in copies:
        landing.wait_recv()
    for plane in range(3):
        tap = taps_ref.at[plane]

        def back(at, carry, plane=plane, tap=tap):
            lanes = head_lanes(at)
            grad = landed[plane, :, lanes].astype(F32)
            one = pltpu.roll(grad, tall - 1, 0)[:rows_here]
            two = pltpu.roll(grad, tall - 2, 0)[:rows_here]
            here = grad[:rows_here]
            grad_ref[plane, :, lanes] = (
                tap[0:1, lanes] * here
                + jnp.where(masks_ref[plane, 2] > 0.5, tap[1:2, lanes] * one, 0.0)
                + jnp.where(masks_ref[plane, 3] > 0.5, tap[2:3, lanes] * two, 0.0)
            ).astype(LOW)
            values = raw[plane, :, lanes]
            before = pltpu.roll(values, 1, 0)[halo:]
            before_two = pltpu.roll(values, 2, 0)[halo:]
            products = (
                here * values[halo:],
                jnp.where(masks_ref[plane, 0] > 0.5, here * before, 0.0),
                jnp.where(masks_ref[plane, 1] > 0.5, here * before_two, 0.0),
            )
            for row, product in enumerate(products):
                sums_ref[plane, row : row + 1, lanes] = jnp.sum(product, axis=0, keepdims=True)
            sums_ref[plane, 3:8, lanes] = jnp.zeros((5, 128), F32)
            return carry

        lax.fori_loop(0, heads, back, 0)

    def pair(at):
        return pl.ds(pl.multiple_of(at * 256, 256), 256)

    def qk_part(at):
        return (
            left_t_right(grad_ref[0, :, pair(at)], normed_ref[0])
            + left_t_right(grad_ref[1, :, pair(at)], normed_ref[1])
        ).astype(LOW)

    def v_part(at):
        side = grad_ref[2, :, pair(at)]
        zero, one = left_t_right(side, normed_ref[0]), left_t_right(side, normed_ref[1])
        return jnp.concatenate(
            [zero[:HD] + one[HD : 2 * HD], zero[2 * HD : 3 * HD] + one[3 * HD :]], axis=0
        ).astype(LOW)

    stream_out(heads // 2, qk_part, wide, qk_part_ref, part_sem)
    stream_out(heads // 2, v_part, narrow, v_part_ref, part_sem)
    for leaving, _ in copies:
        leaving.wait_send()
    for copy in carries:
        copy.wait()


def project_back(x, raw, taps, masks, normed, attended, branch, carried):
    mp = lax.axis_size("mp")
    rows_here, depth = normed.shape[1:]
    tall = raw.shape[1]
    anywhere = pl.BlockSpec(memory_space=pl.ANY)
    dma = pltpu.SemaphoreType.DMA
    vmem = pl.BlockSpec(memory_space=pltpu.VMEM)
    return pl.pallas_call(
        partial(project_back_kernel, tuple(way for way, _ in carried)),
        in_specs=[vmem, anywhere] + [vmem] * 5 + [anywhere] * len(carried),
        out_specs=[vmem] * 2 + [anywhere] * (3 + len(carried)),
        out_shape=[
            jax.ShapeDtypeStruct((3, rows_here, mp * 128), LOW),
            jax.ShapeDtypeStruct((3, 8, mp * 128), F32),
            jax.ShapeDtypeStruct((mp // 2, 4 * HD, depth), LOW),
            jax.ShapeDtypeStruct((mp // 2, 2 * HD, depth), LOW),
            jax.ShapeDtypeStruct((mp // 2, 2 * HD, depth), LOW),
        ]
        + [jax.ShapeDtypeStruct(block.shape, block.dtype) for _, block in carried],
        scratch_shapes=[
            pltpu.VMEM((3, tall, mp * 128), LOW),
            pltpu.VMEM((3, tall, mp * 128), F32),
            pltpu.VMEM((2, 4 * HD, depth), LOW),
            pltpu.VMEM((2, 2 * HD, depth), LOW),
            dma((2,)),
            dma((2,)),
            dma((mp,)),
            dma((mp,)),
            dma((len(carried),)),
            dma((len(carried),)),
        ],
        compiler_params=pltpu.CompilerParams(
            collective_id=7, has_side_effects=True, vmem_limit_bytes=VMEM_LIMIT
        ),
        cost_estimate=pl.CostEstimate(flops=2**35, bytes_accessed=2**24, transcendentals=0),
        name="project_back",
    )(x, raw, taps, masks, normed, attended, branch, *(block for _, block in carried))


def attended_kernel(x_ref, o_ref, landed, local, send, recv):
    me = lax.axis_index("mp")
    tall = o_ref.shape[1]

    def source(at):
        return x_ref.at[:, pl.ds(pl.multiple_of(at * tall, 16), tall), :]

    def target(at):
        return landed.at[:, :, head_lanes(at)]

    own = pltpu.make_async_copy(source(me), target(me), local.at[0])
    own.start()
    greet_members(())
    copies = member_copies(source, target, send, recv)
    for leaving, _ in copies:
        leaving.start()
    own.wait()
    for _, landing in copies:
        landing.wait_recv()
    save = pltpu.make_async_copy(landed, o_ref, local.at[1])
    save.start()
    for leaving, _ in copies:
        leaving.wait_send()
    save.wait()


def attended_back(x, rows_here):
    mp = lax.axis_size("mp")
    shape = (x.shape[0], rows_here, mp * 128)
    dma = pltpu.SemaphoreType.DMA
    return pl.pallas_call(
        attended_kernel,
        in_specs=[pl.BlockSpec(memory_space=pltpu.VMEM)],
        out_specs=pl.BlockSpec(memory_space=pl.ANY),
        out_shape=jax.ShapeDtypeStruct(shape, x.dtype),
        scratch_shapes=[pltpu.VMEM(shape, x.dtype), dma((2,)), dma((mp,)), dma((mp,))],
        compiler_params=pltpu.CompilerParams(
            collective_id=5, has_side_effects=True, vmem_limit_bytes=48 * 2**20
        ),
        cost_estimate=pl.CostEstimate(flops=2**34, bytes_accessed=2**24, transcendentals=0),
        name="attended_back",
    )(x)


def line_blocks(place, sources, local, send, recv):
    z, core = mesh_place()
    count = lax.axis_size("mp") // 2
    out = []
    for number, (step, way, ref) in enumerate(sources):
        at = z - way * step
        there = (at >= 0) & (at < count)
        at = jnp.clip(at, 0, count - 1)
        sems = (send.at[number], recv.at[number], other_core())
        out.append(
            (
                there,
                pltpu.make_async_copy(ref, place(at, core), local.at[number]),
                wire(ref, place(at, core), *sems),
                wire(ref, place(at, 1 - core), *sems),
            )
        )
    return out


def feed_in_kernel(
    late, second_ref, up_ref, down_ref, cot_0, cot_1, cot_2, cot_3, cot_4, cot_5, cot_6, *refs
):
    late_sources = [(step, way, ref) for (step, way), ref in zip(late, refs)]
    (
        all_ref, relu_ref, hidden_ref, down_all_ref, up_all_ref, down_part_ref,
        rows, up, relu, hidden, down, cot, tiles, sums, before, local, outs, send, recv, cot_sem, tile_sem, sum_sem,
        before_sem, late_local, late_send, late_recv, *line_sems,
    ) = refs[len(late) :]
    count = lax.axis_size("mp") // 2
    depth = rows.shape[3]
    units = up.shape[0]
    share = down_ref.shape[0]
    z, core = mesh_place()
    lanes = (pl.ds(0, depth // 2), pl.ds(depth // 2, depth // 2))
    to_x, to_y = plane_partners()
    pieces = (cot_0, cot_1, cot_2, cot_3, cot_4, cot_5, cot_6)

    def line_place(ref):
        return lambda at, at_core: ref.at[
            pl.ds(pl.multiple_of((2 * at + at_core) * share, 16), share), :
        ]

    own = [pltpu.make_async_copy(second_ref.at[s], rows.at[s, 0], local.at[s]) for s in range(2)]
    own.append(pltpu.make_async_copy(up_ref, up, local.at[2]))
    own.append(pltpu.make_async_copy(down_ref, line_place(down)(z, core), local.at[3]))
    for copy in own:
        copy.start()
    for copy in own:
        copy.wait()
    greet_line(True)
    late_blocks = line_blocks(line_place(up), late_sources, late_local, late_send, late_recv)
    down_line = LineGather(line_place(down), *line_sems)

    def remote(s, source, target, half, partner, number):
        return wire(
            rows.at[s, source, :, lanes[half]], rows.at[s, target, :, lanes[half]],
            send.at[s, number], recv.at[s, number], partner,
        )

    copies = [
        [
            remote(s, 0, 1, 0, to_x, 0),
            remote(s, 0, 2, 1, to_y, 1),
            remote(s, 0, 2, 0, to_y, 2),
            remote(s, 0, 1, 1, to_x, 3),
            remote(s, 1, 3, 0, to_y, 4),
            remote(s, 2, 3, 1, to_x, 5),
        ]
        for s in range(2)
    ]
    pending = [None, None]
    done = [0]

    def settle(slot):
        if pending[slot] is not None:
            for copy in pending[slot]:
                copy.wait()
        pending[slot] = None

    def tile(s, m):
        slot = done[0] % 2
        done[0] += 1
        settle(slot)

        def one(at, carry):
            columns = pl.ds(pl.multiple_of(at * CHUNK, CHUNK), CHUNK)
            kept = jnp.maximum(dot_nt(rows[s, m], up[columns, :]), 0.0)
            relu[slot, :, columns] = kept
            hidden[slot, :, columns] = (kept * kept).astype(LOW)
            return carry

        lax.fori_loop(0, units // CHUNK, one, 0)
        pending[slot] = [
            pltpu.make_async_copy(relu.at[slot], relu_ref.at[s, m], outs.at[slot, 0]),
            pltpu.make_async_copy(hidden.at[slot], hidden_ref.at[s, m], outs.at[slot, 1]),
        ]
        for copy in pending[slot]:
            copy.start()

    for number in range(4):
        copies[0][number].start()
    for there, here, leaving, _ in late_blocks:

        @pl.when(there)
        def _(here=here, leaving=leaving):
            here.start()
            leaving.start()

    down_line.start(1)
    down_line.swap_own()

    def cot_loads(s):
        copies = []
        for m in range(4):
            copies += piece_copies(pieces, s, m, cot.at[m], cot_sem.at[m])
        return copies

    for copy in cot_loads(0):
        copy.start()
    for there, here, leaving, landing in late_blocks:

        @pl.when(there)
        def _(here=here, leaving=leaving, landing=landing):
            here.wait()
            leaving.wait_send()
            landing.wait_recv()

    whole_up = pltpu.make_async_copy(up, up_all_ref, local.at[2])
    whole_up.start()
    tile(0, 0)
    copies[0][0].wait_recv()
    copies[0][4].start()
    copies[0][1].wait_recv()
    copies[0][5].start()
    copies[1][0].start()
    copies[1][1].start()
    tile(1, 0)
    down_line.arrive(1)
    down_line.start(2)
    copies[0][3].wait_recv()
    tile(0, 1)
    copies[0][2].wait_recv()
    copies[1][2].start()
    copies[1][3].start()
    tile(0, 2)
    copies[1][0].wait_recv()
    copies[1][4].start()
    copies[1][1].wait_recv()
    copies[1][5].start()
    copies[0][4].wait_recv()
    copies[0][5].wait_recv()
    tile(0, 3)
    for step in range(3, count):
        down_line.arrive(step - 1)
        down_line.start(step)
    settle(0)
    settle(1)
    for copy in cot_loads(0):
        copy.wait()
    gradient_tiles(hidden_ref.at[0], cot, tiles, sums, down_part_ref, tile_sem, sum_sem)
    for copy in cot_loads(1):
        copy.start()
    copies[1][3].wait_recv()
    tile(1, 1)
    copies[1][2].wait_recv()
    tile(1, 2)
    copies[1][4].wait_recv()
    copies[1][5].wait_recv()
    gathered = pltpu.make_async_copy(rows, all_ref, local.at[0])
    gathered.start()
    tile(1, 3)
    down_line.arrive(count - 1)
    down_line.finish(range(1, count), True)
    whole_down = pltpu.make_async_copy(down, down_all_ref, local.at[1])
    whole_down.start()
    settle(0)
    settle(1)
    for copy in cot_loads(1):
        copy.wait()
    gradient_tiles(
        hidden_ref.at[1], cot, tiles, sums, down_part_ref, tile_sem, sum_sem,
        (down_part_ref, before, before_sem),
    )
    for s in range(2):
        for copy in copies[s]:
            copy.wait_send()
    gathered.wait()
    whole_up.wait()
    whole_down.wait()


def gradient_tiles(
    left_ref, right, tiles, sums, out_ref, tile_sem, sum_sem, before=None, span=None
):
    wide = tiles.shape[-1]
    first, steps = span if span is not None else (0, left_ref.shape[-1] // wide)
    lead = (slice(None),) * (len(left_ref.shape) - 1)
    tall = math.prod(tiles.shape[1:-1])

    def load(at, slot):
        columns = pl.ds(pl.multiple_of(at * wide, wide), wide)
        return pltpu.make_async_copy(
            left_ref.at[lead + (columns,)], tiles.at[slot], tile_sem.at[slot]
        )

    def rows_of(at):
        return pl.ds(pl.multiple_of(at * wide, wide), wide)

    def save(at, slot):
        return pltpu.make_async_copy(sums.at[slot], out_ref.at[rows_of(at), :], sum_sem.at[slot])

    def load_before(at, slot):
        before_ref, buffer, sem = before
        return pltpu.make_async_copy(before_ref.at[rows_of(at), :], buffer.at[slot], sem.at[slot])

    load(first, first % 2).start()
    if before is not None:
        load_before(first, first % 2).start()

    def one(at, carry):
        slot = lax.rem(at, 2)
        load(at, slot).wait()
        if before is not None:
            load_before(at, slot).wait()

        @pl.when(at + 1 < steps)
        def _():
            load(at + 1, 1 - slot).start()
            if before is not None:
                load_before(at + 1, 1 - slot).start()

        @pl.when(at >= first + 2)
        def _():
            save(at - 2, slot).wait()

        result = lax.dot_general(
            tiles[slot].reshape(tall, wide),
            right[...].reshape(tall, right.shape[-1]),
            (((0,), (0,)), ((), ())),
            preferred_element_type=F32,
        )
        if before is not None:
            result = result + before[1][slot].astype(F32)
        sums[slot] = result.astype(LOW)
        save(at, slot).start()
        return carry

    lax.fori_loop(first, steps, one, 0)
    save(steps - 2, (steps - 2) % 2).wait()
    save(steps - 1, (steps - 1) % 2).wait()


def feed_in(second, up_early, down, cot_pieces, up_late):
    rows_here, depth = second.shape[1:]
    units = up_early.shape[0]
    count = lax.axis_size("mp") // 2
    anywhere = pl.BlockSpec(memory_space=pl.ANY)
    dma = pltpu.SemaphoreType.DMA
    return pl.pallas_call(
        partial(feed_in_kernel, tuple(up_late)),
        in_specs=[anywhere] * (10 + len(up_late)),
        out_specs=[anywhere] * 6,
        out_shape=[
            jax.ShapeDtypeStruct((2, 4, rows_here, depth), LOW),
            jax.ShapeDtypeStruct((2, 4, rows_here, units), F32),
            jax.ShapeDtypeStruct((2, 4, rows_here, units), LOW),
            jax.ShapeDtypeStruct((units, depth), LOW),
            jax.ShapeDtypeStruct((units, depth), LOW),
            jax.ShapeDtypeStruct((units, depth), LOW),
        ],
        scratch_shapes=[
            pltpu.VMEM((2, 4, rows_here, depth), LOW),
            pltpu.VMEM((units, depth), LOW),
            pltpu.VMEM((2, rows_here, units), F32),
            pltpu.VMEM((2, rows_here, units), LOW),
            pltpu.VMEM((units, depth), LOW),
            pltpu.VMEM((4, rows_here, depth), LOW),
            pltpu.VMEM((2, 4, rows_here, WIDE), LOW),
            pltpu.VMEM((2, WIDE, depth), LOW),
            pltpu.VMEM((2, WIDE, depth), LOW),
            dma((4,)),
            dma((2, 2)),
            dma((2, 6)),
            dma((2, 6)),
            dma((4, 2)),
            dma((2,)),
            dma((2,)),
            dma((2,)),
        ]
        + [dma((len(up_late),))] * 3
        + line_semaphores(count),
        compiler_params=pltpu.CompilerParams(
            collective_id=1, has_side_effects=True, vmem_limit_bytes=VMEM_LIMIT
        ),
        cost_estimate=pl.CostEstimate(
            flops=2 * 8 * rows_here * depth * units * 3,
            bytes_accessed=60 * 2**20,
            transcendentals=0,
        ),
        name="feed_in",
    )(second, up_early, down, *cot_pieces, *up_late.values())


def piece_copies(pieces, s, m, target, sems):
    half = target.shape[-1] // 2
    if m == 0:
        return [pltpu.make_async_copy(pieces[0].at[s], target, sems.at[0])]
    return [
        pltpu.make_async_copy(
            pieces[2 * m - 1 + side].at[s], target.at[:, pl.ds(side * half, half)], sems.at[side]
        )
        for side in range(2)
    ]


def feed_out_kernel(
    cot_0, cot_1, cot_2, cot_3, cot_4, cot_5, cot_6, relu_ref, second_ref, up_ref, down_ref,
    grad_ref, up_part_ref, back_ref,
    up, shared, cot, relu, grad, part, arrived, tiles, sums, result, local, loads, outs, send, recv,
    tile_sem, sum_sem,
):
    units, depth = up.shape
    down = shared.at[pl.ds(0, units), :]
    second = shared.at[pl.ds(0, 8 * cot.shape[1]), :]
    half = depth // 2
    lanes = (pl.ds(0, half), pl.ds(half, half))
    to_x, to_y = plane_partners()
    weights = [
        pltpu.make_async_copy(down_ref, down, local.at[0]),
        pltpu.make_async_copy(up_ref, up, local.at[1]),
    ]
    order = [(s, m) for s in range(2) for m in (3, 1, 2, 0)]
    pieces = (cot_0, cot_1, cot_2, cot_3, cot_4, cot_5, cot_6)

    def load(at):
        s, m = order[at]
        slot = at % 2
        return piece_copies(pieces, s, m, cot.at[slot], loads.at[slot]) + [
            pltpu.make_async_copy(relu_ref.at[s, m], relu.at[slot], loads.at[slot, 2]),
        ]

    for copy in load(0) + weights:
        copy.start()
    greet([to_x, to_y])
    for copy in weights:
        copy.wait()
    def remote(s, source, number, side, partner):
        return pltpu.make_async_remote_copy(
            src_ref=part.at[s, source, :, lanes[side]],
            dst_ref=arrived.at[s, number],
            send_sem=send.at[s, number],
            recv_sem=recv.at[s, number],
            device_id=partner,
            device_id_type=MESH,
        )

    copies = [
        [
            remote(s, 1, 0, 0, to_x),
            remote(s, 3, 1, 0, to_x),
            remote(s, 2, 2, 1, to_y),
            remote(s, 3, 3, 1, to_y),
            remote(s, 2, 4, 0, to_y),
            remote(s, 1, 5, 1, to_x),
        ]
        for s in range(2)
    ]
    saving = [None, None]
    load_second = pltpu.make_async_copy(second_ref, second, local.at[0])

    def tile(at):
        s, m = order[at]
        slot = at % 2
        for copy in load(at):
            copy.wait()
        if at + 1 < len(order):
            for copy in load(at + 1):
                copy.start()
        if saving[slot] is not None:
            saving[slot].wait()

        def back(step, carry):
            columns = pl.ds(pl.multiple_of(step * CHUNK, CHUNK), CHUNK)
            product = dot_nt(cot[slot], down[columns, :])
            grad[slot, :, columns] = (product * 2.0 * relu[slot, :, columns]).astype(LOW)
            return carry

        lax.fori_loop(0, units // CHUNK, back, 0)
        if at + 1 == len(order):
            load_second.start()
        saving[slot] = pltpu.make_async_copy(grad.at[slot], grad_ref.at[s, m], outs.at[slot])
        saving[slot].start()

        def through(step, carry):
            columns = pl.ds(pl.multiple_of(step * CHUNK, CHUNK), CHUNK)
            part[s, m, :, columns] = dot(grad[slot], up[:, columns]).astype(LOW)
            return carry

        lax.fori_loop(0, depth // CHUNK, through, 0)

    def second_leg(s):
        copies[s][1].wait_recv()
        part[s, 2, :, lanes[0]] = (
            part[s, 2, :, lanes[0]].astype(F32) + arrived[s, 1].astype(F32)
        ).astype(LOW)
        copies[s][4].start()
        copies[s][3].wait_recv()
        part[s, 1, :, lanes[1]] = (
            part[s, 1, :, lanes[1]].astype(F32) + arrived[s, 3].astype(F32)
        ).astype(LOW)
        copies[s][5].start()

    def finish(s):
        for side, near, last in ((0, 0, 4), (1, 2, 5)):
            copies[s][near].wait_recv()
            copies[s][last].wait_recv()
            result[:, lanes[side]] = (
                part[s, 0, :, lanes[side]].astype(F32)
                + arrived[s, near].astype(F32)
                + arrived[s, last].astype(F32)
            )
        done = pltpu.make_async_copy(result, back_ref.at[s], local.at[2])
        done.start()
        return done

    def send_after(at):
        s, m = order[at]
        for number in {3: (1, 3), 1: (0,), 2: (2,), 0: ()}[m]:
            copies[s][number].start()

    for at in range(5):
        tile(at)
        send_after(at)
    second_leg(0)
    for at in range(5, 8):
        tile(at)
        send_after(at)
    done = finish(0)

    for slot in range(2):
        saving[slot].wait()
    load_second.wait()
    halves = units // WIDE // 2

    def some(span):
        gradient_tiles(grad_ref, second, tiles, sums, up_part_ref, tile_sem, sum_sem, span=span)

    some((0, halves))
    second_leg(1)
    some((halves, 2 * halves))
    done.wait()
    finish(1).wait()
    for s in range(2):
        for number in range(6):
            copies[s][number].wait_send()


def feed_out(cot_pieces, relu, second_all, up_all, down_all):
    rows_here, units = relu.shape[2:]
    depth = up_all.shape[1]
    anywhere = pl.BlockSpec(memory_space=pl.ANY)
    dma = pltpu.SemaphoreType.DMA
    return pl.pallas_call(
        feed_out_kernel,
        in_specs=[anywhere] * 11,
        out_specs=[anywhere] * 3,
        out_shape=[
            jax.ShapeDtypeStruct((2, 4, rows_here, units), LOW),
            jax.ShapeDtypeStruct((units, depth), LOW),
            jax.ShapeDtypeStruct((2, rows_here, depth), F32),
        ],
        scratch_shapes=[
            pltpu.VMEM((units, depth), LOW),
            pltpu.VMEM((max(units, 8 * rows_here), depth), LOW),
            pltpu.VMEM((2, rows_here, depth), LOW),
            pltpu.VMEM((2, rows_here, units), F32),
            pltpu.VMEM((2, rows_here, units), LOW),
            pltpu.VMEM((2, 4, rows_here, depth), LOW),
            pltpu.VMEM((2, 6, rows_here, depth // 2), LOW),
            pltpu.VMEM((2, 2, 4, rows_here, WIDE), LOW),
            pltpu.VMEM((2, WIDE, depth), LOW),
            pltpu.VMEM((rows_here, depth), F32),
            dma((3,)),
            dma((2, 3)),
            dma((2,)),
            dma((2, 6)),
            dma((2, 6)),
            dma((2,)),
            dma((2,)),
        ],
        compiler_params=pltpu.CompilerParams(
            collective_id=2, has_side_effects=True, vmem_limit_bytes=VMEM_LIMIT
        ),
        cost_estimate=pl.CostEstimate(
            flops=2 * 8 * rows_here * depth * units * 4,
            bytes_accessed=60 * 2**20,
            transcendentals=0,
        ),
        name="feed_out",
    )(*cot_pieces, relu, second_all.reshape(8 * rows_here, depth), up_all, down_all)


def feed_heads_kernel(
    x_ref, hidden_ref, down_ref,
    o_ref, feed_x0_ref, feed_x1_ref, feed_y0_ref, feed_y1_ref, keep_a_ref, keep_b_ref,
    landed, down, hidden, feed, local, send, recv, loads, outs,
):
    me = lax.axis_index("mp")
    units, depth = down.shape
    half = depth // 2
    lanes = (pl.ds(0, half), pl.ds(half, half))
    feed_x_refs, feed_y_refs = (feed_x0_ref, feed_x1_ref), (feed_y0_ref, feed_y1_ref)

    def source(at):
        return x_ref.at[:, :, head_lanes(at)]

    def target(at):
        return landed.at[:, at]

    weights = pltpu.make_async_copy(down_ref, down, local.at[2])
    weights.start()
    own = pltpu.make_async_copy(source(me), target(me), local.at[0])
    own.start()
    greet_members(())
    copies = member_copies(source, target, send, recv)
    for leaving, _ in copies:
        leaving.start()
    order = [(s, m) for s in range(2) for m in (3, 1, 2, 0)]

    def load(at):
        s, m = order[at]
        return pltpu.make_async_copy(hidden_ref.at[s, m], hidden.at[at % 2], loads.at[at % 2])

    load(0).start()
    weights.wait()
    feeding = [None, None]
    for at, (s, m) in enumerate(order):
        slot = at % 2
        load(at).wait()
        if at + 1 < len(order):
            load(at + 1).start()
        if feeding[slot] is not None:
            for copy in feeding[slot]:
                copy.wait()

        def one(step, carry, slot=slot):
            columns = pl.ds(pl.multiple_of(step * CHUNK, CHUNK), CHUNK)
            feed[slot, :, columns] = dot(hidden[slot], down[:, columns]).astype(LOW)
            return carry

        lax.fori_loop(0, depth // CHUNK, one, 0)
        targets = (
            (keep_a_ref.at[s, 0], feed_x_refs[s].at[0], keep_a_ref.at[s, 1], feed_x_refs[s].at[1])[m],
            (keep_b_ref.at[s, 0], keep_b_ref.at[s, 1], feed_y_refs[s].at[0], feed_y_refs[s].at[1])[m],
        )
        feeding[slot] = [
            pltpu.make_async_copy(feed.at[slot, :, lanes[side]], there, outs.at[slot, side])
            for side, there in enumerate(targets)
        ]
        for copy in feeding[slot]:
            copy.start()
    own.wait()
    for _, landing in copies:
        landing.wait_recv()
    save = pltpu.make_async_copy(landed, o_ref, local.at[1])
    save.start()
    for leaving, _ in copies:
        leaving.wait_send()
    for slot in feeding:
        for copy in slot:
            copy.wait()
    save.wait()


def feed_heads(x, hidden, down_all):
    parts, rows_here, width = x.shape
    mp = lax.axis_size("mp")
    units, depth = down_all.shape
    anywhere = pl.BlockSpec(memory_space=pl.ANY)
    dma = pltpu.SemaphoreType.DMA
    shape = (parts, mp, rows_here, 128)
    out, *terms = pl.pallas_call(
        feed_heads_kernel,
        in_specs=[pl.BlockSpec(memory_space=pltpu.VMEM)] + [anywhere] * 2,
        out_specs=[anywhere] * 7,
        out_shape=[jax.ShapeDtypeStruct(shape, LOW)]
        + [jax.ShapeDtypeStruct((2, rows_here, depth // 2), LOW)] * 4
        + [jax.ShapeDtypeStruct((2, 2, rows_here, depth // 2), LOW)] * 2,
        scratch_shapes=[
            pltpu.VMEM(shape, LOW),
            pltpu.VMEM((units, depth), LOW),
            pltpu.VMEM((2, rows_here, units), LOW),
            pltpu.VMEM((2, rows_here, depth), LOW),
            dma((3,)),
            dma((mp,)),
            dma((mp,)),
            dma((2,)),
            dma((2, 2)),
        ],
        compiler_params=pltpu.CompilerParams(
            collective_id=6, has_side_effects=True, vmem_limit_bytes=48 * 2**20
        ),
        cost_estimate=pl.CostEstimate(flops=2**35, bytes_accessed=2**24, transcendentals=0),
        name="feed_heads",
    )(x, hidden, down_all)
    return [out.reshape(parts, mp * rows_here, 128)] + terms


def finish_kernel(
    ways, qk_ref, v_ref, out_ref, norms_ref, taps_ref, *refs
):
    carried, refs = list(zip(ways, refs[: len(ways)])), refs[len(ways) :]
    joint_ref, norms_sum_ref, taps_sum_ref = refs[:3]
    targets, refs = refs[3 : 3 + len(ways)], refs[3 + len(ways) :]
    (
    acc, got, plane_in, line_in, gathered, norms_all, taps_all, norms_dp, taps_dp,
    local, swap_send, swap_recv, plane_send_sem, plane_recv_sem, line_send_sem, line_recv_sem,
    gather_send, gather_recv, small_send, small_recv, carry_send, carry_recv,
    ) = refs
    mp = lax.axis_size("mp")
    dp = lax.axis_index("dp")
    me = lax.axis_index("mp")
    z, core = mesh_place()
    count = mp // 2
    depth = acc.shape[3]
    half = depth // 2
    lanes = (pl.ds(0, half), pl.ds(half, half))
    to_x, to_y = plane_partners()
    dp_x = dp + 1 - 2 * lax.rem(dp, 2)
    dp_y = dp + 2 - 4 * (dp // 2)
    dp_xy = dp_x + 2 - 4 * (dp_x // 2)
    parts = (qk_ref, v_ref, out_ref)
    spans = (pl.ds(0, HD // 2), pl.ds(HD // 2, HD // 4), pl.ds(3 * HD // 4, HD // 4))
    loads = [
        pltpu.make_async_copy(part.at[:, core], acc.at[:, :, span, :], local.at[at])
        for at, (part, span) in enumerate(zip(parts, spans))
    ]
    for copy in loads:
        copy.start()

    barrier = pltpu.get_barrier_semaphore()
    for step in range(1, mp):
        pl.semaphore_signal(
            barrier, inc=1, device_id={"mp": lax.rem(me + step, mp)}, device_id_type=MESH
        )
    for step in range(1, 4):
        pl.semaphore_signal(
            barrier, inc=1, device_id={"dp": lax.rem(dp + step, 4)}, device_id_type=MESH
        )
    pl.semaphore_wait(barrier, mp + 2)

    swaps = [
        [
            wire(
                part.at[:, 1 - core, quarter], got.at[:, quarter, span, :],
                swap_send.at[at, number], swap_recv.at[at, number], other_core(),
            )
            for at, (part, span) in enumerate(zip(parts, spans))
        ]
        for number, quarter in enumerate((dp_xy, dp_x, dp_y, dp))
    ]
    for group in swaps:
        for copy in group:
            copy.start()

    def small(axis, at, others, source, target, number, first):
        out = []
        for step in range(1, others):
            to = lax.rem(at + step, others)
            frm = lax.rem(at + others - step, others)
            sems = (small_send.at[number, step], small_recv.at[number, step], {axis: to})
            out.append((wire(source(to), target.at[at], *sems), wire(source(to), target.at[frm], *sems)))
        return out

    own_small = [
        pltpu.make_async_copy(norms_ref, norms_all.at[me], local.at[3]),
        pltpu.make_async_copy(taps_ref.at[me], taps_all.at[me], local.at[4]),
    ]
    over_mp = small("mp", me, mp, lambda to: norms_ref, norms_all, 0, None) + small(
        "mp", me, mp, lambda to: taps_ref.at[to], taps_all, 1, None
    )

    for copy in own_small:
        copy.start()
    for leaving, _ in over_mp:
        leaving.start()

    def add(quarter, side, number):
        acc[:, quarter, :, lanes[side]] = (
            acc[:, quarter, :, lanes[side]].astype(F32) + plane_in[number].astype(F32)
        ).astype(LOW)

    def add_core(number, quarter):
        for copy in swaps[number]:
            copy.wait_recv()
        acc[:, quarter] = (acc[:, quarter].astype(F32) + got[:, quarter].astype(F32)).astype(LOW)

    def plane(quarter, side, partner, number):
        return wire(
            acc.at[:, quarter, :, lanes[side]], plane_in.at[number],
            plane_send_sem.at[number], plane_recv_sem.at[number], partner,
        )

    sends = [
        plane(dp_x, 0, to_x, 0),
        plane(dp_xy, 0, to_x, 1),
        plane(dp_y, 1, to_y, 2),
        plane(dp_xy, 1, to_y, 3),
        plane(dp_y, 0, to_y, 4),
        plane(dp_x, 1, to_x, 5),
    ]
    for copy in loads:
        copy.wait()
    add_core(0, dp_xy)
    sends[1].start()
    sends[3].start()
    add_core(1, dp_x)
    sends[0].start()
    add_core(2, dp_y)
    sends[2].start()
    add_core(3, dp)
    sends[1].wait_recv()
    add(dp_y, 0, 1)
    sends[4].start()
    sends[3].wait_recv()
    add(dp_x, 1, 3)
    sends[5].start()
    for _, landing in over_mp:
        landing.wait_recv()
    for copy in own_small:
        copy.wait()
    norms_dp[dp] = jnp.sum(norms_all[...], axis=0)
    taps_dp[dp] = jnp.sum(taps_all[...], axis=0)
    over_dp = small("dp", dp, 4, lambda to: norms_dp.at[dp], norms_dp, 2, None) + small(
        "dp", dp, 4, lambda to: taps_dp.at[dp], taps_dp, 3, None
    )
    for leaving, _ in over_dp:
        leaving.start()
    sends[0].wait_recv()
    add(dp, 0, 0)
    sends[2].wait_recv()
    add(dp, 1, 2)
    sends[4].wait_recv()
    add(dp, 0, 4)
    sends[5].wait_recv()
    add(dp, 1, 5)

    carries = carry_copies(carried, targets, carry_send, carry_recv)
    for copy in carries:
        copy.start()

    def line(step):
        out = []
        for way, turn in enumerate((1, -1)):
            target = z + turn * (count - step)
            far = z + turn
            lands = far - 2 * turn + turn * (count - step)
            sends = (target >= 0) & (target < count)
            receives = (lands >= 0) & (lands < count) & (z - turn >= 0) & (z - turn < count)
            at = jnp.clip(target, 0, count - 1)
            to = jnp.clip(lands, 0, count - 1)
            copy = wire(
                acc.at[at, dp], line_in.at[way, step - 1],
                line_send_sem.at[way, step - 1], line_recv_sem.at[way, step - 1],
                line_partner(z, turn),
            )
            out.append((sends, receives, to, copy))
        return out

    for step in range(1, count):
        legs = line(step)
        for sends_now, _, _, copy in legs:
            pl.when(sends_now)(copy.start)
        for way, (_, receives, to, copy) in enumerate(legs):

            @pl.when(receives)
            def _(to=to, copy=copy, way=way):
                copy.wait_recv()
                acc[to, dp] = (
                    acc[to, dp].astype(F32) + line_in[way, step - 1].astype(F32)
                ).astype(LOW)

    gathered[dp] = acc[z, dp]

    def gather(quarter, side, partner, number):
        block = gathered.at[quarter, :, lanes[side]]
        return wire(block, block, gather_send.at[number], gather_recv.at[number], partner)

    leaving = [
        gather(dp, 0, to_x, 0), gather(dp, 1, to_y, 1), gather(dp, 0, to_y, 2), gather(dp, 1, to_x, 3),
        gather(dp_x, 0, to_y, 4), gather(dp_y, 1, to_x, 5),
    ]
    landing = [
        gather(dp_x, 0, to_x, 0), gather(dp_y, 1, to_y, 1), gather(dp_y, 0, to_y, 2), gather(dp_x, 1, to_x, 3),
        gather(dp_xy, 0, to_y, 4), gather(dp_xy, 1, to_x, 5),
    ]
    for number in range(4):
        leaving[number].start()
    for _, landed in over_dp:
        landed.wait_recv()
    norms_sum_ref[...] = jnp.sum(norms_dp[...], axis=0)
    taps_sum_ref[...] = jnp.sum(taps_dp[...], axis=0)
    landing[0].wait_recv()
    leaving[4].start()
    landing[1].wait_recv()
    leaving[5].start()
    for number in range(2, 6):
        landing[number].wait_recv()
    save = pltpu.make_async_copy(gathered, joint_ref, local.at[5])
    save.start()
    for group in swaps:
        for copy in group:
            copy.wait_send()
    for copy in sends:
        copy.wait_send()
    for step in range(1, count):
        for sends_now, _, _, copy in line(step):
            pl.when(sends_now)(copy.wait_send)
    for copy in leaving:
        copy.wait_send()
    for copy, _ in over_mp + over_dp:
        copy.wait_send()
    for copy in carries:
        copy.wait()
    save.wait()


def finish(qk, v, out, norms, taps, carried):
    mp = lax.axis_size("mp")
    count = mp // 2
    depth = qk.shape[-1]
    anywhere = pl.BlockSpec(memory_space=pl.ANY)
    vmem = pl.BlockSpec(memory_space=pltpu.VMEM)
    dma = pltpu.SemaphoreType.DMA
    return pl.pallas_call(
        partial(finish_kernel, tuple(way for way, _ in carried)),
        in_specs=[anywhere] * 3 + [vmem] * 2 + [anywhere] * len(carried),
        out_specs=[anywhere, vmem, vmem] + [anywhere] * len(carried),
        out_shape=[
            jax.ShapeDtypeStruct((4, HD, depth), LOW),
            jax.ShapeDtypeStruct(norms.shape, F32),
            jax.ShapeDtypeStruct(taps.shape[1:], F32),
        ]
        + [jax.ShapeDtypeStruct(block.shape, block.dtype) for _, block in carried],
        scratch_shapes=[
            pltpu.VMEM((count, 4, HD, depth), LOW),
            pltpu.VMEM((count, 4, HD, depth), LOW),
            pltpu.VMEM((6, count, HD, depth // 2), LOW),
            pltpu.VMEM((2, count - 1, HD, depth), LOW),
            pltpu.VMEM((4, HD, depth), LOW),
            pltpu.VMEM((mp,) + norms.shape, F32),
            pltpu.VMEM(taps.shape, F32),
            pltpu.VMEM((4,) + norms.shape, F32),
            pltpu.VMEM((4,) + taps.shape[1:], F32),
            dma((6,)),
            dma((3, 4)),
            dma((3, 4)),
            dma((6,)),
            dma((6,)),
            dma((2, count)),
            dma((2, count)),
            dma((6,)),
            dma((6,)),
            dma((4, mp)),
            dma((4, mp)),
            dma((len(carried),)),
            dma((len(carried),)),
        ],
        compiler_params=pltpu.CompilerParams(
            collective_id=8, has_side_effects=True, vmem_limit_bytes=VMEM_LIMIT
        ),
        cost_estimate=pl.CostEstimate(flops=2**36, bytes_accessed=2**26, transcendentals=0),
        name="finish",
    )(
        qk, v, out, norms, taps, *(block for _, block in carried),
    )


def plane_send(block, mask):
    return lax.ppermute(block, "dp", [(d, d ^ mask) for d in range(lax.axis_size("dp"))])


def placed(own, legs, last, me, turn):
    one_x, two_y, one_y, two_x = legs
    units, width = own.shape
    wide = 256
    steps = width // 2 // wide

    def kernel(me_ref, own_ref, one_x, two_x, one_y, two_y, one_xy, two_xy, o_ref):
        first = pl.program_id(0) < steps
        blocks = [own_ref[...]] + [
            jnp.where(first, one[...], two[...])
            for one, two in ((one_x, two_x), (one_y, two_y), (one_xy, two_xy))
        ]
        odd, high = lax.rem(me_ref[0], 2) == 1, me_ref[0] >= 2
        blocks = [jnp.where(odd, blocks[at ^ 1], blocks[at]) for at in range(4)]
        blocks = [jnp.where(high, blocks[at ^ 2], blocks[at]) for at in range(4)]
        for at, block in enumerate(blocks):
            if turn:
                o_ref[:, at * units : (at + 1) * units] = block.astype(F32).T
            else:
                o_ref[at * units : (at + 1) * units, :] = block.astype(F32)

    def half(side):
        if side == 0:
            return pl.BlockSpec((units, wide), lambda i, me: (0, jnp.minimum(i, steps - 1)))
        return pl.BlockSpec((units, wide), lambda i, me: (0, jnp.maximum(i - steps, 0)))

    if turn:
        shape = (width, 4 * units)
        out_spec = pl.BlockSpec((wide, 4 * units), lambda i, me: (i, 0))
    else:
        shape = (4 * units, width)
        out_spec = pl.BlockSpec((4 * units, wide), lambda i, me: (0, i))
    return pl.pallas_call(
        kernel,
        grid_spec=pltpu.PrefetchScalarGridSpec(
            num_scalar_prefetch=1,
            grid=(2 * steps,),
            in_specs=[pl.BlockSpec((units, wide), lambda i, me: (0, i))] + [half(0), half(1)] * 3,
            out_specs=out_spec,
        ),
        out_shape=jax.ShapeDtypeStruct(shape, F32),
        compiler_params=pltpu.CompilerParams(vmem_limit_bytes=32 * 2**20),
        cost_estimate=pl.CostEstimate(flops=0, bytes_accessed=2**24, transcendentals=0),
        name="placed",
    )(me.reshape(1).astype(jnp.int32), own, one_x, two_x, one_y, two_y, *last)


def plane_gather_begin(block, axis=-1):
    half = block.shape[axis] // 2
    one, two = jnp.split(block, [half], axis=axis)
    return plane_send(one, 1), plane_send(two, 2), plane_send(one, 2), plane_send(two, 1)


def plane_gather_end(legs):
    one_x, two_y, one_y, two_x = legs
    return plane_send(one_x, 2), plane_send(two_y, 1)


def line_step(blocks, step):
    count = lax.axis_size("mp") // 2
    up = [(2 * z + c, 2 * z + 2 + c) for z in range(step - 1, count - 1) for c in range(2)]
    down = [(2 * z + c, 2 * z - 2 + c) for z in range(1, count - step + 1) for c in range(2)]
    return lax.ppermute(blocks[0], "mp", up), lax.ppermute(blocks[1], "mp", down)


def per_device(
    inputs,
    cotangent,
    short_lengths,
    long_lengths,
    norm1_gain,
    norm1_bias,
    query_weight,
    key_weight,
    value_weight,
    query_kernel,
    key_kernel,
    value_kernel,
    out_weight,
    norm2_gain,
    norm2_bias,
    up_weight,
    down_weight,
):
    rows_here = inputs.shape[1]
    width = inputs.shape[2]
    mp = lax.axis_size("mp")
    dp = lax.axis_size("dp")
    me_dp = lax.axis_index("dp")
    me_mp = lax.axis_index("mp")
    group = rows_here * mp
    chips = mp // 2
    hidden_here = up_weight.shape[1]
    share = hidden_here // dp

    starts = jnp.stack(
        [document_starts(short_lengths[0], group), document_starts(long_lengths[0], group)]
    )
    rows = inputs.astype(F32)

    def quarters(weight):
        return weight.reshape(4, weight.shape[0] // 4, width)

    qk_own = jnp.concatenate([query_weight, key_weight], axis=1).T
    up_own = lax.dynamic_slice_in_dim(up_weight, me_dp * share, share, 1).T
    down_own = lax.dynamic_slice_in_dim(down_weight, me_dp * share, share, 0)
    qk_taps = jnp.concatenate([query_kernel, key_kernel], axis=1)
    v_taps = jnp.concatenate([value_kernel, value_kernel], axis=1)
    taps_own = jnp.pad(jnp.stack([qk_taps, qk_taps, v_taps]), ((0, 0), (0, 5), (0, 0)))
    places = jnp.arange(group, dtype=jnp.int32)
    offsets = lax.dynamic_slice_in_dim(
        jnp.pad(places[None, :] - starts, ((0, 0), (0, HALO))), me_mp * rows_here, rows_here + HALO, 1
    )
    masks = jnp.stack(
        [
            offsets[:, :rows_here] >= 1,
            offsets[:, :rows_here] >= 2,
            offsets[:, 1 : rows_here + 1] >= 1,
            offsets[:, 2 : rows_here + 2] >= 2,
        ],
        axis=1,
    ).astype(F32)[..., None]
    wide_masks = jnp.broadcast_to(masks, masks.shape[:3] + (HD,))
    masks = jnp.stack(
        [
            jnp.concatenate([wide_masks[left], wide_masks[right]], axis=2)
            for left, right in ((0, 0), (1, 1), (0, 1))
        ]
    )

    qk_all, v_all, out_all, taps, normed, up_early, raw, mixed, one_x, two_y = front(
        inputs, norm1_gain, norm1_bias, quarters(qk_own), quarters(value_weight.T), quarters(out_weight), taps_own, up_own,
        masks, cotangent,
    )
    qk_all = qk_all.reshape(mp * 2 * HD, width)
    v_all = v_all.reshape(mp * HD, width)
    out_all = out_all.reshape(mp * HD, width)
    mixed = mixed.reshape(3, group, 128)
    cot, mixed, up_early = lax.optimization_barrier((cotangent, mixed, up_early))

    def early_block(at):
        start = (2 * jnp.clip(at, 0, chips - 1) + me_mp % 2) * share
        return lax.dynamic_slice_in_dim(up_early, start, share, 0)

    late = range(early_steps(chips)[-1] + 1, chips)
    up_late = {}
    blocks = (early_block(me_mp // 2 - late[0] + 1), early_block(me_mp // 2 + late[0] - 1))
    for step in late:
        blocks = line_step(blocks, step)
        up_late[step, 1], up_late[step, -1] = blocks
    one_y, two_x = plane_send(cot[:, :, : width // 2], 2), plane_send(cot[:, :, width // 2 :], 1)
    one_xy, two_xy = plane_send(one_x, 2), plane_send(two_y, 1)

    def side_by_side(pair):
        split = pair.reshape(2, rows_here, mp, HD)
        return split.transpose(1, 2, 0, 3).reshape(1, rows_here, mp * 2 * HD)

    def apart(joint):
        split = joint.reshape(joint.shape[1], mp, 2, HD)
        return split.transpose(2, 0, 1, 3).reshape(2, joint.shape[1], mp * HD)

    attended_head, wide, total = attend(mixed, starts)
    attended_head, up_late = lax.optimization_barrier((attended_head, up_late))
    attended = apart(attended_back(attended_head, rows_here))
    middle = rows + dot(attended, out_all)
    second = layer_norm(middle, norm2_gain, norm2_bias).astype(LOW)

    second, one_y, two_x, one_xy, two_xy = lax.optimization_barrier(
        (second, one_y, two_x, one_xy, two_xy)
    )
    cot_pieces = (cot, one_x, two_x, one_y, two_y, one_xy, two_xy)
    second_all, relu, hidden, down_all, up_all, down_part = feed_in(
        second, up_early, down_own, cot_pieces, up_late
    )
    down_mine = lax.psum_scatter(down_part, "mp", scatter_dimension=0, tiled=True)
    grad_pre, up_part, grad_second = feed_out(
        cot_pieces, relu, second_all, up_all, down_all
    )
    up_mine = lax.psum_scatter(up_part, "mp", scatter_dimension=0, tiled=True)
    grad_second, down_mine = lax.optimization_barrier((grad_second, down_mine))
    down_legs = plane_gather_begin(down_mine)

    def norm_back(values, gain, grad):
        flat = values.reshape(-1, width)
        unused, pull = jax.vjp(layer_norm, flat, gain, norm1_bias)
        grad_rows, grad_gain, grad_shift = pull(grad.reshape(-1, width))
        return grad_rows.reshape(values.shape), grad_gain, grad_shift

    grad_middle, gain_two, shift_two = norm_back(middle, norm2_gain, grad_second)
    grad_middle = grad_middle + cotangent.astype(F32)
    branch = grad_middle.astype(LOW)
    grad_attended = jnp.einsum("srd,hd->srh", branch, out_all, preferred_element_type=F32).astype(LOW)
    grad_head, feed_x0, feed_x1, feed_y0, feed_y1, keep_a, keep_b = feed_heads(
        side_by_side(grad_attended), hidden, down_all
    )
    grad_head, down_legs, feed_x0, feed_y0 = lax.optimization_barrier(
        (grad_head, down_legs, feed_x0, feed_y0)
    )
    down_last = plane_gather_end(down_legs)
    x_first, y_first = plane_send(feed_x0, 1), plane_send(feed_y0, 2)
    grad_mixed_head = attend_back(mixed, grad_head, wide, total, starts, HALO)
    grad_mixed_head, down_last, x_first, y_first = lax.optimization_barrier(
        (grad_mixed_head, down_last, x_first, y_first)
    )
    down_grad = placed(down_mine, down_legs, down_last, me_dp, False)

    def add(left, right):
        return left.astype(F32) + right.astype(F32)

    feed_a0, feed_b0 = add(keep_a[0, 1], x_first[1]).astype(LOW), add(keep_b[0, 1], y_first[1]).astype(LOW)
    grad_raw, tap_sums, qk_part, v_part, out_part, x_second, y_second, feed_a0, feed_b0 = project_back(
        grad_mixed_head, raw, taps, masks, normed, attended, branch,
        ((0, feed_x1), (1, feed_y1), (1, feed_a0), (0, feed_b0)),
    )
    grad_raw, down_last = lax.optimization_barrier((grad_raw, down_last))
    grad_raw, up_mine = lax.optimization_barrier((grad_raw, up_mine))
    up_legs = plane_gather_begin(up_mine)
    feed_a1, feed_b1 = add(keep_a[1, 1], x_second[1]).astype(LOW), add(keep_b[1, 1], y_second[1]).astype(LOW)

    def split_parts(part):
        return part.reshape(mp // 2, 2, 4, part.shape[1] // 8, width)

    grad_normed = dot(grad_raw[:2], qk_all) + dot(apart(grad_raw[2:]), v_all)
    grad_input, gain_one, shift_one = norm_back(rows, norm1_gain, grad_normed)
    input_grads = grad_middle + grad_input
    norms = jnp.pad(jnp.stack([gain_one, shift_one, gain_two, shift_two]), ((0, 4), (0, 0)))
    qk_sums = (tap_sums[0] + tap_sums[1]).reshape(8, mp, 2 * HD)
    v_sums = tap_sums[2].reshape(8, mp, 2, HD).sum(axis=2)
    taps_part = jnp.concatenate([qk_sums, v_sums, jnp.zeros_like(v_sums)], axis=2)
    taps_part = taps_part.transpose(1, 0, 2)
    norms, up_legs = lax.optimization_barrier((norms, up_legs))
    joint_grad, small_sum, taps_sum, feed_a1, feed_b1, one_xy, two_xy = finish(
        split_parts(qk_part), split_parts(v_part), split_parts(out_part), norms, taps_part,
        ((1, feed_a1), (0, feed_b1), (1, up_legs[0]), (0, up_legs[1])),
    )
    results = jnp.stack(
        [
            middle[s]
            + jnp.concatenate(
                [
                    add(keep_a[s, 0], x_in[0]) + a_in.astype(F32),
                    add(keep_b[s, 0], y_in[0]) + b_in.astype(F32),
                ],
                axis=1,
            )
            for s, (x_in, y_in, a_in, b_in) in enumerate(
                ((x_first, y_first, feed_a0, feed_b0), (x_second, y_second, feed_a1, feed_b1))
            )
        ]
    ).astype(LOW)
    up_grad = placed(up_mine, up_legs, (one_xy, two_xy), me_dp, True)
    joint_grad = joint_grad.astype(F32)
    qk_grad = joint_grad[:, : HD // 2].reshape(2 * HD, width).T
    v_grad = joint_grad[:, HD // 2 : 3 * HD // 4].reshape(HD, width).T
    out_grad = joint_grad[:, 3 * HD // 4 :].reshape(HD, width)
    taps_sum = taps_sum[:3]
    return (
        results,
        input_grads,
        small_sum[0],
        small_sum[1],
        qk_grad[:, :HD],
        qk_grad[:, HD:],
        v_grad,
        taps_sum[:, :HD],
        taps_sum[:, HD : 2 * HD],
        taps_sum[:, 2 * HD : 3 * HD],
        out_grad,
        small_sum[2],
        small_sum[3],
        up_grad,
        down_grad,
    )


def solution(mesh):
    return jax.shard_map(
        per_device,
        mesh=mesh,
        in_specs=(
            P(None, ("dp", "mp"), None),
            P(None, ("dp", "mp"), None),
            P("dp", None),
            P("dp", None),
            P(),
            P(),
            P(None, "mp"),
            P(None, "mp"),
            P(None, "mp"),
            P(None, "mp"),
            P(None, "mp"),
            P(None, "mp"),
            P("mp", None),
            P(),
            P(),
            P(None, "mp"),
            P("mp", None),
        ),
        out_specs=(
            P(None, ("dp", "mp"), None),
            P(None, ("dp", "mp"), None),
            P(),
            P(),
            P(None, "mp"),
            P(None, "mp"),
            P(None, "mp"),
            P(None, "mp"),
            P(None, "mp"),
            P(None, "mp"),
            P("mp", None),
            P(),
            P(),
            P(None, "mp"),
            P("mp", None),
        ),
        check_vma=False,
    )
```

```python
import math
from functools import partial

import jax
import jax.numpy as jnp
from jax import lax
from jax.experimental import pallas as pl
from jax.experimental.pallas import tpu as pltpu
from jax.sharding import PartitionSpec as P

HD = 64
QUERIES, KEYS = 512, 512
WIDE = 256
CHUNK = 512
VMEM_LIMIT = 63 * 1024 * 1024
MESH = pl.DeviceIdType.MESH
LOW = jnp.bfloat16
F32 = jnp.float32


def dot(left, right):
    return jnp.dot(left, right, preferred_element_type=F32)


def layer_norm(rows, gain, shift):
    row_mean = jnp.mean(rows, axis=-1, keepdims=True)
    centered = rows - row_mean
    variance = jnp.mean(centered * centered, axis=-1, keepdims=True)
    return centered * lax.rsqrt(variance + 1e-05) * gain + shift


def document_starts(lengths, count):
    places = jnp.arange(count, dtype=jnp.int32)
    starts, end = jnp.zeros_like(places), 0
    for at in range(lengths.shape[0]):
        end = end + lengths[at]
        starts = starts + jnp.where(places >= end, lengths[at], 0)
    return starts


def allowed_pairs(start_row, key_block, query_block):
    shape = (KEYS, QUERIES)
    keys = key_block * KEYS + lax.broadcasted_iota(jnp.int32, shape, 0)
    queries = query_block * QUERIES + lax.broadcasted_iota(jnp.int32, (1, QUERIES), 1)
    return (keys <= queries) & (keys >= start_row)


def key_blocks(first_ref, s, step):
    return first_ref[s, step], ((step + 1) * QUERIES + KEYS - 1) // KEYS


def attend_kernel(
    first_ref, start_ref, qk_ref, v_ref, out_ref, wide_ref, total_ref, values_t
):
    s, step = pl.program_id(0), pl.program_id(1)

    @pl.when(step == 0)
    def _():
        def turn(at, carry):
            rows = pl.ds(pl.multiple_of(at * KEYS, KEYS), KEYS)
            both = v_ref[0, rows, :].T
            values_t[at] = jnp.where(s == 0, both[:HD], both[HD:])
            return carry

        lax.fori_loop(0, values_t.shape[0], turn, 0)

    here = pl.ds(pl.multiple_of(step * QUERIES, QUERIES), QUERIES)
    query_t = (qk_ref[0, here, 0:HD] * HD ** (-0.5)).astype(LOW).T
    start_row = start_ref[0]

    def one(at, carry):
        top, summed, acc = carry
        rows = pl.ds(pl.multiple_of(at * KEYS, KEYS), KEYS)
        scores = dot(qk_ref[0, rows, HD : 2 * HD], query_t)
        scores = jnp.where(allowed_pairs(start_row, at, step), scores, -1e30)
        new_top = jnp.maximum(top, jnp.max(scores, axis=0, keepdims=True))
        powered = jnp.exp(scores - new_top)
        shrink = jnp.exp(top - new_top)
        summed = summed * shrink + jnp.sum(powered, axis=0, keepdims=True)
        acc = acc * shrink + dot(values_t[at], powered.astype(LOW))
        return new_top, summed, acc

    top, summed, acc = lax.fori_loop(
        *key_blocks(first_ref, s, step),
        one,
        (
            jnp.full((1, QUERIES), -1e30, F32),
            jnp.zeros((1, QUERIES), F32),
            jnp.zeros((HD, QUERIES), F32),
        ),
    )
    result = acc / summed
    wide_ref[0] = result
    total_ref[0] = top + jnp.log(summed)
    low = result.T.astype(LOW)

    @pl.when(s == 0)
    def _():
        out_ref[0, here, 0:HD] = low

    @pl.when(s == 1)
    def _():
        out_ref[0, here, HD : 2 * HD] = low


def attend(mixed, starts):
    group = mixed.shape[1]
    steps = group // QUERIES
    row = pl.BlockSpec((1, 1, QUERIES), lambda s, i, first: (s, 0, i))
    return pl.pallas_call(
        attend_kernel,
        grid_spec=pltpu.PrefetchScalarGridSpec(
            num_scalar_prefetch=1,
            grid=(2, steps),
            in_specs=[
                row,
                pl.BlockSpec((1, group, 2 * HD), lambda s, i, first: (s, 0, 0)),
                pl.BlockSpec((1, group, 2 * HD), lambda s, i, first: (2, 0, 0)),
            ],
            out_specs=[
                pl.BlockSpec((1, group, 2 * HD), lambda s, i, first: (0, 0, 0)),
                pl.BlockSpec((1, HD, QUERIES), lambda s, i, first: (s, 0, i)),
                row,
            ],
            scratch_shapes=[pltpu.VMEM((group // KEYS, HD, KEYS), LOW)],
        ),
        out_shape=[
            jax.ShapeDtypeStruct((1, group, 2 * HD), LOW),
            jax.ShapeDtypeStruct((2, HD, group), F32),
            jax.ShapeDtypeStruct((2, 1, group), F32),
        ],
        compiler_params=pltpu.CompilerParams(vmem_limit_bytes=32 * 1024 * 1024),
        cost_estimate=pl.CostEstimate(
            flops=2**34, bytes_accessed=group * 2048, transcendentals=group * group // 4
        ),
        name="attend",
    )(starts[:, ::QUERIES] // KEYS, starts[:, None, :], mixed, mixed)


def attend_back_kernel(
    first_ref, start_ref, qk_ref, v_ref, grad_ref, wide_ref, total_ref, out_ref,
    keys_t, values, grad_keys, grad_values,
):
    s, step = pl.program_id(0), pl.program_id(1)
    group = qk_ref.shape[1]

    @pl.when(step == 0)
    def _():
        def turn(at, carry):
            rows = pl.ds(pl.multiple_of(at * KEYS, KEYS), KEYS)
            keys_t[at] = qk_ref[0, rows, HD : 2 * HD].T
            both = v_ref[0, rows, :]
            values[rows, :] = jnp.where(s == 0, both[:, :HD], both[:, HD:])
            return carry

        lax.fori_loop(0, keys_t.shape[0], turn, 0)
        grad_keys[...] = jnp.zeros(grad_keys.shape, F32)
        grad_values[...] = jnp.zeros(grad_values.shape, F32)

    here = pl.ds(pl.multiple_of(step * QUERIES, QUERIES), QUERIES)
    query = (qk_ref[0, here, 0:HD] * HD ** (-0.5)).astype(LOW)
    query_t = query.T
    both = grad_ref[0]
    grad = jnp.where(s == 0, both[:, :HD], both[:, HD:])
    grad_t = grad.T
    start_row = start_ref[0]
    total = total_ref[0]
    inner = jnp.sum(grad_t.astype(F32) * wide_ref[0], axis=0, keepdims=True)

    def one(at, acc):
        rows = pl.ds(pl.multiple_of(at * KEYS, KEYS), KEYS)
        scores = dot(qk_ref[0, rows, HD : 2 * HD], query_t)
        scores = jnp.where(allowed_pairs(start_row, at, step), scores, -1e30)
        probs = jnp.exp(scores - total)
        grad_probs = dot(values[rows, :], grad_t)
        grad_scores = (probs * (grad_probs - inner)).astype(LOW)
        grad_values[rows, :] += dot(probs.astype(LOW), grad)
        grad_keys[rows, :] += dot(grad_scores, query)
        return acc + dot(keys_t[at], grad_scores)

    acc = lax.fori_loop(
        *key_blocks(first_ref, s, step), one, jnp.zeros((HD, QUERIES), F32)
    )
    out_ref[s, here, 0:HD] = (acc * HD ** (-0.5)).T.astype(out_ref.dtype)

    @pl.when(step == pl.num_programs(1) - 1)
    def _():
        out_ref[s, 0:group, HD : 2 * HD] = grad_keys[...].astype(out_ref.dtype)
        out_ref[s, group:, :] = jnp.zeros((out_ref.shape[1] - group, 2 * HD), out_ref.dtype)

        @pl.when(s == 0)
        def _():
            out_ref[2, 0:group, 0:HD] = grad_values[...].astype(out_ref.dtype)

        @pl.when(s == 1)
        def _():
            out_ref[2, 0:group, HD : 2 * HD] = grad_values[...].astype(out_ref.dtype)
            out_ref[2, group:, :] = jnp.zeros((out_ref.shape[1] - group, 2 * HD), out_ref.dtype)


def attend_back(mixed, grad, wide, total, starts, halo):
    group = mixed.shape[1]
    steps = group // QUERIES
    row = pl.BlockSpec((1, 1, QUERIES), lambda s, i, first: (s, 0, i))
    return pl.pallas_call(
        attend_back_kernel,
        grid_spec=pltpu.PrefetchScalarGridSpec(
            num_scalar_prefetch=1,
            grid=(2, steps),
            in_specs=[
                row,
                pl.BlockSpec((1, group, 2 * HD), lambda s, i, first: (s, 0, 0)),
                pl.BlockSpec((1, group, 2 * HD), lambda s, i, first: (2, 0, 0)),
                pl.BlockSpec((1, QUERIES, 2 * HD), lambda s, i, first: (0, i, 0)),
                pl.BlockSpec((1, HD, QUERIES), lambda s, i, first: (s, 0, i)),
                row,
            ],
            out_specs=pl.BlockSpec((3, group + halo, 2 * HD), lambda s, i, first: (0, 0, 0)),
            scratch_shapes=[
                pltpu.VMEM((group // KEYS, HD, KEYS), LOW),
                pltpu.VMEM((group, HD), LOW),
                pltpu.VMEM((group, HD), F32),
                pltpu.VMEM((group, HD), F32),
            ],
        ),
        out_shape=jax.ShapeDtypeStruct((3, group + halo, 2 * HD), LOW),
        compiler_params=pltpu.CompilerParams(vmem_limit_bytes=32 * 1024 * 1024),
        cost_estimate=pl.CostEstimate(
            flops=2**35, bytes_accessed=group * 2048, transcendentals=group * group // 4
        ),
        name="attend_back",
    )(starts[:, ::QUERIES] // KEYS, starts[:, None, :], mixed, mixed, grad, wide, total)


def plane_partners():
    me = lax.axis_index("dp")
    return {"dp": me + 1 - 2 * lax.rem(me, 2)}, {"dp": me + 2 - 4 * (me // 2)}


def dot_nt(left, right):
    return lax.dot_general(left, right, (((1,), (1,)), ((), ())), preferred_element_type=F32)


def mesh_place():
    me = lax.axis_index("mp")
    return me // 2, lax.rem(me, 2)


def wire(source, target, send, recv, partner):
    return pltpu.make_async_remote_copy(
        src_ref=source,
        dst_ref=target,
        send_sem=send,
        recv_sem=recv,
        device_id=partner,
        device_id_type=MESH,
    )


def line_partner(z, step):
    _, core = mesh_place()
    return {"mp": 2 * (z + step) + core}


def other_core():
    z, core = mesh_place()
    return {"mp": 2 * z + 1 - core}


def greet(partners):
    barrier = pltpu.get_barrier_semaphore()
    for partner in partners:
        pl.semaphore_signal(barrier, inc=1, device_id=partner, device_id_type=MESH)
    pl.semaphore_wait(barrier, len(partners))


def greet_line(with_plane):
    z, _ = mesh_place()
    count = lax.axis_size("mp") // 2
    barrier = pltpu.get_barrier_semaphore()
    partners = [other_core()]
    if with_plane:
        partners += list(plane_partners())
    for partner in partners:
        pl.semaphore_signal(barrier, inc=1, device_id=partner, device_id_type=MESH)
    for turn in (1, -1):

        @pl.when((z + turn >= 0) & (z + turn < count))
        def _(turn=turn):
            pl.semaphore_signal(barrier, inc=1, device_id=line_partner(z, turn), device_id_type=MESH)

    near = jnp.where(z > 0, 1, 0) + jnp.where(z < count - 1, 1, 0)
    pl.semaphore_wait(barrier, near + len(partners))


class LineGather:
    def __init__(self, place, send, recv, swap_send, swap_recv):
        self.z, self.core = mesh_place()
        self.count = lax.axis_size("mp") // 2
        self.place, self.send, self.recv = place, send, recv
        self.swap_send, self.swap_recv = swap_send, swap_recv

    def copies(self, step):
        z, count = self.z, self.count
        out = []
        for way, turn in enumerate((1, -1)):
            leaves = z - turn * (step - 1)
            lands = z - turn * step
            far = z + turn
            sends = (leaves >= 0) & (leaves < count) & (far >= 0) & (far < count)
            receives = (lands >= 0) & (lands < count)
            at = jnp.clip(leaves, 0, count - 1)
            to = jnp.clip(lands, 0, count - 1)
            sems = (self.send.at[way, step - 1], self.recv.at[way, step - 1], line_partner(z, turn))
            leaving = wire(self.place(at, self.core), self.place(at, self.core), *sems)
            landing = wire(self.place(to, self.core), self.place(to, self.core), *sems)
            out.append((sends, leaving, receives, landing, to))
        return out

    def start(self, step):
        for sends, leaving, _, _, _ in self.copies(step):
            pl.when(sends)(leaving.start)

    def swap(self, at, number):
        sems = (self.swap_send.at[number], self.swap_recv.at[number], other_core())
        leaving = wire(self.place(at, self.core), self.place(at, self.core), *sems)
        landing = wire(self.place(at, 1 - self.core), self.place(at, 1 - self.core), *sems)
        return leaving, landing

    def swap_own(self):
        self.swap(self.z, 0)[0].start()

    def arrive(self, step):
        for way, (_, _, receives, landing, at) in enumerate(self.copies(step)):

            @pl.when(receives)
            def _(landing=landing, at=at, way=way):
                landing.wait_recv()
                self.swap(at, 1 + 2 * (step - 1) + way)[0].start()

    def swapped(self, at, number):
        leaving, landing = self.swap(at, number)
        leaving.wait_send()
        landing.wait_recv()

    def finish(self, steps, own):
        if own:
            self.swapped(self.z, 0)
        for step in steps:
            for way, (sends, leaving, receives, _, at) in enumerate(self.copies(step)):
                pl.when(sends)(leaving.wait_send)
                pl.when(receives)(
                    lambda at=at, way=way, step=step: self.swapped(at, 1 + 2 * (step - 1) + way)
                )


def line_semaphores(count):
    return [
        pltpu.SemaphoreType.DMA((2, count)),
        pltpu.SemaphoreType.DMA((2, count)),
        pltpu.SemaphoreType.DMA((2 * count,)),
        pltpu.SemaphoreType.DMA((2 * count,)),
    ]


def early_steps(count):
    return range(1, count // 2 + 1)


HALO = 16


def carry_copies(carried, targets, send, recv):
    partners = plane_partners()
    return [
        wire(ref, target, send.at[at], recv.at[at], partners[way])
        for at, ((way, ref), target) in enumerate(zip(carried, targets))
    ]


def greet_members(ways):
    mp = lax.axis_size("mp")
    me = lax.axis_index("mp")
    barrier = pltpu.get_barrier_semaphore()
    for step in range(1, mp):
        pl.semaphore_signal(
            barrier, inc=1, device_id={"mp": lax.rem(me + step, mp)}, device_id_type=MESH
        )
    partners = plane_partners() if ways else ()
    for partner in partners:
        pl.semaphore_signal(barrier, inc=1, device_id=partner, device_id_type=MESH)
    pl.semaphore_wait(barrier, mp - 1 + len(partners))


def member_copies(source, target, send, recv):
    mp = lax.axis_size("mp")
    me = lax.axis_index("mp")
    copies = []
    for step in range(1, mp):
        to = lax.rem(me + step, mp)
        sems = (send.at[step], recv.at[step], {"mp": to})
        copies.append(
            (
                wire(source(to), target(me), *sems),
                wire(source(to), target(lax.rem(me + mp - step, mp)), *sems),
            )
        )
    return copies


def head_lanes(at):
    return pl.ds(pl.multiple_of(at * 128, 128), 128)


def front_kernel(
    inputs_ref, gain_ref, shift_ref, qk_ref, v_ref, out_ref, taps_ref, up_ref, masks_ref, cot_ref,
    all_qk_ref, all_v_ref, all_out_ref, all_taps_ref, normed_ref, up_all_ref, raw_ref, o_ref, cot_x_ref, cot_y_ref,
    inputs, rows, all_qk, all_v, all_out, all_taps, up_all, raw, mixed, landed, local, *sems,
):
    mp = lax.axis_size("mp")
    dp = lax.axis_index("dp")
    me = lax.axis_index("mp")
    z, core = mesh_place()
    count = mp // 2
    rows_here, depth = inputs.shape[1:]
    halo = rows.shape[1] - rows_here
    to_x, to_y = plane_partners()
    share = up_ref.shape[0]
    owned = (qk_ref, v_ref, out_ref)
    whole = (all_qk, all_v, all_out)
    (plane_send_sem, plane_recv_sem, plane_swap_send, plane_swap_recv) = sems[:4]
    taps_send, taps_recv, halo_send, halo_recv, carry_send, carry_recv, head_send, head_recv = sems[4:12]
    line_sems = [sems[12 + 4 * part : 16 + 4 * part] for part in range(4)]

    def up_place(at, at_core):
        start = pl.multiple_of((2 * at + at_core) * share, 16)
        return up_all.at[pl.ds(start, share), :]

    def taps_place(at):
        return all_taps.at[:, :, head_lanes(at)]

    loads = [
        pltpu.make_async_copy(inputs_ref, inputs, local.at[0]),
        pltpu.make_async_copy(taps_ref, taps_place(me), local.at[1]),
        pltpu.make_async_copy(up_ref, up_place(z, core), local.at[2]),
    ] + [
        pltpu.make_async_copy(
            owned[part].at[dp], whole[part].at[z, core, dp], local.at[3 + part]
        )
        for part in range(3)
    ]
    for copy in loads:
        copy.start()
    greet_members((0, 1))
    for copy in loads[1:]:
        copy.wait()

    lines = [
        LineGather(lambda at, at_core, part=part: whole[part].at[at, at_core, dp], *line_sems[part])
        for part in range(3)
    ]
    up_line = LineGather(up_place, *line_sems[3])
    for line in lines:
        line.start(1)
    tap_copies = member_copies(lambda to: taps_ref, taps_place, taps_send, taps_recv)
    for copy, _ in tap_copies:
        copy.start()
    for line in lines:
        line.swap_own()

    loads[0].wait()
    tall = 16

    def norm(s):
        def some(at, carry):
            here = pl.ds(pl.multiple_of(at * tall, tall), tall)
            there = pl.ds(pl.multiple_of(halo + at * tall, tall), tall)
            values = inputs[s, here, :].astype(F32)
            centered = values - jnp.mean(values, axis=1, keepdims=True)
            variance = jnp.mean(centered * centered, axis=1, keepdims=True)
            rows[s, there, :] = (
                centered * lax.rsqrt(variance + 1e-05) * gain_ref[...] + shift_ref[...]
            ).astype(LOW)
            return carry

        lax.fori_loop(0, rows_here // tall, some, 0)

    norm(0)
    for step in range(1, count):
        for line in lines:
            line.arrive(step)
        if step + 1 < count:
            for line in lines:
                line.start(step + 1)

    half = depth // 2
    lanes = (pl.ds(0, half), pl.ds(half, half))
    dp_x = dp + 1 - 2 * lax.rem(dp, 2)
    dp_y = dp + 2 - 4 * (dp // 2)
    dp_xy = dp_x + 2 - 4 * (dp_x // 2)
    legs = ((0, to_x), (1, to_y), (0, to_y), (1, to_x), (0, to_y), (1, to_x))

    def plane(number, quarter):
        side, partner = legs[number]
        out = []
        for part in range(3):
            block = whole[part].at[:, core, quarter, :, lanes[side]]
            out.append(
                wire(
                    block, block, plane_send_sem.at[part, number], plane_recv_sem.at[part, number], partner
                )
            )
        return out

    leaving = [plane(number, quarter) for number, quarter in enumerate((dp, dp, dp, dp, dp_x, dp_y))]
    landing = [
        plane(number, quarter) for number, quarter in enumerate((dp_x, dp_y, dp_y, dp_x, dp_xy, dp_xy))
    ]

    def pass_on(number, at_core):
        quarter = (dp_x, dp_y, dp_xy)[number]
        out = []
        for part in range(3):
            block = whole[part].at[:, at_core, quarter]
            out.append(
                wire(
                    block, block, plane_swap_send.at[part, number], plane_swap_recv.at[part, number],
                    other_core(),
                )
            )
        return out

    def each(copies, what):
        for copy in copies:
            getattr(copy, what)()

    for number in range(4):
        each(leaving[number], "start")
    early = early_steps(count)
    up_line.start(1)
    up_line.swap_own()
    norm(1)
    own_rows = rows.at[:, pl.ds(halo, rows_here), :]
    save = pltpu.make_async_copy(own_rows, normed_ref, local.at[0])
    save.start()
    halo_copy = wire(
        rows.at[:, pl.ds(rows_here, halo), :], rows.at[:, pl.ds(0, halo), :], halo_send, halo_recv,
        {"mp": lax.rem(me + 1, mp)},
    )
    halo_copy.start()
    each(landing[0], "wait_recv")
    each(leaving[4], "start")
    each(landing[1], "wait_recv")
    each(leaving[5], "start")
    each(landing[3], "wait_recv")
    each(pass_on(0, core), "start")
    each(landing[2], "wait_recv")
    each(pass_on(1, core), "start")
    up_line.arrive(1)
    up_line.start(2)
    each(landing[4], "wait_recv")
    each(landing[5], "wait_recv")
    each(pass_on(2, core), "start")
    for step in early[1:-1]:
        up_line.arrive(step)
        up_line.start(step + 1)
    carries = [
        wire(cot_ref.at[:, :, lanes[0]], cot_x_ref, carry_send.at[0], carry_recv.at[0], to_x),
        wire(cot_ref.at[:, :, lanes[1]], cot_y_ref, carry_send.at[1], carry_recv.at[1], to_y),
    ]
    for copy in carries:
        copy.start()
    for line in lines:
        line.finish(range(1, count), True)
    for number in range(3):
        each(pass_on(number, 1 - core), "wait_recv")
    for _, landed_taps in tap_copies:
        landed_taps.wait_recv()
    halo_copy.wait_recv()
    saves = [
        pltpu.make_async_copy(here, there, local.at[2 + at])
        for at, (here, there) in enumerate(
            ((all_qk, all_qk_ref), (all_v, all_v_ref), (all_out, all_out_ref), (all_taps, all_taps_ref))
        )
    ]
    for copy in saves:
        copy.start()

    def chip(at, carry):
        weights = all_qk[at].reshape(4 * HD, depth)
        columns = pl.ds(pl.multiple_of(at * 4 * HD, 4 * HD), 4 * HD)
        for s in range(2):
            raw[s, :, columns] = dot_nt(rows[s], weights)
        return carry

    lax.fori_loop(0, count, chip, 0)
    lane = lax.broadcasted_iota(jnp.int32, (rows.shape[1], 128), 1)

    def two_heads(at, carry):
        weights = all_v[at].reshape(2 * HD, depth)
        zero, one = dot_nt(rows[0], weights), dot_nt(rows[1], weights)
        raw[2, :, head_lanes(2 * at)] = jnp.where(lane < HD, zero, pltpu.roll(one, HD, 1))
        raw[2, :, head_lanes(2 * at + 1)] = jnp.where(lane < HD, pltpu.roll(zero, HD, 1), one)
        return carry

    lax.fori_loop(0, count, two_heads, 0)
    save_raw = pltpu.make_async_copy(raw, raw_ref, local.at[6])
    save_raw.start()
    for plane_at in range(3):
        tap = all_taps.at[plane_at]

        def conv(at, carry, plane_at=plane_at, tap=tap):
            lanes_at = head_lanes(at)
            values = raw[plane_at, :, lanes_at]
            one = pltpu.roll(values, 1, 0)[halo:]
            two = pltpu.roll(values, 2, 0)[halo:]
            mixed[plane_at, :, lanes_at] = (
                tap[0:1, lanes_at] * values[halo:]
                + jnp.where(masks_ref[plane_at, 0] > 0.5, tap[1:2, lanes_at] * one, 0.0)
                + jnp.where(masks_ref[plane_at, 1] > 0.5, tap[2:3, lanes_at] * two, 0.0)
            ).astype(LOW)
            return carry

        lax.fori_loop(0, mp, conv, 0)

    def source(at):
        return mixed.at[:, :, head_lanes(at)]

    def target(at):
        return landed.at[:, at]

    own = pltpu.make_async_copy(source(me), target(me), local.at[7])
    own.start()
    copies = member_copies(source, target, head_send, head_recv)
    for copy, _ in copies:
        copy.start()
    up_line.arrive(early[-1])
    up_line.finish(early, True)
    save_up = pltpu.make_async_copy(up_all, up_all_ref, local.at[8])
    save_up.start()
    own.wait()
    for _, copy in copies:
        copy.wait_recv()
    save_heads = pltpu.make_async_copy(landed, o_ref, local.at[9])
    save_heads.start()
    for number in range(6):
        each(leaving[number], "wait_send")
    for number in range(3):
        each(pass_on(number, core), "wait_send")
    for copy, _ in tap_copies + copies:
        copy.wait_send()
    halo_copy.wait_send()
    for copy in carries:
        copy.wait()
    save.wait()
    for copy in saves:
        copy.wait()
    save_raw.wait()
    save_up.wait()
    save_heads.wait()


def front(inputs, gain, shift, qk, v, out, taps, up, masks, cot):
    mp = lax.axis_size("mp")
    count = mp // 2
    rows_here, depth = inputs.shape[1:]
    tall = rows_here + HALO
    anywhere = pl.BlockSpec(memory_space=pl.ANY)
    vmem = pl.BlockSpec(memory_space=pltpu.VMEM)
    dma = pltpu.SemaphoreType.DMA
    whole = [((count, 2) + part.shape, LOW) for part in (qk, v, out)]
    whole.append(((3, 8, mp * 128), F32))
    kept = [
        ((2, rows_here, depth), LOW),
        ((mp * up.shape[0], depth), LOW),
        ((3, tall, mp * 128), F32),
        ((3, mp, rows_here, 128), LOW),
        ((2, rows_here, depth // 2), LOW),
        ((2, rows_here, depth // 2), LOW),
    ]
    return pl.pallas_call(
        front_kernel,
        in_specs=[anywhere, vmem, vmem] + [anywhere] * 5 + [vmem, anywhere],
        out_specs=[anywhere] * 10,
        out_shape=[jax.ShapeDtypeStruct(*shape) for shape in whole + kept],
        scratch_shapes=[
            pltpu.VMEM(inputs.shape, LOW),
            pltpu.VMEM((2, tall, depth), LOW),
        ]
        + [pltpu.VMEM(*shape) for shape in whole]
        + [
            pltpu.VMEM(*kept[1]),
            pltpu.VMEM(*kept[2]),
            pltpu.VMEM((3, rows_here, mp * 128), LOW),
            pltpu.VMEM(*kept[3]),
            dma((10,)),
            dma((3, 6)),
            dma((3, 6)),
            dma((3, 3)),
            dma((3, 3)),
            dma((mp,)),
            dma((mp,)),
            dma,
            dma,
            dma((2,)),
            dma((2,)),
            dma((mp,)),
            dma((mp,)),
        ]
        + line_semaphores(count) * 4,
        compiler_params=pltpu.CompilerParams(
            collective_id=3, has_side_effects=True, vmem_limit_bytes=VMEM_LIMIT
        ),
        cost_estimate=pl.CostEstimate(flops=2**36, bytes_accessed=2**26, transcendentals=0),
        name="front",
    )(inputs, gain.reshape(1, depth), shift.reshape(1, depth), qk, v, out, taps, up, masks, cot)


def left_t_right(left, right):
    return lax.dot_general(left, right, (((0,), (0,)), ((), ())), preferred_element_type=F32)


def stream_out(steps, compute, buffer, ref, sem):
    def save(at, slot):
        return pltpu.make_async_copy(buffer.at[slot], ref.at[at], sem.at[slot])

    def one(at, carry):
        slot = lax.rem(at, 2)

        @pl.when(at >= 2)
        def _():
            save(at - 2, slot).wait()

        buffer[slot] = compute(at)
        save(at, slot).start()
        return carry

    lax.fori_loop(0, steps, one, 0)
    save(steps - 2, (steps - 2) % 2).wait()
    save(steps - 1, (steps - 1) % 2).wait()


def project_back_kernel(
    ways, x_ref, raw_ref, taps_ref, masks_ref, normed_ref, attended_ref, branch_ref, *refs
):
    carried, refs = list(zip(ways, refs[: len(ways)])), refs[len(ways) :]
    grad_ref, sums_ref, qk_part_ref, v_part_ref, out_part_ref = refs[:5]
    targets, refs = refs[5 : 5 + len(ways)], refs[5 + len(ways) :]
    landed, raw, wide, narrow, part_sem, local, send, recv, carry_send, carry_recv = refs
    me = lax.axis_index("mp")
    tall = landed.shape[1]
    rows_here = grad_ref.shape[1]
    halo = tall - rows_here
    heads = landed.shape[2] // 128

    def source(at):
        return x_ref.at[:, pl.ds(pl.multiple_of(at * rows_here, 16), tall), :]

    def target(at):
        return landed.at[:, :, head_lanes(at)]

    own = pltpu.make_async_copy(source(me), target(me), local.at[0])
    own.start()
    load = pltpu.make_async_copy(raw_ref, raw, local.at[1])
    load.start()
    greet_members(ways)
    copies = member_copies(source, target, send, recv)
    for leaving, _ in copies:
        leaving.start()
    carries = carry_copies(carried, targets, carry_send, carry_recv)
    for copy in carries:
        copy.start()

    def out_part(at):
        lanes = head_lanes(at)
        return (
            left_t_right(attended_ref[0, :, lanes], branch_ref[0])
            + left_t_right(attended_ref[1, :, lanes], branch_ref[1])
        ).astype(LOW)

    stream_out(heads // 2, out_part, narrow, out_part_ref, part_sem)
    own.wait()
    load.wait()
    for _, landing in copies:
        landing.wait_recv()
    for plane in range(3):
        tap = taps_ref.at[plane]

        def back(at, carry, plane=plane, tap=tap):
            lanes = head_lanes(at)
            grad = landed[plane, :, lanes].astype(F32)
            one = pltpu.roll(grad, tall - 1, 0)[:rows_here]
            two = pltpu.roll(grad, tall - 2, 0)[:rows_here]
            here = grad[:rows_here]
            grad_ref[plane, :, lanes] = (
                tap[0:1, lanes] * here
                + jnp.where(masks_ref[plane, 2] > 0.5, tap[1:2, lanes] * one, 0.0)
                + jnp.where(masks_ref[plane, 3] > 0.5, tap[2:3, lanes] * two, 0.0)
            ).astype(LOW)
            values = raw[plane, :, lanes]
            before = pltpu.roll(values, 1, 0)[halo:]
            before_two = pltpu.roll(values, 2, 0)[halo:]
            products = (
                here * values[halo:],
                jnp.where(masks_ref[plane, 0] > 0.5, here * before, 0.0),
                jnp.where(masks_ref[plane, 1] > 0.5, here * before_two, 0.0),
            )
            for row, product in enumerate(products):
                sums_ref[plane, row : row + 1, lanes] = jnp.sum(product, axis=0, keepdims=True)
            sums_ref[plane, 3:8, lanes] = jnp.zeros((5, 128), F32)
            return carry

        lax.fori_loop(0, heads, back, 0)

    def pair(at):
        return pl.ds(pl.multiple_of(at * 256, 256), 256)

    def qk_part(at):
        return (
            left_t_right(grad_ref[0, :, pair(at)], normed_ref[0])
            + left_t_right(grad_ref[1, :, pair(at)], normed_ref[1])
        ).astype(LOW)

    def v_part(at):
        side = grad_ref[2, :, pair(at)]
        zero, one = left_t_right(side, normed_ref[0]), left_t_right(side, normed_ref[1])
        return jnp.concatenate(
            [zero[:HD] + one[HD : 2 * HD], zero[2 * HD : 3 * HD] + one[3 * HD :]], axis=0
        ).astype(LOW)

    stream_out(heads // 2, qk_part, wide, qk_part_ref, part_sem)
    stream_out(heads // 2, v_part, narrow, v_part_ref, part_sem)
    for leaving, _ in copies:
        leaving.wait_send()
    for copy in carries:
        copy.wait()


def project_back(x, raw, taps, masks, normed, attended, branch, carried):
    mp = lax.axis_size("mp")
    rows_here, depth = normed.shape[1:]
    tall = raw.shape[1]
    anywhere = pl.BlockSpec(memory_space=pl.ANY)
    dma = pltpu.SemaphoreType.DMA
    vmem = pl.BlockSpec(memory_space=pltpu.VMEM)
    return pl.pallas_call(
        partial(project_back_kernel, tuple(way for way, _ in carried)),
        in_specs=[vmem, anywhere] + [vmem] * 5 + [anywhere] * len(carried),
        out_specs=[vmem] * 2 + [anywhere] * (3 + len(carried)),
        out_shape=[
            jax.ShapeDtypeStruct((3, rows_here, mp * 128), LOW),
            jax.ShapeDtypeStruct((3, 8, mp * 128), F32),
            jax.ShapeDtypeStruct((mp // 2, 4 * HD, depth), LOW),
            jax.ShapeDtypeStruct((mp // 2, 2 * HD, depth), LOW),
            jax.ShapeDtypeStruct((mp // 2, 2 * HD, depth), LOW),
        ]
        + [jax.ShapeDtypeStruct(block.shape, block.dtype) for _, block in carried],
        scratch_shapes=[
            pltpu.VMEM((3, tall, mp * 128), LOW),
            pltpu.VMEM((3, tall, mp * 128), F32),
            pltpu.VMEM((2, 4 * HD, depth), LOW),
            pltpu.VMEM((2, 2 * HD, depth), LOW),
            dma((2,)),
            dma((2,)),
            dma((mp,)),
            dma((mp,)),
            dma((len(carried),)),
            dma((len(carried),)),
        ],
        compiler_params=pltpu.CompilerParams(
            collective_id=7, has_side_effects=True, vmem_limit_bytes=VMEM_LIMIT
        ),
        cost_estimate=pl.CostEstimate(flops=2**35, bytes_accessed=2**24, transcendentals=0),
        name="project_back",
    )(x, raw, taps, masks, normed, attended, branch, *(block for _, block in carried))


def attended_kernel(x_ref, o_ref, landed, local, send, recv):
    me = lax.axis_index("mp")
    tall = o_ref.shape[1]

    def source(at):
        return x_ref.at[:, pl.ds(pl.multiple_of(at * tall, 16), tall), :]

    def target(at):
        return landed.at[:, :, head_lanes(at)]

    own = pltpu.make_async_copy(source(me), target(me), local.at[0])
    own.start()
    greet_members(())
    copies = member_copies(source, target, send, recv)
    for leaving, _ in copies:
        leaving.start()
    own.wait()
    for _, landing in copies:
        landing.wait_recv()
    save = pltpu.make_async_copy(landed, o_ref, local.at[1])
    save.start()
    for leaving, _ in copies:
        leaving.wait_send()
    save.wait()


def attended_back(x, rows_here):
    mp = lax.axis_size("mp")
    shape = (x.shape[0], rows_here, mp * 128)
    dma = pltpu.SemaphoreType.DMA
    return pl.pallas_call(
        attended_kernel,
        in_specs=[pl.BlockSpec(memory_space=pltpu.VMEM)],
        out_specs=pl.BlockSpec(memory_space=pl.ANY),
        out_shape=jax.ShapeDtypeStruct(shape, x.dtype),
        scratch_shapes=[pltpu.VMEM(shape, x.dtype), dma((2,)), dma((mp,)), dma((mp,))],
        compiler_params=pltpu.CompilerParams(
            collective_id=5, has_side_effects=True, vmem_limit_bytes=48 * 2**20
        ),
        cost_estimate=pl.CostEstimate(flops=2**34, bytes_accessed=2**24, transcendentals=0),
        name="attended_back",
    )(x)


def line_blocks(place, sources, local, send, recv):
    z, core = mesh_place()
    count = lax.axis_size("mp") // 2
    out = []
    for number, (step, way, ref) in enumerate(sources):
        at = z - way * step
        there = (at >= 0) & (at < count)
        at = jnp.clip(at, 0, count - 1)
        sems = (send.at[number], recv.at[number], other_core())
        out.append(
            (
                there,
                pltpu.make_async_copy(ref, place(at, core), local.at[number]),
                wire(ref, place(at, core), *sems),
                wire(ref, place(at, 1 - core), *sems),
            )
        )
    return out


def feed_in_kernel(
    late, second_ref, up_ref, down_ref, cot_0, cot_1, cot_2, cot_3, cot_4, cot_5, cot_6, *refs
):
    late_sources = [(step, way, ref) for (step, way), ref in zip(late, refs)]
    (
        all_ref, relu_ref, hidden_ref, down_all_ref, up_all_ref, down_part_ref,
        rows, up, relu, hidden, down, cot, tiles, sums, before, local, outs, send, recv, cot_sem, tile_sem, sum_sem,
        before_sem, late_local, late_send, late_recv, *line_sems,
    ) = refs[len(late) :]
    count = lax.axis_size("mp") // 2
    depth = rows.shape[3]
    units = up.shape[0]
    share = down_ref.shape[0]
    z, core = mesh_place()
    lanes = (pl.ds(0, depth // 2), pl.ds(depth // 2, depth // 2))
    to_x, to_y = plane_partners()
    pieces = (cot_0, cot_1, cot_2, cot_3, cot_4, cot_5, cot_6)

    def line_place(ref):
        return lambda at, at_core: ref.at[
            pl.ds(pl.multiple_of((2 * at + at_core) * share, 16), share), :
        ]

    own = [pltpu.make_async_copy(second_ref.at[s], rows.at[s, 0], local.at[s]) for s in range(2)]
    own.append(pltpu.make_async_copy(up_ref, up, local.at[2]))
    own.append(pltpu.make_async_copy(down_ref, line_place(down)(z, core), local.at[3]))
    for copy in own:
        copy.start()
    for copy in own:
        copy.wait()
    greet_line(True)
    late_blocks = line_blocks(line_place(up), late_sources, late_local, late_send, late_recv)
    down_line = LineGather(line_place(down), *line_sems)

    def remote(s, source, target, half, partner, number):
        return wire(
            rows.at[s, source, :, lanes[half]], rows.at[s, target, :, lanes[half]],
            send.at[s, number], recv.at[s, number], partner,
        )

    copies = [
        [
            remote(s, 0, 1, 0, to_x, 0),
            remote(s, 0, 2, 1, to_y, 1),
            remote(s, 0, 2, 0, to_y, 2),
            remote(s, 0, 1, 1, to_x, 3),
            remote(s, 1, 3, 0, to_y, 4),
            remote(s, 2, 3, 1, to_x, 5),
        ]
        for s in range(2)
    ]
    pending = [None, None]
    done = [0]

    def settle(slot):
        if pending[slot] is not None:
            for copy in pending[slot]:
                copy.wait()
        pending[slot] = None

    def tile(s, m):
        slot = done[0] % 2
        done[0] += 1
        settle(slot)

        def one(at, carry):
            columns = pl.ds(pl.multiple_of(at * CHUNK, CHUNK), CHUNK)
            kept = jnp.maximum(dot_nt(rows[s, m], up[columns, :]), 0.0)
            relu[slot, :, columns] = kept
            hidden[slot, :, columns] = (kept * kept).astype(LOW)
            return carry

        lax.fori_loop(0, units // CHUNK, one, 0)
        pending[slot] = [
            pltpu.make_async_copy(relu.at[slot], relu_ref.at[s, m], outs.at[slot, 0]),
            pltpu.make_async_copy(hidden.at[slot], hidden_ref.at[s, m], outs.at[slot, 1]),
        ]
        for copy in pending[slot]:
            copy.start()

    for number in range(4):
        copies[0][number].start()
    for there, here, leaving, _ in late_blocks:

        @pl.when(there)
        def _(here=here, leaving=leaving):
            here.start()
            leaving.start()

    down_line.start(1)
    down_line.swap_own()

    def cot_loads(s):
        copies = []
        for m in range(4):
            copies += piece_copies(pieces, s, m, cot.at[m], cot_sem.at[m])
        return copies

    for copy in cot_loads(0):
        copy.start()
    for there, here, leaving, landing in late_blocks:

        @pl.when(there)
        def _(here=here, leaving=leaving, landing=landing):
            here.wait()
            leaving.wait_send()
            landing.wait_recv()

    whole_up = pltpu.make_async_copy(up, up_all_ref, local.at[2])
    whole_up.start()
    tile(0, 0)
    copies[0][0].wait_recv()
    copies[0][4].start()
    copies[0][1].wait_recv()
    copies[0][5].start()
    copies[1][0].start()
    copies[1][1].start()
    tile(1, 0)
    down_line.arrive(1)
    down_line.start(2)
    copies[0][3].wait_recv()
    tile(0, 1)
    copies[0][2].wait_recv()
    copies[1][2].start()
    copies[1][3].start()
    tile(0, 2)
    copies[1][0].wait_recv()
    copies[1][4].start()
    copies[1][1].wait_recv()
    copies[1][5].start()
    copies[0][4].wait_recv()
    copies[0][5].wait_recv()
    tile(0, 3)
    for step in range(3, count):
        down_line.arrive(step - 1)
        down_line.start(step)
    settle(0)
    settle(1)
    for copy in cot_loads(0):
        copy.wait()
    gradient_tiles(hidden_ref.at[0], cot, tiles, sums, down_part_ref, tile_sem, sum_sem)
    for copy in cot_loads(1):
        copy.start()
    copies[1][3].wait_recv()
    tile(1, 1)
    copies[1][2].wait_recv()
    tile(1, 2)
    copies[1][4].wait_recv()
    copies[1][5].wait_recv()
    gathered = pltpu.make_async_copy(rows, all_ref, local.at[0])
    gathered.start()
    tile(1, 3)
    down_line.arrive(count - 1)
    down_line.finish(range(1, count), True)
    whole_down = pltpu.make_async_copy(down, down_all_ref, local.at[1])
    whole_down.start()
    settle(0)
    settle(1)
    for copy in cot_loads(1):
        copy.wait()
    gradient_tiles(
        hidden_ref.at[1], cot, tiles, sums, down_part_ref, tile_sem, sum_sem,
        (down_part_ref, before, before_sem),
    )
    for s in range(2):
        for copy in copies[s]:
            copy.wait_send()
    gathered.wait()
    whole_up.wait()
    whole_down.wait()


def gradient_tiles(
    left_ref, right, tiles, sums, out_ref, tile_sem, sum_sem, before=None, span=None
):
    wide = tiles.shape[-1]
    first, steps = span if span is not None else (0, left_ref.shape[-1] // wide)
    lead = (slice(None),) * (len(left_ref.shape) - 1)
    tall = math.prod(tiles.shape[1:-1])

    def load(at, slot):
        columns = pl.ds(pl.multiple_of(at * wide, wide), wide)
        return pltpu.make_async_copy(
            left_ref.at[lead + (columns,)], tiles.at[slot], tile_sem.at[slot]
        )

    def rows_of(at):
        return pl.ds(pl.multiple_of(at * wide, wide), wide)

    def save(at, slot):
        return pltpu.make_async_copy(sums.at[slot], out_ref.at[rows_of(at), :], sum_sem.at[slot])

    def load_before(at, slot):
        before_ref, buffer, sem = before
        return pltpu.make_async_copy(before_ref.at[rows_of(at), :], buffer.at[slot], sem.at[slot])

    load(first, first % 2).start()
    if before is not None:
        load_before(first, first % 2).start()

    def one(at, carry):
        slot = lax.rem(at, 2)
        load(at, slot).wait()
        if before is not None:
            load_before(at, slot).wait()

        @pl.when(at + 1 < steps)
        def _():
            load(at + 1, 1 - slot).start()
            if before is not None:
                load_before(at + 1, 1 - slot).start()

        @pl.when(at >= first + 2)
        def _():
            save(at - 2, slot).wait()

        result = lax.dot_general(
            tiles[slot].reshape(tall, wide),
            right[...].reshape(tall, right.shape[-1]),
            (((0,), (0,)), ((), ())),
            preferred_element_type=F32,
        )
        if before is not None:
            result = result + before[1][slot].astype(F32)
        sums[slot] = result.astype(LOW)
        save(at, slot).start()
        return carry

    lax.fori_loop(first, steps, one, 0)
    save(steps - 2, (steps - 2) % 2).wait()
    save(steps - 1, (steps - 1) % 2).wait()


def feed_in(second, up_early, down, cot_pieces, up_late):
    rows_here, depth = second.shape[1:]
    units = up_early.shape[0]
    count = lax.axis_size("mp") // 2
    anywhere = pl.BlockSpec(memory_space=pl.ANY)
    dma = pltpu.SemaphoreType.DMA
    return pl.pallas_call(
        partial(feed_in_kernel, tuple(up_late)),
        in_specs=[anywhere] * (10 + len(up_late)),
        out_specs=[anywhere] * 6,
        out_shape=[
            jax.ShapeDtypeStruct((2, 4, rows_here, depth), LOW),
            jax.ShapeDtypeStruct((2, 4, rows_here, units), F32),
            jax.ShapeDtypeStruct((2, 4, rows_here, units), LOW),
            jax.ShapeDtypeStruct((units, depth), LOW),
            jax.ShapeDtypeStruct((units, depth), LOW),
            jax.ShapeDtypeStruct((units, depth), LOW),
        ],
        scratch_shapes=[
            pltpu.VMEM((2, 4, rows_here, depth), LOW),
            pltpu.VMEM((units, depth), LOW),
            pltpu.VMEM((2, rows_here, units), F32),
            pltpu.VMEM((2, rows_here, units), LOW),
            pltpu.VMEM((units, depth), LOW),
            pltpu.VMEM((4, rows_here, depth), LOW),
            pltpu.VMEM((2, 4, rows_here, WIDE), LOW),
            pltpu.VMEM((2, WIDE, depth), LOW),
            pltpu.VMEM((2, WIDE, depth), LOW),
            dma((4,)),
            dma((2, 2)),
            dma((2, 6)),
            dma((2, 6)),
            dma((4, 2)),
            dma((2,)),
            dma((2,)),
            dma((2,)),
        ]
        + [dma((len(up_late),))] * 3
        + line_semaphores(count),
        compiler_params=pltpu.CompilerParams(
            collective_id=1, has_side_effects=True, vmem_limit_bytes=VMEM_LIMIT
        ),
        cost_estimate=pl.CostEstimate(
            flops=2 * 8 * rows_here * depth * units * 3,
            bytes_accessed=60 * 2**20,
            transcendentals=0,
        ),
        name="feed_in",
    )(second, up_early, down, *cot_pieces, *up_late.values())


def piece_copies(pieces, s, m, target, sems):
    half = target.shape[-1] // 2
    if m == 0:
        return [pltpu.make_async_copy(pieces[0].at[s], target, sems.at[0])]
    return [
        pltpu.make_async_copy(
            pieces[2 * m - 1 + side].at[s], target.at[:, pl.ds(side * half, half)], sems.at[side]
        )
        for side in range(2)
    ]


def feed_out_kernel(
    cot_0, cot_1, cot_2, cot_3, cot_4, cot_5, cot_6, relu_ref, second_ref, up_ref, down_ref,
    grad_ref, up_part_ref, back_ref,
    up, shared, cot, relu, grad, part, arrived, tiles, sums, result, local, loads, outs, send, recv,
    tile_sem, sum_sem,
):
    units, depth = up.shape
    down = shared.at[pl.ds(0, units), :]
    second = shared.at[pl.ds(0, 8 * cot.shape[1]), :]
    half = depth // 2
    lanes = (pl.ds(0, half), pl.ds(half, half))
    to_x, to_y = plane_partners()
    weights = [
        pltpu.make_async_copy(down_ref, down, local.at[0]),
        pltpu.make_async_copy(up_ref, up, local.at[1]),
    ]
    order = [(s, m) for s in range(2) for m in (3, 1, 2, 0)]
    pieces = (cot_0, cot_1, cot_2, cot_3, cot_4, cot_5, cot_6)

    def load(at):
        s, m = order[at]
        slot = at % 2
        return piece_copies(pieces, s, m, cot.at[slot], loads.at[slot]) + [
            pltpu.make_async_copy(relu_ref.at[s, m], relu.at[slot], loads.at[slot, 2]),
        ]

    for copy in load(0) + weights:
        copy.start()
    greet([to_x, to_y])
    for copy in weights:
        copy.wait()
    def remote(s, source, number, side, partner):
        return pltpu.make_async_remote_copy(
            src_ref=part.at[s, source, :, lanes[side]],
            dst_ref=arrived.at[s, number],
            send_sem=send.at[s, number],
            recv_sem=recv.at[s, number],
            device_id=partner,
            device_id_type=MESH,
        )

    copies = [
        [
            remote(s, 1, 0, 0, to_x),
            remote(s, 3, 1, 0, to_x),
            remote(s, 2, 2, 1, to_y),
            remote(s, 3, 3, 1, to_y),
            remote(s, 2, 4, 0, to_y),
            remote(s, 1, 5, 1, to_x),
        ]
        for s in range(2)
    ]
    saving = [None, None]
    load_second = pltpu.make_async_copy(second_ref, second, local.at[0])

    def tile(at):
        s, m = order[at]
        slot = at % 2
        for copy in load(at):
            copy.wait()
        if at + 1 < len(order):
            for copy in load(at + 1):
                copy.start()
        if saving[slot] is not None:
            saving[slot].wait()

        def back(step, carry):
            columns = pl.ds(pl.multiple_of(step * CHUNK, CHUNK), CHUNK)
            product = dot_nt(cot[slot], down[columns, :])
            grad[slot, :, columns] = (product * 2.0 * relu[slot, :, columns]).astype(LOW)
            return carry

        lax.fori_loop(0, units // CHUNK, back, 0)
        if at + 1 == len(order):
            load_second.start()
        saving[slot] = pltpu.make_async_copy(grad.at[slot], grad_ref.at[s, m], outs.at[slot])
        saving[slot].start()

        def through(step, carry):
            columns = pl.ds(pl.multiple_of(step * CHUNK, CHUNK), CHUNK)
            part[s, m, :, columns] = dot(grad[slot], up[:, columns]).astype(LOW)
            return carry

        lax.fori_loop(0, depth // CHUNK, through, 0)

    def second_leg(s):
        copies[s][1].wait_recv()
        part[s, 2, :, lanes[0]] = (
            part[s, 2, :, lanes[0]].astype(F32) + arrived[s, 1].astype(F32)
        ).astype(LOW)
        copies[s][4].start()
        copies[s][3].wait_recv()
        part[s, 1, :, lanes[1]] = (
            part[s, 1, :, lanes[1]].astype(F32) + arrived[s, 3].astype(F32)
        ).astype(LOW)
        copies[s][5].start()

    def finish(s):
        for side, near, last in ((0, 0, 4), (1, 2, 5)):
            copies[s][near].wait_recv()
            copies[s][last].wait_recv()
            result[:, lanes[side]] = (
                part[s, 0, :, lanes[side]].astype(F32)
                + arrived[s, near].astype(F32)
                + arrived[s, last].astype(F32)
            )
        done = pltpu.make_async_copy(result, back_ref.at[s], local.at[2])
        done.start()
        return done

    def send_after(at):
        s, m = order[at]
        for number in {3: (1, 3), 1: (0,), 2: (2,), 0: ()}[m]:
            copies[s][number].start()

    for at in range(5):
        tile(at)
        send_after(at)
    second_leg(0)
    for at in range(5, 8):
        tile(at)
        send_after(at)
    done = finish(0)

    for slot in range(2):
        saving[slot].wait()
    load_second.wait()
    halves = units // WIDE // 2

    def some(span):
        gradient_tiles(grad_ref, second, tiles, sums, up_part_ref, tile_sem, sum_sem, span=span)

    some((0, halves))
    second_leg(1)
    some((halves, 2 * halves))
    done.wait()
    finish(1).wait()
    for s in range(2):
        for number in range(6):
            copies[s][number].wait_send()


def feed_out(cot_pieces, relu, second_all, up_all, down_all):
    rows_here, units = relu.shape[2:]
    depth = up_all.shape[1]
    anywhere = pl.BlockSpec(memory_space=pl.ANY)
    dma = pltpu.SemaphoreType.DMA
    return pl.pallas_call(
        feed_out_kernel,
        in_specs=[anywhere] * 11,
        out_specs=[anywhere] * 3,
        out_shape=[
            jax.ShapeDtypeStruct((2, 4, rows_here, units), LOW),
            jax.ShapeDtypeStruct((units, depth), LOW),
            jax.ShapeDtypeStruct((2, rows_here, depth), F32),
        ],
        scratch_shapes=[
            pltpu.VMEM((units, depth), LOW),
            pltpu.VMEM((max(units, 8 * rows_here), depth), LOW),
            pltpu.VMEM((2, rows_here, depth), LOW),
            pltpu.VMEM((2, rows_here, units), F32),
            pltpu.VMEM((2, rows_here, units), LOW),
            pltpu.VMEM((2, 4, rows_here, depth), LOW),
            pltpu.VMEM((2, 6, rows_here, depth // 2), LOW),
            pltpu.VMEM((2, 2, 4, rows_here, WIDE), LOW),
            pltpu.VMEM((2, WIDE, depth), LOW),
            pltpu.VMEM((rows_here, depth), F32),
            dma((3,)),
            dma((2, 3)),
            dma((2,)),
            dma((2, 6)),
            dma((2, 6)),
            dma((2,)),
            dma((2,)),
        ],
        compiler_params=pltpu.CompilerParams(
            collective_id=2, has_side_effects=True, vmem_limit_bytes=VMEM_LIMIT
        ),
        cost_estimate=pl.CostEstimate(
            flops=2 * 8 * rows_here * depth * units * 4,
            bytes_accessed=60 * 2**20,
            transcendentals=0,
        ),
        name="feed_out",
    )(*cot_pieces, relu, second_all.reshape(8 * rows_here, depth), up_all, down_all)


def feed_heads_kernel(
    x_ref, hidden_ref, down_ref,
    o_ref, feed_x0_ref, feed_x1_ref, feed_y0_ref, feed_y1_ref, keep_a_ref, keep_b_ref,
    landed, down, hidden, feed, local, send, recv, loads, outs,
):
    me = lax.axis_index("mp")
    units, depth = down.shape
    half = depth // 2
    lanes = (pl.ds(0, half), pl.ds(half, half))
    feed_x_refs, feed_y_refs = (feed_x0_ref, feed_x1_ref), (feed_y0_ref, feed_y1_ref)

    def source(at):
        return x_ref.at[:, :, head_lanes(at)]

    def target(at):
        return landed.at[:, at]

    weights = pltpu.make_async_copy(down_ref, down, local.at[2])
    weights.start()
    own = pltpu.make_async_copy(source(me), target(me), local.at[0])
    own.start()
    greet_members(())
    copies = member_copies(source, target, send, recv)
    for leaving, _ in copies:
        leaving.start()
    order = [(s, m) for s in range(2) for m in (3, 1, 2, 0)]

    def load(at):
        s, m = order[at]
        return pltpu.make_async_copy(hidden_ref.at[s, m], hidden.at[at % 2], loads.at[at % 2])

    load(0).start()
    weights.wait()
    feeding = [None, None]
    for at, (s, m) in enumerate(order):
        slot = at % 2
        load(at).wait()
        if at + 1 < len(order):
            load(at + 1).start()
        if feeding[slot] is not None:
            for copy in feeding[slot]:
                copy.wait()

        def one(step, carry, slot=slot):
            columns = pl.ds(pl.multiple_of(step * CHUNK, CHUNK), CHUNK)
            feed[slot, :, columns] = dot(hidden[slot], down[:, columns]).astype(LOW)
            return carry

        lax.fori_loop(0, depth // CHUNK, one, 0)
        targets = (
            (keep_a_ref.at[s, 0], feed_x_refs[s].at[0], keep_a_ref.at[s, 1], feed_x_refs[s].at[1])[m],
            (keep_b_ref.at[s, 0], keep_b_ref.at[s, 1], feed_y_refs[s].at[0], feed_y_refs[s].at[1])[m],
        )
        feeding[slot] = [
            pltpu.make_async_copy(feed.at[slot, :, lanes[side]], there, outs.at[slot, side])
            for side, there in enumerate(targets)
        ]
        for copy in feeding[slot]:
            copy.start()
    own.wait()
    for _, landing in copies:
        landing.wait_recv()
    save = pltpu.make_async_copy(landed, o_ref, local.at[1])
    save.start()
    for leaving, _ in copies:
        leaving.wait_send()
    for slot in feeding:
        for copy in slot:
            copy.wait()
    save.wait()


def feed_heads(x, hidden, down_all):
    parts, rows_here, width = x.shape
    mp = lax.axis_size("mp")
    units, depth = down_all.shape
    anywhere = pl.BlockSpec(memory_space=pl.ANY)
    dma = pltpu.SemaphoreType.DMA
    shape = (parts, mp, rows_here, 128)
    out, *terms = pl.pallas_call(
        feed_heads_kernel,
        in_specs=[pl.BlockSpec(memory_space=pltpu.VMEM)] + [anywhere] * 2,
        out_specs=[anywhere] * 7,
        out_shape=[jax.ShapeDtypeStruct(shape, LOW)]
        + [jax.ShapeDtypeStruct((2, rows_here, depth // 2), LOW)] * 4
        + [jax.ShapeDtypeStruct((2, 2, rows_here, depth // 2), LOW)] * 2,
        scratch_shapes=[
            pltpu.VMEM(shape, LOW),
            pltpu.VMEM((units, depth), LOW),
            pltpu.VMEM((2, rows_here, units), LOW),
            pltpu.VMEM((2, rows_here, depth), LOW),
            dma((3,)),
            dma((mp,)),
            dma((mp,)),
            dma((2,)),
            dma((2, 2)),
        ],
        compiler_params=pltpu.CompilerParams(
            collective_id=6, has_side_effects=True, vmem_limit_bytes=48 * 2**20
        ),
        cost_estimate=pl.CostEstimate(flops=2**35, bytes_accessed=2**24, transcendentals=0),
        name="feed_heads",
    )(x, hidden, down_all)
    return [out.reshape(parts, mp * rows_here, 128)] + terms


def finish_kernel(
    ways, qk_ref, v_ref, out_ref, norms_ref, taps_ref, grad_raw_ref, inputs_ref, gain_ref,
    qk_all_ref, v_all_ref, middle_ref, *refs
):
    carried, refs = list(zip(ways, refs[: len(ways)])), refs[len(ways) :]
    joint_ref, norms_sum_ref, taps_sum_ref, input_grad_ref = refs[:4]
    targets, refs = refs[4 : 4 + len(ways)], refs[4 + len(ways) :]
    (
    acc, got, plane_in, line_in, gathered, norms_all, taps_all, norms_dp, taps_dp,
    weights, result, middle, norms, sums, weight_sem,
    local, swap_send, swap_recv, plane_send_sem, plane_recv_sem, line_send_sem, line_recv_sem,
    gather_send, gather_recv, small_send, small_recv, carry_send, carry_recv,
    ) = refs
    mp = lax.axis_size("mp")
    dp = lax.axis_index("dp")
    me = lax.axis_index("mp")
    z, core = mesh_place()
    count = mp // 2
    depth = acc.shape[3]
    half = depth // 2
    lanes = (pl.ds(0, half), pl.ds(half, half))
    to_x, to_y = plane_partners()
    dp_x = dp + 1 - 2 * lax.rem(dp, 2)
    dp_y = dp + 2 - 4 * (dp // 2)
    dp_xy = dp_x + 2 - 4 * (dp_x // 2)
    parts = (qk_ref, v_ref, out_ref)
    spans = (pl.ds(0, HD // 2), pl.ds(HD // 2, HD // 4), pl.ds(3 * HD // 4, HD // 4))
    loads = [
        pltpu.make_async_copy(part.at[:, core], acc.at[:, :, span, :], local.at[at])
        for at, (part, span) in enumerate(zip(parts, spans))
    ]
    for copy in loads:
        copy.start()

    barrier = pltpu.get_barrier_semaphore()
    for step in range(1, mp):
        pl.semaphore_signal(
            barrier, inc=1, device_id={"mp": lax.rem(me + step, mp)}, device_id_type=MESH
        )
    for step in range(1, 4):
        pl.semaphore_signal(
            barrier, inc=1, device_id={"dp": lax.rem(dp + step, 4)}, device_id_type=MESH
        )
    pl.semaphore_wait(barrier, mp + 2)

    swaps = [
        [
            wire(
                part.at[:, 1 - core, quarter], got.at[:, quarter, span, :],
                swap_send.at[at, number], swap_recv.at[at, number], other_core(),
            )
            for at, (part, span) in enumerate(zip(parts, spans))
        ]
        for number, quarter in enumerate((dp_xy, dp_x, dp_y, dp))
    ]
    for group in swaps:
        for copy in group:
            copy.start()

    def small(axis, at, others, source, target, number, first):
        out = []
        for step in range(1, others):
            to = lax.rem(at + step, others)
            frm = lax.rem(at + others - step, others)
            sems = (small_send.at[number, step], small_recv.at[number, step], {axis: to})
            out.append((wire(source(to), target.at[at], *sems), wire(source(to), target.at[frm], *sems)))
        return out

    load_middle = pltpu.make_async_copy(middle_ref, middle, local.at[6])
    load_middle.start()
    own_small = [
        pltpu.make_async_copy(norms, norms_all.at[me], local.at[3]),
        pltpu.make_async_copy(taps_ref.at[me], taps_all.at[me], local.at[4]),
    ]
    over_mp = small("mp", me, mp, lambda to: norms, norms_all, 0, None) + small(
        "mp", me, mp, lambda to: taps_ref.at[to], taps_all, 1, None
    )

    rows_here = inputs_ref.shape[1]
    slots = weights.shape[0]

    def load_weights(at, slot):
        return [
            pltpu.make_async_copy(
                qk_all_ref.at[at], weights.at[slot, pl.ds(0, 4 * HD), :], weight_sem.at[slot, 0]
            )
        ] + [
            pltpu.make_async_copy(
                v_all_ref.at[at, pl.ds(head * HD, HD), :],
                weights.at[slot, pl.ds((4 + 2 * head + copy) * HD, HD), :],
                weight_sem.at[slot, 1 + 2 * head + copy],
            )
            for head in range(2)
            for copy in range(2)
        ]

    def normed_grad():
        if slots == 2:
            for copy in load_weights(0, 0):
                copy.start()
        lane = lax.rem(lax.broadcasted_iota(jnp.int32, (rows_here, 4 * HD), 1), 2 * HD)

        def one(at, carry):
            slot = lax.rem(at, slots)
            if slots == 1:
                for copy in load_weights(at, slot):
                    copy.start()
            for copy in load_weights(at, slot):
                copy.wait()
            if slots == 2:

                @pl.when(at + 1 < count)
                def _():
                    for copy in load_weights(at + 1, 1 - slot):
                        copy.start()

            pair = pl.ds(pl.multiple_of(at * 4 * HD, 4 * HD), 4 * HD)
            side = grad_raw_ref[2, :, pair]
            for s in range(2):
                mine = lane < HD if s == 0 else lane >= HD
                left = jnp.concatenate(
                    [grad_raw_ref[s, :, pair], jnp.where(mine, side, jnp.zeros_like(side))], axis=1
                )
                for first in range(0, depth, CHUNK):
                    columns = pl.ds(first, CHUNK)
                    product = dot(left, weights[slot, :, columns])

                    @pl.when(at == 0)
                    def _(s=s, columns=columns, product=product):
                        result[s, :, columns] = product

                    @pl.when(at > 0)
                    def _(s=s, columns=columns, product=product):
                        result[s, :, columns] += product

            return carry

        lax.fori_loop(0, count, one, 0)

    tall = 16
    tiles = rows_here // tall

    def norm_back(s, first, last):
        def some(at, carry):
            here = pl.ds(pl.multiple_of(at * tall, tall), tall)
            values = inputs_ref[s, here, :].astype(F32)
            centered = values - jnp.mean(values, axis=1, keepdims=True)
            scale = lax.rsqrt(jnp.mean(centered * centered, axis=1, keepdims=True) + 1e-05)
            hat = centered * scale
            grad = result[s, here, :]
            wide = grad * gain_ref[...]
            back = wide - jnp.mean(wide, axis=1, keepdims=True)
            back = scale * (back - hat * jnp.mean(wide * hat, axis=1, keepdims=True))
            result[s, here, :] = middle[s, here, :] + back
            product = grad * hat
            sums[0] += product[:8] + product[8:]
            sums[1] += grad[:8] + grad[8:]
            return carry

        lax.fori_loop(first, last, some, 0)

    def add(quarter, side, number):
        acc[:, quarter, :, lanes[side]] = (
            acc[:, quarter, :, lanes[side]].astype(F32) + plane_in[number].astype(F32)
        ).astype(LOW)

    def add_core(number, quarter):
        for copy in swaps[number]:
            copy.wait_recv()
        acc[:, quarter] = (acc[:, quarter].astype(F32) + got[:, quarter].astype(F32)).astype(LOW)

    def plane(quarter, side, partner, number):
        return wire(
            acc.at[:, quarter, :, lanes[side]], plane_in.at[number],
            plane_send_sem.at[number], plane_recv_sem.at[number], partner,
        )

    sends = [
        plane(dp_x, 0, to_x, 0),
        plane(dp_xy, 0, to_x, 1),
        plane(dp_y, 1, to_y, 2),
        plane(dp_xy, 1, to_y, 3),
        plane(dp_y, 0, to_y, 4),
        plane(dp_x, 1, to_x, 5),
    ]
    for copy in loads:
        copy.wait()
    add_core(0, dp_xy)
    sends[1].start()
    sends[3].start()
    add_core(1, dp_x)
    sends[0].start()
    add_core(2, dp_y)
    sends[2].start()
    add_core(3, dp)
    normed_grad()
    load_middle.wait()
    sums[...] = jnp.zeros(sums.shape, F32)
    norm_back(0, 0, tiles)
    saved_rows = [
        pltpu.make_async_copy(result.at[s], input_grad_ref.at[s], local.at[7 + s]) for s in range(2)
    ]
    saved_rows[0].start()
    sends[1].wait_recv()
    add(dp_y, 0, 1)
    sends[4].start()
    sends[3].wait_recv()
    add(dp_x, 1, 3)
    sends[5].start()
    norm_back(1, 0, tiles // 2)
    sends[0].wait_recv()
    add(dp, 0, 0)
    sends[2].wait_recv()
    add(dp, 1, 2)
    sends[4].wait_recv()
    add(dp, 0, 4)
    sends[5].wait_recv()
    add(dp, 1, 5)

    carries = carry_copies(carried, targets, carry_send, carry_recv)
    for copy in carries:
        copy.start()

    def line(step):
        out = []
        for way, turn in enumerate((1, -1)):
            target = z + turn * (count - step)
            far = z + turn
            lands = far - 2 * turn + turn * (count - step)
            sends = (target >= 0) & (target < count)
            receives = (lands >= 0) & (lands < count) & (z - turn >= 0) & (z - turn < count)
            at = jnp.clip(target, 0, count - 1)
            to = jnp.clip(lands, 0, count - 1)
            copy = wire(
                acc.at[at, dp], line_in.at[way, step - 1],
                line_send_sem.at[way, step - 1], line_recv_sem.at[way, step - 1],
                line_partner(z, turn),
            )
            out.append((sends, receives, to, copy))
        return out

    over_dp = []
    for step in range(1, count):
        legs = line(step)
        for sends_now, _, _, copy in legs:
            pl.when(sends_now)(copy.start)
        if step == 1:
            norm_back(1, tiles // 2, tiles)
            saved_rows[1].start()
            norms[...] = norms_ref[...]
            norms[0:1, :] = jnp.sum(sums[0], axis=0, keepdims=True)
            norms[1:2, :] = jnp.sum(sums[1], axis=0, keepdims=True)
            for copy in own_small:
                copy.start()
            for leaving, _ in over_mp:
                leaving.start()
        if step == count - 1:
            for _, landed in over_mp:
                landed.wait_recv()
            for copy in own_small:
                copy.wait()
            norms_dp[dp] = jnp.sum(norms_all[...], axis=0)
            taps_dp[dp] = jnp.sum(taps_all[...], axis=0)
            over_dp = small("dp", dp, 4, lambda to: norms_dp.at[dp], norms_dp, 2, None) + small(
                "dp", dp, 4, lambda to: taps_dp.at[dp], taps_dp, 3, None
            )
            for leaving, _ in over_dp:
                leaving.start()
        for way, (_, receives, to, copy) in enumerate(legs):

            @pl.when(receives)
            def _(to=to, copy=copy, way=way):
                copy.wait_recv()
                acc[to, dp] = (
                    acc[to, dp].astype(F32) + line_in[way, step - 1].astype(F32)
                ).astype(LOW)

    gathered[dp] = acc[z, dp]

    def gather(quarter, side, partner, number):
        block = gathered.at[quarter, :, lanes[side]]
        return wire(block, block, gather_send.at[number], gather_recv.at[number], partner)

    leaving = [
        gather(dp, 0, to_x, 0), gather(dp, 1, to_y, 1), gather(dp, 0, to_y, 2), gather(dp, 1, to_x, 3),
        gather(dp_x, 0, to_y, 4), gather(dp_y, 1, to_x, 5),
    ]
    landing = [
        gather(dp_x, 0, to_x, 0), gather(dp_y, 1, to_y, 1), gather(dp_y, 0, to_y, 2), gather(dp_x, 1, to_x, 3),
        gather(dp_xy, 0, to_y, 4), gather(dp_xy, 1, to_x, 5),
    ]
    for number in range(4):
        leaving[number].start()
    for _, landed in over_dp:
        landed.wait_recv()
    norms_sum_ref[...] = jnp.sum(norms_dp[...], axis=0)
    taps_sum_ref[...] = jnp.sum(taps_dp[...], axis=0)
    landing[0].wait_recv()
    leaving[4].start()
    landing[1].wait_recv()
    leaving[5].start()
    for number in range(2, 6):
        landing[number].wait_recv()
    save = pltpu.make_async_copy(gathered, joint_ref, local.at[5])
    save.start()
    for group in swaps:
        for copy in group:
            copy.wait_send()
    for copy in sends:
        copy.wait_send()
    for step in range(1, count):
        for sends_now, _, _, copy in line(step):
            pl.when(sends_now)(copy.wait_send)
    for copy in leaving:
        copy.wait_send()
    for copy, _ in over_mp + over_dp:
        copy.wait_send()
    for copy in carries + saved_rows:
        copy.wait()
    save.wait()


def finish(qk, v, out, norms, taps, grad_raw, inputs, gain, qk_all, v_all, middle, carried):
    mp = lax.axis_size("mp")
    count = mp // 2
    depth = qk.shape[-1]
    anywhere = pl.BlockSpec(memory_space=pl.ANY)
    vmem = pl.BlockSpec(memory_space=pltpu.VMEM)
    dma = pltpu.SemaphoreType.DMA
    return pl.pallas_call(
        partial(finish_kernel, tuple(way for way, _ in carried)),
        in_specs=[anywhere] * 3 + [vmem] * 5 + [anywhere] * (3 + len(carried)),
        out_specs=[anywhere, vmem, vmem, anywhere] + [anywhere] * len(carried),
        out_shape=[
            jax.ShapeDtypeStruct((4, HD, depth), LOW),
            jax.ShapeDtypeStruct(norms.shape, F32),
            jax.ShapeDtypeStruct(taps.shape[1:], F32),
            jax.ShapeDtypeStruct(middle.shape, F32),
        ]
        + [jax.ShapeDtypeStruct(block.shape, block.dtype) for _, block in carried],
        scratch_shapes=[
            pltpu.VMEM((count, 4, HD, depth), LOW),
            pltpu.VMEM((count, 4, HD, depth), LOW),
            pltpu.VMEM((6, count, HD, depth // 2), LOW),
            pltpu.VMEM((2, count - 1, HD, depth), LOW),
            pltpu.VMEM((4, HD, depth), LOW),
            pltpu.VMEM((mp,) + norms.shape, F32),
            pltpu.VMEM(taps.shape, F32),
            pltpu.VMEM((4,) + norms.shape, F32),
            pltpu.VMEM((4,) + taps.shape[1:], F32),
            pltpu.VMEM((2 if count <= 8 else 1, 8 * HD, depth), LOW),
            pltpu.VMEM(middle.shape, F32),
            pltpu.VMEM(middle.shape, F32),
            pltpu.VMEM(norms.shape, F32),
            pltpu.VMEM((2, 8, depth), F32),
            dma((2, 5)),
            dma((9,)),
            dma((3, 4)),
            dma((3, 4)),
            dma((6,)),
            dma((6,)),
            dma((2, count)),
            dma((2, count)),
            dma((6,)),
            dma((6,)),
            dma((4, mp)),
            dma((4, mp)),
            dma((len(carried),)),
            dma((len(carried),)),
        ],
        compiler_params=pltpu.CompilerParams(
            collective_id=8, has_side_effects=True, vmem_limit_bytes=VMEM_LIMIT + 2**19
        ),
        cost_estimate=pl.CostEstimate(flops=2**36, bytes_accessed=2**26, transcendentals=0),
        name="finish",
    )(
        qk, v, out, norms, taps, grad_raw, inputs, gain.reshape(1, depth), qk_all, v_all, middle, *(block for _, block in carried),
    )


def plane_send(block, mask):
    return lax.ppermute(block, "dp", [(d, d ^ mask) for d in range(lax.axis_size("dp"))])


def placed(own, legs, last, me, turn):
    one_x, two_y, one_y, two_x = legs
    units, width = own.shape
    wide = 256
    steps = width // 2 // wide

    def kernel(me_ref, own_ref, one_x, two_x, one_y, two_y, one_xy, two_xy, o_ref):
        first = pl.program_id(0) < steps
        blocks = [own_ref[...]] + [
            jnp.where(first, one[...], two[...])
            for one, two in ((one_x, two_x), (one_y, two_y), (one_xy, two_xy))
        ]
        odd, high = lax.rem(me_ref[0], 2) == 1, me_ref[0] >= 2
        blocks = [jnp.where(odd, blocks[at ^ 1], blocks[at]) for at in range(4)]
        blocks = [jnp.where(high, blocks[at ^ 2], blocks[at]) for at in range(4)]
        for at, block in enumerate(blocks):
            if turn:
                o_ref[:, at * units : (at + 1) * units] = block.astype(F32).T
            else:
                o_ref[at * units : (at + 1) * units, :] = block.astype(F32)

    def half(side):
        if side == 0:
            return pl.BlockSpec((units, wide), lambda i, me: (0, jnp.minimum(i, steps - 1)))
        return pl.BlockSpec((units, wide), lambda i, me: (0, jnp.maximum(i - steps, 0)))

    if turn:
        shape = (width, 4 * units)
        out_spec = pl.BlockSpec((wide, 4 * units), lambda i, me: (i, 0))
    else:
        shape = (4 * units, width)
        out_spec = pl.BlockSpec((4 * units, wide), lambda i, me: (0, i))
    return pl.pallas_call(
        kernel,
        grid_spec=pltpu.PrefetchScalarGridSpec(
            num_scalar_prefetch=1,
            grid=(2 * steps,),
            in_specs=[pl.BlockSpec((units, wide), lambda i, me: (0, i))] + [half(0), half(1)] * 3,
            out_specs=out_spec,
        ),
        out_shape=jax.ShapeDtypeStruct(shape, F32),
        compiler_params=pltpu.CompilerParams(vmem_limit_bytes=32 * 2**20),
        cost_estimate=pl.CostEstimate(flops=0, bytes_accessed=2**24, transcendentals=0),
        name="placed",
    )(me.reshape(1).astype(jnp.int32), own, one_x, two_x, one_y, two_y, *last)


def plane_gather_begin(block, axis=-1):
    half = block.shape[axis] // 2
    one, two = jnp.split(block, [half], axis=axis)
    return plane_send(one, 1), plane_send(two, 2), plane_send(one, 2), plane_send(two, 1)


def plane_gather_end(legs):
    one_x, two_y, one_y, two_x = legs
    return plane_send(one_x, 2), plane_send(two_y, 1)


def line_step(blocks, step):
    count = lax.axis_size("mp") // 2
    up = [(2 * z + c, 2 * z + 2 + c) for z in range(step - 1, count - 1) for c in range(2)]
    down = [(2 * z + c, 2 * z - 2 + c) for z in range(1, count - step + 1) for c in range(2)]
    return lax.ppermute(blocks[0], "mp", up), lax.ppermute(blocks[1], "mp", down)


def per_device(
    inputs,
    cotangent,
    short_lengths,
    long_lengths,
    norm1_gain,
    norm1_bias,
    query_weight,
    key_weight,
    value_weight,
    query_kernel,
    key_kernel,
    value_kernel,
    out_weight,
    norm2_gain,
    norm2_bias,
    up_weight,
    down_weight,
):
    rows_here = inputs.shape[1]
    width = inputs.shape[2]
    mp = lax.axis_size("mp")
    dp = lax.axis_size("dp")
    me_dp = lax.axis_index("dp")
    me_mp = lax.axis_index("mp")
    group = rows_here * mp
    chips = mp // 2
    hidden_here = up_weight.shape[1]
    share = hidden_here // dp

    starts = jnp.stack(
        [document_starts(short_lengths[0], group), document_starts(long_lengths[0], group)]
    )
    rows = inputs.astype(F32)

    def quarters(weight):
        return weight.reshape(4, weight.shape[0] // 4, width)

    qk_own = jnp.concatenate([query_weight, key_weight], axis=1).T
    up_own = lax.dynamic_slice_in_dim(up_weight, me_dp * share, share, 1).T
    down_own = lax.dynamic_slice_in_dim(down_weight, me_dp * share, share, 0)
    qk_taps = jnp.concatenate([query_kernel, key_kernel], axis=1)
    v_taps = jnp.concatenate([value_kernel, value_kernel], axis=1)
    taps_own = jnp.pad(jnp.stack([qk_taps, qk_taps, v_taps]), ((0, 0), (0, 5), (0, 0)))
    places = jnp.arange(group, dtype=jnp.int32)
    offsets = lax.dynamic_slice_in_dim(
        jnp.pad(places[None, :] - starts, ((0, 0), (0, HALO))), me_mp * rows_here, rows_here + HALO, 1
    )
    masks = jnp.stack(
        [
            offsets[:, :rows_here] >= 1,
            offsets[:, :rows_here] >= 2,
            offsets[:, 1 : rows_here + 1] >= 1,
            offsets[:, 2 : rows_here + 2] >= 2,
        ],
        axis=1,
    ).astype(F32)[..., None]
    wide_masks = jnp.broadcast_to(masks, masks.shape[:3] + (HD,))
    masks = jnp.stack(
        [
            jnp.concatenate([wide_masks[left], wide_masks[right]], axis=2)
            for left, right in ((0, 0), (1, 1), (0, 1))
        ]
    )

    qk_all, v_all, out_all, taps, normed, up_early, raw, mixed, one_x, two_y = front(
        inputs, norm1_gain, norm1_bias, quarters(qk_own), quarters(value_weight.T), quarters(out_weight), taps_own, up_own,
        masks, cotangent,
    )
    qk_all = qk_all.reshape(mp * 2 * HD, width)
    v_all = v_all.reshape(mp * HD, width)
    out_all = out_all.reshape(mp * HD, width)
    mixed = mixed.reshape(3, group, 128)
    cot, mixed, up_early = lax.optimization_barrier((cotangent, mixed, up_early))

    def early_block(at):
        start = (2 * jnp.clip(at, 0, chips - 1) + me_mp % 2) * share
        return lax.dynamic_slice_in_dim(up_early, start, share, 0)

    late = range(early_steps(chips)[-1] + 1, chips)
    up_late = {}
    blocks = (early_block(me_mp // 2 - late[0] + 1), early_block(me_mp // 2 + late[0] - 1))
    for step in late:
        blocks = line_step(blocks, step)
        up_late[step, 1], up_late[step, -1] = blocks
    one_y, two_x = plane_send(cot[:, :, : width // 2], 2), plane_send(cot[:, :, width // 2 :], 1)
    one_xy, two_xy = plane_send(one_x, 2), plane_send(two_y, 1)

    def side_by_side(pair):
        split = pair.reshape(2, rows_here, mp, HD)
        return split.transpose(1, 2, 0, 3).reshape(1, rows_here, mp * 2 * HD)

    def apart(joint):
        split = joint.reshape(joint.shape[1], mp, 2, HD)
        return split.transpose(2, 0, 1, 3).reshape(2, joint.shape[1], mp * HD)

    attended_head, wide, total = attend(mixed, starts)
    attended_head, up_late = lax.optimization_barrier((attended_head, up_late))
    attended = apart(attended_back(attended_head, rows_here))
    middle = rows + dot(attended, out_all)
    second = layer_norm(middle, norm2_gain, norm2_bias).astype(LOW)

    second, one_y, two_x, one_xy, two_xy = lax.optimization_barrier(
        (second, one_y, two_x, one_xy, two_xy)
    )
    cot_pieces = (cot, one_x, two_x, one_y, two_y, one_xy, two_xy)
    second_all, relu, hidden, down_all, up_all, down_part = feed_in(
        second, up_early, down_own, cot_pieces, up_late
    )
    down_mine = lax.psum_scatter(down_part, "mp", scatter_dimension=0, tiled=True)
    grad_pre, up_part, grad_second = feed_out(
        cot_pieces, relu, second_all, up_all, down_all
    )
    up_mine = lax.psum_scatter(up_part, "mp", scatter_dimension=0, tiled=True)
    grad_second, down_mine = lax.optimization_barrier((grad_second, down_mine))
    down_legs = plane_gather_begin(down_mine)

    def norm_back(values, gain, grad):
        flat = values.reshape(-1, width)
        unused, pull = jax.vjp(layer_norm, flat, gain, norm1_bias)
        grad_rows, grad_gain, grad_shift = pull(grad.reshape(-1, width))
        return grad_rows.reshape(values.shape), grad_gain, grad_shift

    grad_middle, gain_two, shift_two = norm_back(middle, norm2_gain, grad_second)
    grad_middle = grad_middle + cotangent.astype(F32)
    branch = grad_middle.astype(LOW)
    grad_attended = jnp.einsum("srd,hd->srh", branch, out_all, preferred_element_type=F32).astype(LOW)
    grad_head, feed_x0, feed_x1, feed_y0, feed_y1, keep_a, keep_b = feed_heads(
        side_by_side(grad_attended), hidden, down_all
    )
    grad_head, down_legs, feed_x0, feed_y0 = lax.optimization_barrier(
        (grad_head, down_legs, feed_x0, feed_y0)
    )
    down_last = plane_gather_end(down_legs)
    x_first, y_first = plane_send(feed_x0, 1), plane_send(feed_y0, 2)
    grad_mixed_head = attend_back(mixed, grad_head, wide, total, starts, HALO)
    grad_mixed_head, down_last, x_first, y_first = lax.optimization_barrier(
        (grad_mixed_head, down_last, x_first, y_first)
    )
    down_grad = placed(down_mine, down_legs, down_last, me_dp, False)

    def add(left, right):
        return left.astype(F32) + right.astype(F32)

    feed_a0, feed_b0 = add(keep_a[0, 1], x_first[1]).astype(LOW), add(keep_b[0, 1], y_first[1]).astype(LOW)
    grad_raw, tap_sums, qk_part, v_part, out_part, x_second, y_second, feed_a0, feed_b0 = project_back(
        grad_mixed_head, raw, taps, masks, normed, attended, branch,
        ((0, feed_x1), (1, feed_y1), (1, feed_a0), (0, feed_b0)),
    )
    grad_raw, down_last = lax.optimization_barrier((grad_raw, down_last))
    grad_raw, up_mine = lax.optimization_barrier((grad_raw, up_mine))
    up_legs = plane_gather_begin(up_mine)
    feed_a1, feed_b1 = add(keep_a[1, 1], x_second[1]).astype(LOW), add(keep_b[1, 1], y_second[1]).astype(LOW)

    def split_parts(part):
        return part.reshape(mp // 2, 2, 4, part.shape[1] // 8, width)

    norms = jnp.pad(jnp.stack([gain_two, shift_two]), ((2, 4), (0, 0)))
    qk_sums = (tap_sums[0] + tap_sums[1]).reshape(8, mp, 2 * HD)
    v_sums = tap_sums[2].reshape(8, mp, 2, HD).sum(axis=2)
    taps_part = jnp.concatenate([qk_sums, v_sums, jnp.zeros_like(v_sums)], axis=2)
    taps_part = taps_part.transpose(1, 0, 2)
    norms, up_legs = lax.optimization_barrier((norms, up_legs))
    joint_grad, small_sum, taps_sum, input_grads, feed_a1, feed_b1, one_xy, two_xy = finish(
        split_parts(qk_part), split_parts(v_part), split_parts(out_part), norms, taps_part,
        grad_raw, inputs, norm1_gain, qk_all.reshape(chips, 4 * HD, width), v_all.reshape(chips, 2 * HD, width),
        grad_middle,
        ((1, feed_a1), (0, feed_b1), (1, up_legs[0]), (0, up_legs[1])),
    )
    results = jnp.stack(
        [
            middle[s]
            + jnp.concatenate(
                [
                    add(keep_a[s, 0], x_in[0]) + a_in.astype(F32),
                    add(keep_b[s, 0], y_in[0]) + b_in.astype(F32),
                ],
                axis=1,
            )
            for s, (x_in, y_in, a_in, b_in) in enumerate(
                ((x_first, y_first, feed_a0, feed_b0), (x_second, y_second, feed_a1, feed_b1))
            )
        ]
    ).astype(LOW)
    up_grad = placed(up_mine, up_legs, (one_xy, two_xy), me_dp, True)
    joint_grad = joint_grad.astype(F32)
    qk_grad = joint_grad[:, : HD // 2].reshape(2 * HD, width).T
    v_grad = joint_grad[:, HD // 2 : 3 * HD // 4].reshape(HD, width).T
    out_grad = joint_grad[:, 3 * HD // 4 :].reshape(HD, width)
    taps_sum = taps_sum[:3]
    return (
        results,
        input_grads,
        small_sum[0],
        small_sum[1],
        qk_grad[:, :HD],
        qk_grad[:, HD:],
        v_grad,
        taps_sum[:, :HD],
        taps_sum[:, HD : 2 * HD],
        taps_sum[:, 2 * HD : 3 * HD],
        out_grad,
        small_sum[2],
        small_sum[3],
        up_grad,
        down_grad,
    )


def solution(mesh):
    return jax.shard_map(
        per_device,
        mesh=mesh,
        in_specs=(
            P(None, ("dp", "mp"), None),
            P(None, ("dp", "mp"), None),
            P("dp", None),
            P("dp", None),
            P(),
            P(),
            P(None, "mp"),
            P(None, "mp"),
            P(None, "mp"),
            P(None, "mp"),
            P(None, "mp"),
            P(None, "mp"),
            P("mp", None),
            P(),
            P(),
            P(None, "mp"),
            P("mp", None),
        ),
        out_specs=(
            P(None, ("dp", "mp"), None),
            P(None, ("dp", "mp"), None),
            P(),
            P(),
            P(None, "mp"),
            P(None, "mp"),
            P(None, "mp"),
            P(None, "mp"),
            P(None, "mp"),
            P(None, "mp"),
            P("mp", None),
            P(),
            P(),
            P(None, "mp"),
            P("mp", None),
        ),
        check_vma=False,
    )
```

```python
import math
from functools import partial

import jax
import jax.numpy as jnp
from jax import lax
from jax.experimental import pallas as pl
from jax.experimental.pallas import tpu as pltpu
from jax.sharding import PartitionSpec as P

HD = 64
QUERIES, KEYS = 512, 512
WIDE = 256
CHUNK = 512
VMEM_LIMIT = 63 * 1024 * 1024
MESH = pl.DeviceIdType.MESH
LOW = jnp.bfloat16
F32 = jnp.float32


def dot(left, right):
    return jnp.dot(left, right, preferred_element_type=F32)


def layer_norm(rows, gain, shift):
    row_mean = jnp.mean(rows, axis=-1, keepdims=True)
    centered = rows - row_mean
    variance = jnp.mean(centered * centered, axis=-1, keepdims=True)
    return centered * lax.rsqrt(variance + 1e-05) * gain + shift


def document_starts(lengths, count):
    ends = jnp.cumsum(lengths)
    places = jnp.arange(count, dtype=jnp.int32)
    passed = (places[:, None] >= ends[None, :]).astype(jnp.int32)
    return jnp.sum(passed * lengths[None, :], axis=1)


def allowed_pairs(start_row, key_block, query_block):
    shape = (KEYS, QUERIES)
    keys = key_block * KEYS + lax.broadcasted_iota(jnp.int32, shape, 0)
    queries = query_block * QUERIES + lax.broadcasted_iota(jnp.int32, (1, QUERIES), 1)
    return (keys <= queries) & (keys >= start_row)


def key_blocks(first_ref, s, step):
    return first_ref[s, step], ((step + 1) * QUERIES + KEYS - 1) // KEYS


def attend_kernel(
    first_ref, start_ref, qk_ref, v_ref, out_ref, wide_ref, total_ref, values_t
):
    s, step = pl.program_id(0), pl.program_id(1)

    @pl.when(step == 0)
    def _():
        def turn(at, carry):
            rows = pl.ds(pl.multiple_of(at * KEYS, KEYS), KEYS)
            both = v_ref[0, rows, :].T
            values_t[at] = jnp.where(s == 0, both[:HD], both[HD:])
            return carry

        lax.fori_loop(0, values_t.shape[0], turn, 0)

    here = pl.ds(pl.multiple_of(step * QUERIES, QUERIES), QUERIES)
    query_t = (qk_ref[0, here, 0:HD] * HD ** (-0.5)).astype(LOW).T
    start_row = start_ref[0]

    def one(at, carry):
        top, summed, acc = carry
        rows = pl.ds(pl.multiple_of(at * KEYS, KEYS), KEYS)
        scores = dot(qk_ref[0, rows, HD : 2 * HD], query_t)
        scores = jnp.where(allowed_pairs(start_row, at, step), scores, -1e30)
        new_top = jnp.maximum(top, jnp.max(scores, axis=0, keepdims=True))
        powered = jnp.exp(scores - new_top)
        shrink = jnp.exp(top - new_top)
        summed = summed * shrink + jnp.sum(powered, axis=0, keepdims=True)
        acc = acc * shrink + dot(values_t[at], powered.astype(LOW))
        return new_top, summed, acc

    top, summed, acc = lax.fori_loop(
        *key_blocks(first_ref, s, step),
        one,
        (
            jnp.full((1, QUERIES), -1e30, F32),
            jnp.zeros((1, QUERIES), F32),
            jnp.zeros((HD, QUERIES), F32),
        ),
    )
    result = acc / summed
    wide_ref[0] = result
    total_ref[0] = top + jnp.log(summed)
    low = result.T.astype(LOW)

    @pl.when(s == 0)
    def _():
        out_ref[0, here, 0:HD] = low

    @pl.when(s == 1)
    def _():
        out_ref[0, here, HD : 2 * HD] = low


def attend(mixed, starts):
    group = mixed.shape[1]
    steps = group // QUERIES
    row = pl.BlockSpec((1, 1, QUERIES), lambda s, i, first: (s, 0, i))
    return pl.pallas_call(
        attend_kernel,
        grid_spec=pltpu.PrefetchScalarGridSpec(
            num_scalar_prefetch=1,
            grid=(2, steps),
            in_specs=[
                row,
                pl.BlockSpec((1, group, 2 * HD), lambda s, i, first: (s, 0, 0)),
                pl.BlockSpec((1, group, 2 * HD), lambda s, i, first: (2, 0, 0)),
            ],
            out_specs=[
                pl.BlockSpec((1, group, 2 * HD), lambda s, i, first: (0, 0, 0)),
                pl.BlockSpec((1, HD, QUERIES), lambda s, i, first: (s, 0, i)),
                row,
            ],
            scratch_shapes=[pltpu.VMEM((group // KEYS, HD, KEYS), LOW)],
        ),
        out_shape=[
            jax.ShapeDtypeStruct((1, group, 2 * HD), LOW),
            jax.ShapeDtypeStruct((2, HD, group), F32),
            jax.ShapeDtypeStruct((2, 1, group), F32),
        ],
        compiler_params=pltpu.CompilerParams(vmem_limit_bytes=32 * 1024 * 1024),
        cost_estimate=pl.CostEstimate(
            flops=2**34, bytes_accessed=group * 2048, transcendentals=group * group // 4
        ),
        name="attend",
    )(starts[:, ::QUERIES] // KEYS, starts[:, None, :], mixed, mixed)


def attend_back_kernel(
    first_ref, start_ref, qk_ref, v_ref, grad_ref, wide_ref, total_ref, out_ref,
    keys_t, values, grad_keys, grad_values,
):
    s, step = pl.program_id(0), pl.program_id(1)
    group = qk_ref.shape[1]

    @pl.when(step == 0)
    def _():
        def turn(at, carry):
            rows = pl.ds(pl.multiple_of(at * KEYS, KEYS), KEYS)
            keys_t[at] = qk_ref[0, rows, HD : 2 * HD].T
            both = v_ref[0, rows, :]
            values[rows, :] = jnp.where(s == 0, both[:, :HD], both[:, HD:])
            return carry

        lax.fori_loop(0, keys_t.shape[0], turn, 0)
        grad_keys[...] = jnp.zeros(grad_keys.shape, F32)
        grad_values[...] = jnp.zeros(grad_values.shape, F32)

    here = pl.ds(pl.multiple_of(step * QUERIES, QUERIES), QUERIES)
    query = (qk_ref[0, here, 0:HD] * HD ** (-0.5)).astype(LOW)
    query_t = query.T
    both = grad_ref[0]
    grad = jnp.where(s == 0, both[:, :HD], both[:, HD:])
    grad_t = grad.T
    start_row = start_ref[0]
    total = total_ref[0]
    inner = jnp.sum(grad_t.astype(F32) * wide_ref[0], axis=0, keepdims=True)

    def one(at, acc):
        rows = pl.ds(pl.multiple_of(at * KEYS, KEYS), KEYS)
        scores = dot(qk_ref[0, rows, HD : 2 * HD], query_t)
        scores = jnp.where(allowed_pairs(start_row, at, step), scores, -1e30)
        probs = jnp.exp(scores - total)
        grad_probs = dot(values[rows, :], grad_t)
        grad_scores = (probs * (grad_probs - inner)).astype(LOW)
        grad_values[rows, :] += dot(probs.astype(LOW), grad)
        grad_keys[rows, :] += dot(grad_scores, query)
        return acc + dot(keys_t[at], grad_scores)

    acc = lax.fori_loop(
        *key_blocks(first_ref, s, step), one, jnp.zeros((HD, QUERIES), F32)
    )
    out_ref[s, here, 0:HD] = (acc * HD ** (-0.5)).T.astype(out_ref.dtype)

    @pl.when(step == pl.num_programs(1) - 1)
    def _():
        out_ref[s, 0:group, HD : 2 * HD] = grad_keys[...].astype(out_ref.dtype)
        out_ref[s, group:, :] = jnp.zeros((out_ref.shape[1] - group, 2 * HD), out_ref.dtype)

        @pl.when(s == 0)
        def _():
            out_ref[2, 0:group, 0:HD] = grad_values[...].astype(out_ref.dtype)

        @pl.when(s == 1)
        def _():
            out_ref[2, 0:group, HD : 2 * HD] = grad_values[...].astype(out_ref.dtype)
            out_ref[2, group:, :] = jnp.zeros((out_ref.shape[1] - group, 2 * HD), out_ref.dtype)


def attend_back(mixed, grad, wide, total, starts, halo):
    group = mixed.shape[1]
    steps = group // QUERIES
    row = pl.BlockSpec((1, 1, QUERIES), lambda s, i, first: (s, 0, i))
    return pl.pallas_call(
        attend_back_kernel,
        grid_spec=pltpu.PrefetchScalarGridSpec(
            num_scalar_prefetch=1,
            grid=(2, steps),
            in_specs=[
                row,
                pl.BlockSpec((1, group, 2 * HD), lambda s, i, first: (s, 0, 0)),
                pl.BlockSpec((1, group, 2 * HD), lambda s, i, first: (2, 0, 0)),
                pl.BlockSpec((1, QUERIES, 2 * HD), lambda s, i, first: (0, i, 0)),
                pl.BlockSpec((1, HD, QUERIES), lambda s, i, first: (s, 0, i)),
                row,
            ],
            out_specs=pl.BlockSpec((3, group + halo, 2 * HD), lambda s, i, first: (0, 0, 0)),
            scratch_shapes=[
                pltpu.VMEM((group // KEYS, HD, KEYS), LOW),
                pltpu.VMEM((group, HD), LOW),
                pltpu.VMEM((group, HD), F32),
                pltpu.VMEM((group, HD), F32),
            ],
        ),
        out_shape=jax.ShapeDtypeStruct((3, group + halo, 2 * HD), LOW),
        compiler_params=pltpu.CompilerParams(vmem_limit_bytes=32 * 1024 * 1024),
        cost_estimate=pl.CostEstimate(
            flops=2**35, bytes_accessed=group * 2048, transcendentals=group * group // 4
        ),
        name="attend_back",
    )(starts[:, ::QUERIES] // KEYS, starts[:, None, :], mixed, mixed, grad, wide, total)


def plane_partners():
    me = lax.axis_index("dp")
    return {"dp": me + 1 - 2 * lax.rem(me, 2)}, {"dp": me + 2 - 4 * (me // 2)}


def dot_nt(left, right):
    return lax.dot_general(left, right, (((1,), (1,)), ((), ())), preferred_element_type=F32)


def mesh_place():
    me = lax.axis_index("mp")
    return me // 2, lax.rem(me, 2)


def wire(source, target, send, recv, partner):
    return pltpu.make_async_remote_copy(
        src_ref=source,
        dst_ref=target,
        send_sem=send,
        recv_sem=recv,
        device_id=partner,
        device_id_type=MESH,
    )


def line_partner(z, step):
    _, core = mesh_place()
    return {"mp": 2 * (z + step) + core}


def other_core():
    z, core = mesh_place()
    return {"mp": 2 * z + 1 - core}


def greet(partners):
    barrier = pltpu.get_barrier_semaphore()
    for partner in partners:
        pl.semaphore_signal(barrier, inc=1, device_id=partner, device_id_type=MESH)
    pl.semaphore_wait(barrier, len(partners))


def greet_line(with_plane):
    z, _ = mesh_place()
    count = lax.axis_size("mp") // 2
    barrier = pltpu.get_barrier_semaphore()
    partners = [other_core()]
    if with_plane:
        partners += list(plane_partners())
    for partner in partners:
        pl.semaphore_signal(barrier, inc=1, device_id=partner, device_id_type=MESH)
    for turn in (1, -1):

        @pl.when((z + turn >= 0) & (z + turn < count))
        def _(turn=turn):
            pl.semaphore_signal(barrier, inc=1, device_id=line_partner(z, turn), device_id_type=MESH)

    near = jnp.where(z > 0, 1, 0) + jnp.where(z < count - 1, 1, 0)
    pl.semaphore_wait(barrier, near + len(partners))


class LineGather:
    def __init__(self, place, send, recv, swap_send, swap_recv):
        self.z, self.core = mesh_place()
        self.count = lax.axis_size("mp") // 2
        self.place, self.send, self.recv = place, send, recv
        self.swap_send, self.swap_recv = swap_send, swap_recv

    def copies(self, step):
        z, count = self.z, self.count
        out = []
        for way, turn in enumerate((1, -1)):
            leaves = z - turn * (step - 1)
            lands = z - turn * step
            far = z + turn
            sends = (leaves >= 0) & (leaves < count) & (far >= 0) & (far < count)
            receives = (lands >= 0) & (lands < count)
            at = jnp.clip(leaves, 0, count - 1)
            to = jnp.clip(lands, 0, count - 1)
            sems = (self.send.at[way, step - 1], self.recv.at[way, step - 1], line_partner(z, turn))
            leaving = wire(self.place(at, self.core), self.place(at, self.core), *sems)
            landing = wire(self.place(to, self.core), self.place(to, self.core), *sems)
            out.append((sends, leaving, receives, landing, to))
        return out

    def start(self, step):
        for sends, leaving, _, _, _ in self.copies(step):
            pl.when(sends)(leaving.start)

    def swap(self, at, number):
        sems = (self.swap_send.at[number], self.swap_recv.at[number], other_core())
        leaving = wire(self.place(at, self.core), self.place(at, self.core), *sems)
        landing = wire(self.place(at, 1 - self.core), self.place(at, 1 - self.core), *sems)
        return leaving, landing

    def swap_own(self):
        self.swap(self.z, 0)[0].start()

    def arrive(self, step):
        for way, (_, _, receives, landing, at) in enumerate(self.copies(step)):

            @pl.when(receives)
            def _(landing=landing, at=at, way=way):
                landing.wait_recv()
                self.swap(at, 1 + 2 * (step - 1) + way)[0].start()

    def swapped(self, at, number):
        leaving, landing = self.swap(at, number)
        leaving.wait_send()
        landing.wait_recv()

    def finish(self, steps, own):
        if own:
            self.swapped(self.z, 0)
        for step in steps:
            for way, (sends, leaving, receives, _, at) in enumerate(self.copies(step)):
                pl.when(sends)(leaving.wait_send)
                pl.when(receives)(
                    lambda at=at, way=way, step=step: self.swapped(at, 1 + 2 * (step - 1) + way)
                )


def line_semaphores(count):
    return [
        pltpu.SemaphoreType.DMA((2, count)),
        pltpu.SemaphoreType.DMA((2, count)),
        pltpu.SemaphoreType.DMA((2 * count,)),
        pltpu.SemaphoreType.DMA((2 * count,)),
    ]


def early_steps(count):
    return range(1, count // 2 + 1)


HALO = 16


def carry_copies(carried, targets, send, recv):
    partners = plane_partners()
    return [
        wire(ref, target, send.at[at], recv.at[at], partners[way])
        for at, ((way, ref), target) in enumerate(zip(carried, targets))
    ]


def greet_members(ways):
    mp = lax.axis_size("mp")
    me = lax.axis_index("mp")
    barrier = pltpu.get_barrier_semaphore()
    for step in range(1, mp):
        pl.semaphore_signal(
            barrier, inc=1, device_id={"mp": lax.rem(me + step, mp)}, device_id_type=MESH
        )
    partners = plane_partners() if ways else ()
    for partner in partners:
        pl.semaphore_signal(barrier, inc=1, device_id=partner, device_id_type=MESH)
    pl.semaphore_wait(barrier, mp - 1 + len(partners))


def member_copies(source, target, send, recv):
    mp = lax.axis_size("mp")
    me = lax.axis_index("mp")
    copies = []
    for step in range(1, mp):
        to = lax.rem(me + step, mp)
        sems = (send.at[step], recv.at[step], {"mp": to})
        copies.append(
            (
                wire(source(to), target(me), *sems),
                wire(source(to), target(lax.rem(me + mp - step, mp)), *sems),
            )
        )
    return copies


def head_lanes(at):
    return pl.ds(pl.multiple_of(at * 128, 128), 128)


def front_kernel(
    inputs_ref, gain_ref, shift_ref, qk_ref, v_ref, out_ref, taps_ref, up_ref, masks_ref, cot_ref,
    all_qk_ref, all_v_ref, all_out_ref, all_taps_ref, normed_ref, up_all_ref, raw_ref, o_ref, cot_x_ref, cot_y_ref,
    inputs, rows, all_qk, all_v, all_out, all_taps, up_all, raw, mixed, landed, local, *sems,
):
    mp = lax.axis_size("mp")
    dp = lax.axis_index("dp")
    me = lax.axis_index("mp")
    z, core = mesh_place()
    count = mp // 2
    rows_here, depth = inputs.shape[1:]
    halo = rows.shape[1] - rows_here
    to_x, to_y = plane_partners()
    share = up_ref.shape[0]
    owned = (qk_ref, v_ref, out_ref)
    whole = (all_qk, all_v, all_out)
    (plane_send_sem, plane_recv_sem, plane_swap_send, plane_swap_recv) = sems[:4]
    taps_send, taps_recv, halo_send, halo_recv, carry_send, carry_recv, head_send, head_recv = sems[4:12]
    line_sems = [sems[12 + 4 * part : 16 + 4 * part] for part in range(4)]

    def up_place(at, at_core):
        start = pl.multiple_of((2 * at + at_core) * share, 16)
        return up_all.at[pl.ds(start, share), :]

    def taps_place(at):
        return all_taps.at[:, :, head_lanes(at)]

    loads = [
        pltpu.make_async_copy(inputs_ref, inputs, local.at[0]),
        pltpu.make_async_copy(taps_ref, taps_place(me), local.at[1]),
        pltpu.make_async_copy(up_ref, up_place(z, core), local.at[2]),
    ] + [
        pltpu.make_async_copy(
            owned[part].at[dp], whole[part].at[z, core, dp], local.at[3 + part]
        )
        for part in range(3)
    ]
    for copy in loads:
        copy.start()
    greet_members((0, 1))
    for copy in loads[1:]:
        copy.wait()

    lines = [
        LineGather(lambda at, at_core, part=part: whole[part].at[at, at_core, dp], *line_sems[part])
        for part in range(3)
    ]
    up_line = LineGather(up_place, *line_sems[3])
    for line in lines:
        line.start(1)
    tap_copies = member_copies(lambda to: taps_ref, taps_place, taps_send, taps_recv)
    for copy, _ in tap_copies:
        copy.start()
    for line in lines:
        line.swap_own()

    loads[0].wait()
    tall = 16

    def norm(s):
        def some(at, carry):
            here = pl.ds(pl.multiple_of(at * tall, tall), tall)
            there = pl.ds(pl.multiple_of(halo + at * tall, tall), tall)
            values = inputs[s, here, :].astype(F32)
            centered = values - jnp.mean(values, axis=1, keepdims=True)
            variance = jnp.mean(centered * centered, axis=1, keepdims=True)
            rows[s, there, :] = (
                centered * lax.rsqrt(variance + 1e-05) * gain_ref[...] + shift_ref[...]
            ).astype(LOW)
            return carry

        lax.fori_loop(0, rows_here // tall, some, 0)

    norm(0)
    for step in range(1, count):
        for line in lines:
            line.arrive(step)
        if step + 1 < count:
            for line in lines:
                line.start(step + 1)

    half = depth // 2
    lanes = (pl.ds(0, half), pl.ds(half, half))
    dp_x = dp + 1 - 2 * lax.rem(dp, 2)
    dp_y = dp + 2 - 4 * (dp // 2)
    dp_xy = dp_x + 2 - 4 * (dp_x // 2)
    legs = ((0, to_x), (1, to_y), (0, to_y), (1, to_x), (0, to_y), (1, to_x))

    def plane(number, quarter):
        side, partner = legs[number]
        out = []
        for part in range(3):
            block = whole[part].at[:, core, quarter, :, lanes[side]]
            out.append(
                wire(
                    block, block, plane_send_sem.at[part, number], plane_recv_sem.at[part, number], partner
                )
            )
        return out

    leaving = [plane(number, quarter) for number, quarter in enumerate((dp, dp, dp, dp, dp_x, dp_y))]
    landing = [
        plane(number, quarter) for number, quarter in enumerate((dp_x, dp_y, dp_y, dp_x, dp_xy, dp_xy))
    ]

    def pass_on(number, at_core):
        quarter = (dp_x, dp_y, dp_xy)[number]
        out = []
        for part in range(3):
            block = whole[part].at[:, at_core, quarter]
            out.append(
                wire(
                    block, block, plane_swap_send.at[part, number], plane_swap_recv.at[part, number],
                    other_core(),
                )
            )
        return out

    def each(copies, what):
        for copy in copies:
            getattr(copy, what)()

    for number in range(4):
        each(leaving[number], "start")
    early = early_steps(count)
    up_line.start(1)
    up_line.swap_own()
    norm(1)
    own_rows = rows.at[:, pl.ds(halo, rows_here), :]
    save = pltpu.make_async_copy(own_rows, normed_ref, local.at[0])
    save.start()
    halo_copy = wire(
        rows.at[:, pl.ds(rows_here, halo), :], rows.at[:, pl.ds(0, halo), :], halo_send, halo_recv,
        {"mp": lax.rem(me + 1, mp)},
    )
    halo_copy.start()
    each(landing[0], "wait_recv")
    each(leaving[4], "start")
    each(landing[1], "wait_recv")
    each(leaving[5], "start")
    each(landing[3], "wait_recv")
    each(pass_on(0, core), "start")
    each(landing[2], "wait_recv")
    each(pass_on(1, core), "start")
    up_line.arrive(1)
    up_line.start(2)
    each(landing[4], "wait_recv")
    each(landing[5], "wait_recv")
    each(pass_on(2, core), "start")
    for step in early[1:-1]:
        up_line.arrive(step)
        up_line.start(step + 1)
    carries = [
        wire(cot_ref.at[:, :, lanes[0]], cot_x_ref, carry_send.at[0], carry_recv.at[0], to_x),
        wire(cot_ref.at[:, :, lanes[1]], cot_y_ref, carry_send.at[1], carry_recv.at[1], to_y),
    ]
    for copy in carries:
        copy.start()
    for line in lines:
        line.finish(range(1, count), True)
    for number in range(3):
        each(pass_on(number, 1 - core), "wait_recv")
    for _, landed_taps in tap_copies:
        landed_taps.wait_recv()
    halo_copy.wait_recv()
    saves = [
        pltpu.make_async_copy(here, there, local.at[2 + at])
        for at, (here, there) in enumerate(
            ((all_qk, all_qk_ref), (all_v, all_v_ref), (all_out, all_out_ref), (all_taps, all_taps_ref))
        )
    ]
    for copy in saves:
        copy.start()

    def chip(at, carry):
        weights = all_qk[at].reshape(4 * HD, depth)
        columns = pl.ds(pl.multiple_of(at * 4 * HD, 4 * HD), 4 * HD)
        for s in range(2):
            raw[s, :, columns] = dot_nt(rows[s], weights)
        return carry

    lax.fori_loop(0, count, chip, 0)
    lane = lax.broadcasted_iota(jnp.int32, (rows.shape[1], 128), 1)

    def two_heads(at, carry):
        weights = all_v[at].reshape(2 * HD, depth)
        zero, one = dot_nt(rows[0], weights), dot_nt(rows[1], weights)
        raw[2, :, head_lanes(2 * at)] = jnp.where(lane < HD, zero, pltpu.roll(one, HD, 1))
        raw[2, :, head_lanes(2 * at + 1)] = jnp.where(lane < HD, pltpu.roll(zero, HD, 1), one)
        return carry

    lax.fori_loop(0, count, two_heads, 0)
    save_raw = pltpu.make_async_copy(raw, raw_ref, local.at[6])
    save_raw.start()
    for plane_at in range(3):
        tap = all_taps.at[plane_at]

        def conv(at, carry, plane_at=plane_at, tap=tap):
            lanes_at = head_lanes(at)
            values = raw[plane_at, :, lanes_at]
            one = pltpu.roll(values, 1, 0)[halo:]
            two = pltpu.roll(values, 2, 0)[halo:]
            mixed[plane_at, :, lanes_at] = (
                tap[0:1, lanes_at] * values[halo:]
                + jnp.where(masks_ref[plane_at, 0] > 0.5, tap[1:2, lanes_at] * one, 0.0)
                + jnp.where(masks_ref[plane_at, 1] > 0.5, tap[2:3, lanes_at] * two, 0.0)
            ).astype(LOW)
            return carry

        lax.fori_loop(0, mp, conv, 0)

    def source(at):
        return mixed.at[:, :, head_lanes(at)]

    def target(at):
        return landed.at[:, at]

    own = pltpu.make_async_copy(source(me), target(me), local.at[7])
    own.start()
    copies = member_copies(source, target, head_send, head_recv)
    for copy, _ in copies:
        copy.start()
    up_line.arrive(early[-1])
    up_line.finish(early, True)
    save_up = pltpu.make_async_copy(up_all, up_all_ref, local.at[8])
    save_up.start()
    own.wait()
    for _, copy in copies:
        copy.wait_recv()
    save_heads = pltpu.make_async_copy(landed, o_ref, local.at[9])
    save_heads.start()
    for number in range(6):
        each(leaving[number], "wait_send")
    for number in range(3):
        each(pass_on(number, core), "wait_send")
    for copy, _ in tap_copies + copies:
        copy.wait_send()
    halo_copy.wait_send()
    for copy in carries:
        copy.wait()
    save.wait()
    for copy in saves:
        copy.wait()
    save_raw.wait()
    save_up.wait()
    save_heads.wait()


def front(inputs, gain, shift, qk, v, out, taps, up, masks, cot):
    mp = lax.axis_size("mp")
    count = mp // 2
    rows_here, depth = inputs.shape[1:]
    tall = rows_here + HALO
    anywhere = pl.BlockSpec(memory_space=pl.ANY)
    vmem = pl.BlockSpec(memory_space=pltpu.VMEM)
    dma = pltpu.SemaphoreType.DMA
    whole = [((count, 2) + part.shape, LOW) for part in (qk, v, out)]
    whole.append(((3, 8, mp * 128), F32))
    kept = [
        ((2, rows_here, depth), LOW),
        ((mp * up.shape[0], depth), LOW),
        ((3, tall, mp * 128), F32),
        ((3, mp, rows_here, 128), LOW),
        ((2, rows_here, depth // 2), LOW),
        ((2, rows_here, depth // 2), LOW),
    ]
    return pl.pallas_call(
        front_kernel,
        in_specs=[anywhere, vmem, vmem] + [anywhere] * 5 + [vmem, anywhere],
        out_specs=[anywhere] * 10,
        out_shape=[jax.ShapeDtypeStruct(*shape) for shape in whole + kept],
        scratch_shapes=[
            pltpu.VMEM(inputs.shape, LOW),
            pltpu.VMEM((2, tall, depth), LOW),
        ]
        + [pltpu.VMEM(*shape) for shape in whole]
        + [
            pltpu.VMEM(*kept[1]),
            pltpu.VMEM(*kept[2]),
            pltpu.VMEM((3, rows_here, mp * 128), LOW),
            pltpu.VMEM(*kept[3]),
            dma((10,)),
            dma((3, 6)),
            dma((3, 6)),
            dma((3, 3)),
            dma((3, 3)),
            dma((mp,)),
            dma((mp,)),
            dma,
            dma,
            dma((2,)),
            dma((2,)),
            dma((mp,)),
            dma((mp,)),
        ]
        + line_semaphores(count) * 4,
        compiler_params=pltpu.CompilerParams(
            collective_id=3, has_side_effects=True, vmem_limit_bytes=VMEM_LIMIT
        ),
        cost_estimate=pl.CostEstimate(flops=2**36, bytes_accessed=2**26, transcendentals=0),
        name="front",
    )(inputs, gain.reshape(1, depth), shift.reshape(1, depth), qk, v, out, taps, up, masks, cot)


def left_t_right(left, right):
    return lax.dot_general(left, right, (((0,), (0,)), ((), ())), preferred_element_type=F32)


def stream_out(steps, compute, buffer, ref, sem):
    def save(at, slot):
        return pltpu.make_async_copy(buffer.at[slot], ref.at[at], sem.at[slot])

    def one(at, carry):
        slot = lax.rem(at, 2)

        @pl.when(at >= 2)
        def _():
            save(at - 2, slot).wait()

        buffer[slot] = compute(at)
        save(at, slot).start()
        return carry

    lax.fori_loop(0, steps, one, 0)
    save(steps - 2, (steps - 2) % 2).wait()
    save(steps - 1, (steps - 1) % 2).wait()


def project_back_kernel(
    ways, x_ref, raw_ref, taps_ref, masks_ref, normed_ref, attended_ref, branch_ref, *refs
):
    carried, refs = list(zip(ways, refs[: len(ways)])), refs[len(ways) :]
    grad_ref, sums_ref, qk_part_ref, v_part_ref, out_part_ref = refs[:5]
    targets, refs = refs[5 : 5 + len(ways)], refs[5 + len(ways) :]
    landed, raw, wide, narrow, part_sem, local, send, recv, carry_send, carry_recv = refs
    me = lax.axis_index("mp")
    tall = landed.shape[1]
    rows_here = grad_ref.shape[1]
    halo = tall - rows_here
    heads = landed.shape[2] // 128

    def source(at):
        return x_ref.at[:, pl.ds(pl.multiple_of(at * rows_here, 16), tall), :]

    def target(at):
        return landed.at[:, :, head_lanes(at)]

    own = pltpu.make_async_copy(source(me), target(me), local.at[0])
    own.start()
    load = pltpu.make_async_copy(raw_ref, raw, local.at[1])
    load.start()
    greet_members(ways)
    copies = member_copies(source, target, send, recv)
    for leaving, _ in copies:
        leaving.start()
    carries = carry_copies(carried, targets, carry_send, carry_recv)
    for copy in carries:
        copy.start()

    def out_part(at):
        lanes = head_lanes(at)
        return (
            left_t_right(attended_ref[0, :, lanes], branch_ref[0])
            + left_t_right(attended_ref[1, :, lanes], branch_ref[1])
        ).astype(LOW)

    stream_out(heads // 2, out_part, narrow, out_part_ref, part_sem)
    own.wait()
    load.wait()
    for _, landing in copies:
        landing.wait_recv()
    for plane in range(3):
        tap = taps_ref.at[plane]

        def back(at, carry, plane=plane, tap=tap):
            lanes = head_lanes(at)
            grad = landed[plane, :, lanes].astype(F32)
            one = pltpu.roll(grad, tall - 1, 0)[:rows_here]
            two = pltpu.roll(grad, tall - 2, 0)[:rows_here]
            here = grad[:rows_here]
            grad_ref[plane, :, lanes] = (
                tap[0:1, lanes] * here
                + jnp.where(masks_ref[plane, 2] > 0.5, tap[1:2, lanes] * one, 0.0)
                + jnp.where(masks_ref[plane, 3] > 0.5, tap[2:3, lanes] * two, 0.0)
            ).astype(LOW)
            values = raw[plane, :, lanes]
            before = pltpu.roll(values, 1, 0)[halo:]
            before_two = pltpu.roll(values, 2, 0)[halo:]
            products = (
                here * values[halo:],
                jnp.where(masks_ref[plane, 0] > 0.5, here * before, 0.0),
                jnp.where(masks_ref[plane, 1] > 0.5, here * before_two, 0.0),
            )
            for row, product in enumerate(products):
                sums_ref[plane, row : row + 1, lanes] = jnp.sum(product, axis=0, keepdims=True)
            sums_ref[plane, 3:8, lanes] = jnp.zeros((5, 128), F32)
            return carry

        lax.fori_loop(0, heads, back, 0)

    def pair(at):
        return pl.ds(pl.multiple_of(at * 256, 256), 256)

    def qk_part(at):
        return (
            left_t_right(grad_ref[0, :, pair(at)], normed_ref[0])
            + left_t_right(grad_ref[1, :, pair(at)], normed_ref[1])
        ).astype(LOW)

    def v_part(at):
        side = grad_ref[2, :, pair(at)]
        zero, one = left_t_right(side, normed_ref[0]), left_t_right(side, normed_ref[1])
        return jnp.concatenate(
            [zero[:HD] + one[HD : 2 * HD], zero[2 * HD : 3 * HD] + one[3 * HD :]], axis=0
        ).astype(LOW)

    stream_out(heads // 2, qk_part, wide, qk_part_ref, part_sem)
    stream_out(heads // 2, v_part, narrow, v_part_ref, part_sem)
    for leaving, _ in copies:
        leaving.wait_send()
    for copy in carries:
        copy.wait()


def project_back(x, raw, taps, masks, normed, attended, branch, carried):
    mp = lax.axis_size("mp")
    rows_here, depth = normed.shape[1:]
    tall = raw.shape[1]
    anywhere = pl.BlockSpec(memory_space=pl.ANY)
    dma = pltpu.SemaphoreType.DMA
    vmem = pl.BlockSpec(memory_space=pltpu.VMEM)
    return pl.pallas_call(
        partial(project_back_kernel, tuple(way for way, _ in carried)),
        in_specs=[vmem, anywhere] + [vmem] * 5 + [anywhere] * len(carried),
        out_specs=[vmem] * 2 + [anywhere] * (3 + len(carried)),
        out_shape=[
            jax.ShapeDtypeStruct((3, rows_here, mp * 128), LOW),
            jax.ShapeDtypeStruct((3, 8, mp * 128), F32),
            jax.ShapeDtypeStruct((mp // 2, 4 * HD, depth), LOW),
            jax.ShapeDtypeStruct((mp // 2, 2 * HD, depth), LOW),
            jax.ShapeDtypeStruct((mp // 2, 2 * HD, depth), LOW),
        ]
        + [jax.ShapeDtypeStruct(block.shape, block.dtype) for _, block in carried],
        scratch_shapes=[
            pltpu.VMEM((3, tall, mp * 128), LOW),
            pltpu.VMEM((3, tall, mp * 128), F32),
            pltpu.VMEM((2, 4 * HD, depth), LOW),
            pltpu.VMEM((2, 2 * HD, depth), LOW),
            dma((2,)),
            dma((2,)),
            dma((mp,)),
            dma((mp,)),
            dma((len(carried),)),
            dma((len(carried),)),
        ],
        compiler_params=pltpu.CompilerParams(
            collective_id=7, has_side_effects=True, vmem_limit_bytes=VMEM_LIMIT
        ),
        cost_estimate=pl.CostEstimate(flops=2**35, bytes_accessed=2**24, transcendentals=0),
        name="project_back",
    )(x, raw, taps, masks, normed, attended, branch, *(block for _, block in carried))


def attended_kernel(x_ref, o_ref, landed, local, send, recv):
    me = lax.axis_index("mp")
    tall = o_ref.shape[1]

    def source(at):
        return x_ref.at[:, pl.ds(pl.multiple_of(at * tall, 16), tall), :]

    def target(at):
        return landed.at[:, :, head_lanes(at)]

    own = pltpu.make_async_copy(source(me), target(me), local.at[0])
    own.start()
    greet_members(())
    copies = member_copies(source, target, send, recv)
    for leaving, _ in copies:
        leaving.start()
    own.wait()
    for _, landing in copies:
        landing.wait_recv()
    save = pltpu.make_async_copy(landed, o_ref, local.at[1])
    save.start()
    for leaving, _ in copies:
        leaving.wait_send()
    save.wait()


def attended_back(x, rows_here):
    mp = lax.axis_size("mp")
    shape = (x.shape[0], rows_here, mp * 128)
    dma = pltpu.SemaphoreType.DMA
    return pl.pallas_call(
        attended_kernel,
        in_specs=[pl.BlockSpec(memory_space=pltpu.VMEM)],
        out_specs=pl.BlockSpec(memory_space=pl.ANY),
        out_shape=jax.ShapeDtypeStruct(shape, x.dtype),
        scratch_shapes=[pltpu.VMEM(shape, x.dtype), dma((2,)), dma((mp,)), dma((mp,))],
        compiler_params=pltpu.CompilerParams(
            collective_id=5, has_side_effects=True, vmem_limit_bytes=48 * 2**20
        ),
        cost_estimate=pl.CostEstimate(flops=2**34, bytes_accessed=2**24, transcendentals=0),
        name="attended_back",
    )(x)


def line_blocks(place, sources, local, send, recv):
    z, core = mesh_place()
    count = lax.axis_size("mp") // 2
    out = []
    for number, (step, way, ref) in enumerate(sources):
        at = z - way * step
        there = (at >= 0) & (at < count)
        at = jnp.clip(at, 0, count - 1)
        sems = (send.at[number], recv.at[number], other_core())
        out.append(
            (
                there,
                pltpu.make_async_copy(ref, place(at, core), local.at[number]),
                wire(ref, place(at, core), *sems),
                wire(ref, place(at, 1 - core), *sems),
            )
        )
    return out


def feed_in_kernel(
    late, second_ref, up_ref, down_ref, cot_0, cot_1, cot_2, cot_3, cot_4, cot_5, cot_6, *refs
):
    late_sources = [(step, way, ref) for (step, way), ref in zip(late, refs)]
    (
        all_ref, relu_ref, hidden_ref, down_all_ref, up_all_ref, down_part_ref,
        rows, up, relu, hidden, down, cot, tiles, sums, before, local, outs, send, recv, cot_sem, tile_sem, sum_sem,
        before_sem, late_local, late_send, late_recv, *line_sems,
    ) = refs[len(late) :]
    count = lax.axis_size("mp") // 2
    depth = rows.shape[3]
    units = up.shape[0]
    share = down_ref.shape[0]
    z, core = mesh_place()
    lanes = (pl.ds(0, depth // 2), pl.ds(depth // 2, depth // 2))
    to_x, to_y = plane_partners()
    pieces = (cot_0, cot_1, cot_2, cot_3, cot_4, cot_5, cot_6)

    def line_place(ref):
        return lambda at, at_core: ref.at[
            pl.ds(pl.multiple_of((2 * at + at_core) * share, 16), share), :
        ]

    own = [pltpu.make_async_copy(second_ref.at[s], rows.at[s, 0], local.at[s]) for s in range(2)]
    own.append(pltpu.make_async_copy(up_ref, up, local.at[2]))
    own.append(pltpu.make_async_copy(down_ref, line_place(down)(z, core), local.at[3]))
    for copy in own:
        copy.start()
    for copy in own:
        copy.wait()
    greet_line(True)
    late_blocks = line_blocks(line_place(up), late_sources, late_local, late_send, late_recv)
    down_line = LineGather(line_place(down), *line_sems)

    def remote(s, source, target, half, partner, number):
        return wire(
            rows.at[s, source, :, lanes[half]], rows.at[s, target, :, lanes[half]],
            send.at[s, number], recv.at[s, number], partner,
        )

    copies = [
        [
            remote(s, 0, 1, 0, to_x, 0),
            remote(s, 0, 2, 1, to_y, 1),
            remote(s, 0, 2, 0, to_y, 2),
            remote(s, 0, 1, 1, to_x, 3),
            remote(s, 1, 3, 0, to_y, 4),
            remote(s, 2, 3, 1, to_x, 5),
        ]
        for s in range(2)
    ]
    pending = [None, None]
    done = [0]

    def settle(slot):
        if pending[slot] is not None:
            for copy in pending[slot]:
                copy.wait()
        pending[slot] = None

    def tile(s, m):
        slot = done[0] % 2
        done[0] += 1
        settle(slot)

        def one(at, carry):
            columns = pl.ds(pl.multiple_of(at * CHUNK, CHUNK), CHUNK)
            kept = jnp.maximum(dot_nt(rows[s, m], up[columns, :]), 0.0)
            relu[slot, :, columns] = kept
            hidden[slot, :, columns] = (kept * kept).astype(LOW)
            return carry

        lax.fori_loop(0, units // CHUNK, one, 0)
        pending[slot] = [
            pltpu.make_async_copy(relu.at[slot], relu_ref.at[s, m], outs.at[slot, 0]),
            pltpu.make_async_copy(hidden.at[slot], hidden_ref.at[s, m], outs.at[slot, 1]),
        ]
        for copy in pending[slot]:
            copy.start()

    for number in range(4):
        copies[0][number].start()
    for there, here, leaving, _ in late_blocks:

        @pl.when(there)
        def _(here=here, leaving=leaving):
            here.start()
            leaving.start()

    down_line.start(1)
    down_line.swap_own()

    def cot_loads(s):
        copies = []
        for m in range(4):
            copies += piece_copies(pieces, s, m, cot.at[m], cot_sem.at[m])
        return copies

    for copy in cot_loads(0):
        copy.start()
    for there, here, leaving, landing in late_blocks:

        @pl.when(there)
        def _(here=here, leaving=leaving, landing=landing):
            here.wait()
            leaving.wait_send()
            landing.wait_recv()

    whole_up = pltpu.make_async_copy(up, up_all_ref, local.at[2])
    whole_up.start()
    tile(0, 0)
    copies[0][0].wait_recv()
    copies[0][4].start()
    copies[0][1].wait_recv()
    copies[0][5].start()
    copies[1][0].start()
    copies[1][1].start()
    tile(1, 0)
    down_line.arrive(1)
    down_line.start(2)
    copies[0][3].wait_recv()
    tile(0, 1)
    copies[0][2].wait_recv()
    copies[1][2].start()
    copies[1][3].start()
    tile(0, 2)
    copies[1][0].wait_recv()
    copies[1][4].start()
    copies[1][1].wait_recv()
    copies[1][5].start()
    copies[0][4].wait_recv()
    copies[0][5].wait_recv()
    tile(0, 3)
    for step in range(3, count):
        down_line.arrive(step - 1)
        down_line.start(step)
    settle(0)
    settle(1)
    for copy in cot_loads(0):
        copy.wait()
    gradient_tiles(hidden_ref.at[0], cot, tiles, sums, down_part_ref, tile_sem, sum_sem)
    for copy in cot_loads(1):
        copy.start()
    copies[1][3].wait_recv()
    tile(1, 1)
    copies[1][2].wait_recv()
    tile(1, 2)
    copies[1][4].wait_recv()
    copies[1][5].wait_recv()
    gathered = pltpu.make_async_copy(rows, all_ref, local.at[0])
    gathered.start()
    tile(1, 3)
    down_line.arrive(count - 1)
    down_line.finish(range(1, count), True)
    whole_down = pltpu.make_async_copy(down, down_all_ref, local.at[1])
    whole_down.start()
    settle(0)
    settle(1)
    for copy in cot_loads(1):
        copy.wait()
    gradient_tiles(
        hidden_ref.at[1], cot, tiles, sums, down_part_ref, tile_sem, sum_sem,
        (down_part_ref, before, before_sem),
    )
    for s in range(2):
        for copy in copies[s]:
            copy.wait_send()
    gathered.wait()
    whole_up.wait()
    whole_down.wait()


def gradient_tiles(
    left_ref, right, tiles, sums, out_ref, tile_sem, sum_sem, before=None, span=None
):
    wide = tiles.shape[-1]
    first, steps = span if span is not None else (0, left_ref.shape[-1] // wide)
    lead = (slice(None),) * (len(left_ref.shape) - 1)
    tall = math.prod(tiles.shape[1:-1])

    def load(at, slot):
        columns = pl.ds(pl.multiple_of(at * wide, wide), wide)
        return pltpu.make_async_copy(
            left_ref.at[lead + (columns,)], tiles.at[slot], tile_sem.at[slot]
        )

    def rows_of(at):
        return pl.ds(pl.multiple_of(at * wide, wide), wide)

    def save(at, slot):
        return pltpu.make_async_copy(sums.at[slot], out_ref.at[rows_of(at), :], sum_sem.at[slot])

    def load_before(at, slot):
        before_ref, buffer, sem = before
        return pltpu.make_async_copy(before_ref.at[rows_of(at), :], buffer.at[slot], sem.at[slot])

    load(first, first % 2).start()
    if before is not None:
        load_before(first, first % 2).start()

    def one(at, carry):
        slot = lax.rem(at, 2)
        load(at, slot).wait()
        if before is not None:
            load_before(at, slot).wait()

        @pl.when(at + 1 < steps)
        def _():
            load(at + 1, 1 - slot).start()
            if before is not None:
                load_before(at + 1, 1 - slot).start()

        @pl.when(at >= first + 2)
        def _():
            save(at - 2, slot).wait()

        result = lax.dot_general(
            tiles[slot].reshape(tall, wide),
            right[...].reshape(tall, right.shape[-1]),
            (((0,), (0,)), ((), ())),
            preferred_element_type=F32,
        )
        if before is not None:
            result = result + before[1][slot].astype(F32)
        sums[slot] = result.astype(LOW)
        save(at, slot).start()
        return carry

    lax.fori_loop(first, steps, one, 0)
    save(steps - 2, (steps - 2) % 2).wait()
    save(steps - 1, (steps - 1) % 2).wait()


def feed_in(second, up_early, down, cot_pieces, up_late):
    rows_here, depth = second.shape[1:]
    units = up_early.shape[0]
    count = lax.axis_size("mp") // 2
    anywhere = pl.BlockSpec(memory_space=pl.ANY)
    dma = pltpu.SemaphoreType.DMA
    return pl.pallas_call(
        partial(feed_in_kernel, tuple(up_late)),
        in_specs=[anywhere] * (10 + len(up_late)),
        out_specs=[anywhere] * 6,
        out_shape=[
            jax.ShapeDtypeStruct((2, 4, rows_here, depth), LOW),
            jax.ShapeDtypeStruct((2, 4, rows_here, units), F32),
            jax.ShapeDtypeStruct((2, 4, rows_here, units), LOW),
            jax.ShapeDtypeStruct((units, depth), LOW),
            jax.ShapeDtypeStruct((units, depth), LOW),
            jax.ShapeDtypeStruct((units, depth), LOW),
        ],
        scratch_shapes=[
            pltpu.VMEM((2, 4, rows_here, depth), LOW),
            pltpu.VMEM((units, depth), LOW),
            pltpu.VMEM((2, rows_here, units), F32),
            pltpu.VMEM((2, rows_here, units), LOW),
            pltpu.VMEM((units, depth), LOW),
            pltpu.VMEM((4, rows_here, depth), LOW),
            pltpu.VMEM((2, 4, rows_here, WIDE), LOW),
            pltpu.VMEM((2, WIDE, depth), LOW),
            pltpu.VMEM((2, WIDE, depth), LOW),
            dma((4,)),
            dma((2, 2)),
            dma((2, 6)),
            dma((2, 6)),
            dma((4, 2)),
            dma((2,)),
            dma((2,)),
            dma((2,)),
        ]
        + [dma((len(up_late),))] * 3
        + line_semaphores(count),
        compiler_params=pltpu.CompilerParams(
            collective_id=1, has_side_effects=True, vmem_limit_bytes=VMEM_LIMIT
        ),
        cost_estimate=pl.CostEstimate(
            flops=2 * 8 * rows_here * depth * units * 3,
            bytes_accessed=60 * 2**20,
            transcendentals=0,
        ),
        name="feed_in",
    )(second, up_early, down, *cot_pieces, *up_late.values())


def piece_copies(pieces, s, m, target, sems):
    half = target.shape[-1] // 2
    if m == 0:
        return [pltpu.make_async_copy(pieces[0].at[s], target, sems.at[0])]
    return [
        pltpu.make_async_copy(
            pieces[2 * m - 1 + side].at[s], target.at[:, pl.ds(side * half, half)], sems.at[side]
        )
        for side in range(2)
    ]


def feed_out_kernel(
    cot_0, cot_1, cot_2, cot_3, cot_4, cot_5, cot_6, relu_ref, second_ref, up_ref, down_ref,
    grad_ref, up_part_ref, back_ref,
    up, shared, cot, relu, grad, part, arrived, tiles, sums, result, local, loads, outs, send, recv,
    tile_sem, sum_sem,
):
    units, depth = up.shape
    down = shared.at[pl.ds(0, units), :]
    second = shared.at[pl.ds(0, 8 * cot.shape[1]), :]
    half = depth // 2
    lanes = (pl.ds(0, half), pl.ds(half, half))
    to_x, to_y = plane_partners()
    weights = [
        pltpu.make_async_copy(down_ref, down, local.at[0]),
        pltpu.make_async_copy(up_ref, up, local.at[1]),
    ]
    order = [(s, m) for s in range(2) for m in (3, 1, 2, 0)]
    pieces = (cot_0, cot_1, cot_2, cot_3, cot_4, cot_5, cot_6)

    def load(at):
        s, m = order[at]
        slot = at % 2
        return piece_copies(pieces, s, m, cot.at[slot], loads.at[slot]) + [
            pltpu.make_async_copy(relu_ref.at[s, m], relu.at[slot], loads.at[slot, 2]),
        ]

    for copy in load(0) + weights:
        copy.start()
    greet([to_x, to_y])
    for copy in weights:
        copy.wait()
    def remote(s, source, number, side, partner):
        return pltpu.make_async_remote_copy(
            src_ref=part.at[s, source, :, lanes[side]],
            dst_ref=arrived.at[s, number],
            send_sem=send.at[s, number],
            recv_sem=recv.at[s, number],
            device_id=partner,
            device_id_type=MESH,
        )

    copies = [
        [
            remote(s, 1, 0, 0, to_x),
            remote(s, 3, 1, 0, to_x),
            remote(s, 2, 2, 1, to_y),
            remote(s, 3, 3, 1, to_y),
            remote(s, 2, 4, 0, to_y),
            remote(s, 1, 5, 1, to_x),
        ]
        for s in range(2)
    ]
    saving = [None, None]
    load_second = pltpu.make_async_copy(second_ref, second, local.at[0])

    def tile(at):
        s, m = order[at]
        slot = at % 2
        for copy in load(at):
            copy.wait()
        if at + 1 < len(order):
            for copy in load(at + 1):
                copy.start()
        if saving[slot] is not None:
            saving[slot].wait()

        def back(step, carry):
            columns = pl.ds(pl.multiple_of(step * CHUNK, CHUNK), CHUNK)
            product = dot_nt(cot[slot], down[columns, :])
            grad[slot, :, columns] = (product * 2.0 * relu[slot, :, columns]).astype(LOW)
            return carry

        lax.fori_loop(0, units // CHUNK, back, 0)
        if at + 1 == len(order):
            load_second.start()
        saving[slot] = pltpu.make_async_copy(grad.at[slot], grad_ref.at[s, m], outs.at[slot])
        saving[slot].start()

        def through(step, carry):
            columns = pl.ds(pl.multiple_of(step * CHUNK, CHUNK), CHUNK)
            part[s, m, :, columns] = dot(grad[slot], up[:, columns]).astype(LOW)
            return carry

        lax.fori_loop(0, depth // CHUNK, through, 0)

    def second_leg(s):
        copies[s][1].wait_recv()
        part[s, 2, :, lanes[0]] = (
            part[s, 2, :, lanes[0]].astype(F32) + arrived[s, 1].astype(F32)
        ).astype(LOW)
        copies[s][4].start()
        copies[s][3].wait_recv()
        part[s, 1, :, lanes[1]] = (
            part[s, 1, :, lanes[1]].astype(F32) + arrived[s, 3].astype(F32)
        ).astype(LOW)
        copies[s][5].start()

    def finish(s):
        for side, near, last in ((0, 0, 4), (1, 2, 5)):
            copies[s][near].wait_recv()
            copies[s][last].wait_recv()
            result[:, lanes[side]] = (
                part[s, 0, :, lanes[side]].astype(F32)
                + arrived[s, near].astype(F32)
                + arrived[s, last].astype(F32)
            )
        done = pltpu.make_async_copy(result, back_ref.at[s], local.at[2])
        done.start()
        return done

    def send_after(at):
        s, m = order[at]
        for number in {3: (1, 3), 1: (0,), 2: (2,), 0: ()}[m]:
            copies[s][number].start()

    for at in range(5):
        tile(at)
        send_after(at)
    second_leg(0)
    for at in range(5, 8):
        tile(at)
        send_after(at)
    done = finish(0)

    for slot in range(2):
        saving[slot].wait()
    load_second.wait()
    halves = units // WIDE // 2

    def some(span):
        gradient_tiles(grad_ref, second, tiles, sums, up_part_ref, tile_sem, sum_sem, span=span)

    some((0, halves))
    second_leg(1)
    some((halves, 2 * halves))
    done.wait()
    finish(1).wait()
    for s in range(2):
        for number in range(6):
            copies[s][number].wait_send()


def feed_out(cot_pieces, relu, second_all, up_all, down_all):
    rows_here, units = relu.shape[2:]
    depth = up_all.shape[1]
    anywhere = pl.BlockSpec(memory_space=pl.ANY)
    dma = pltpu.SemaphoreType.DMA
    return pl.pallas_call(
        feed_out_kernel,
        in_specs=[anywhere] * 11,
        out_specs=[anywhere] * 3,
        out_shape=[
            jax.ShapeDtypeStruct((2, 4, rows_here, units), LOW),
            jax.ShapeDtypeStruct((units, depth), LOW),
            jax.ShapeDtypeStruct((2, rows_here, depth), F32),
        ],
        scratch_shapes=[
            pltpu.VMEM((units, depth), LOW),
            pltpu.VMEM((max(units, 8 * rows_here), depth), LOW),
            pltpu.VMEM((2, rows_here, depth), LOW),
            pltpu.VMEM((2, rows_here, units), F32),
            pltpu.VMEM((2, rows_here, units), LOW),
            pltpu.VMEM((2, 4, rows_here, depth), LOW),
            pltpu.VMEM((2, 6, rows_here, depth // 2), LOW),
            pltpu.VMEM((2, 2, 4, rows_here, WIDE), LOW),
            pltpu.VMEM((2, WIDE, depth), LOW),
            pltpu.VMEM((rows_here, depth), F32),
            dma((3,)),
            dma((2, 3)),
            dma((2,)),
            dma((2, 6)),
            dma((2, 6)),
            dma((2,)),
            dma((2,)),
        ],
        compiler_params=pltpu.CompilerParams(
            collective_id=2, has_side_effects=True, vmem_limit_bytes=VMEM_LIMIT
        ),
        cost_estimate=pl.CostEstimate(
            flops=2 * 8 * rows_here * depth * units * 4,
            bytes_accessed=60 * 2**20,
            transcendentals=0,
        ),
        name="feed_out",
    )(*cot_pieces, relu, second_all.reshape(8 * rows_here, depth), up_all, down_all)


def feed_heads_kernel(
    x_ref, hidden_ref, down_ref,
    o_ref, feed_x0_ref, feed_x1_ref, feed_y0_ref, feed_y1_ref, keep_a_ref, keep_b_ref,
    landed, down, hidden, feed, local, send, recv, loads, outs,
):
    me = lax.axis_index("mp")
    units, depth = down.shape
    half = depth // 2
    lanes = (pl.ds(0, half), pl.ds(half, half))
    feed_x_refs, feed_y_refs = (feed_x0_ref, feed_x1_ref), (feed_y0_ref, feed_y1_ref)

    def source(at):
        return x_ref.at[:, :, head_lanes(at)]

    def target(at):
        return landed.at[:, at]

    weights = pltpu.make_async_copy(down_ref, down, local.at[2])
    weights.start()
    own = pltpu.make_async_copy(source(me), target(me), local.at[0])
    own.start()
    greet_members(())
    copies = member_copies(source, target, send, recv)
    for leaving, _ in copies:
        leaving.start()
    order = [(s, m) for s in range(2) for m in (3, 1, 2, 0)]

    def load(at):
        s, m = order[at]
        return pltpu.make_async_copy(hidden_ref.at[s, m], hidden.at[at % 2], loads.at[at % 2])

    load(0).start()
    weights.wait()
    feeding = [None, None]
    for at, (s, m) in enumerate(order):
        slot = at % 2
        load(at).wait()
        if at + 1 < len(order):
            load(at + 1).start()
        if feeding[slot] is not None:
            for copy in feeding[slot]:
                copy.wait()

        def one(step, carry, slot=slot):
            columns = pl.ds(pl.multiple_of(step * CHUNK, CHUNK), CHUNK)
            feed[slot, :, columns] = dot(hidden[slot], down[:, columns]).astype(LOW)
            return carry

        lax.fori_loop(0, depth // CHUNK, one, 0)
        targets = (
            (keep_a_ref.at[s, 0], feed_x_refs[s].at[0], keep_a_ref.at[s, 1], feed_x_refs[s].at[1])[m],
            (keep_b_ref.at[s, 0], keep_b_ref.at[s, 1], feed_y_refs[s].at[0], feed_y_refs[s].at[1])[m],
        )
        feeding[slot] = [
            pltpu.make_async_copy(feed.at[slot, :, lanes[side]], there, outs.at[slot, side])
            for side, there in enumerate(targets)
        ]
        for copy in feeding[slot]:
            copy.start()
    own.wait()
    for _, landing in copies:
        landing.wait_recv()
    save = pltpu.make_async_copy(landed, o_ref, local.at[1])
    save.start()
    for leaving, _ in copies:
        leaving.wait_send()
    for slot in feeding:
        for copy in slot:
            copy.wait()
    save.wait()


def feed_heads(x, hidden, down_all):
    parts, rows_here, width = x.shape
    mp = lax.axis_size("mp")
    units, depth = down_all.shape
    anywhere = pl.BlockSpec(memory_space=pl.ANY)
    dma = pltpu.SemaphoreType.DMA
    shape = (parts, mp, rows_here, 128)
    out, *terms = pl.pallas_call(
        feed_heads_kernel,
        in_specs=[pl.BlockSpec(memory_space=pltpu.VMEM)] + [anywhere] * 2,
        out_specs=[anywhere] * 7,
        out_shape=[jax.ShapeDtypeStruct(shape, LOW)]
        + [jax.ShapeDtypeStruct((2, rows_here, depth // 2), LOW)] * 4
        + [jax.ShapeDtypeStruct((2, 2, rows_here, depth // 2), LOW)] * 2,
        scratch_shapes=[
            pltpu.VMEM(shape, LOW),
            pltpu.VMEM((units, depth), LOW),
            pltpu.VMEM((2, rows_here, units), LOW),
            pltpu.VMEM((2, rows_here, depth), LOW),
            dma((3,)),
            dma((mp,)),
            dma((mp,)),
            dma((2,)),
            dma((2, 2)),
        ],
        compiler_params=pltpu.CompilerParams(
            collective_id=6, has_side_effects=True, vmem_limit_bytes=48 * 2**20
        ),
        cost_estimate=pl.CostEstimate(flops=2**35, bytes_accessed=2**24, transcendentals=0),
        name="feed_heads",
    )(x, hidden, down_all)
    return [out.reshape(parts, mp * rows_here, 128)] + terms


def finish_kernel(
    ways, qk_ref, v_ref, out_ref, norms_ref, taps_ref, grad_raw_ref, inputs_ref, gain_ref,
    qk_all_ref, v_all_ref, middle_ref, *refs
):
    carried, refs = list(zip(ways, refs[: len(ways)])), refs[len(ways) :]
    joint_ref, norms_sum_ref, taps_sum_ref, input_grad_ref = refs[:4]
    targets, refs = refs[4 : 4 + len(ways)], refs[4 + len(ways) :]
    (
    acc, got, plane_in, line_in, gathered, norms_all, taps_all, norms_dp, taps_dp,
    weights, result, middle, norms, sums, weight_sem,
    local, swap_send, swap_recv, plane_send_sem, plane_recv_sem, line_send_sem, line_recv_sem,
    gather_send, gather_recv, small_send, small_recv, carry_send, carry_recv,
    ) = refs
    mp = lax.axis_size("mp")
    dp = lax.axis_index("dp")
    me = lax.axis_index("mp")
    z, core = mesh_place()
    count = mp // 2
    depth = acc.shape[3]
    half = depth // 2
    lanes = (pl.ds(0, half), pl.ds(half, half))
    to_x, to_y = plane_partners()
    dp_x = dp + 1 - 2 * lax.rem(dp, 2)
    dp_y = dp + 2 - 4 * (dp // 2)
    dp_xy = dp_x + 2 - 4 * (dp_x // 2)
    parts = (qk_ref, v_ref, out_ref)
    spans = (pl.ds(0, HD // 2), pl.ds(HD // 2, HD // 4), pl.ds(3 * HD // 4, HD // 4))
    loads = [
        pltpu.make_async_copy(part.at[:, core], acc.at[:, :, span, :], local.at[at])
        for at, (part, span) in enumerate(zip(parts, spans))
    ]
    for copy in loads:
        copy.start()

    barrier = pltpu.get_barrier_semaphore()
    for step in range(1, mp):
        pl.semaphore_signal(
            barrier, inc=1, device_id={"mp": lax.rem(me + step, mp)}, device_id_type=MESH
        )
    for step in range(1, 4):
        pl.semaphore_signal(
            barrier, inc=1, device_id={"dp": lax.rem(dp + step, 4)}, device_id_type=MESH
        )
    pl.semaphore_wait(barrier, mp + 2)

    swaps = [
        [
            wire(
                part.at[:, 1 - core, quarter], got.at[:, quarter, span, :],
                swap_send.at[at, number], swap_recv.at[at, number], other_core(),
            )
            for at, (part, span) in enumerate(zip(parts, spans))
        ]
        for number, quarter in enumerate((dp_xy, dp_x, dp_y, dp))
    ]
    for group in swaps:
        for copy in group:
            copy.start()

    def small(axis, at, others, source, target, number, first):
        out = []
        for step in range(1, others):
            to = lax.rem(at + step, others)
            frm = lax.rem(at + others - step, others)
            sems = (small_send.at[number, step], small_recv.at[number, step], {axis: to})
            out.append((wire(source(to), target.at[at], *sems), wire(source(to), target.at[frm], *sems)))
        return out

    load_middle = pltpu.make_async_copy(middle_ref, middle, local.at[6])
    load_middle.start()
    own_small = [
        pltpu.make_async_copy(norms, norms_all.at[me], local.at[3]),
        pltpu.make_async_copy(taps_ref.at[me], taps_all.at[me], local.at[4]),
    ]
    over_mp = small("mp", me, mp, lambda to: norms, norms_all, 0, None) + small(
        "mp", me, mp, lambda to: taps_ref.at[to], taps_all, 1, None
    )

    rows_here = inputs_ref.shape[1]
    slots = weights.shape[0]

    def load_weights(at, slot):
        return [
            pltpu.make_async_copy(
                qk_all_ref.at[at], weights.at[slot, pl.ds(0, 4 * HD), :], weight_sem.at[slot, 0]
            )
        ] + [
            pltpu.make_async_copy(
                v_all_ref.at[at, pl.ds(head * HD, HD), :],
                weights.at[slot, pl.ds((4 + 2 * head + copy) * HD, HD), :],
                weight_sem.at[slot, 1 + 2 * head + copy],
            )
            for head in range(2)
            for copy in range(2)
        ]

    def normed_grad():
        if slots == 2:
            for copy in load_weights(0, 0):
                copy.start()
        lane = lax.rem(lax.broadcasted_iota(jnp.int32, (rows_here, 4 * HD), 1), 2 * HD)

        def one(at, carry):
            slot = lax.rem(at, slots)
            if slots == 1:
                for copy in load_weights(at, slot):
                    copy.start()
            for copy in load_weights(at, slot):
                copy.wait()
            if slots == 2:

                @pl.when(at + 1 < count)
                def _():
                    for copy in load_weights(at + 1, 1 - slot):
                        copy.start()

            pair = pl.ds(pl.multiple_of(at * 4 * HD, 4 * HD), 4 * HD)
            side = grad_raw_ref[2, :, pair]
            for s in range(2):
                mine = lane < HD if s == 0 else lane >= HD
                left = jnp.concatenate(
                    [grad_raw_ref[s, :, pair], jnp.where(mine, side, jnp.zeros_like(side))], axis=1
                )
                for first in range(0, depth, CHUNK):
                    columns = pl.ds(first, CHUNK)
                    product = dot(left, weights[slot, :, columns])

                    @pl.when(at == 0)
                    def _(s=s, columns=columns, product=product):
                        result[s, :, columns] = product

                    @pl.when(at > 0)
                    def _(s=s, columns=columns, product=product):
                        result[s, :, columns] += product

            return carry

        lax.fori_loop(0, count, one, 0)

    tall = 16
    tiles = rows_here // tall

    def norm_back(s, first, last):
        def some(at, carry):
            here = pl.ds(pl.multiple_of(at * tall, tall), tall)
            values = inputs_ref[s, here, :].astype(F32)
            centered = values - jnp.mean(values, axis=1, keepdims=True)
            scale = lax.rsqrt(jnp.mean(centered * centered, axis=1, keepdims=True) + 1e-05)
            hat = centered * scale
            grad = result[s, here, :]
            wide = grad * gain_ref[...]
            back = wide - jnp.mean(wide, axis=1, keepdims=True)
            back = scale * (back - hat * jnp.mean(wide * hat, axis=1, keepdims=True))
            result[s, here, :] = middle[s, here, :] + back
            product = grad * hat
            sums[0] += product[:8] + product[8:]
            sums[1] += grad[:8] + grad[8:]
            return carry

        lax.fori_loop(first, last, some, 0)

    def add(quarter, side, number):
        acc[:, quarter, :, lanes[side]] = (
            acc[:, quarter, :, lanes[side]].astype(F32) + plane_in[number].astype(F32)
        ).astype(LOW)

    def add_core(number, quarter):
        for copy in swaps[number]:
            copy.wait_recv()
        acc[:, quarter] = (acc[:, quarter].astype(F32) + got[:, quarter].astype(F32)).astype(LOW)

    def plane(quarter, side, partner, number):
        return wire(
            acc.at[:, quarter, :, lanes[side]], plane_in.at[number],
            plane_send_sem.at[number], plane_recv_sem.at[number], partner,
        )

    sends = [
        plane(dp_x, 0, to_x, 0),
        plane(dp_xy, 0, to_x, 1),
        plane(dp_y, 1, to_y, 2),
        plane(dp_xy, 1, to_y, 3),
        plane(dp_y, 0, to_y, 4),
        plane(dp_x, 1, to_x, 5),
    ]
    for copy in loads:
        copy.wait()
    add_core(0, dp_xy)
    sends[1].start()
    sends[3].start()
    add_core(1, dp_x)
    sends[0].start()
    add_core(2, dp_y)
    sends[2].start()
    add_core(3, dp)
    normed_grad()
    load_middle.wait()
    sums[...] = jnp.zeros(sums.shape, F32)
    norm_back(0, 0, tiles)
    saved_rows = [
        pltpu.make_async_copy(result.at[s], input_grad_ref.at[s], local.at[7 + s]) for s in range(2)
    ]
    saved_rows[0].start()
    sends[1].wait_recv()
    add(dp_y, 0, 1)
    sends[4].start()
    sends[3].wait_recv()
    add(dp_x, 1, 3)
    sends[5].start()
    norm_back(1, 0, tiles // 2)
    sends[0].wait_recv()
    add(dp, 0, 0)
    sends[2].wait_recv()
    add(dp, 1, 2)
    sends[4].wait_recv()
    add(dp, 0, 4)
    sends[5].wait_recv()
    add(dp, 1, 5)

    carries = carry_copies(carried, targets, carry_send, carry_recv)
    for copy in carries:
        copy.start()

    def line(step):
        out = []
        for way, turn in enumerate((1, -1)):
            target = z + turn * (count - step)
            far = z + turn
            lands = far - 2 * turn + turn * (count - step)
            sends = (target >= 0) & (target < count)
            receives = (lands >= 0) & (lands < count) & (z - turn >= 0) & (z - turn < count)
            at = jnp.clip(target, 0, count - 1)
            to = jnp.clip(lands, 0, count - 1)
            copy = wire(
                acc.at[at, dp], line_in.at[way, step - 1],
                line_send_sem.at[way, step - 1], line_recv_sem.at[way, step - 1],
                line_partner(z, turn),
            )
            out.append((sends, receives, to, copy))
        return out

    over_dp = []
    for step in range(1, count):
        legs = line(step)
        for sends_now, _, _, copy in legs:
            pl.when(sends_now)(copy.start)
        if step == 1:
            norm_back(1, tiles // 2, tiles)
            saved_rows[1].start()
            norms[...] = norms_ref[...]
            norms[0:1, :] = jnp.sum(sums[0], axis=0, keepdims=True)
            norms[1:2, :] = jnp.sum(sums[1], axis=0, keepdims=True)
            for copy in own_small:
                copy.start()
            for leaving, _ in over_mp:
                leaving.start()
        if step == count - 1:
            for _, landed in over_mp:
                landed.wait_recv()
            for copy in own_small:
                copy.wait()
            norms_dp[dp] = jnp.sum(norms_all[...], axis=0)
            taps_dp[dp] = jnp.sum(taps_all[...], axis=0)
            over_dp = small("dp", dp, 4, lambda to: norms_dp.at[dp], norms_dp, 2, None) + small(
                "dp", dp, 4, lambda to: taps_dp.at[dp], taps_dp, 3, None
            )
            for leaving, _ in over_dp:
                leaving.start()
        for way, (_, receives, to, copy) in enumerate(legs):

            @pl.when(receives)
            def _(to=to, copy=copy, way=way):
                copy.wait_recv()
                acc[to, dp] = (
                    acc[to, dp].astype(F32) + line_in[way, step - 1].astype(F32)
                ).astype(LOW)

    gathered[dp] = acc[z, dp]

    def gather(quarter, side, partner, number):
        block = gathered.at[quarter, :, lanes[side]]
        return wire(block, block, gather_send.at[number], gather_recv.at[number], partner)

    leaving = [
        gather(dp, 0, to_x, 0), gather(dp, 1, to_y, 1), gather(dp, 0, to_y, 2), gather(dp, 1, to_x, 3),
        gather(dp_x, 0, to_y, 4), gather(dp_y, 1, to_x, 5),
    ]
    landing = [
        gather(dp_x, 0, to_x, 0), gather(dp_y, 1, to_y, 1), gather(dp_y, 0, to_y, 2), gather(dp_x, 1, to_x, 3),
        gather(dp_xy, 0, to_y, 4), gather(dp_xy, 1, to_x, 5),
    ]
    for number in range(4):
        leaving[number].start()
    for _, landed in over_dp:
        landed.wait_recv()
    norms_sum_ref[...] = jnp.sum(norms_dp[...], axis=0)
    taps_sum_ref[...] = jnp.sum(taps_dp[...], axis=0)
    landing[0].wait_recv()
    leaving[4].start()
    landing[1].wait_recv()
    leaving[5].start()
    for number in range(2, 6):
        landing[number].wait_recv()
    save = pltpu.make_async_copy(gathered, joint_ref, local.at[5])
    save.start()
    for group in swaps:
        for copy in group:
            copy.wait_send()
    for copy in sends:
        copy.wait_send()
    for step in range(1, count):
        for sends_now, _, _, copy in line(step):
            pl.when(sends_now)(copy.wait_send)
    for copy in leaving:
        copy.wait_send()
    for copy, _ in over_mp + over_dp:
        copy.wait_send()
    for copy in carries + saved_rows:
        copy.wait()
    save.wait()


def finish(qk, v, out, norms, taps, grad_raw, inputs, gain, qk_all, v_all, middle, carried):
    mp = lax.axis_size("mp")
    count = mp // 2
    depth = qk.shape[-1]
    anywhere = pl.BlockSpec(memory_space=pl.ANY)
    vmem = pl.BlockSpec(memory_space=pltpu.VMEM)
    dma = pltpu.SemaphoreType.DMA
    return pl.pallas_call(
        partial(finish_kernel, tuple(way for way, _ in carried)),
        in_specs=[anywhere] * 3 + [vmem] * 5 + [anywhere] * (3 + len(carried)),
        out_specs=[anywhere, vmem, vmem, anywhere] + [anywhere] * len(carried),
        out_shape=[
            jax.ShapeDtypeStruct((4, HD, depth), LOW),
            jax.ShapeDtypeStruct(norms.shape, F32),
            jax.ShapeDtypeStruct(taps.shape[1:], F32),
            jax.ShapeDtypeStruct(middle.shape, F32),
        ]
        + [jax.ShapeDtypeStruct(block.shape, block.dtype) for _, block in carried],
        scratch_shapes=[
            pltpu.VMEM((count, 4, HD, depth), LOW),
            pltpu.VMEM((count, 4, HD, depth), LOW),
            pltpu.VMEM((6, count, HD, depth // 2), LOW),
            pltpu.VMEM((2, count - 1, HD, depth), LOW),
            pltpu.VMEM((4, HD, depth), LOW),
            pltpu.VMEM((mp,) + norms.shape, F32),
            pltpu.VMEM(taps.shape, F32),
            pltpu.VMEM((4,) + norms.shape, F32),
            pltpu.VMEM((4,) + taps.shape[1:], F32),
            pltpu.VMEM((2 if count <= 8 else 1, 8 * HD, depth), LOW),
            pltpu.VMEM(middle.shape, F32),
            pltpu.VMEM(middle.shape, F32),
            pltpu.VMEM(norms.shape, F32),
            pltpu.VMEM((2, 8, depth), F32),
            dma((2, 5)),
            dma((9,)),
            dma((3, 4)),
            dma((3, 4)),
            dma((6,)),
            dma((6,)),
            dma((2, count)),
            dma((2, count)),
            dma((6,)),
            dma((6,)),
            dma((4, mp)),
            dma((4, mp)),
            dma((len(carried),)),
            dma((len(carried),)),
        ],
        compiler_params=pltpu.CompilerParams(
            collective_id=8, has_side_effects=True, vmem_limit_bytes=VMEM_LIMIT + 2**19
        ),
        cost_estimate=pl.CostEstimate(flops=2**36, bytes_accessed=2**26, transcendentals=0),
        name="finish",
    )(
        qk, v, out, norms, taps, grad_raw, inputs, gain.reshape(1, depth), qk_all, v_all, middle, *(block for _, block in carried),
    )


def plane_send(block, mask):
    return lax.ppermute(block, "dp", [(d, d ^ mask) for d in range(lax.axis_size("dp"))])


def placed(own, legs, last, me, turn):
    one_x, two_y, one_y, two_x = legs
    units, width = own.shape
    wide = 256
    steps = width // 2 // wide

    def kernel(me_ref, own_ref, one_x, two_x, one_y, two_y, one_xy, two_xy, o_ref):
        first = pl.program_id(0) < steps
        blocks = [own_ref[...]] + [
            jnp.where(first, one[...], two[...])
            for one, two in ((one_x, two_x), (one_y, two_y), (one_xy, two_xy))
        ]
        odd, high = lax.rem(me_ref[0], 2) == 1, me_ref[0] >= 2
        blocks = [jnp.where(odd, blocks[at ^ 1], blocks[at]) for at in range(4)]
        blocks = [jnp.where(high, blocks[at ^ 2], blocks[at]) for at in range(4)]
        for at, block in enumerate(blocks):
            if turn:
                o_ref[:, at * units : (at + 1) * units] = block.astype(F32).T
            else:
                o_ref[at * units : (at + 1) * units, :] = block.astype(F32)

    def half(side):
        if side == 0:
            return pl.BlockSpec((units, wide), lambda i, me: (0, jnp.minimum(i, steps - 1)))
        return pl.BlockSpec((units, wide), lambda i, me: (0, jnp.maximum(i - steps, 0)))

    if turn:
        shape = (width, 4 * units)
        out_spec = pl.BlockSpec((wide, 4 * units), lambda i, me: (i, 0))
    else:
        shape = (4 * units, width)
        out_spec = pl.BlockSpec((4 * units, wide), lambda i, me: (0, i))
    return pl.pallas_call(
        kernel,
        grid_spec=pltpu.PrefetchScalarGridSpec(
            num_scalar_prefetch=1,
            grid=(2 * steps,),
            in_specs=[pl.BlockSpec((units, wide), lambda i, me: (0, i))] + [half(0), half(1)] * 3,
            out_specs=out_spec,
        ),
        out_shape=jax.ShapeDtypeStruct(shape, F32),
        compiler_params=pltpu.CompilerParams(vmem_limit_bytes=32 * 2**20),
        cost_estimate=pl.CostEstimate(flops=0, bytes_accessed=2**24, transcendentals=0),
        name="placed",
    )(me.reshape(1).astype(jnp.int32), own, one_x, two_x, one_y, two_y, *last)


def plane_gather_begin(block, axis=-1):
    half = block.shape[axis] // 2
    one, two = jnp.split(block, [half], axis=axis)
    return plane_send(one, 1), plane_send(two, 2), plane_send(one, 2), plane_send(two, 1)


def plane_gather_end(legs):
    one_x, two_y, one_y, two_x = legs
    return plane_send(one_x, 2), plane_send(two_y, 1)


def line_step(blocks, step):
    count = lax.axis_size("mp") // 2
    up = [(2 * z + c, 2 * z + 2 + c) for z in range(step - 1, count - 1) for c in range(2)]
    down = [(2 * z + c, 2 * z - 2 + c) for z in range(1, count - step + 1) for c in range(2)]
    return lax.ppermute(blocks[0], "mp", up), lax.ppermute(blocks[1], "mp", down)


def per_device(
    inputs,
    cotangent,
    short_lengths,
    long_lengths,
    norm1_gain,
    norm1_bias,
    query_weight,
    key_weight,
    value_weight,
    query_kernel,
    key_kernel,
    value_kernel,
    out_weight,
    norm2_gain,
    norm2_bias,
    up_weight,
    down_weight,
):
    rows_here = inputs.shape[1]
    width = inputs.shape[2]
    mp = lax.axis_size("mp")
    dp = lax.axis_size("dp")
    me_dp = lax.axis_index("dp")
    me_mp = lax.axis_index("mp")
    group = rows_here * mp
    chips = mp // 2
    hidden_here = up_weight.shape[1]
    share = hidden_here // dp

    starts = jnp.stack(
        [document_starts(short_lengths[0], group), document_starts(long_lengths[0], group)]
    )
    rows = inputs.astype(F32)

    def quarters(weight):
        return weight.reshape(4, weight.shape[0] // 4, width)

    qk_own = jnp.concatenate([query_weight, key_weight], axis=1).T
    up_own = lax.dynamic_slice_in_dim(up_weight, me_dp * share, share, 1).T
    down_own = lax.dynamic_slice_in_dim(down_weight, me_dp * share, share, 0)
    qk_taps = jnp.concatenate([query_kernel, key_kernel], axis=1)
    v_taps = jnp.concatenate([value_kernel, value_kernel], axis=1)
    taps_own = jnp.pad(jnp.stack([qk_taps, qk_taps, v_taps]), ((0, 0), (0, 5), (0, 0)))
    places = jnp.arange(group, dtype=jnp.int32)
    offsets = lax.dynamic_slice_in_dim(
        jnp.pad(places[None, :] - starts, ((0, 0), (0, HALO))), me_mp * rows_here, rows_here + HALO, 1
    )
    masks = jnp.stack(
        [
            offsets[:, :rows_here] >= 1,
            offsets[:, :rows_here] >= 2,
            offsets[:, 1 : rows_here + 1] >= 1,
            offsets[:, 2 : rows_here + 2] >= 2,
        ],
        axis=1,
    ).astype(F32)[..., None]
    wide_masks = jnp.broadcast_to(masks, masks.shape[:3] + (HD,))
    masks = jnp.stack(
        [
            jnp.concatenate([wide_masks[left], wide_masks[right]], axis=2)
            for left, right in ((0, 0), (1, 1), (0, 1))
        ]
    )

    qk_all, v_all, out_all, taps, normed, up_early, raw, mixed, one_x, two_y = front(
        inputs, norm1_gain, norm1_bias, quarters(qk_own), quarters(value_weight.T), quarters(out_weight), taps_own, up_own,
        masks, cotangent,
    )
    qk_all = qk_all.reshape(mp * 2 * HD, width)
    v_all = v_all.reshape(mp * HD, width)
    out_all = out_all.reshape(mp * HD, width)
    mixed = mixed.reshape(3, group, 128)
    cot, mixed, up_early = lax.optimization_barrier((cotangent, mixed, up_early))

    def early_block(at):
        start = (2 * jnp.clip(at, 0, chips - 1) + me_mp % 2) * share
        return lax.dynamic_slice_in_dim(up_early, start, share, 0)

    late = range(early_steps(chips)[-1] + 1, chips)
    up_late = {}
    blocks = (early_block(me_mp // 2 - late[0] + 1), early_block(me_mp // 2 + late[0] - 1))
    for step in late:
        blocks = line_step(blocks, step)
        up_late[step, 1], up_late[step, -1] = blocks
    one_y, two_x = plane_send(cot[:, :, : width // 2], 2), plane_send(cot[:, :, width // 2 :], 1)
    one_xy, two_xy = plane_send(one_x, 2), plane_send(two_y, 1)

    def side_by_side(pair):
        split = pair.reshape(2, rows_here, mp, HD)
        return split.transpose(1, 2, 0, 3).reshape(1, rows_here, mp * 2 * HD)

    def apart(joint):
        split = joint.reshape(joint.shape[1], mp, 2, HD)
        return split.transpose(2, 0, 1, 3).reshape(2, joint.shape[1], mp * HD)

    attended_head, wide, total = attend(mixed, starts)
    attended_head, up_late = lax.optimization_barrier((attended_head, up_late))
    attended = apart(attended_back(attended_head, rows_here))
    middle = rows + dot(attended, out_all)
    second = layer_norm(middle, norm2_gain, norm2_bias).astype(LOW)

    second, one_y, two_x, one_xy, two_xy = lax.optimization_barrier(
        (second, one_y, two_x, one_xy, two_xy)
    )
    cot_pieces = (cot, one_x, two_x, one_y, two_y, one_xy, two_xy)
    second_all, relu, hidden, down_all, up_all, down_part = feed_in(
        second, up_early, down_own, cot_pieces, up_late
    )
    down_mine = lax.psum_scatter(down_part, "mp", scatter_dimension=0, tiled=True)
    grad_pre, up_part, grad_second = feed_out(
        cot_pieces, relu, second_all, up_all, down_all
    )
    up_mine = lax.psum_scatter(up_part, "mp", scatter_dimension=0, tiled=True)
    grad_second, down_mine = lax.optimization_barrier((grad_second, down_mine))
    down_legs = plane_gather_begin(down_mine)

    def norm_back(values, gain, grad):
        flat = values.reshape(-1, width)
        unused, pull = jax.vjp(layer_norm, flat, gain, norm1_bias)
        grad_rows, grad_gain, grad_shift = pull(grad.reshape(-1, width))
        return grad_rows.reshape(values.shape), grad_gain, grad_shift

    grad_middle, gain_two, shift_two = norm_back(middle, norm2_gain, grad_second)
    grad_middle = grad_middle + cotangent.astype(F32)
    branch = grad_middle.astype(LOW)
    grad_attended = jnp.einsum("srd,hd->srh", branch, out_all, preferred_element_type=F32).astype(LOW)
    grad_head, feed_x0, feed_x1, feed_y0, feed_y1, keep_a, keep_b = feed_heads(
        side_by_side(grad_attended), hidden, down_all
    )
    grad_head, down_legs, feed_x0, feed_y0 = lax.optimization_barrier(
        (grad_head, down_legs, feed_x0, feed_y0)
    )
    down_last = plane_gather_end(down_legs)
    x_first, y_first = plane_send(feed_x0, 1), plane_send(feed_y0, 2)
    grad_mixed_head = attend_back(mixed, grad_head, wide, total, starts, HALO)
    grad_mixed_head, x_first, y_first = lax.optimization_barrier(
        (grad_mixed_head, x_first, y_first)
    )

    def add(left, right):
        return left.astype(F32) + right.astype(F32)

    feed_a0, feed_b0 = add(keep_a[0, 1], x_first[1]).astype(LOW), add(keep_b[0, 1], y_first[1]).astype(LOW)
    grad_raw, tap_sums, qk_part, v_part, out_part, x_second, y_second, feed_a0, feed_b0 = project_back(
        grad_mixed_head, raw, taps, masks, normed, attended, branch,
        ((0, feed_x1), (1, feed_y1), (1, feed_a0), (0, feed_b0)),
    )
    grad_raw, down_last = lax.optimization_barrier((grad_raw, down_last))
    grad_raw, up_mine, down_last = lax.optimization_barrier((grad_raw, up_mine, down_last))
    down_grad = placed(down_mine, down_legs, down_last, me_dp, False)
    up_legs = plane_gather_begin(up_mine)
    feed_a1, feed_b1 = add(keep_a[1, 1], x_second[1]).astype(LOW), add(keep_b[1, 1], y_second[1]).astype(LOW)

    def split_parts(part):
        return part.reshape(mp // 2, 2, 4, part.shape[1] // 8, width)

    norms = jnp.pad(jnp.stack([gain_two, shift_two]), ((2, 4), (0, 0)))
    qk_sums = (tap_sums[0] + tap_sums[1]).reshape(8, mp, 2 * HD)
    v_sums = tap_sums[2].reshape(8, mp, 2, HD).sum(axis=2)
    taps_part = jnp.concatenate([qk_sums, v_sums, jnp.zeros_like(v_sums)], axis=2)
    taps_part = taps_part.transpose(1, 0, 2)
    norms, up_legs = lax.optimization_barrier((norms, up_legs))
    joint_grad, small_sum, taps_sum, input_grads, feed_a1, feed_b1, one_xy, two_xy = finish(
        split_parts(qk_part), split_parts(v_part), split_parts(out_part), norms, taps_part,
        grad_raw, inputs, norm1_gain, qk_all.reshape(chips, 4 * HD, width), v_all.reshape(chips, 2 * HD, width),
        grad_middle,
        ((1, feed_a1), (0, feed_b1), (1, up_legs[0]), (0, up_legs[1])),
    )
    results = jnp.stack(
        [
            middle[s]
            + jnp.concatenate(
                [
                    add(keep_a[s, 0], x_in[0]) + a_in.astype(F32),
                    add(keep_b[s, 0], y_in[0]) + b_in.astype(F32),
                ],
                axis=1,
            )
            for s, (x_in, y_in, a_in, b_in) in enumerate(
                ((x_first, y_first, feed_a0, feed_b0), (x_second, y_second, feed_a1, feed_b1))
            )
        ]
    ).astype(LOW)
    up_grad = placed(up_mine, up_legs, (one_xy, two_xy), me_dp, True)
    joint_grad = joint_grad.astype(F32)
    qk_grad = joint_grad[:, : HD // 2].reshape(2 * HD, width).T
    v_grad = joint_grad[:, HD // 2 : 3 * HD // 4].reshape(HD, width).T
    out_grad = joint_grad[:, 3 * HD // 4 :].reshape(HD, width)
    taps_sum = taps_sum[:3]
    return (
        results,
        input_grads,
        small_sum[0],
        small_sum[1],
        qk_grad[:, :HD],
        qk_grad[:, HD:],
        v_grad,
        taps_sum[:, :HD],
        taps_sum[:, HD : 2 * HD],
        taps_sum[:, 2 * HD : 3 * HD],
        out_grad,
        small_sum[2],
        small_sum[3],
        up_grad,
        down_grad,
    )


def solution(mesh):
    return jax.shard_map(
        per_device,
        mesh=mesh,
        in_specs=(
            P(None, ("dp", "mp"), None),
            P(None, ("dp", "mp"), None),
            P("dp", None),
            P("dp", None),
            P(),
            P(),
            P(None, "mp"),
            P(None, "mp"),
            P(None, "mp"),
            P(None, "mp"),
            P(None, "mp"),
            P(None, "mp"),
            P("mp", None),
            P(),
            P(),
            P(None, "mp"),
            P("mp", None),
        ),
        out_specs=(
            P(None, ("dp", "mp"), None),
            P(None, ("dp", "mp"), None),
            P(),
            P(),
            P(None, "mp"),
            P(None, "mp"),
            P(None, "mp"),
            P(None, "mp"),
            P(None, "mp"),
            P(None, "mp"),
            P("mp", None),
            P(),
            P(),
            P(None, "mp"),
            P("mp", None),
        ),
        check_vma=False,
    )
```

```python
import math
from functools import partial

import jax
import jax.numpy as jnp
from jax import lax
from jax.experimental import pallas as pl
from jax.experimental.pallas import tpu as pltpu
from jax.sharding import PartitionSpec as P

HD = 64
QUERIES, KEYS = 512, 512
WIDE = 256
CHUNK = 512
VMEM_LIMIT = 63 * 1024 * 1024
MESH = pl.DeviceIdType.MESH
LOW = jnp.bfloat16
F32 = jnp.float32


def dot(left, right):
    return jnp.dot(left, right, preferred_element_type=F32)


def layer_norm(rows, gain, shift):
    row_mean = jnp.mean(rows, axis=-1, keepdims=True)
    centered = rows - row_mean
    variance = jnp.mean(centered * centered, axis=-1, keepdims=True)
    return centered * lax.rsqrt(variance + 1e-05) * gain + shift


def document_starts(lengths, count):
    ends = jnp.cumsum(lengths)
    places = jnp.arange(count, dtype=jnp.int32)
    passed = (places[:, None] >= ends[None, :]).astype(jnp.int32)
    return jnp.sum(passed * lengths[None, :], axis=1)


def allowed_pairs(start_row, key_block, query_block):
    shape = (KEYS, QUERIES)
    keys = key_block * KEYS + lax.broadcasted_iota(jnp.int32, shape, 0)
    queries = query_block * QUERIES + lax.broadcasted_iota(jnp.int32, (1, QUERIES), 1)
    return (keys <= queries) & (keys >= start_row)


def key_blocks(first_ref, s, step):
    return first_ref[s, step], ((step + 1) * QUERIES + KEYS - 1) // KEYS


def attend_kernel(
    first_ref, start_ref, qk_ref, v_ref, out_ref, wide_ref, total_ref, values_t
):
    s, step = pl.program_id(0), pl.program_id(1)

    @pl.when(step == 0)
    def _():
        def turn(at, carry):
            rows = pl.ds(pl.multiple_of(at * KEYS, KEYS), KEYS)
            both = v_ref[0, rows, :].T
            values_t[at] = jnp.where(s == 0, both[:HD], both[HD:])
            return carry

        lax.fori_loop(0, values_t.shape[0], turn, 0)

    here = pl.ds(pl.multiple_of(step * QUERIES, QUERIES), QUERIES)
    query_t = (qk_ref[0, here, 0:HD] * HD ** (-0.5)).astype(LOW).T
    start_row = start_ref[0]

    def one(at, carry):
        top, summed, acc = carry
        rows = pl.ds(pl.multiple_of(at * KEYS, KEYS), KEYS)
        scores = dot(qk_ref[0, rows, HD : 2 * HD], query_t)
        scores = jnp.where(allowed_pairs(start_row, at, step), scores, -1e30)
        new_top = jnp.maximum(top, jnp.max(scores, axis=0, keepdims=True))
        powered = jnp.exp(scores - new_top)
        shrink = jnp.exp(top - new_top)
        summed = summed * shrink + jnp.sum(powered, axis=0, keepdims=True)
        acc = acc * shrink + dot(values_t[at], powered.astype(LOW))
        return new_top, summed, acc

    top, summed, acc = lax.fori_loop(
        *key_blocks(first_ref, s, step),
        one,
        (
            jnp.full((1, QUERIES), -1e30, F32),
            jnp.zeros((1, QUERIES), F32),
            jnp.zeros((HD, QUERIES), F32),
        ),
    )
    result = acc / summed
    wide_ref[0] = result
    total_ref[0] = top + jnp.log(summed)
    low = result.T.astype(LOW)

    @pl.when(s == 0)
    def _():
        out_ref[0, here, 0:HD] = low

    @pl.when(s == 1)
    def _():
        out_ref[0, here, HD : 2 * HD] = low


def attend(mixed, starts):
    group = mixed.shape[1]
    steps = group // QUERIES
    row = pl.BlockSpec((1, 1, QUERIES), lambda s, i, first: (s, 0, i))
    return pl.pallas_call(
        attend_kernel,
        grid_spec=pltpu.PrefetchScalarGridSpec(
            num_scalar_prefetch=1,
            grid=(2, steps),
            in_specs=[
                row,
                pl.BlockSpec((1, group, 2 * HD), lambda s, i, first: (s, 0, 0)),
                pl.BlockSpec((1, group, 2 * HD), lambda s, i, first: (2, 0, 0)),
            ],
            out_specs=[
                pl.BlockSpec((1, group, 2 * HD), lambda s, i, first: (0, 0, 0)),
                pl.BlockSpec((1, HD, QUERIES), lambda s, i, first: (s, 0, i)),
                row,
            ],
            scratch_shapes=[pltpu.VMEM((group // KEYS, HD, KEYS), LOW)],
        ),
        out_shape=[
            jax.ShapeDtypeStruct((1, group, 2 * HD), LOW),
            jax.ShapeDtypeStruct((2, HD, group), F32),
            jax.ShapeDtypeStruct((2, 1, group), F32),
        ],
        compiler_params=pltpu.CompilerParams(vmem_limit_bytes=32 * 1024 * 1024),
        cost_estimate=pl.CostEstimate(
            flops=2**34, bytes_accessed=group * 2048, transcendentals=group * group // 4
        ),
        name="attend",
    )(starts[:, ::QUERIES] // KEYS, starts[:, None, :], mixed, mixed)


def attend_back_kernel(
    first_ref, start_ref, qk_ref, v_ref, grad_ref, wide_ref, total_ref, out_ref,
    keys_t, values, grad_keys, grad_values,
):
    s, step = pl.program_id(0), pl.program_id(1)
    group = qk_ref.shape[1]

    @pl.when(step == 0)
    def _():
        def turn(at, carry):
            rows = pl.ds(pl.multiple_of(at * KEYS, KEYS), KEYS)
            keys_t[at] = qk_ref[0, rows, HD : 2 * HD].T
            both = v_ref[0, rows, :]
            values[rows, :] = jnp.where(s == 0, both[:, :HD], both[:, HD:])
            return carry

        lax.fori_loop(0, keys_t.shape[0], turn, 0)
        grad_keys[...] = jnp.zeros(grad_keys.shape, F32)
        grad_values[...] = jnp.zeros(grad_values.shape, F32)

    here = pl.ds(pl.multiple_of(step * QUERIES, QUERIES), QUERIES)
    query = (qk_ref[0, here, 0:HD] * HD ** (-0.5)).astype(LOW)
    query_t = query.T
    both = grad_ref[0]
    grad = jnp.where(s == 0, both[:, :HD], both[:, HD:])
    grad_t = grad.T
    start_row = start_ref[0]
    total = total_ref[0]
    inner = jnp.sum(grad_t.astype(F32) * wide_ref[0], axis=0, keepdims=True)

    def one(at, acc):
        rows = pl.ds(pl.multiple_of(at * KEYS, KEYS), KEYS)
        scores = dot(qk_ref[0, rows, HD : 2 * HD], query_t)
        scores = jnp.where(allowed_pairs(start_row, at, step), scores, -1e30)
        probs = jnp.exp(scores - total)
        grad_probs = dot(values[rows, :], grad_t)
        grad_scores = (probs * (grad_probs - inner)).astype(LOW)
        grad_values[rows, :] += dot(probs.astype(LOW), grad)
        grad_keys[rows, :] += dot(grad_scores, query)
        return acc + dot(keys_t[at], grad_scores)

    acc = lax.fori_loop(
        *key_blocks(first_ref, s, step), one, jnp.zeros((HD, QUERIES), F32)
    )
    out_ref[s, here, 0:HD] = (acc * HD ** (-0.5)).T.astype(out_ref.dtype)

    @pl.when(step == pl.num_programs(1) - 1)
    def _():
        out_ref[s, 0:group, HD : 2 * HD] = grad_keys[...].astype(out_ref.dtype)
        out_ref[s, group:, :] = jnp.zeros((out_ref.shape[1] - group, 2 * HD), out_ref.dtype)

        @pl.when(s == 0)
        def _():
            out_ref[2, 0:group, 0:HD] = grad_values[...].astype(out_ref.dtype)

        @pl.when(s == 1)
        def _():
            out_ref[2, 0:group, HD : 2 * HD] = grad_values[...].astype(out_ref.dtype)
            out_ref[2, group:, :] = jnp.zeros((out_ref.shape[1] - group, 2 * HD), out_ref.dtype)


def attend_back(mixed, grad, wide, total, starts, halo):
    group = mixed.shape[1]
    steps = group // QUERIES
    row = pl.BlockSpec((1, 1, QUERIES), lambda s, i, first: (s, 0, i))
    return pl.pallas_call(
        attend_back_kernel,
        grid_spec=pltpu.PrefetchScalarGridSpec(
            num_scalar_prefetch=1,
            grid=(2, steps),
            in_specs=[
                row,
                pl.BlockSpec((1, group, 2 * HD), lambda s, i, first: (s, 0, 0)),
                pl.BlockSpec((1, group, 2 * HD), lambda s, i, first: (2, 0, 0)),
                pl.BlockSpec((1, QUERIES, 2 * HD), lambda s, i, first: (0, i, 0)),
                pl.BlockSpec((1, HD, QUERIES), lambda s, i, first: (s, 0, i)),
                row,
            ],
            out_specs=pl.BlockSpec((3, group + halo, 2 * HD), lambda s, i, first: (0, 0, 0)),
            scratch_shapes=[
                pltpu.VMEM((group // KEYS, HD, KEYS), LOW),
                pltpu.VMEM((group, HD), LOW),
                pltpu.VMEM((group, HD), F32),
                pltpu.VMEM((group, HD), F32),
            ],
        ),
        out_shape=jax.ShapeDtypeStruct((3, group + halo, 2 * HD), LOW),
        compiler_params=pltpu.CompilerParams(vmem_limit_bytes=32 * 1024 * 1024),
        cost_estimate=pl.CostEstimate(
            flops=2**35, bytes_accessed=group * 2048, transcendentals=group * group // 4
        ),
        name="attend_back",
    )(starts[:, ::QUERIES] // KEYS, starts[:, None, :], mixed, mixed, grad, wide, total)


def plane_partners():
    me = lax.axis_index("dp")
    return {"dp": me + 1 - 2 * lax.rem(me, 2)}, {"dp": me + 2 - 4 * (me // 2)}


def dot_nt(left, right):
    return lax.dot_general(left, right, (((1,), (1,)), ((), ())), preferred_element_type=F32)


def mesh_place():
    me = lax.axis_index("mp")
    return me // 2, lax.rem(me, 2)


def wire(source, target, send, recv, partner):
    return pltpu.make_async_remote_copy(
        src_ref=source,
        dst_ref=target,
        send_sem=send,
        recv_sem=recv,
        device_id=partner,
        device_id_type=MESH,
    )


def line_partner(z, step):
    _, core = mesh_place()
    return {"mp": 2 * (z + step) + core}


def other_core():
    z, core = mesh_place()
    return {"mp": 2 * z + 1 - core}


def greet(partners):
    barrier = pltpu.get_barrier_semaphore()
    for partner in partners:
        pl.semaphore_signal(barrier, inc=1, device_id=partner, device_id_type=MESH)
    pl.semaphore_wait(barrier, len(partners))


def greet_line(with_plane):
    z, _ = mesh_place()
    count = lax.axis_size("mp") // 2
    barrier = pltpu.get_barrier_semaphore()
    partners = [other_core()]
    if with_plane:
        partners += list(plane_partners())
    for partner in partners:
        pl.semaphore_signal(barrier, inc=1, device_id=partner, device_id_type=MESH)
    for turn in (1, -1):

        @pl.when((z + turn >= 0) & (z + turn < count))
        def _(turn=turn):
            pl.semaphore_signal(barrier, inc=1, device_id=line_partner(z, turn), device_id_type=MESH)

    near = jnp.where(z > 0, 1, 0) + jnp.where(z < count - 1, 1, 0)
    pl.semaphore_wait(barrier, near + len(partners))


class LineGather:
    def __init__(self, place, send, recv, swap_send, swap_recv):
        self.z, self.core = mesh_place()
        self.count = lax.axis_size("mp") // 2
        self.place, self.send, self.recv = place, send, recv
        self.swap_send, self.swap_recv = swap_send, swap_recv

    def copies(self, step):
        z, count = self.z, self.count
        out = []
        for way, turn in enumerate((1, -1)):
            leaves = z - turn * (step - 1)
            lands = z - turn * step
            far = z + turn
            sends = (leaves >= 0) & (leaves < count) & (far >= 0) & (far < count)
            receives = (lands >= 0) & (lands < count)
            at = jnp.clip(leaves, 0, count - 1)
            to = jnp.clip(lands, 0, count - 1)
            sems = (self.send.at[way, step - 1], self.recv.at[way, step - 1], line_partner(z, turn))
            leaving = wire(self.place(at, self.core), self.place(at, self.core), *sems)
            landing = wire(self.place(to, self.core), self.place(to, self.core), *sems)
            out.append((sends, leaving, receives, landing, to))
        return out

    def start(self, step):
        for sends, leaving, _, _, _ in self.copies(step):
            pl.when(sends)(leaving.start)

    def swap(self, at, number):
        sems = (self.swap_send.at[number], self.swap_recv.at[number], other_core())
        leaving = wire(self.place(at, self.core), self.place(at, self.core), *sems)
        landing = wire(self.place(at, 1 - self.core), self.place(at, 1 - self.core), *sems)
        return leaving, landing

    def swap_own(self):
        self.swap(self.z, 0)[0].start()

    def arrive(self, step):
        for way, (_, _, receives, landing, at) in enumerate(self.copies(step)):

            @pl.when(receives)
            def _(landing=landing, at=at, way=way):
                landing.wait_recv()
                self.swap(at, 1 + 2 * (step - 1) + way)[0].start()

    def swapped(self, at, number):
        leaving, landing = self.swap(at, number)
        leaving.wait_send()
        landing.wait_recv()

    def finish(self, steps, own):
        if own:
            self.swapped(self.z, 0)
        for step in steps:
            for way, (sends, leaving, receives, _, at) in enumerate(self.copies(step)):
                pl.when(sends)(leaving.wait_send)
                pl.when(receives)(
                    lambda at=at, way=way, step=step: self.swapped(at, 1 + 2 * (step - 1) + way)
                )


def line_semaphores(count):
    return [
        pltpu.SemaphoreType.DMA((2, count)),
        pltpu.SemaphoreType.DMA((2, count)),
        pltpu.SemaphoreType.DMA((2 * count,)),
        pltpu.SemaphoreType.DMA((2 * count,)),
    ]


def early_steps(count):
    return range(1, count // 2 + 1)


HALO = 16


def carry_copies(carried, targets, send, recv):
    partners = plane_partners()
    return [
        wire(ref, target, send.at[at], recv.at[at], partners[way])
        for at, ((way, ref), target) in enumerate(zip(carried, targets))
    ]


def greet_members(ways):
    mp = lax.axis_size("mp")
    me = lax.axis_index("mp")
    barrier = pltpu.get_barrier_semaphore()
    for step in range(1, mp):
        pl.semaphore_signal(
            barrier, inc=1, device_id={"mp": lax.rem(me + step, mp)}, device_id_type=MESH
        )
    partners = plane_partners() if ways else ()
    for partner in partners:
        pl.semaphore_signal(barrier, inc=1, device_id=partner, device_id_type=MESH)
    pl.semaphore_wait(barrier, mp - 1 + len(partners))


def member_copies(source, target, send, recv):
    mp = lax.axis_size("mp")
    me = lax.axis_index("mp")
    copies = []
    for step in range(1, mp):
        to = lax.rem(me + step, mp)
        sems = (send.at[step], recv.at[step], {"mp": to})
        copies.append(
            (
                wire(source(to), target(me), *sems),
                wire(source(to), target(lax.rem(me + mp - step, mp)), *sems),
            )
        )
    return copies


def head_lanes(at):
    return pl.ds(pl.multiple_of(at * 128, 128), 128)


def front_kernel(
    inputs_ref, gain_ref, shift_ref, qk_ref, v_ref, out_ref, taps_ref, up_ref, masks_ref, cot_ref,
    all_qk_ref, all_v_ref, all_out_ref, all_taps_ref, normed_ref, up_all_ref, raw_ref, o_ref, cot_x_ref, cot_y_ref,
    inputs, rows, all_qk, all_v, all_out, all_taps, up_all, raw, mixed, landed, local, *sems,
):
    mp = lax.axis_size("mp")
    dp = lax.axis_index("dp")
    me = lax.axis_index("mp")
    z, core = mesh_place()
    count = mp // 2
    rows_here, depth = inputs.shape[1:]
    halo = rows.shape[1] - rows_here
    to_x, to_y = plane_partners()
    share = up_ref.shape[0]
    owned = (qk_ref, v_ref, out_ref)
    whole = (all_qk, all_v, all_out)
    (plane_send_sem, plane_recv_sem, plane_swap_send, plane_swap_recv) = sems[:4]
    taps_send, taps_recv, halo_send, halo_recv, carry_send, carry_recv, head_send, head_recv = sems[4:12]
    line_sems = [sems[12 + 4 * part : 16 + 4 * part] for part in range(4)]

    def up_place(at, at_core):
        start = pl.multiple_of((2 * at + at_core) * share, 16)
        return up_all.at[pl.ds(start, share), :]

    def taps_place(at):
        return all_taps.at[:, :, head_lanes(at)]

    loads = [
        pltpu.make_async_copy(inputs_ref, inputs, local.at[0]),
        pltpu.make_async_copy(taps_ref, taps_place(me), local.at[1]),
        pltpu.make_async_copy(up_ref, up_place(z, core), local.at[2]),
    ] + [
        pltpu.make_async_copy(
            owned[part].at[dp], whole[part].at[z, core, dp], local.at[3 + part]
        )
        for part in range(3)
    ]
    for copy in loads:
        copy.start()
    greet_members((0, 1))
    for copy in loads[1:]:
        copy.wait()

    lines = [
        LineGather(lambda at, at_core, part=part: whole[part].at[at, at_core, dp], *line_sems[part])
        for part in range(3)
    ]
    up_line = LineGather(up_place, *line_sems[3])
    for line in lines:
        line.start(1)
    tap_copies = member_copies(lambda to: taps_ref, taps_place, taps_send, taps_recv)
    for copy, _ in tap_copies:
        copy.start()
    for line in lines:
        line.swap_own()

    loads[0].wait()
    tall = 16

    def norm(s):
        def some(at, carry):
            here = pl.ds(pl.multiple_of(at * tall, tall), tall)
            there = pl.ds(pl.multiple_of(halo + at * tall, tall), tall)
            values = inputs[s, here, :].astype(F32)
            centered = values - jnp.mean(values, axis=1, keepdims=True)
            variance = jnp.mean(centered * centered, axis=1, keepdims=True)
            rows[s, there, :] = (
                centered * lax.rsqrt(variance + 1e-05) * gain_ref[...] + shift_ref[...]
            ).astype(LOW)
            return carry

        lax.fori_loop(0, rows_here // tall, some, 0)

    norm(0)
    for step in range(1, count):
        for line in lines:
            line.arrive(step)
        if step + 1 < count:
            for line in lines:
                line.start(step + 1)

    half = depth // 2
    lanes = (pl.ds(0, half), pl.ds(half, half))
    dp_x = dp + 1 - 2 * lax.rem(dp, 2)
    dp_y = dp + 2 - 4 * (dp // 2)
    dp_xy = dp_x + 2 - 4 * (dp_x // 2)
    legs = ((0, to_x), (1, to_y), (0, to_y), (1, to_x), (0, to_y), (1, to_x))

    def plane(number, quarter):
        side, partner = legs[number]
        out = []
        for part in range(3):
            block = whole[part].at[:, core, quarter, :, lanes[side]]
            out.append(
                wire(
                    block, block, plane_send_sem.at[part, number], plane_recv_sem.at[part, number], partner
                )
            )
        return out

    leaving = [plane(number, quarter) for number, quarter in enumerate((dp, dp, dp, dp, dp_x, dp_y))]
    landing = [
        plane(number, quarter) for number, quarter in enumerate((dp_x, dp_y, dp_y, dp_x, dp_xy, dp_xy))
    ]

    def pass_on(number, at_core):
        quarter = (dp_x, dp_y, dp_xy)[number]
        out = []
        for part in range(3):
            block = whole[part].at[:, at_core, quarter]
            out.append(
                wire(
                    block, block, plane_swap_send.at[part, number], plane_swap_recv.at[part, number],
                    other_core(),
                )
            )
        return out

    def each(copies, what):
        for copy in copies:
            getattr(copy, what)()

    for number in range(4):
        each(leaving[number], "start")
    early = early_steps(count)
    up_line.start(1)
    up_line.swap_own()
    norm(1)
    own_rows = rows.at[:, pl.ds(halo, rows_here), :]
    save = pltpu.make_async_copy(own_rows, normed_ref, local.at[0])
    save.start()
    halo_copy = wire(
        rows.at[:, pl.ds(rows_here, halo), :], rows.at[:, pl.ds(0, halo), :], halo_send, halo_recv,
        {"mp": lax.rem(me + 1, mp)},
    )
    halo_copy.start()
    each(landing[0], "wait_recv")
    each(leaving[4], "start")
    each(landing[1], "wait_recv")
    each(leaving[5], "start")
    each(landing[3], "wait_recv")
    each(pass_on(0, core), "start")
    each(landing[2], "wait_recv")
    each(pass_on(1, core), "start")
    up_line.arrive(1)
    up_line.start(2)
    each(landing[4], "wait_recv")
    each(landing[5], "wait_recv")
    each(pass_on(2, core), "start")
    for step in early[1:-1]:
        up_line.arrive(step)
        up_line.start(step + 1)
    carries = [
        wire(cot_ref.at[:, :, lanes[0]], cot_x_ref, carry_send.at[0], carry_recv.at[0], to_x),
        wire(cot_ref.at[:, :, lanes[1]], cot_y_ref, carry_send.at[1], carry_recv.at[1], to_y),
    ]
    for copy in carries:
        copy.start()
    for line in lines:
        line.finish(range(1, count), True)
    for number in range(3):
        each(pass_on(number, 1 - core), "wait_recv")
    for _, landed_taps in tap_copies:
        landed_taps.wait_recv()
    halo_copy.wait_recv()
    saves = [
        pltpu.make_async_copy(here, there, local.at[2 + at])
        for at, (here, there) in enumerate(
            ((all_qk, all_qk_ref), (all_v, all_v_ref), (all_out, all_out_ref), (all_taps, all_taps_ref))
        )
    ]
    for copy in saves:
        copy.start()

    def chip(at, carry):
        weights = all_qk[at].reshape(4 * HD, depth)
        columns = pl.ds(pl.multiple_of(at * 4 * HD, 4 * HD), 4 * HD)
        for s in range(2):
            raw[s, :, columns] = dot_nt(rows[s], weights)
        return carry

    lax.fori_loop(0, count, chip, 0)
    lane = lax.broadcasted_iota(jnp.int32, (rows.shape[1], 128), 1)

    def two_heads(at, carry):
        weights = all_v[at].reshape(2 * HD, depth)
        zero, one = dot_nt(rows[0], weights), dot_nt(rows[1], weights)
        raw[2, :, head_lanes(2 * at)] = jnp.where(lane < HD, zero, pltpu.roll(one, HD, 1))
        raw[2, :, head_lanes(2 * at + 1)] = jnp.where(lane < HD, pltpu.roll(zero, HD, 1), one)
        return carry

    lax.fori_loop(0, count, two_heads, 0)
    save_raw = pltpu.make_async_copy(raw, raw_ref, local.at[6])
    save_raw.start()
    for plane_at in range(3):
        tap = all_taps.at[plane_at]

        def conv(at, carry, plane_at=plane_at, tap=tap):
            lanes_at = head_lanes(at)
            values = raw[plane_at, :, lanes_at]
            one = pltpu.roll(values, 1, 0)[halo:]
            two = pltpu.roll(values, 2, 0)[halo:]
            mixed[plane_at, :, lanes_at] = (
                tap[0:1, lanes_at] * values[halo:]
                + jnp.where(masks_ref[plane_at, 0] > 0.5, tap[1:2, lanes_at] * one, 0.0)
                + jnp.where(masks_ref[plane_at, 1] > 0.5, tap[2:3, lanes_at] * two, 0.0)
            ).astype(LOW)
            return carry

        lax.fori_loop(0, mp, conv, 0)

    def source(at):
        return mixed.at[:, :, head_lanes(at)]

    def target(at):
        return landed.at[:, at]

    own = pltpu.make_async_copy(source(me), target(me), local.at[7])
    own.start()
    copies = member_copies(source, target, head_send, head_recv)
    for copy, _ in copies:
        copy.start()
    up_line.arrive(early[-1])
    up_line.finish(early, True)
    save_up = pltpu.make_async_copy(up_all, up_all_ref, local.at[8])
    save_up.start()
    own.wait()
    for _, copy in copies:
        copy.wait_recv()
    save_heads = pltpu.make_async_copy(landed, o_ref, local.at[9])
    save_heads.start()
    for number in range(6):
        each(leaving[number], "wait_send")
    for number in range(3):
        each(pass_on(number, core), "wait_send")
    for copy, _ in tap_copies + copies:
        copy.wait_send()
    halo_copy.wait_send()
    for copy in carries:
        copy.wait()
    save.wait()
    for copy in saves:
        copy.wait()
    save_raw.wait()
    save_up.wait()
    save_heads.wait()


def front(inputs, gain, shift, qk, v, out, taps, up, masks, cot):
    mp = lax.axis_size("mp")
    count = mp // 2
    rows_here, depth = inputs.shape[1:]
    tall = rows_here + HALO
    anywhere = pl.BlockSpec(memory_space=pl.ANY)
    vmem = pl.BlockSpec(memory_space=pltpu.VMEM)
    dma = pltpu.SemaphoreType.DMA
    whole = [((count, 2) + part.shape, LOW) for part in (qk, v, out)]
    whole.append(((3, 8, mp * 128), F32))
    kept = [
        ((2, rows_here, depth), LOW),
        ((mp * up.shape[0], depth), LOW),
        ((3, tall, mp * 128), F32),
        ((3, mp, rows_here, 128), LOW),
        ((2, rows_here, depth // 2), LOW),
        ((2, rows_here, depth // 2), LOW),
    ]
    return pl.pallas_call(
        front_kernel,
        in_specs=[anywhere, vmem, vmem] + [anywhere] * 5 + [vmem, anywhere],
        out_specs=[anywhere] * 10,
        out_shape=[jax.ShapeDtypeStruct(*shape) for shape in whole + kept],
        scratch_shapes=[
            pltpu.VMEM(inputs.shape, LOW),
            pltpu.VMEM((2, tall, depth), LOW),
        ]
        + [pltpu.VMEM(*shape) for shape in whole]
        + [
            pltpu.VMEM(*kept[1]),
            pltpu.VMEM(*kept[2]),
            pltpu.VMEM((3, rows_here, mp * 128), LOW),
            pltpu.VMEM(*kept[3]),
            dma((10,)),
            dma((3, 6)),
            dma((3, 6)),
            dma((3, 3)),
            dma((3, 3)),
            dma((mp,)),
            dma((mp,)),
            dma,
            dma,
            dma((2,)),
            dma((2,)),
            dma((mp,)),
            dma((mp,)),
        ]
        + line_semaphores(count) * 4,
        compiler_params=pltpu.CompilerParams(
            collective_id=3, has_side_effects=True, vmem_limit_bytes=VMEM_LIMIT
        ),
        cost_estimate=pl.CostEstimate(flops=2**36, bytes_accessed=2**26, transcendentals=0),
        name="front",
    )(inputs, gain.reshape(1, depth), shift.reshape(1, depth), qk, v, out, taps, up, masks, cot)


def left_t_right(left, right):
    return lax.dot_general(left, right, (((0,), (0,)), ((), ())), preferred_element_type=F32)


def stream_out(steps, compute, buffer, ref, sem):
    def save(at, slot):
        return pltpu.make_async_copy(buffer.at[slot], ref.at[at], sem.at[slot])

    def one(at, carry):
        slot = lax.rem(at, 2)

        @pl.when(at >= 2)
        def _():
            save(at - 2, slot).wait()

        buffer[slot] = compute(at)
        save(at, slot).start()
        return carry

    lax.fori_loop(0, steps, one, 0)
    save(steps - 2, (steps - 2) % 2).wait()
    save(steps - 1, (steps - 1) % 2).wait()


def project_back_kernel(
    ways, x_ref, raw_ref, taps_ref, masks_ref, normed_ref, attended_ref, branch_ref, *refs
):
    carried, refs = list(zip(ways, refs[: len(ways)])), refs[len(ways) :]
    grad_ref, sums_ref, qk_part_ref, v_part_ref, out_part_ref = refs[:5]
    targets, refs = refs[5 : 5 + len(ways)], refs[5 + len(ways) :]
    landed, raw, wide, narrow, part_sem, local, send, recv, carry_send, carry_recv = refs
    me = lax.axis_index("mp")
    tall = landed.shape[1]
    rows_here = grad_ref.shape[1]
    halo = tall - rows_here
    heads = landed.shape[2] // 128

    def source(at):
        return x_ref.at[:, pl.ds(pl.multiple_of(at * rows_here, 16), tall), :]

    def target(at):
        return landed.at[:, :, head_lanes(at)]

    own = pltpu.make_async_copy(source(me), target(me), local.at[0])
    own.start()
    load = pltpu.make_async_copy(raw_ref, raw, local.at[1])
    load.start()
    greet_members(ways)
    copies = member_copies(source, target, send, recv)
    for leaving, _ in copies:
        leaving.start()
    carries = carry_copies(carried, targets, carry_send, carry_recv)
    for copy in carries:
        copy.start()

    def out_part(at):
        lanes = head_lanes(at)
        return (
            left_t_right(attended_ref[0, :, lanes], branch_ref[0])
            + left_t_right(attended_ref[1, :, lanes], branch_ref[1])
        ).astype(LOW)

    stream_out(heads // 2, out_part, narrow, out_part_ref, part_sem)
    own.wait()
    load.wait()
    for _, landing in copies:
        landing.wait_recv()
    for plane in range(3):
        tap = taps_ref.at[plane]

        def back(at, carry, plane=plane, tap=tap):
            lanes = head_lanes(at)
            grad = landed[plane, :, lanes].astype(F32)
            one = pltpu.roll(grad, tall - 1, 0)[:rows_here]
            two = pltpu.roll(grad, tall - 2, 0)[:rows_here]
            here = grad[:rows_here]
            grad_ref[plane, :, lanes] = (
                tap[0:1, lanes] * here
                + jnp.where(masks_ref[plane, 2] > 0.5, tap[1:2, lanes] * one, 0.0)
                + jnp.where(masks_ref[plane, 3] > 0.5, tap[2:3, lanes] * two, 0.0)
            ).astype(LOW)
            values = raw[plane, :, lanes]
            before = pltpu.roll(values, 1, 0)[halo:]
            before_two = pltpu.roll(values, 2, 0)[halo:]
            products = (
                here * values[halo:],
                jnp.where(masks_ref[plane, 0] > 0.5, here * before, 0.0),
                jnp.where(masks_ref[plane, 1] > 0.5, here * before_two, 0.0),
            )
            for row, product in enumerate(products):
                sums_ref[plane, row : row + 1, lanes] = jnp.sum(product, axis=0, keepdims=True)
            sums_ref[plane, 3:8, lanes] = jnp.zeros((5, 128), F32)
            return carry

        lax.fori_loop(0, heads, back, 0)

    def pair(at):
        return pl.ds(pl.multiple_of(at * 256, 256), 256)

    def qk_part(at):
        return (
            left_t_right(grad_ref[0, :, pair(at)], normed_ref[0])
            + left_t_right(grad_ref[1, :, pair(at)], normed_ref[1])
        ).astype(LOW)

    def v_part(at):
        side = grad_ref[2, :, pair(at)]
        zero, one = left_t_right(side, normed_ref[0]), left_t_right(side, normed_ref[1])
        return jnp.concatenate(
            [zero[:HD] + one[HD : 2 * HD], zero[2 * HD : 3 * HD] + one[3 * HD :]], axis=0
        ).astype(LOW)

    stream_out(heads // 2, qk_part, wide, qk_part_ref, part_sem)
    stream_out(heads // 2, v_part, narrow, v_part_ref, part_sem)
    for leaving, _ in copies:
        leaving.wait_send()
    for copy in carries:
        copy.wait()


def project_back(x, raw, taps, masks, normed, attended, branch, carried):
    mp = lax.axis_size("mp")
    rows_here, depth = normed.shape[1:]
    tall = raw.shape[1]
    anywhere = pl.BlockSpec(memory_space=pl.ANY)
    dma = pltpu.SemaphoreType.DMA
    vmem = pl.BlockSpec(memory_space=pltpu.VMEM)
    return pl.pallas_call(
        partial(project_back_kernel, tuple(way for way, _ in carried)),
        in_specs=[vmem, anywhere] + [vmem] * 5 + [anywhere] * len(carried),
        out_specs=[vmem] * 2 + [anywhere] * (3 + len(carried)),
        out_shape=[
            jax.ShapeDtypeStruct((3, rows_here, mp * 128), LOW),
            jax.ShapeDtypeStruct((3, 8, mp * 128), F32),
            jax.ShapeDtypeStruct((mp // 2, 4 * HD, depth), LOW),
            jax.ShapeDtypeStruct((mp // 2, 2 * HD, depth), LOW),
            jax.ShapeDtypeStruct((mp // 2, 2 * HD, depth), LOW),
        ]
        + [jax.ShapeDtypeStruct(block.shape, block.dtype) for _, block in carried],
        scratch_shapes=[
            pltpu.VMEM((3, tall, mp * 128), LOW),
            pltpu.VMEM((3, tall, mp * 128), F32),
            pltpu.VMEM((2, 4 * HD, depth), LOW),
            pltpu.VMEM((2, 2 * HD, depth), LOW),
            dma((2,)),
            dma((2,)),
            dma((mp,)),
            dma((mp,)),
            dma((len(carried),)),
            dma((len(carried),)),
        ],
        compiler_params=pltpu.CompilerParams(
            collective_id=7, has_side_effects=True, vmem_limit_bytes=VMEM_LIMIT
        ),
        cost_estimate=pl.CostEstimate(flops=2**35, bytes_accessed=2**24, transcendentals=0),
        name="project_back",
    )(x, raw, taps, masks, normed, attended, branch, *(block for _, block in carried))


def attended_kernel(x_ref, o_ref, landed, local, send, recv):
    me = lax.axis_index("mp")
    tall = o_ref.shape[1]

    def source(at):
        return x_ref.at[:, pl.ds(pl.multiple_of(at * tall, 16), tall), :]

    def target(at):
        return landed.at[:, :, head_lanes(at)]

    own = pltpu.make_async_copy(source(me), target(me), local.at[0])
    own.start()
    greet_members(())
    copies = member_copies(source, target, send, recv)
    for leaving, _ in copies:
        leaving.start()
    own.wait()
    for _, landing in copies:
        landing.wait_recv()
    save = pltpu.make_async_copy(landed, o_ref, local.at[1])
    save.start()
    for leaving, _ in copies:
        leaving.wait_send()
    save.wait()


def attended_back(x, rows_here):
    mp = lax.axis_size("mp")
    shape = (x.shape[0], rows_here, mp * 128)
    dma = pltpu.SemaphoreType.DMA
    return pl.pallas_call(
        attended_kernel,
        in_specs=[pl.BlockSpec(memory_space=pltpu.VMEM)],
        out_specs=pl.BlockSpec(memory_space=pl.ANY),
        out_shape=jax.ShapeDtypeStruct(shape, x.dtype),
        scratch_shapes=[pltpu.VMEM(shape, x.dtype), dma((2,)), dma((mp,)), dma((mp,))],
        compiler_params=pltpu.CompilerParams(
            collective_id=5, has_side_effects=True, vmem_limit_bytes=48 * 2**20
        ),
        cost_estimate=pl.CostEstimate(flops=2**34, bytes_accessed=2**24, transcendentals=0),
        name="attended_back",
    )(x)


def line_blocks(place, sources, local, send, recv):
    z, core = mesh_place()
    count = lax.axis_size("mp") // 2
    out = []
    for number, (step, way, ref) in enumerate(sources):
        at = z - way * step
        there = (at >= 0) & (at < count)
        at = jnp.clip(at, 0, count - 1)
        sems = (send.at[number], recv.at[number], other_core())
        out.append(
            (
                there,
                pltpu.make_async_copy(ref, place(at, core), local.at[number]),
                wire(ref, place(at, core), *sems),
                wire(ref, place(at, 1 - core), *sems),
            )
        )
    return out


def feed_in_kernel(
    late, second_ref, up_ref, down_ref, cot_0, cot_1, cot_2, cot_3, cot_4, cot_5, cot_6, *refs
):
    late_sources = [(step, way, ref) for (step, way), ref in zip(late, refs)]
    (
        all_ref, relu_ref, hidden_ref, down_all_ref, up_all_ref, down_part_ref,
        rows, up, relu, hidden, down, cot, tiles, sums, before, local, outs, send, recv, cot_sem, tile_sem, sum_sem,
        before_sem, late_local, late_send, late_recv, *line_sems,
    ) = refs[len(late) :]
    count = lax.axis_size("mp") // 2
    depth = rows.shape[3]
    units = up.shape[0]
    share = down_ref.shape[0]
    z, core = mesh_place()
    lanes = (pl.ds(0, depth // 2), pl.ds(depth // 2, depth // 2))
    to_x, to_y = plane_partners()
    pieces = (cot_0, cot_1, cot_2, cot_3, cot_4, cot_5, cot_6)

    def line_place(ref):
        return lambda at, at_core: ref.at[
            pl.ds(pl.multiple_of((2 * at + at_core) * share, 16), share), :
        ]

    own = [pltpu.make_async_copy(second_ref.at[s], rows.at[s, 0], local.at[s]) for s in range(2)]
    own.append(pltpu.make_async_copy(up_ref, up, local.at[2]))
    own.append(pltpu.make_async_copy(down_ref, line_place(down)(z, core), local.at[3]))
    for copy in own:
        copy.start()
    for copy in own:
        copy.wait()
    greet_line(True)
    late_blocks = line_blocks(line_place(up), late_sources, late_local, late_send, late_recv)
    down_line = LineGather(line_place(down), *line_sems)

    def remote(s, source, target, half, partner, number):
        return wire(
            rows.at[s, source, :, lanes[half]], rows.at[s, target, :, lanes[half]],
            send.at[s, number], recv.at[s, number], partner,
        )

    copies = [
        [
            remote(s, 0, 1, 0, to_x, 0),
            remote(s, 0, 2, 1, to_y, 1),
            remote(s, 0, 2, 0, to_y, 2),
            remote(s, 0, 1, 1, to_x, 3),
            remote(s, 1, 3, 0, to_y, 4),
            remote(s, 2, 3, 1, to_x, 5),
        ]
        for s in range(2)
    ]
    pending = [None, None]
    done = [0]

    def settle(slot):
        if pending[slot] is not None:
            for copy in pending[slot]:
                copy.wait()
        pending[slot] = None

    def tile(s, m):
        slot = done[0] % 2
        done[0] += 1
        settle(slot)

        def one(at, carry):
            columns = pl.ds(pl.multiple_of(at * CHUNK, CHUNK), CHUNK)
            kept = jnp.maximum(dot_nt(rows[s, m], up[columns, :]), 0.0)
            relu[slot, :, columns] = kept
            hidden[slot, :, columns] = (kept * kept).astype(LOW)
            return carry

        lax.fori_loop(0, units // CHUNK, one, 0)
        pending[slot] = [
            pltpu.make_async_copy(relu.at[slot], relu_ref.at[s, m], outs.at[slot, 0]),
            pltpu.make_async_copy(hidden.at[slot], hidden_ref.at[s, m], outs.at[slot, 1]),
        ]
        for copy in pending[slot]:
            copy.start()

    for number in range(4):
        copies[0][number].start()
    for there, here, leaving, _ in late_blocks:

        @pl.when(there)
        def _(here=here, leaving=leaving):
            here.start()
            leaving.start()

    down_line.start(1)
    down_line.swap_own()

    def cot_loads(s):
        copies = []
        for m in range(4):
            copies += piece_copies(pieces, s, m, cot.at[m], cot_sem.at[m])
        return copies

    for copy in cot_loads(0):
        copy.start()
    for there, here, leaving, landing in late_blocks:

        @pl.when(there)
        def _(here=here, leaving=leaving, landing=landing):
            here.wait()
            leaving.wait_send()
            landing.wait_recv()

    whole_up = pltpu.make_async_copy(up, up_all_ref, local.at[2])
    whole_up.start()
    tile(0, 0)
    copies[0][0].wait_recv()
    copies[0][4].start()
    copies[0][1].wait_recv()
    copies[0][5].start()
    copies[1][0].start()
    copies[1][1].start()
    tile(1, 0)
    down_line.arrive(1)
    down_line.start(2)
    copies[0][3].wait_recv()
    tile(0, 1)
    copies[0][2].wait_recv()
    copies[1][2].start()
    copies[1][3].start()
    tile(0, 2)
    copies[1][0].wait_recv()
    copies[1][4].start()
    copies[1][1].wait_recv()
    copies[1][5].start()
    copies[0][4].wait_recv()
    copies[0][5].wait_recv()
    tile(0, 3)
    for step in range(3, count):
        down_line.arrive(step - 1)
        down_line.start(step)
    settle(0)
    settle(1)
    for copy in cot_loads(0):
        copy.wait()
    gradient_tiles(hidden_ref.at[0], cot, tiles, sums, down_part_ref, tile_sem, sum_sem)
    for copy in cot_loads(1):
        copy.start()
    copies[1][3].wait_recv()
    tile(1, 1)
    copies[1][2].wait_recv()
    tile(1, 2)
    copies[1][4].wait_recv()
    copies[1][5].wait_recv()
    gathered = pltpu.make_async_copy(rows, all_ref, local.at[0])
    gathered.start()
    tile(1, 3)
    down_line.arrive(count - 1)
    down_line.finish(range(1, count), True)
    whole_down = pltpu.make_async_copy(down, down_all_ref, local.at[1])
    whole_down.start()
    settle(0)
    settle(1)
    for copy in cot_loads(1):
        copy.wait()
    gradient_tiles(
        hidden_ref.at[1], cot, tiles, sums, down_part_ref, tile_sem, sum_sem,
        (down_part_ref, before, before_sem),
    )
    for s in range(2):
        for copy in copies[s]:
            copy.wait_send()
    gathered.wait()
    whole_up.wait()
    whole_down.wait()


def gradient_tiles(
    left_ref, right, tiles, sums, out_ref, tile_sem, sum_sem, before=None, span=None
):
    wide = tiles.shape[-1]
    first, steps = span if span is not None else (0, left_ref.shape[-1] // wide)
    lead = (slice(None),) * (len(left_ref.shape) - 1)
    tall = math.prod(tiles.shape[1:-1])

    def load(at, slot):
        columns = pl.ds(pl.multiple_of(at * wide, wide), wide)
        return pltpu.make_async_copy(
            left_ref.at[lead + (columns,)], tiles.at[slot], tile_sem.at[slot]
        )

    def rows_of(at):
        return pl.ds(pl.multiple_of(at * wide, wide), wide)

    def save(at, slot):
        return pltpu.make_async_copy(sums.at[slot], out_ref.at[rows_of(at), :], sum_sem.at[slot])

    def load_before(at, slot):
        before_ref, buffer, sem = before
        return pltpu.make_async_copy(before_ref.at[rows_of(at), :], buffer.at[slot], sem.at[slot])

    load(first, first % 2).start()
    if before is not None:
        load_before(first, first % 2).start()

    def one(at, carry):
        slot = lax.rem(at, 2)
        load(at, slot).wait()
        if before is not None:
            load_before(at, slot).wait()

        @pl.when(at + 1 < steps)
        def _():
            load(at + 1, 1 - slot).start()
            if before is not None:
                load_before(at + 1, 1 - slot).start()

        @pl.when(at >= first + 2)
        def _():
            save(at - 2, slot).wait()

        result = lax.dot_general(
            tiles[slot].reshape(tall, wide),
            right[...].reshape(tall, right.shape[-1]),
            (((0,), (0,)), ((), ())),
            preferred_element_type=F32,
        )
        if before is not None:
            result = result + before[1][slot].astype(F32)
        sums[slot] = result.astype(LOW)
        save(at, slot).start()
        return carry

    lax.fori_loop(first, steps, one, 0)
    save(steps - 2, (steps - 2) % 2).wait()
    save(steps - 1, (steps - 1) % 2).wait()


def feed_in(second, up_early, down, cot_pieces, up_late):
    rows_here, depth = second.shape[1:]
    units = up_early.shape[0]
    count = lax.axis_size("mp") // 2
    anywhere = pl.BlockSpec(memory_space=pl.ANY)
    dma = pltpu.SemaphoreType.DMA
    return pl.pallas_call(
        partial(feed_in_kernel, tuple(up_late)),
        in_specs=[anywhere] * (10 + len(up_late)),
        out_specs=[anywhere] * 6,
        out_shape=[
            jax.ShapeDtypeStruct((2, 4, rows_here, depth), LOW),
            jax.ShapeDtypeStruct((2, 4, rows_here, units), F32),
            jax.ShapeDtypeStruct((2, 4, rows_here, units), LOW),
            jax.ShapeDtypeStruct((units, depth), LOW),
            jax.ShapeDtypeStruct((units, depth), LOW),
            jax.ShapeDtypeStruct((units, depth), LOW),
        ],
        scratch_shapes=[
            pltpu.VMEM((2, 4, rows_here, depth), LOW),
            pltpu.VMEM((units, depth), LOW),
            pltpu.VMEM((2, rows_here, units), F32),
            pltpu.VMEM((2, rows_here, units), LOW),
            pltpu.VMEM((units, depth), LOW),
            pltpu.VMEM((4, rows_here, depth), LOW),
            pltpu.VMEM((2, 4, rows_here, WIDE), LOW),
            pltpu.VMEM((2, WIDE, depth), LOW),
            pltpu.VMEM((2, WIDE, depth), LOW),
            dma((4,)),
            dma((2, 2)),
            dma((2, 6)),
            dma((2, 6)),
            dma((4, 2)),
            dma((2,)),
            dma((2,)),
            dma((2,)),
        ]
        + [dma((len(up_late),))] * 3
        + line_semaphores(count),
        compiler_params=pltpu.CompilerParams(
            collective_id=1, has_side_effects=True, vmem_limit_bytes=VMEM_LIMIT
        ),
        cost_estimate=pl.CostEstimate(
            flops=2 * 8 * rows_here * depth * units * 3,
            bytes_accessed=60 * 2**20,
            transcendentals=0,
        ),
        name="feed_in",
    )(second, up_early, down, *cot_pieces, *up_late.values())


def piece_copies(pieces, s, m, target, sems):
    half = target.shape[-1] // 2
    if m == 0:
        return [pltpu.make_async_copy(pieces[0].at[s], target, sems.at[0])]
    return [
        pltpu.make_async_copy(
            pieces[2 * m - 1 + side].at[s], target.at[:, pl.ds(side * half, half)], sems.at[side]
        )
        for side in range(2)
    ]


def feed_out_kernel(
    cot_0, cot_1, cot_2, cot_3, cot_4, cot_5, cot_6, relu_ref, second_ref, up_ref, down_ref,
    grad_ref, up_part_ref, back_ref,
    up, shared, cot, relu, grad, part, arrived, tiles, sums, result, local, loads, outs, send, recv,
    tile_sem, sum_sem,
):
    units, depth = up.shape
    down = shared.at[pl.ds(0, units), :]
    second = shared.at[pl.ds(0, 8 * cot.shape[1]), :]
    half = depth // 2
    lanes = (pl.ds(0, half), pl.ds(half, half))
    to_x, to_y = plane_partners()
    weights = [
        pltpu.make_async_copy(down_ref, down, local.at[0]),
        pltpu.make_async_copy(up_ref, up, local.at[1]),
    ]
    order = [(s, m) for s in range(2) for m in (3, 1, 2, 0)]
    pieces = (cot_0, cot_1, cot_2, cot_3, cot_4, cot_5, cot_6)

    def load(at):
        s, m = order[at]
        slot = at % 2
        return piece_copies(pieces, s, m, cot.at[slot], loads.at[slot]) + [
            pltpu.make_async_copy(relu_ref.at[s, m], relu.at[slot], loads.at[slot, 2]),
        ]

    for copy in load(0) + weights:
        copy.start()
    greet([to_x, to_y])
    for copy in weights:
        copy.wait()
    def remote(s, source, number, side, partner):
        return pltpu.make_async_remote_copy(
            src_ref=part.at[s, source, :, lanes[side]],
            dst_ref=arrived.at[s, number],
            send_sem=send.at[s, number],
            recv_sem=recv.at[s, number],
            device_id=partner,
            device_id_type=MESH,
        )

    copies = [
        [
            remote(s, 1, 0, 0, to_x),
            remote(s, 3, 1, 0, to_x),
            remote(s, 2, 2, 1, to_y),
            remote(s, 3, 3, 1, to_y),
            remote(s, 2, 4, 0, to_y),
            remote(s, 1, 5, 1, to_x),
        ]
        for s in range(2)
    ]
    saving = [None, None]
    load_second = pltpu.make_async_copy(second_ref, second, local.at[0])

    def tile(at):
        s, m = order[at]
        slot = at % 2
        for copy in load(at):
            copy.wait()
        if at + 1 < len(order):
            for copy in load(at + 1):
                copy.start()
        if saving[slot] is not None:
            saving[slot].wait()

        def back(step, carry):
            columns = pl.ds(pl.multiple_of(step * CHUNK, CHUNK), CHUNK)
            product = dot_nt(cot[slot], down[columns, :])
            grad[slot, :, columns] = (product * 2.0 * relu[slot, :, columns]).astype(LOW)
            return carry

        lax.fori_loop(0, units // CHUNK, back, 0)
        if at + 1 == len(order):
            load_second.start()
        saving[slot] = pltpu.make_async_copy(grad.at[slot], grad_ref.at[s, m], outs.at[slot])
        saving[slot].start()

        def through(step, carry):
            columns = pl.ds(pl.multiple_of(step * CHUNK, CHUNK), CHUNK)
            part[s, m, :, columns] = dot(grad[slot], up[:, columns]).astype(LOW)
            return carry

        lax.fori_loop(0, depth // CHUNK, through, 0)

    def second_leg(s):
        copies[s][1].wait_recv()
        part[s, 2, :, lanes[0]] = (
            part[s, 2, :, lanes[0]].astype(F32) + arrived[s, 1].astype(F32)
        ).astype(LOW)
        copies[s][4].start()
        copies[s][3].wait_recv()
        part[s, 1, :, lanes[1]] = (
            part[s, 1, :, lanes[1]].astype(F32) + arrived[s, 3].astype(F32)
        ).astype(LOW)
        copies[s][5].start()

    def finish(s):
        for side, near, last in ((0, 0, 4), (1, 2, 5)):
            copies[s][near].wait_recv()
            copies[s][last].wait_recv()
            result[:, lanes[side]] = (
                part[s, 0, :, lanes[side]].astype(F32)
                + arrived[s, near].astype(F32)
                + arrived[s, last].astype(F32)
            )
        done = pltpu.make_async_copy(result, back_ref.at[s], local.at[2])
        done.start()
        return done

    def send_after(at):
        s, m = order[at]
        for number in {3: (1, 3), 1: (0,), 2: (2,), 0: ()}[m]:
            copies[s][number].start()

    for at in range(5):
        tile(at)
        send_after(at)
    second_leg(0)
    for at in range(5, 8):
        tile(at)
        send_after(at)
    done = finish(0)

    for slot in range(2):
        saving[slot].wait()
    load_second.wait()
    halves = units // WIDE // 2

    def some(span):
        gradient_tiles(grad_ref, second, tiles, sums, up_part_ref, tile_sem, sum_sem, span=span)

    some((0, halves))
    second_leg(1)
    some((halves, 2 * halves))
    done.wait()
    finish(1).wait()
    for s in range(2):
        for number in range(6):
            copies[s][number].wait_send()


def feed_out(cot_pieces, relu, second_all, up_all, down_all):
    rows_here, units = relu.shape[2:]
    depth = up_all.shape[1]
    anywhere = pl.BlockSpec(memory_space=pl.ANY)
    dma = pltpu.SemaphoreType.DMA
    return pl.pallas_call(
        feed_out_kernel,
        in_specs=[anywhere] * 11,
        out_specs=[anywhere] * 3,
        out_shape=[
            jax.ShapeDtypeStruct((2, 4, rows_here, units), LOW),
            jax.ShapeDtypeStruct((units, depth), LOW),
            jax.ShapeDtypeStruct((2, rows_here, depth), F32),
        ],
        scratch_shapes=[
            pltpu.VMEM((units, depth), LOW),
            pltpu.VMEM((max(units, 8 * rows_here), depth), LOW),
            pltpu.VMEM((2, rows_here, depth), LOW),
            pltpu.VMEM((2, rows_here, units), F32),
            pltpu.VMEM((2, rows_here, units), LOW),
            pltpu.VMEM((2, 4, rows_here, depth), LOW),
            pltpu.VMEM((2, 6, rows_here, depth // 2), LOW),
            pltpu.VMEM((2, 2, 4, rows_here, WIDE), LOW),
            pltpu.VMEM((2, WIDE, depth), LOW),
            pltpu.VMEM((rows_here, depth), F32),
            dma((3,)),
            dma((2, 3)),
            dma((2,)),
            dma((2, 6)),
            dma((2, 6)),
            dma((2,)),
            dma((2,)),
        ],
        compiler_params=pltpu.CompilerParams(
            collective_id=2, has_side_effects=True, vmem_limit_bytes=VMEM_LIMIT
        ),
        cost_estimate=pl.CostEstimate(
            flops=2 * 8 * rows_here * depth * units * 4,
            bytes_accessed=60 * 2**20,
            transcendentals=0,
        ),
        name="feed_out",
    )(*cot_pieces, relu, second_all.reshape(8 * rows_here, depth), up_all, down_all)


def feed_heads_kernel(
    x_ref, hidden_ref, down_ref,
    o_ref, feed_x0_ref, feed_x1_ref, feed_y0_ref, feed_y1_ref, keep_a_ref, keep_b_ref,
    landed, down, hidden, feed, local, send, recv, loads, outs,
):
    me = lax.axis_index("mp")
    units, depth = down.shape
    half = depth // 2
    lanes = (pl.ds(0, half), pl.ds(half, half))
    feed_x_refs, feed_y_refs = (feed_x0_ref, feed_x1_ref), (feed_y0_ref, feed_y1_ref)

    def source(at):
        return x_ref.at[:, :, head_lanes(at)]

    def target(at):
        return landed.at[:, at]

    weights = pltpu.make_async_copy(down_ref, down, local.at[2])
    weights.start()
    own = pltpu.make_async_copy(source(me), target(me), local.at[0])
    own.start()
    greet_members(())
    copies = member_copies(source, target, send, recv)
    for leaving, _ in copies:
        leaving.start()
    order = [(s, m) for s in range(2) for m in (3, 1, 2, 0)]

    def load(at):
        s, m = order[at]
        return pltpu.make_async_copy(hidden_ref.at[s, m], hidden.at[at % 2], loads.at[at % 2])

    load(0).start()
    weights.wait()
    feeding = [None, None]
    for at, (s, m) in enumerate(order):
        slot = at % 2
        load(at).wait()
        if at + 1 < len(order):
            load(at + 1).start()
        if feeding[slot] is not None:
            for copy in feeding[slot]:
                copy.wait()

        def one(step, carry, slot=slot):
            columns = pl.ds(pl.multiple_of(step * CHUNK, CHUNK), CHUNK)
            feed[slot, :, columns] = dot(hidden[slot], down[:, columns]).astype(LOW)
            return carry

        lax.fori_loop(0, depth // CHUNK, one, 0)
        targets = (
            (keep_a_ref.at[s, 0], feed_x_refs[s].at[0], keep_a_ref.at[s, 1], feed_x_refs[s].at[1])[m],
            (keep_b_ref.at[s, 0], keep_b_ref.at[s, 1], feed_y_refs[s].at[0], feed_y_refs[s].at[1])[m],
        )
        feeding[slot] = [
            pltpu.make_async_copy(feed.at[slot, :, lanes[side]], there, outs.at[slot, side])
            for side, there in enumerate(targets)
        ]
        for copy in feeding[slot]:
            copy.start()
    own.wait()
    for _, landing in copies:
        landing.wait_recv()
    save = pltpu.make_async_copy(landed, o_ref, local.at[1])
    save.start()
    for leaving, _ in copies:
        leaving.wait_send()
    for slot in feeding:
        for copy in slot:
            copy.wait()
    save.wait()


def feed_heads(x, hidden, down_all):
    parts, rows_here, width = x.shape
    mp = lax.axis_size("mp")
    units, depth = down_all.shape
    anywhere = pl.BlockSpec(memory_space=pl.ANY)
    dma = pltpu.SemaphoreType.DMA
    shape = (parts, mp, rows_here, 128)
    out, *terms = pl.pallas_call(
        feed_heads_kernel,
        in_specs=[pl.BlockSpec(memory_space=pltpu.VMEM)] + [anywhere] * 2,
        out_specs=[anywhere] * 7,
        out_shape=[jax.ShapeDtypeStruct(shape, LOW)]
        + [jax.ShapeDtypeStruct((2, rows_here, depth // 2), LOW)] * 4
        + [jax.ShapeDtypeStruct((2, 2, rows_here, depth // 2), LOW)] * 2,
        scratch_shapes=[
            pltpu.VMEM(shape, LOW),
            pltpu.VMEM((units, depth), LOW),
            pltpu.VMEM((2, rows_here, units), LOW),
            pltpu.VMEM((2, rows_here, depth), LOW),
            dma((3,)),
            dma((mp,)),
            dma((mp,)),
            dma((2,)),
            dma((2, 2)),
        ],
        compiler_params=pltpu.CompilerParams(
            collective_id=6, has_side_effects=True, vmem_limit_bytes=48 * 2**20
        ),
        cost_estimate=pl.CostEstimate(flops=2**35, bytes_accessed=2**24, transcendentals=0),
        name="feed_heads",
    )(x, hidden, down_all)
    return [out.reshape(parts, mp * rows_here, 128)] + terms


def finish_kernel(
    ways, qk_ref, v_ref, out_ref, norms_ref, taps_ref, grad_raw_ref, inputs_ref, gain_ref,
    qk_all_ref, v_all_ref, middle_ref, *refs
):
    carried, refs = list(zip(ways, refs[: len(ways)])), refs[len(ways) :]
    joint_ref, norms_sum_ref, taps_sum_ref, input_grad_ref = refs[:4]
    targets, refs = refs[4 : 4 + len(ways)], refs[4 + len(ways) :]
    (
    acc, got, plane_in, line_in, gathered, norms_all, taps_all, norms_dp, taps_dp,
    weights, result, middle, norms, sums, weight_sem,
    local, swap_send, swap_recv, plane_send_sem, plane_recv_sem, line_send_sem, line_recv_sem,
    gather_send, gather_recv, small_send, small_recv, carry_send, carry_recv,
    ) = refs
    mp = lax.axis_size("mp")
    dp = lax.axis_index("dp")
    me = lax.axis_index("mp")
    z, core = mesh_place()
    count = mp // 2
    depth = acc.shape[3]
    half = depth // 2
    lanes = (pl.ds(0, half), pl.ds(half, half))
    to_x, to_y = plane_partners()
    dp_x = dp + 1 - 2 * lax.rem(dp, 2)
    dp_y = dp + 2 - 4 * (dp // 2)
    dp_xy = dp_x + 2 - 4 * (dp_x // 2)
    parts = (qk_ref, v_ref, out_ref)
    spans = (pl.ds(0, HD // 2), pl.ds(HD // 2, HD // 4), pl.ds(3 * HD // 4, HD // 4))
    loads = [
        pltpu.make_async_copy(part.at[:, core], acc.at[:, :, span, :], local.at[at])
        for at, (part, span) in enumerate(zip(parts, spans))
    ]
    for copy in loads:
        copy.start()

    barrier = pltpu.get_barrier_semaphore()
    for step in range(1, mp):
        pl.semaphore_signal(
            barrier, inc=1, device_id={"mp": lax.rem(me + step, mp)}, device_id_type=MESH
        )
    for step in range(1, 4):
        pl.semaphore_signal(
            barrier, inc=1, device_id={"dp": lax.rem(dp + step, 4)}, device_id_type=MESH
        )
    pl.semaphore_wait(barrier, mp + 2)

    swaps = [
        [
            wire(
                part.at[:, 1 - core, quarter], got.at[:, quarter, span, :],
                swap_send.at[at, number], swap_recv.at[at, number], other_core(),
            )
            for at, (part, span) in enumerate(zip(parts, spans))
        ]
        for number, quarter in enumerate((dp_xy, dp_x, dp_y, dp))
    ]
    for group in swaps:
        for copy in group:
            copy.start()

    def small(axis, at, others, source, target, number, first):
        out = []
        for step in range(1, others):
            to = lax.rem(at + step, others)
            frm = lax.rem(at + others - step, others)
            sems = (small_send.at[number, step], small_recv.at[number, step], {axis: to})
            out.append((wire(source(to), target.at[at], *sems), wire(source(to), target.at[frm], *sems)))
        return out

    load_middle = pltpu.make_async_copy(middle_ref, middle, local.at[6])
    load_middle.start()
    own_small = [
        pltpu.make_async_copy(norms, norms_all.at[me], local.at[3]),
        pltpu.make_async_copy(taps_ref.at[me], taps_all.at[me], local.at[4]),
    ]
    over_mp = small("mp", me, mp, lambda to: norms, norms_all, 0, None) + small(
        "mp", me, mp, lambda to: taps_ref.at[to], taps_all, 1, None
    )

    rows_here = inputs_ref.shape[1]
    slots = weights.shape[0]

    def load_weights(at, slot):
        return [
            pltpu.make_async_copy(
                qk_all_ref.at[at], weights.at[slot, pl.ds(0, 4 * HD), :], weight_sem.at[slot, 0]
            )
        ] + [
            pltpu.make_async_copy(
                v_all_ref.at[at, pl.ds(head * HD, HD), :],
                weights.at[slot, pl.ds((4 + 2 * head + copy) * HD, HD), :],
                weight_sem.at[slot, 1 + 2 * head + copy],
            )
            for head in range(2)
            for copy in range(2)
        ]

    def normed_grad():
        if slots == 2:
            for copy in load_weights(0, 0):
                copy.start()
        lane = lax.rem(lax.broadcasted_iota(jnp.int32, (rows_here, 4 * HD), 1), 2 * HD)

        def one(at, carry):
            slot = lax.rem(at, slots)
            if slots == 1:
                for copy in load_weights(at, slot):
                    copy.start()
            for copy in load_weights(at, slot):
                copy.wait()
            if slots == 2:

                @pl.when(at + 1 < count)
                def _():
                    for copy in load_weights(at + 1, 1 - slot):
                        copy.start()

            pair = pl.ds(pl.multiple_of(at * 4 * HD, 4 * HD), 4 * HD)
            side = grad_raw_ref[2, :, pair]
            for s in range(2):
                mine = lane < HD if s == 0 else lane >= HD
                left = jnp.concatenate(
                    [grad_raw_ref[s, :, pair], jnp.where(mine, side, jnp.zeros_like(side))], axis=1
                )
                for first in range(0, depth, CHUNK):
                    columns = pl.ds(first, CHUNK)
                    product = dot(left, weights[slot, :, columns])

                    @pl.when(at == 0)
                    def _(s=s, columns=columns, product=product):
                        result[s, :, columns] = product

                    @pl.when(at > 0)
                    def _(s=s, columns=columns, product=product):
                        result[s, :, columns] += product

            return carry

        lax.fori_loop(0, count, one, 0)

    tall = 16
    tiles = rows_here // tall

    def norm_back(s, first, last):
        def some(at, carry):
            here = pl.ds(pl.multiple_of(at * tall, tall), tall)
            values = inputs_ref[s, here, :].astype(F32)
            centered = values - jnp.mean(values, axis=1, keepdims=True)
            scale = lax.rsqrt(jnp.mean(centered * centered, axis=1, keepdims=True) + 1e-05)
            hat = centered * scale
            grad = result[s, here, :]
            wide = grad * gain_ref[...]
            back = wide - jnp.mean(wide, axis=1, keepdims=True)
            back = scale * (back - hat * jnp.mean(wide * hat, axis=1, keepdims=True))
            result[s, here, :] = middle[s, here, :] + back
            product = grad * hat
            sums[0] += product[:8] + product[8:]
            sums[1] += grad[:8] + grad[8:]
            return carry

        lax.fori_loop(first, last, some, 0)

    def add(quarter, side, number):
        acc[:, quarter, :, lanes[side]] = (
            acc[:, quarter, :, lanes[side]].astype(F32) + plane_in[number].astype(F32)
        ).astype(LOW)

    def add_core(number, quarter):
        for copy in swaps[number]:
            copy.wait_recv()
        acc[:, quarter] = (acc[:, quarter].astype(F32) + got[:, quarter].astype(F32)).astype(LOW)

    def plane(quarter, side, partner, number):
        return wire(
            acc.at[:, quarter, :, lanes[side]], plane_in.at[number],
            plane_send_sem.at[number], plane_recv_sem.at[number], partner,
        )

    sends = [
        plane(dp_x, 0, to_x, 0),
        plane(dp_xy, 0, to_x, 1),
        plane(dp_y, 1, to_y, 2),
        plane(dp_xy, 1, to_y, 3),
        plane(dp_y, 0, to_y, 4),
        plane(dp_x, 1, to_x, 5),
    ]
    for copy in loads:
        copy.wait()
    add_core(0, dp_xy)
    sends[1].start()
    sends[3].start()
    add_core(1, dp_x)
    sends[0].start()
    add_core(2, dp_y)
    sends[2].start()
    add_core(3, dp)
    normed_grad()
    load_middle.wait()
    sums[...] = jnp.zeros(sums.shape, F32)
    norm_back(0, 0, tiles)
    saved_rows = [
        pltpu.make_async_copy(result.at[s], input_grad_ref.at[s], local.at[7 + s]) for s in range(2)
    ]
    saved_rows[0].start()
    sends[1].wait_recv()
    add(dp_y, 0, 1)
    sends[4].start()
    sends[3].wait_recv()
    add(dp_x, 1, 3)
    sends[5].start()
    norm_back(1, 0, tiles // 2)
    sends[0].wait_recv()
    add(dp, 0, 0)
    sends[2].wait_recv()
    add(dp, 1, 2)
    sends[4].wait_recv()
    add(dp, 0, 4)
    sends[5].wait_recv()
    add(dp, 1, 5)

    carries = carry_copies(carried, targets, carry_send, carry_recv)
    for copy in carries:
        copy.start()

    def line(step):
        out = []
        for way, turn in enumerate((1, -1)):
            target = z + turn * (count - step)
            far = z + turn
            lands = far - 2 * turn + turn * (count - step)
            sends = (target >= 0) & (target < count)
            receives = (lands >= 0) & (lands < count) & (z - turn >= 0) & (z - turn < count)
            at = jnp.clip(target, 0, count - 1)
            to = jnp.clip(lands, 0, count - 1)
            copy = wire(
                acc.at[at, dp], line_in.at[way, step - 1],
                line_send_sem.at[way, step - 1], line_recv_sem.at[way, step - 1],
                line_partner(z, turn),
            )
            out.append((sends, receives, to, copy))
        return out

    over_dp = []
    for step in range(1, count):
        legs = line(step)
        for sends_now, _, _, copy in legs:
            pl.when(sends_now)(copy.start)
        if step == 1:
            norm_back(1, tiles // 2, tiles)
            saved_rows[1].start()
            norms[...] = norms_ref[...]
            norms[0:1, :] = jnp.sum(sums[0], axis=0, keepdims=True)
            norms[1:2, :] = jnp.sum(sums[1], axis=0, keepdims=True)
            for copy in own_small:
                copy.start()
            for leaving, _ in over_mp:
                leaving.start()
        if step == count - 1:
            for _, landed in over_mp:
                landed.wait_recv()
            for copy in own_small:
                copy.wait()
            norms_dp[dp] = jnp.sum(norms_all[...], axis=0)
            taps_dp[dp] = jnp.sum(taps_all[...], axis=0)
            over_dp = small("dp", dp, 4, lambda to: norms_dp.at[dp], norms_dp, 2, None) + small(
                "dp", dp, 4, lambda to: taps_dp.at[dp], taps_dp, 3, None
            )
            for leaving, _ in over_dp:
                leaving.start()
        for way, (_, receives, to, copy) in enumerate(legs):

            @pl.when(receives)
            def _(to=to, copy=copy, way=way):
                copy.wait_recv()
                acc[to, dp] = (
                    acc[to, dp].astype(F32) + line_in[way, step - 1].astype(F32)
                ).astype(LOW)

    gathered[dp] = acc[z, dp]

    def gather(quarter, side, partner, number):
        block = gathered.at[quarter, :, lanes[side]]
        return wire(block, block, gather_send.at[number], gather_recv.at[number], partner)

    leaving = [
        gather(dp, 0, to_x, 0), gather(dp, 1, to_y, 1), gather(dp, 0, to_y, 2), gather(dp, 1, to_x, 3),
        gather(dp_x, 0, to_y, 4), gather(dp_y, 1, to_x, 5),
    ]
    landing = [
        gather(dp_x, 0, to_x, 0), gather(dp_y, 1, to_y, 1), gather(dp_y, 0, to_y, 2), gather(dp_x, 1, to_x, 3),
        gather(dp_xy, 0, to_y, 4), gather(dp_xy, 1, to_x, 5),
    ]
    for number in range(4):
        leaving[number].start()
    for _, landed in over_dp:
        landed.wait_recv()
    norms_sum_ref[...] = jnp.sum(norms_dp[...], axis=0)
    taps_sum_ref[...] = jnp.sum(taps_dp[...], axis=0)
    landing[0].wait_recv()
    leaving[4].start()
    landing[1].wait_recv()
    leaving[5].start()
    for number in range(2, 6):
        landing[number].wait_recv()
    save = pltpu.make_async_copy(gathered, joint_ref, local.at[5])
    save.start()
    for group in swaps:
        for copy in group:
            copy.wait_send()
    for copy in sends:
        copy.wait_send()
    for step in range(1, count):
        for sends_now, _, _, copy in line(step):
            pl.when(sends_now)(copy.wait_send)
    for copy in leaving:
        copy.wait_send()
    for copy, _ in over_mp + over_dp:
        copy.wait_send()
    for copy in carries + saved_rows:
        copy.wait()
    save.wait()


def finish(qk, v, out, norms, taps, grad_raw, inputs, gain, qk_all, v_all, middle, carried):
    mp = lax.axis_size("mp")
    count = mp // 2
    depth = qk.shape[-1]
    anywhere = pl.BlockSpec(memory_space=pl.ANY)
    vmem = pl.BlockSpec(memory_space=pltpu.VMEM)
    dma = pltpu.SemaphoreType.DMA
    return pl.pallas_call(
        partial(finish_kernel, tuple(way for way, _ in carried)),
        in_specs=[anywhere] * 3 + [vmem] * 5 + [anywhere] * (3 + len(carried)),
        out_specs=[anywhere, vmem, vmem, anywhere] + [anywhere] * len(carried),
        out_shape=[
            jax.ShapeDtypeStruct((4, HD, depth), LOW),
            jax.ShapeDtypeStruct(norms.shape, F32),
            jax.ShapeDtypeStruct(taps.shape[1:], F32),
            jax.ShapeDtypeStruct(middle.shape, F32),
        ]
        + [jax.ShapeDtypeStruct(block.shape, block.dtype) for _, block in carried],
        scratch_shapes=[
            pltpu.VMEM((count, 4, HD, depth), LOW),
            pltpu.VMEM((count, 4, HD, depth), LOW),
            pltpu.VMEM((6, count, HD, depth // 2), LOW),
            pltpu.VMEM((2, count - 1, HD, depth), LOW),
            pltpu.VMEM((4, HD, depth), LOW),
            pltpu.VMEM((mp,) + norms.shape, F32),
            pltpu.VMEM(taps.shape, F32),
            pltpu.VMEM((4,) + norms.shape, F32),
            pltpu.VMEM((4,) + taps.shape[1:], F32),
            pltpu.VMEM((2 if count <= 8 else 1, 8 * HD, depth), LOW),
            pltpu.VMEM(middle.shape, F32),
            pltpu.VMEM(middle.shape, F32),
            pltpu.VMEM(norms.shape, F32),
            pltpu.VMEM((2, 8, depth), F32),
            dma((2, 5)),
            dma((9,)),
            dma((3, 4)),
            dma((3, 4)),
            dma((6,)),
            dma((6,)),
            dma((2, count)),
            dma((2, count)),
            dma((6,)),
            dma((6,)),
            dma((4, mp)),
            dma((4, mp)),
            dma((len(carried),)),
            dma((len(carried),)),
        ],
        compiler_params=pltpu.CompilerParams(
            collective_id=8, has_side_effects=True, vmem_limit_bytes=VMEM_LIMIT + 2**19
        ),
        cost_estimate=pl.CostEstimate(flops=2**36, bytes_accessed=2**26, transcendentals=0),
        name="finish",
    )(
        qk, v, out, norms, taps, grad_raw, inputs, gain.reshape(1, depth), qk_all, v_all, middle, *(block for _, block in carried),
    )


def plane_send(block, mask):
    return lax.ppermute(block, "dp", [(d, d ^ mask) for d in range(lax.axis_size("dp"))])


def placed(own, legs, last, me, turn):
    one_x, two_y, one_y, two_x = legs
    units, width = own.shape
    wide = 256
    steps = width // 2 // wide

    def kernel(me_ref, own_ref, one_x, two_x, one_y, two_y, one_xy, two_xy, o_ref):
        first = pl.program_id(0) < steps
        blocks = [own_ref[...]] + [
            jnp.where(first, one[...], two[...])
            for one, two in ((one_x, two_x), (one_y, two_y), (one_xy, two_xy))
        ]
        odd, high = lax.rem(me_ref[0], 2) == 1, me_ref[0] >= 2
        blocks = [jnp.where(odd, blocks[at ^ 1], blocks[at]) for at in range(4)]
        blocks = [jnp.where(high, blocks[at ^ 2], blocks[at]) for at in range(4)]
        for at, block in enumerate(blocks):
            if turn:
                o_ref[:, at * units : (at + 1) * units] = block.astype(F32).T
            else:
                o_ref[at * units : (at + 1) * units, :] = block.astype(F32)

    def half(side):
        if side == 0:
            return pl.BlockSpec((units, wide), lambda i, me: (0, jnp.minimum(i, steps - 1)))
        return pl.BlockSpec((units, wide), lambda i, me: (0, jnp.maximum(i - steps, 0)))

    if turn:
        shape = (width, 4 * units)
        out_spec = pl.BlockSpec((wide, 4 * units), lambda i, me: (i, 0))
    else:
        shape = (4 * units, width)
        out_spec = pl.BlockSpec((4 * units, wide), lambda i, me: (0, i))
    return pl.pallas_call(
        kernel,
        grid_spec=pltpu.PrefetchScalarGridSpec(
            num_scalar_prefetch=1,
            grid=(2 * steps,),
            in_specs=[pl.BlockSpec((units, wide), lambda i, me: (0, i))] + [half(0), half(1)] * 3,
            out_specs=out_spec,
        ),
        out_shape=jax.ShapeDtypeStruct(shape, F32),
        compiler_params=pltpu.CompilerParams(vmem_limit_bytes=32 * 2**20),
        cost_estimate=pl.CostEstimate(flops=0, bytes_accessed=2**24, transcendentals=0),
        name="placed",
    )(me.reshape(1).astype(jnp.int32), own, one_x, two_x, one_y, two_y, *last)


def plane_gather_begin(block, axis=-1):
    half = block.shape[axis] // 2
    one, two = jnp.split(block, [half], axis=axis)
    return plane_send(one, 1), plane_send(two, 2), plane_send(one, 2), plane_send(two, 1)


def plane_gather_end(legs):
    one_x, two_y, one_y, two_x = legs
    return plane_send(one_x, 2), plane_send(two_y, 1)


def line_step(blocks, step):
    count = lax.axis_size("mp") // 2
    up = [(2 * z + c, 2 * z + 2 + c) for z in range(step - 1, count - 1) for c in range(2)]
    down = [(2 * z + c, 2 * z - 2 + c) for z in range(1, count - step + 1) for c in range(2)]
    return lax.ppermute(blocks[0], "mp", up), lax.ppermute(blocks[1], "mp", down)


def per_device(
    inputs,
    cotangent,
    short_lengths,
    long_lengths,
    norm1_gain,
    norm1_bias,
    query_weight,
    key_weight,
    value_weight,
    query_kernel,
    key_kernel,
    value_kernel,
    out_weight,
    norm2_gain,
    norm2_bias,
    up_weight,
    down_weight,
):
    rows_here = inputs.shape[1]
    width = inputs.shape[2]
    mp = lax.axis_size("mp")
    dp = lax.axis_size("dp")
    me_dp = lax.axis_index("dp")
    me_mp = lax.axis_index("mp")
    group = rows_here * mp
    chips = mp // 2
    hidden_here = up_weight.shape[1]
    share = hidden_here // dp

    starts = jnp.stack(
        [document_starts(short_lengths[0], group), document_starts(long_lengths[0], group)]
    )
    rows = inputs.astype(F32)

    def quarters(weight):
        return weight.reshape(4, weight.shape[0] // 4, width)

    qk_own = jnp.concatenate([query_weight, key_weight], axis=1).T
    up_own = lax.dynamic_slice_in_dim(up_weight, me_dp * share, share, 1).T
    down_own = lax.dynamic_slice_in_dim(down_weight, me_dp * share, share, 0)
    qk_taps = jnp.concatenate([query_kernel, key_kernel], axis=1)
    v_taps = jnp.concatenate([value_kernel, value_kernel], axis=1)
    taps_own = jnp.pad(jnp.stack([qk_taps, qk_taps, v_taps]), ((0, 0), (0, 5), (0, 0)))
    places = jnp.arange(group, dtype=jnp.int32)
    offsets = lax.dynamic_slice_in_dim(
        jnp.pad(places[None, :] - starts, ((0, 0), (0, HALO))), me_mp * rows_here, rows_here + HALO, 1
    )
    masks = jnp.stack(
        [
            offsets[:, :rows_here] >= 1,
            offsets[:, :rows_here] >= 2,
            offsets[:, 1 : rows_here + 1] >= 1,
            offsets[:, 2 : rows_here + 2] >= 2,
        ],
        axis=1,
    ).astype(F32)[..., None]
    wide_masks = jnp.broadcast_to(masks, masks.shape[:3] + (HD,))
    masks = jnp.stack(
        [
            jnp.concatenate([wide_masks[left], wide_masks[right]], axis=2)
            for left, right in ((0, 0), (1, 1), (0, 1))
        ]
    )

    qk_all, v_all, out_all, taps, normed, up_early, raw, mixed, one_x, two_y = front(
        inputs, norm1_gain, norm1_bias, quarters(qk_own), quarters(value_weight.T), quarters(out_weight), taps_own, up_own,
        masks, cotangent,
    )
    qk_all = qk_all.reshape(mp * 2 * HD, width)
    v_all = v_all.reshape(mp * HD, width)
    out_all = out_all.reshape(mp * HD, width)
    mixed = mixed.reshape(3, group, 128)
    cot, mixed, up_early = lax.optimization_barrier((cotangent, mixed, up_early))

    def early_block(at):
        start = (2 * jnp.clip(at, 0, chips - 1) + me_mp % 2) * share
        return lax.dynamic_slice_in_dim(up_early, start, share, 0)

    late = range(early_steps(chips)[-1] + 1, chips)
    up_late = {}
    blocks = (early_block(me_mp // 2 - late[0] + 1), early_block(me_mp // 2 + late[0] - 1))
    for step in late:
        blocks = line_step(blocks, step)
        up_late[step, 1], up_late[step, -1] = blocks
    one_y, two_x = plane_send(cot[:, :, : width // 2], 2), plane_send(cot[:, :, width // 2 :], 1)
    one_xy, two_xy = plane_send(one_x, 2), plane_send(two_y, 1)

    def side_by_side(pair):
        split = pair.reshape(2, rows_here, mp, HD)
        return split.transpose(1, 2, 0, 3).reshape(1, rows_here, mp * 2 * HD)

    def apart(joint):
        split = joint.reshape(joint.shape[1], mp, 2, HD)
        return split.transpose(2, 0, 1, 3).reshape(2, joint.shape[1], mp * HD)

    attended_head, wide, total = attend(mixed, starts)
    attended_head, up_late = lax.optimization_barrier((attended_head, up_late))
    attended = apart(attended_back(attended_head, rows_here))
    middle = rows + dot(attended, out_all)
    second = layer_norm(middle, norm2_gain, norm2_bias).astype(LOW)

    second, one_y, two_x, one_xy, two_xy = lax.optimization_barrier(
        (second, one_y, two_x, one_xy, two_xy)
    )
    cot_pieces = (cot, one_x, two_x, one_y, two_y, one_xy, two_xy)
    second_all, relu, hidden, down_all, up_all, down_part = feed_in(
        second, up_early, down_own, cot_pieces, up_late
    )
    down_mine = lax.psum_scatter(down_part, "mp", scatter_dimension=0, tiled=True)
    grad_pre, up_part, grad_second = feed_out(
        cot_pieces, relu, second_all, up_all, down_all
    )
    up_mine = lax.psum_scatter(up_part, "mp", scatter_dimension=0, tiled=True)
    grad_second, down_mine = lax.optimization_barrier((grad_second, down_mine))
    down_legs = plane_gather_begin(down_mine)

    def norm_back(values, gain, grad):
        flat = values.reshape(-1, width)
        unused, pull = jax.vjp(layer_norm, flat, gain, norm1_bias)
        grad_rows, grad_gain, grad_shift = pull(grad.reshape(-1, width))
        return grad_rows.reshape(values.shape), grad_gain, grad_shift

    grad_middle, gain_two, shift_two = norm_back(middle, norm2_gain, grad_second)
    grad_middle = grad_middle + cotangent.astype(F32)
    branch = grad_middle.astype(LOW)
    grad_attended = jnp.einsum("srd,hd->srh", branch, out_all, preferred_element_type=F32).astype(LOW)
    grad_head, feed_x0, feed_x1, feed_y0, feed_y1, keep_a, keep_b = feed_heads(
        side_by_side(grad_attended), hidden, down_all
    )
    grad_head, down_legs, feed_x0, feed_y0 = lax.optimization_barrier(
        (grad_head, down_legs, feed_x0, feed_y0)
    )
    x_first, y_first = plane_send(feed_x0, 1), plane_send(feed_y0, 2)
    grad_mixed_head = attend_back(mixed, grad_head, wide, total, starts, HALO)
    grad_mixed_head, x_first, y_first, down_legs = lax.optimization_barrier(
        (grad_mixed_head, x_first, y_first, down_legs)
    )
    down_last = plane_gather_end(down_legs)

    def add(left, right):
        return left.astype(F32) + right.astype(F32)

    feed_a0, feed_b0 = add(keep_a[0, 1], x_first[1]).astype(LOW), add(keep_b[0, 1], y_first[1]).astype(LOW)
    grad_raw, tap_sums, qk_part, v_part, out_part, x_second, y_second, feed_a0, feed_b0 = project_back(
        grad_mixed_head, raw, taps, masks, normed, attended, branch,
        ((0, feed_x1), (1, feed_y1), (1, feed_a0), (0, feed_b0)),
    )
    grad_raw, down_last = lax.optimization_barrier((grad_raw, down_last))
    grad_raw, up_mine, down_last = lax.optimization_barrier((grad_raw, up_mine, down_last))
    down_grad = placed(down_mine, down_legs, down_last, me_dp, False)
    up_legs = plane_gather_begin(up_mine)
    feed_a1, feed_b1 = add(keep_a[1, 1], x_second[1]).astype(LOW), add(keep_b[1, 1], y_second[1]).astype(LOW)

    def split_parts(part):
        return part.reshape(mp // 2, 2, 4, part.shape[1] // 8, width)

    norms = jnp.pad(jnp.stack([gain_two, shift_two]), ((2, 4), (0, 0)))
    qk_sums = (tap_sums[0] + tap_sums[1]).reshape(8, mp, 2 * HD)
    v_sums = tap_sums[2].reshape(8, mp, 2, HD).sum(axis=2)
    taps_part = jnp.concatenate([qk_sums, v_sums, jnp.zeros_like(v_sums)], axis=2)
    taps_part = taps_part.transpose(1, 0, 2)
    norms, up_legs = lax.optimization_barrier((norms, up_legs))
    joint_grad, small_sum, taps_sum, input_grads, feed_a1, feed_b1, one_xy, two_xy = finish(
        split_parts(qk_part), split_parts(v_part), split_parts(out_part), norms, taps_part,
        grad_raw, inputs, norm1_gain, qk_all.reshape(chips, 4 * HD, width), v_all.reshape(chips, 2 * HD, width),
        grad_middle,
        ((1, feed_a1), (0, feed_b1), (1, up_legs[0]), (0, up_legs[1])),
    )
    results = jnp.stack(
        [
            middle[s]
            + jnp.concatenate(
                [
                    add(keep_a[s, 0], x_in[0]) + a_in.astype(F32),
                    add(keep_b[s, 0], y_in[0]) + b_in.astype(F32),
                ],
                axis=1,
            )
            for s, (x_in, y_in, a_in, b_in) in enumerate(
                ((x_first, y_first, feed_a0, feed_b0), (x_second, y_second, feed_a1, feed_b1))
            )
        ]
    ).astype(LOW)
    up_grad = placed(up_mine, up_legs, (one_xy, two_xy), me_dp, True)
    joint_grad = joint_grad.astype(F32)
    qk_grad = joint_grad[:, : HD // 2].reshape(2 * HD, width).T
    v_grad = joint_grad[:, HD // 2 : 3 * HD // 4].reshape(HD, width).T
    out_grad = joint_grad[:, 3 * HD // 4 :].reshape(HD, width)
    taps_sum = taps_sum[:3]
    return (
        results,
        input_grads,
        small_sum[0],
        small_sum[1],
        qk_grad[:, :HD],
        qk_grad[:, HD:],
        v_grad,
        taps_sum[:, :HD],
        taps_sum[:, HD : 2 * HD],
        taps_sum[:, 2 * HD : 3 * HD],
        out_grad,
        small_sum[2],
        small_sum[3],
        up_grad,
        down_grad,
    )


def solution(mesh):
    return jax.shard_map(
        per_device,
        mesh=mesh,
        in_specs=(
            P(None, ("dp", "mp"), None),
            P(None, ("dp", "mp"), None),
            P("dp", None),
            P("dp", None),
            P(),
            P(),
            P(None, "mp"),
            P(None, "mp"),
            P(None, "mp"),
            P(None, "mp"),
            P(None, "mp"),
            P(None, "mp"),
            P("mp", None),
            P(),
            P(),
            P(None, "mp"),
            P("mp", None),
        ),
        out_specs=(
            P(None, ("dp", "mp"), None),
            P(None, ("dp", "mp"), None),
            P(),
            P(),
            P(None, "mp"),
            P(None, "mp"),
            P(None, "mp"),
            P(None, "mp"),
            P(None, "mp"),
            P(None, "mp"),
            P("mp", None),
            P(),
            P(),
            P(None, "mp"),
            P("mp", None),
        ),
        check_vma=False,
    )
```

```python
import math
from functools import partial

import jax
import jax.numpy as jnp
from jax import lax
from jax.experimental import pallas as pl
from jax.experimental.pallas import tpu as pltpu
from jax.sharding import PartitionSpec as P

HD = 64
QUERIES, KEYS = 512, 512
WIDE = 256
CHUNK = 512
VMEM_LIMIT = 63 * 1024 * 1024
MESH = pl.DeviceIdType.MESH
LOW = jnp.bfloat16
F32 = jnp.float32


def dot(left, right):
    return jnp.dot(left, right, preferred_element_type=F32)


def layer_norm(rows, gain, shift):
    row_mean = jnp.mean(rows, axis=-1, keepdims=True)
    centered = rows - row_mean
    variance = jnp.mean(centered * centered, axis=-1, keepdims=True)
    return centered * lax.rsqrt(variance + 1e-05) * gain + shift


def document_starts(lengths, count):
    ends = jnp.cumsum(lengths)
    places = jnp.arange(count, dtype=jnp.int32)
    passed = (places[:, None] >= ends[None, :]).astype(jnp.int32)
    return jnp.sum(passed * lengths[None, :], axis=1)


def allowed_pairs(start_row, key_block, query_block):
    shape = (KEYS, QUERIES)
    keys = key_block * KEYS + lax.broadcasted_iota(jnp.int32, shape, 0)
    queries = query_block * QUERIES + lax.broadcasted_iota(jnp.int32, (1, QUERIES), 1)
    return (keys <= queries) & (keys >= start_row)


def key_blocks(first_ref, s, step):
    return first_ref[s, step], ((step + 1) * QUERIES + KEYS - 1) // KEYS


def attend_kernel(
    first_ref, start_ref, qk_ref, v_ref, out_ref, wide_ref, total_ref, values_t
):
    s, step = pl.program_id(0), pl.program_id(1)

    @pl.when(step == 0)
    def _():
        def turn(at, carry):
            rows = pl.ds(pl.multiple_of(at * KEYS, KEYS), KEYS)
            both = v_ref[0, rows, :].T
            values_t[at] = jnp.where(s == 0, both[:HD], both[HD:])
            return carry

        lax.fori_loop(0, values_t.shape[0], turn, 0)

    here = pl.ds(pl.multiple_of(step * QUERIES, QUERIES), QUERIES)
    query_t = (qk_ref[0, here, 0:HD] * HD ** (-0.5)).astype(LOW).T
    start_row = start_ref[0]

    def one(at, carry):
        top, summed, acc = carry
        rows = pl.ds(pl.multiple_of(at * KEYS, KEYS), KEYS)
        scores = dot(qk_ref[0, rows, HD : 2 * HD], query_t)
        scores = jnp.where(allowed_pairs(start_row, at, step), scores, -1e30)
        new_top = jnp.maximum(top, jnp.max(scores, axis=0, keepdims=True))
        powered = jnp.exp(scores - new_top)
        shrink = jnp.exp(top - new_top)
        summed = summed * shrink + jnp.sum(powered, axis=0, keepdims=True)
        acc = acc * shrink + dot(values_t[at], powered.astype(LOW))
        return new_top, summed, acc

    top, summed, acc = lax.fori_loop(
        *key_blocks(first_ref, s, step),
        one,
        (
            jnp.full((1, QUERIES), -1e30, F32),
            jnp.zeros((1, QUERIES), F32),
            jnp.zeros((HD, QUERIES), F32),
        ),
    )
    result = acc / summed
    wide_ref[0] = result
    total_ref[0] = top + jnp.log(summed)
    low = result.T.astype(LOW)

    @pl.when(s == 0)
    def _():
        out_ref[0, here, 0:HD] = low

    @pl.when(s == 1)
    def _():
        out_ref[0, here, HD : 2 * HD] = low


def attend(mixed, starts):
    group = mixed.shape[1]
    steps = group // QUERIES
    row = pl.BlockSpec((1, 1, QUERIES), lambda s, i, first: (s, 0, i))
    return pl.pallas_call(
        attend_kernel,
        grid_spec=pltpu.PrefetchScalarGridSpec(
            num_scalar_prefetch=1,
            grid=(2, steps),
            in_specs=[
                row,
                pl.BlockSpec((1, group, 2 * HD), lambda s, i, first: (s, 0, 0)),
                pl.BlockSpec((1, group, 2 * HD), lambda s, i, first: (2, 0, 0)),
            ],
            out_specs=[
                pl.BlockSpec((1, group, 2 * HD), lambda s, i, first: (0, 0, 0)),
                pl.BlockSpec((1, HD, QUERIES), lambda s, i, first: (s, 0, i)),
                row,
            ],
            scratch_shapes=[pltpu.VMEM((group // KEYS, HD, KEYS), LOW)],
        ),
        out_shape=[
            jax.ShapeDtypeStruct((1, group, 2 * HD), LOW),
            jax.ShapeDtypeStruct((2, HD, group), F32),
            jax.ShapeDtypeStruct((2, 1, group), F32),
        ],
        compiler_params=pltpu.CompilerParams(vmem_limit_bytes=32 * 1024 * 1024),
        cost_estimate=pl.CostEstimate(
            flops=2**34, bytes_accessed=group * 2048, transcendentals=group * group // 4
        ),
        name="attend",
    )(starts[:, ::QUERIES] // KEYS, starts[:, None, :], mixed, mixed)


def attend_back_kernel(
    first_ref, start_ref, qk_ref, v_ref, grad_ref, wide_ref, total_ref, out_ref,
    keys_t, values, grad_keys, grad_values,
):
    s, step = pl.program_id(0), pl.program_id(1)
    group = qk_ref.shape[1]

    @pl.when(step == 0)
    def _():
        def turn(at, carry):
            rows = pl.ds(pl.multiple_of(at * KEYS, KEYS), KEYS)
            keys_t[at] = qk_ref[0, rows, HD : 2 * HD].T
            both = v_ref[0, rows, :]
            values[rows, :] = jnp.where(s == 0, both[:, :HD], both[:, HD:])
            return carry

        lax.fori_loop(0, keys_t.shape[0], turn, 0)
        grad_keys[...] = jnp.zeros(grad_keys.shape, F32)
        grad_values[...] = jnp.zeros(grad_values.shape, F32)

    here = pl.ds(pl.multiple_of(step * QUERIES, QUERIES), QUERIES)
    query = (qk_ref[0, here, 0:HD] * HD ** (-0.5)).astype(LOW)
    query_t = query.T
    both = grad_ref[0]
    grad = jnp.where(s == 0, both[:, :HD], both[:, HD:])
    grad_t = grad.T
    start_row = start_ref[0]
    total = total_ref[0]
    inner = jnp.sum(grad_t.astype(F32) * wide_ref[0], axis=0, keepdims=True)

    def one(at, acc):
        rows = pl.ds(pl.multiple_of(at * KEYS, KEYS), KEYS)
        scores = dot(qk_ref[0, rows, HD : 2 * HD], query_t)
        scores = jnp.where(allowed_pairs(start_row, at, step), scores, -1e30)
        probs = jnp.exp(scores - total)
        grad_probs = dot(values[rows, :], grad_t)
        grad_scores = (probs * (grad_probs - inner)).astype(LOW)
        grad_values[rows, :] += dot(probs.astype(LOW), grad)
        grad_keys[rows, :] += dot(grad_scores, query)
        return acc + dot(keys_t[at], grad_scores)

    acc = lax.fori_loop(
        *key_blocks(first_ref, s, step), one, jnp.zeros((HD, QUERIES), F32)
    )
    out_ref[s, here, 0:HD] = (acc * HD ** (-0.5)).T.astype(out_ref.dtype)

    @pl.when(step == pl.num_programs(1) - 1)
    def _():
        out_ref[s, 0:group, HD : 2 * HD] = grad_keys[...].astype(out_ref.dtype)
        out_ref[s, group:, :] = jnp.zeros((out_ref.shape[1] - group, 2 * HD), out_ref.dtype)

        @pl.when(s == 0)
        def _():
            out_ref[2, 0:group, 0:HD] = grad_values[...].astype(out_ref.dtype)

        @pl.when(s == 1)
        def _():
            out_ref[2, 0:group, HD : 2 * HD] = grad_values[...].astype(out_ref.dtype)
            out_ref[2, group:, :] = jnp.zeros((out_ref.shape[1] - group, 2 * HD), out_ref.dtype)


def attend_back(mixed, grad, wide, total, starts, halo):
    group = mixed.shape[1]
    steps = group // QUERIES
    row = pl.BlockSpec((1, 1, QUERIES), lambda s, i, first: (s, 0, i))
    return pl.pallas_call(
        attend_back_kernel,
        grid_spec=pltpu.PrefetchScalarGridSpec(
            num_scalar_prefetch=1,
            grid=(2, steps),
            in_specs=[
                row,
                pl.BlockSpec((1, group, 2 * HD), lambda s, i, first: (s, 0, 0)),
                pl.BlockSpec((1, group, 2 * HD), lambda s, i, first: (2, 0, 0)),
                pl.BlockSpec((1, QUERIES, 2 * HD), lambda s, i, first: (0, i, 0)),
                pl.BlockSpec((1, HD, QUERIES), lambda s, i, first: (s, 0, i)),
                row,
            ],
            out_specs=pl.BlockSpec((3, group + halo, 2 * HD), lambda s, i, first: (0, 0, 0)),
            scratch_shapes=[
                pltpu.VMEM((group // KEYS, HD, KEYS), LOW),
                pltpu.VMEM((group, HD), LOW),
                pltpu.VMEM((group, HD), F32),
                pltpu.VMEM((group, HD), F32),
            ],
        ),
        out_shape=jax.ShapeDtypeStruct((3, group + halo, 2 * HD), LOW),
        compiler_params=pltpu.CompilerParams(vmem_limit_bytes=32 * 1024 * 1024),
        cost_estimate=pl.CostEstimate(
            flops=2**35, bytes_accessed=group * 2048, transcendentals=group * group // 4
        ),
        name="attend_back",
    )(starts[:, ::QUERIES] // KEYS, starts[:, None, :], mixed, mixed, grad, wide, total)


def plane_partners():
    me = lax.axis_index("dp")
    return {"dp": me + 1 - 2 * lax.rem(me, 2)}, {"dp": me + 2 - 4 * (me // 2)}


def dot_nt(left, right):
    return lax.dot_general(left, right, (((1,), (1,)), ((), ())), preferred_element_type=F32)


def mesh_place():
    me = lax.axis_index("mp")
    return me // 2, lax.rem(me, 2)


def wire(source, target, send, recv, partner):
    return pltpu.make_async_remote_copy(
        src_ref=source,
        dst_ref=target,
        send_sem=send,
        recv_sem=recv,
        device_id=partner,
        device_id_type=MESH,
    )


def line_partner(z, step):
    _, core = mesh_place()
    return {"mp": 2 * (z + step) + core}


def other_core():
    z, core = mesh_place()
    return {"mp": 2 * z + 1 - core}


def greet(partners):
    barrier = pltpu.get_barrier_semaphore()
    for partner in partners:
        pl.semaphore_signal(barrier, inc=1, device_id=partner, device_id_type=MESH)
    pl.semaphore_wait(barrier, len(partners))


def greet_line(with_plane):
    z, _ = mesh_place()
    count = lax.axis_size("mp") // 2
    barrier = pltpu.get_barrier_semaphore()
    partners = [other_core()]
    if with_plane:
        partners += list(plane_partners())
    for partner in partners:
        pl.semaphore_signal(barrier, inc=1, device_id=partner, device_id_type=MESH)
    for turn in (1, -1):

        @pl.when((z + turn >= 0) & (z + turn < count))
        def _(turn=turn):
            pl.semaphore_signal(barrier, inc=1, device_id=line_partner(z, turn), device_id_type=MESH)

    near = jnp.where(z > 0, 1, 0) + jnp.where(z < count - 1, 1, 0)
    pl.semaphore_wait(barrier, near + len(partners))


class LineGather:
    def __init__(self, place, send, recv, swap_send, swap_recv):
        self.z, self.core = mesh_place()
        self.count = lax.axis_size("mp") // 2
        self.place, self.send, self.recv = place, send, recv
        self.swap_send, self.swap_recv = swap_send, swap_recv

    def copies(self, step):
        z, count = self.z, self.count
        out = []
        for way, turn in enumerate((1, -1)):
            leaves = z - turn * (step - 1)
            lands = z - turn * step
            far = z + turn
            sends = (leaves >= 0) & (leaves < count) & (far >= 0) & (far < count)
            receives = (lands >= 0) & (lands < count)
            at = jnp.clip(leaves, 0, count - 1)
            to = jnp.clip(lands, 0, count - 1)
            sems = (self.send.at[way, step - 1], self.recv.at[way, step - 1], line_partner(z, turn))
            leaving = wire(self.place(at, self.core), self.place(at, self.core), *sems)
            landing = wire(self.place(to, self.core), self.place(to, self.core), *sems)
            out.append((sends, leaving, receives, landing, to))
        return out

    def start(self, step):
        for sends, leaving, _, _, _ in self.copies(step):
            pl.when(sends)(leaving.start)

    def swap(self, at, number):
        sems = (self.swap_send.at[number], self.swap_recv.at[number], other_core())
        leaving = wire(self.place(at, self.core), self.place(at, self.core), *sems)
        landing = wire(self.place(at, 1 - self.core), self.place(at, 1 - self.core), *sems)
        return leaving, landing

    def swap_own(self):
        self.swap(self.z, 0)[0].start()

    def arrive(self, step):
        for way, (_, _, receives, landing, at) in enumerate(self.copies(step)):

            @pl.when(receives)
            def _(landing=landing, at=at, way=way):
                landing.wait_recv()
                self.swap(at, 1 + 2 * (step - 1) + way)[0].start()

    def swapped(self, at, number):
        leaving, landing = self.swap(at, number)
        leaving.wait_send()
        landing.wait_recv()

    def finish(self, steps, own):
        if own:
            self.swapped(self.z, 0)
        for step in steps:
            for way, (sends, leaving, receives, _, at) in enumerate(self.copies(step)):
                pl.when(sends)(leaving.wait_send)
                pl.when(receives)(
                    lambda at=at, way=way, step=step: self.swapped(at, 1 + 2 * (step - 1) + way)
                )


def line_semaphores(count):
    return [
        pltpu.SemaphoreType.DMA((2, count)),
        pltpu.SemaphoreType.DMA((2, count)),
        pltpu.SemaphoreType.DMA((2 * count,)),
        pltpu.SemaphoreType.DMA((2 * count,)),
    ]


def early_steps(count):
    return range(1, count // 2 + 1)


HALO = 16


def carry_copies(carried, targets, send, recv):
    partners = plane_partners()
    return [
        wire(ref, target, send.at[at], recv.at[at], partners[way])
        for at, ((way, ref), target) in enumerate(zip(carried, targets))
    ]


def greet_members(ways):
    mp = lax.axis_size("mp")
    me = lax.axis_index("mp")
    barrier = pltpu.get_barrier_semaphore()
    for step in range(1, mp):
        pl.semaphore_signal(
            barrier, inc=1, device_id={"mp": lax.rem(me + step, mp)}, device_id_type=MESH
        )
    partners = plane_partners() if ways else ()
    for partner in partners:
        pl.semaphore_signal(barrier, inc=1, device_id=partner, device_id_type=MESH)
    pl.semaphore_wait(barrier, mp - 1 + len(partners))


def member_copies(source, target, send, recv):
    mp = lax.axis_size("mp")
    me = lax.axis_index("mp")
    copies = []
    for step in range(1, mp):
        to = lax.rem(me + step, mp)
        sems = (send.at[step], recv.at[step], {"mp": to})
        copies.append(
            (
                wire(source(to), target(me), *sems),
                wire(source(to), target(lax.rem(me + mp - step, mp)), *sems),
            )
        )
    return copies


def head_lanes(at):
    return pl.ds(pl.multiple_of(at * 128, 128), 128)


def front_kernel(
    inputs_ref, gain_ref, shift_ref, qk_ref, v_ref, out_ref, taps_ref, up_ref, masks_ref, cot_ref,
    all_qk_ref, all_v_ref, all_out_ref, all_taps_ref, normed_ref, up_all_ref, raw_ref, o_ref, cot_x_ref, cot_y_ref,
    inputs, rows, all_qk, all_v, all_out, all_taps, up_all, raw, mixed, landed, local, *sems,
):
    mp = lax.axis_size("mp")
    dp = lax.axis_index("dp")
    me = lax.axis_index("mp")
    z, core = mesh_place()
    count = mp // 2
    rows_here, depth = inputs.shape[1:]
    halo = rows.shape[1] - rows_here
    to_x, to_y = plane_partners()
    share = up_ref.shape[0]
    owned = (qk_ref, v_ref, out_ref)
    whole = (all_qk, all_v, all_out)
    (plane_send_sem, plane_recv_sem, plane_swap_send, plane_swap_recv) = sems[:4]
    taps_send, taps_recv, halo_send, halo_recv, carry_send, carry_recv, head_send, head_recv = sems[4:12]
    line_sems = [sems[12 + 4 * part : 16 + 4 * part] for part in range(4)]

    def up_place(at, at_core):
        start = pl.multiple_of((2 * at + at_core) * share, 16)
        return up_all.at[pl.ds(start, share), :]

    def taps_place(at):
        return all_taps.at[:, :, head_lanes(at)]

    loads = [
        pltpu.make_async_copy(inputs_ref, inputs, local.at[0]),
        pltpu.make_async_copy(taps_ref, taps_place(me), local.at[1]),
        pltpu.make_async_copy(up_ref, up_place(z, core), local.at[2]),
    ] + [
        pltpu.make_async_copy(
            owned[part].at[dp], whole[part].at[z, core, dp], local.at[3 + part]
        )
        for part in range(3)
    ]
    for copy in loads:
        copy.start()
    greet_members((0, 1))
    for copy in loads[1:]:
        copy.wait()

    lines = [
        LineGather(lambda at, at_core, part=part: whole[part].at[at, at_core, dp], *line_sems[part])
        for part in range(3)
    ]
    up_line = LineGather(up_place, *line_sems[3])
    for line in lines:
        line.start(1)
    tap_copies = member_copies(lambda to: taps_ref, taps_place, taps_send, taps_recv)
    for copy, _ in tap_copies:
        copy.start()
    for line in lines:
        line.swap_own()

    loads[0].wait()
    tall = 16

    def norm(s):
        def some(at, carry):
            here = pl.ds(pl.multiple_of(at * tall, tall), tall)
            there = pl.ds(pl.multiple_of(halo + at * tall, tall), tall)
            values = inputs[s, here, :].astype(F32)
            centered = values - jnp.mean(values, axis=1, keepdims=True)
            variance = jnp.mean(centered * centered, axis=1, keepdims=True)
            rows[s, there, :] = (
                centered * lax.rsqrt(variance + 1e-05) * gain_ref[...] + shift_ref[...]
            ).astype(LOW)
            return carry

        lax.fori_loop(0, rows_here // tall, some, 0)

    norm(0)
    for step in range(1, count):
        for line in lines:
            line.arrive(step)
        if step + 1 < count:
            for line in lines:
                line.start(step + 1)

    half = depth // 2
    lanes = (pl.ds(0, half), pl.ds(half, half))
    dp_x = dp + 1 - 2 * lax.rem(dp, 2)
    dp_y = dp + 2 - 4 * (dp // 2)
    dp_xy = dp_x + 2 - 4 * (dp_x // 2)
    legs = ((0, to_x), (1, to_y), (0, to_y), (1, to_x), (0, to_y), (1, to_x))

    def plane(number, quarter):
        side, partner = legs[number]
        out = []
        for part in range(3):
            block = whole[part].at[:, core, quarter, :, lanes[side]]
            out.append(
                wire(
                    block, block, plane_send_sem.at[part, number], plane_recv_sem.at[part, number], partner
                )
            )
        return out

    leaving = [plane(number, quarter) for number, quarter in enumerate((dp, dp, dp, dp, dp_x, dp_y))]
    landing = [
        plane(number, quarter) for number, quarter in enumerate((dp_x, dp_y, dp_y, dp_x, dp_xy, dp_xy))
    ]

    def pass_on(number, at_core):
        quarter = (dp_x, dp_y, dp_xy)[number]
        out = []
        for part in range(3):
            block = whole[part].at[:, at_core, quarter]
            out.append(
                wire(
                    block, block, plane_swap_send.at[part, number], plane_swap_recv.at[part, number],
                    other_core(),
                )
            )
        return out

    def each(copies, what):
        for copy in copies:
            getattr(copy, what)()

    for number in range(4):
        each(leaving[number], "start")
    early = early_steps(count)
    up_line.start(1)
    up_line.swap_own()
    norm(1)
    own_rows = rows.at[:, pl.ds(halo, rows_here), :]
    save = pltpu.make_async_copy(own_rows, normed_ref, local.at[0])
    save.start()
    halo_copy = wire(
        rows.at[:, pl.ds(rows_here, halo), :], rows.at[:, pl.ds(0, halo), :], halo_send, halo_recv,
        {"mp": lax.rem(me + 1, mp)},
    )
    halo_copy.start()
    each(landing[0], "wait_recv")
    each(leaving[4], "start")
    each(landing[1], "wait_recv")
    each(leaving[5], "start")
    each(landing[3], "wait_recv")
    each(pass_on(0, core), "start")
    each(landing[2], "wait_recv")
    each(pass_on(1, core), "start")
    up_line.arrive(1)
    up_line.start(2)
    each(landing[4], "wait_recv")
    each(landing[5], "wait_recv")
    each(pass_on(2, core), "start")
    for step in early[1:-1]:
        up_line.arrive(step)
        up_line.start(step + 1)
    carries = [
        wire(cot_ref.at[:, :, lanes[0]], cot_x_ref, carry_send.at[0], carry_recv.at[0], to_x),
        wire(cot_ref.at[:, :, lanes[1]], cot_y_ref, carry_send.at[1], carry_recv.at[1], to_y),
    ]
    for copy in carries:
        copy.start()
    for line in lines:
        line.finish(range(1, count), True)
    for number in range(3):
        each(pass_on(number, 1 - core), "wait_recv")
    for _, landed_taps in tap_copies:
        landed_taps.wait_recv()
    halo_copy.wait_recv()
    saves = [
        pltpu.make_async_copy(here, there, local.at[2 + at])
        for at, (here, there) in enumerate(
            ((all_qk, all_qk_ref), (all_v, all_v_ref), (all_out, all_out_ref), (all_taps, all_taps_ref))
        )
    ]
    for copy in saves:
        copy.start()

    def chip(at, carry):
        weights = all_qk[at].reshape(4 * HD, depth)
        columns = pl.ds(pl.multiple_of(at * 4 * HD, 4 * HD), 4 * HD)
        for s in range(2):
            raw[s, :, columns] = dot_nt(rows[s], weights)
        return carry

    lax.fori_loop(0, count, chip, 0)
    lane = lax.broadcasted_iota(jnp.int32, (rows.shape[1], 128), 1)

    def two_heads(at, carry):
        weights = all_v[at].reshape(2 * HD, depth)
        zero, one = dot_nt(rows[0], weights), dot_nt(rows[1], weights)
        raw[2, :, head_lanes(2 * at)] = jnp.where(lane < HD, zero, pltpu.roll(one, HD, 1))
        raw[2, :, head_lanes(2 * at + 1)] = jnp.where(lane < HD, pltpu.roll(zero, HD, 1), one)
        return carry

    lax.fori_loop(0, count, two_heads, 0)
    save_raw = pltpu.make_async_copy(raw, raw_ref, local.at[6])
    save_raw.start()
    for plane_at in range(3):
        tap = all_taps.at[plane_at]

        def conv(at, carry, plane_at=plane_at, tap=tap):
            lanes_at = head_lanes(at)
            values = raw[plane_at, :, lanes_at]
            one = pltpu.roll(values, 1, 0)[halo:]
            two = pltpu.roll(values, 2, 0)[halo:]
            mixed[plane_at, :, lanes_at] = (
                tap[0:1, lanes_at] * values[halo:]
                + jnp.where(masks_ref[plane_at, 0] > 0.5, tap[1:2, lanes_at] * one, 0.0)
                + jnp.where(masks_ref[plane_at, 1] > 0.5, tap[2:3, lanes_at] * two, 0.0)
            ).astype(LOW)
            return carry

        lax.fori_loop(0, mp, conv, 0)

    def source(at):
        return mixed.at[:, :, head_lanes(at)]

    def target(at):
        return landed.at[:, at]

    own = pltpu.make_async_copy(source(me), target(me), local.at[7])
    own.start()
    copies = member_copies(source, target, head_send, head_recv)
    for copy, _ in copies:
        copy.start()
    up_line.arrive(early[-1])
    up_line.finish(early, True)
    save_up = pltpu.make_async_copy(up_all, up_all_ref, local.at[8])
    save_up.start()
    own.wait()
    for _, copy in copies:
        copy.wait_recv()
    save_heads = pltpu.make_async_copy(landed, o_ref, local.at[9])
    save_heads.start()
    for number in range(6):
        each(leaving[number], "wait_send")
    for number in range(3):
        each(pass_on(number, core), "wait_send")
    for copy, _ in tap_copies + copies:
        copy.wait_send()
    halo_copy.wait_send()
    for copy in carries:
        copy.wait()
    save.wait()
    for copy in saves:
        copy.wait()
    save_raw.wait()
    save_up.wait()
    save_heads.wait()


def front(inputs, gain, shift, qk, v, out, taps, up, masks, cot):
    mp = lax.axis_size("mp")
    count = mp // 2
    rows_here, depth = inputs.shape[1:]
    tall = rows_here + HALO
    anywhere = pl.BlockSpec(memory_space=pl.ANY)
    vmem = pl.BlockSpec(memory_space=pltpu.VMEM)
    dma = pltpu.SemaphoreType.DMA
    whole = [((count, 2) + part.shape, LOW) for part in (qk, v, out)]
    whole.append(((3, 8, mp * 128), F32))
    kept = [
        ((2, rows_here, depth), LOW),
        ((mp * up.shape[0], depth), LOW),
        ((3, tall, mp * 128), F32),
        ((3, mp, rows_here, 128), LOW),
        ((2, rows_here, depth // 2), LOW),
        ((2, rows_here, depth // 2), LOW),
    ]
    return pl.pallas_call(
        front_kernel,
        in_specs=[anywhere, vmem, vmem] + [anywhere] * 5 + [vmem, anywhere],
        out_specs=[anywhere] * 10,
        out_shape=[jax.ShapeDtypeStruct(*shape) for shape in whole + kept],
        scratch_shapes=[
            pltpu.VMEM(inputs.shape, LOW),
            pltpu.VMEM((2, tall, depth), LOW),
        ]
        + [pltpu.VMEM(*shape) for shape in whole]
        + [
            pltpu.VMEM(*kept[1]),
            pltpu.VMEM(*kept[2]),
            pltpu.VMEM((3, rows_here, mp * 128), LOW),
            pltpu.VMEM(*kept[3]),
            dma((10,)),
            dma((3, 6)),
            dma((3, 6)),
            dma((3, 3)),
            dma((3, 3)),
            dma((mp,)),
            dma((mp,)),
            dma,
            dma,
            dma((2,)),
            dma((2,)),
            dma((mp,)),
            dma((mp,)),
        ]
        + line_semaphores(count) * 4,
        compiler_params=pltpu.CompilerParams(
            collective_id=3, has_side_effects=True, vmem_limit_bytes=VMEM_LIMIT
        ),
        cost_estimate=pl.CostEstimate(flops=2**36, bytes_accessed=2**26, transcendentals=0),
        name="front",
    )(inputs, gain.reshape(1, depth), shift.reshape(1, depth), qk, v, out, taps, up, masks, cot)


def left_t_right(left, right):
    return lax.dot_general(left, right, (((0,), (0,)), ((), ())), preferred_element_type=F32)


def stream_out(steps, compute, buffer, ref, sem):
    def save(at, slot):
        return pltpu.make_async_copy(buffer.at[slot], ref.at[at], sem.at[slot])

    def one(at, carry):
        slot = lax.rem(at, 2)

        @pl.when(at >= 2)
        def _():
            save(at - 2, slot).wait()

        buffer[slot] = compute(at)
        save(at, slot).start()
        return carry

    lax.fori_loop(0, steps, one, 0)
    save(steps - 2, (steps - 2) % 2).wait()
    save(steps - 1, (steps - 1) % 2).wait()


def project_back_kernel(
    ways, x_ref, raw_ref, taps_ref, masks_ref, normed_ref, attended_ref, branch_ref, *refs
):
    carried, refs = list(zip(ways, refs[: len(ways)])), refs[len(ways) :]
    grad_ref, sums_ref, qk_part_ref, v_part_ref, out_part_ref = refs[:5]
    targets, refs = refs[5 : 5 + len(ways)], refs[5 + len(ways) :]
    landed, raw, wide, narrow, part_sem, local, send, recv, carry_send, carry_recv = refs
    me = lax.axis_index("mp")
    tall = landed.shape[1]
    rows_here = grad_ref.shape[1]
    halo = tall - rows_here
    heads = landed.shape[2] // 128

    def source(at):
        return x_ref.at[:, pl.ds(pl.multiple_of(at * rows_here, 16), tall), :]

    def target(at):
        return landed.at[:, :, head_lanes(at)]

    own = pltpu.make_async_copy(source(me), target(me), local.at[0])
    own.start()
    load = pltpu.make_async_copy(raw_ref, raw, local.at[1])
    load.start()
    greet_members(ways)
    copies = member_copies(source, target, send, recv)
    for leaving, _ in copies:
        leaving.start()
    carries = carry_copies(carried, targets, carry_send, carry_recv)
    for copy in carries:
        copy.start()

    def out_part(at):
        lanes = head_lanes(at)
        return (
            left_t_right(attended_ref[0, :, lanes], branch_ref[0])
            + left_t_right(attended_ref[1, :, lanes], branch_ref[1])
        ).astype(LOW)

    stream_out(heads // 2, out_part, narrow, out_part_ref, part_sem)
    own.wait()
    load.wait()
    for _, landing in copies:
        landing.wait_recv()
    for plane in range(3):
        tap = taps_ref.at[plane]

        def back(at, carry, plane=plane, tap=tap):
            lanes = head_lanes(at)
            grad = landed[plane, :, lanes].astype(F32)
            one = pltpu.roll(grad, tall - 1, 0)[:rows_here]
            two = pltpu.roll(grad, tall - 2, 0)[:rows_here]
            here = grad[:rows_here]
            grad_ref[plane, :, lanes] = (
                tap[0:1, lanes] * here
                + jnp.where(masks_ref[plane, 2] > 0.5, tap[1:2, lanes] * one, 0.0)
                + jnp.where(masks_ref[plane, 3] > 0.5, tap[2:3, lanes] * two, 0.0)
            ).astype(LOW)
            values = raw[plane, :, lanes]
            before = pltpu.roll(values, 1, 0)[halo:]
            before_two = pltpu.roll(values, 2, 0)[halo:]
            products = (
                here * values[halo:],
                jnp.where(masks_ref[plane, 0] > 0.5, here * before, 0.0),
                jnp.where(masks_ref[plane, 1] > 0.5, here * before_two, 0.0),
            )
            for row, product in enumerate(products):
                sums_ref[plane, row : row + 1, lanes] = jnp.sum(product, axis=0, keepdims=True)
            sums_ref[plane, 3:8, lanes] = jnp.zeros((5, 128), F32)
            return carry

        lax.fori_loop(0, heads, back, 0)

    def pair(at):
        return pl.ds(pl.multiple_of(at * 256, 256), 256)

    def qk_part(at):
        return (
            left_t_right(grad_ref[0, :, pair(at)], normed_ref[0])
            + left_t_right(grad_ref[1, :, pair(at)], normed_ref[1])
        ).astype(LOW)

    def v_part(at):
        side = grad_ref[2, :, pair(at)]
        zero, one = left_t_right(side, normed_ref[0]), left_t_right(side, normed_ref[1])
        return jnp.concatenate(
            [zero[:HD] + one[HD : 2 * HD], zero[2 * HD : 3 * HD] + one[3 * HD :]], axis=0
        ).astype(LOW)

    stream_out(heads // 2, qk_part, wide, qk_part_ref, part_sem)
    stream_out(heads // 2, v_part, narrow, v_part_ref, part_sem)
    for leaving, _ in copies:
        leaving.wait_send()
    for copy in carries:
        copy.wait()


def project_back(x, raw, taps, masks, normed, attended, branch, carried):
    mp = lax.axis_size("mp")
    rows_here, depth = normed.shape[1:]
    tall = raw.shape[1]
    anywhere = pl.BlockSpec(memory_space=pl.ANY)
    dma = pltpu.SemaphoreType.DMA
    vmem = pl.BlockSpec(memory_space=pltpu.VMEM)
    return pl.pallas_call(
        partial(project_back_kernel, tuple(way for way, _ in carried)),
        in_specs=[vmem, anywhere] + [vmem] * 5 + [anywhere] * len(carried),
        out_specs=[vmem] * 2 + [anywhere] * (3 + len(carried)),
        out_shape=[
            jax.ShapeDtypeStruct((3, rows_here, mp * 128), LOW),
            jax.ShapeDtypeStruct((3, 8, mp * 128), F32),
            jax.ShapeDtypeStruct((mp // 2, 4 * HD, depth), LOW),
            jax.ShapeDtypeStruct((mp // 2, 2 * HD, depth), LOW),
            jax.ShapeDtypeStruct((mp // 2, 2 * HD, depth), LOW),
        ]
        + [jax.ShapeDtypeStruct(block.shape, block.dtype) for _, block in carried],
        scratch_shapes=[
            pltpu.VMEM((3, tall, mp * 128), LOW),
            pltpu.VMEM((3, tall, mp * 128), F32),
            pltpu.VMEM((2, 4 * HD, depth), LOW),
            pltpu.VMEM((2, 2 * HD, depth), LOW),
            dma((2,)),
            dma((2,)),
            dma((mp,)),
            dma((mp,)),
            dma((len(carried),)),
            dma((len(carried),)),
        ],
        compiler_params=pltpu.CompilerParams(
            collective_id=7, has_side_effects=True, vmem_limit_bytes=VMEM_LIMIT
        ),
        cost_estimate=pl.CostEstimate(flops=2**35, bytes_accessed=2**24, transcendentals=0),
        name="project_back",
    )(x, raw, taps, masks, normed, attended, branch, *(block for _, block in carried))


def attended_kernel(x_ref, o_ref, landed, local, send, recv):
    me = lax.axis_index("mp")
    tall = o_ref.shape[1]

    def source(at):
        return x_ref.at[:, pl.ds(pl.multiple_of(at * tall, 16), tall), :]

    def target(at):
        return landed.at[:, :, head_lanes(at)]

    own = pltpu.make_async_copy(source(me), target(me), local.at[0])
    own.start()
    greet_members(())
    copies = member_copies(source, target, send, recv)
    for leaving, _ in copies:
        leaving.start()
    own.wait()
    for _, landing in copies:
        landing.wait_recv()
    save = pltpu.make_async_copy(landed, o_ref, local.at[1])
    save.start()
    for leaving, _ in copies:
        leaving.wait_send()
    save.wait()


def attended_back(x, rows_here):
    mp = lax.axis_size("mp")
    shape = (x.shape[0], rows_here, mp * 128)
    dma = pltpu.SemaphoreType.DMA
    return pl.pallas_call(
        attended_kernel,
        in_specs=[pl.BlockSpec(memory_space=pltpu.VMEM)],
        out_specs=pl.BlockSpec(memory_space=pl.ANY),
        out_shape=jax.ShapeDtypeStruct(shape, x.dtype),
        scratch_shapes=[pltpu.VMEM(shape, x.dtype), dma((2,)), dma((mp,)), dma((mp,))],
        compiler_params=pltpu.CompilerParams(
            collective_id=5, has_side_effects=True, vmem_limit_bytes=48 * 2**20
        ),
        cost_estimate=pl.CostEstimate(flops=2**34, bytes_accessed=2**24, transcendentals=0),
        name="attended_back",
    )(x)


def line_blocks(place, sources, local, send, recv):
    z, core = mesh_place()
    count = lax.axis_size("mp") // 2
    out = []
    for number, (step, way, ref) in enumerate(sources):
        at = z - way * step
        there = (at >= 0) & (at < count)
        at = jnp.clip(at, 0, count - 1)
        sems = (send.at[number], recv.at[number], other_core())
        out.append(
            (
                there,
                pltpu.make_async_copy(ref, place(at, core), local.at[number]),
                wire(ref, place(at, core), *sems),
                wire(ref, place(at, 1 - core), *sems),
            )
        )
    return out


def feed_in_kernel(
    late, second_ref, up_ref, down_ref, cot_0, cot_1, cot_2, cot_3, cot_4, cot_5, cot_6, *refs
):
    late_sources = [(step, way, ref) for (step, way), ref in zip(late, refs)]
    (
        all_ref, relu_ref, hidden_ref, down_all_ref, up_all_ref, down_part_ref,
        rows, up, relu, hidden, down, cot, tiles, sums, before, local, outs, send, recv, cot_sem, tile_sem, sum_sem,
        before_sem, late_local, late_send, late_recv, *line_sems,
    ) = refs[len(late) :]
    count = lax.axis_size("mp") // 2
    depth = rows.shape[3]
    units = up.shape[0]
    share = down_ref.shape[0]
    z, core = mesh_place()
    lanes = (pl.ds(0, depth // 2), pl.ds(depth // 2, depth // 2))
    to_x, to_y = plane_partners()
    pieces = (cot_0, cot_1, cot_2, cot_3, cot_4, cot_5, cot_6)

    def line_place(ref):
        return lambda at, at_core: ref.at[
            pl.ds(pl.multiple_of((2 * at + at_core) * share, 16), share), :
        ]

    own = [pltpu.make_async_copy(second_ref.at[s], rows.at[s, 0], local.at[s]) for s in range(2)]
    own.append(pltpu.make_async_copy(up_ref, up, local.at[2]))
    own.append(pltpu.make_async_copy(down_ref, line_place(down)(z, core), local.at[3]))
    for copy in own:
        copy.start()
    for copy in own:
        copy.wait()
    greet_line(True)
    late_blocks = line_blocks(line_place(up), late_sources, late_local, late_send, late_recv)
    down_line = LineGather(line_place(down), *line_sems)

    def remote(s, source, target, half, partner, number):
        return wire(
            rows.at[s, source, :, lanes[half]], rows.at[s, target, :, lanes[half]],
            send.at[s, number], recv.at[s, number], partner,
        )

    copies = [
        [
            remote(s, 0, 1, 0, to_x, 0),
            remote(s, 0, 2, 1, to_y, 1),
            remote(s, 0, 2, 0, to_y, 2),
            remote(s, 0, 1, 1, to_x, 3),
            remote(s, 1, 3, 0, to_y, 4),
            remote(s, 2, 3, 1, to_x, 5),
        ]
        for s in range(2)
    ]
    pending = [None, None]
    done = [0]

    def settle(slot):
        if pending[slot] is not None:
            for copy in pending[slot]:
                copy.wait()
        pending[slot] = None

    def tile(s, m):
        slot = done[0] % 2
        done[0] += 1
        settle(slot)

        def one(at, carry):
            columns = pl.ds(pl.multiple_of(at * CHUNK, CHUNK), CHUNK)
            kept = jnp.maximum(dot_nt(rows[s, m], up[columns, :]), 0.0)
            relu[slot, :, columns] = kept
            hidden[slot, :, columns] = (kept * kept).astype(LOW)
            return carry

        lax.fori_loop(0, units // CHUNK, one, 0)
        pending[slot] = [
            pltpu.make_async_copy(relu.at[slot], relu_ref.at[s, m], outs.at[slot, 0]),
            pltpu.make_async_copy(hidden.at[slot], hidden_ref.at[s, m], outs.at[slot, 1]),
        ]
        for copy in pending[slot]:
            copy.start()

    for number in range(4):
        copies[0][number].start()
    for there, here, leaving, _ in late_blocks:

        @pl.when(there)
        def _(here=here, leaving=leaving):
            here.start()
            leaving.start()

    down_line.start(1)
    down_line.swap_own()

    def cot_loads(s):
        copies = []
        for m in range(4):
            copies += piece_copies(pieces, s, m, cot.at[m], cot_sem.at[m])
        return copies

    for copy in cot_loads(0):
        copy.start()
    for there, here, leaving, landing in late_blocks:

        @pl.when(there)
        def _(here=here, leaving=leaving, landing=landing):
            here.wait()
            leaving.wait_send()
            landing.wait_recv()

    whole_up = pltpu.make_async_copy(up, up_all_ref, local.at[2])
    whole_up.start()
    tile(0, 0)
    copies[0][0].wait_recv()
    copies[0][4].start()
    copies[0][1].wait_recv()
    copies[0][5].start()
    copies[1][0].start()
    copies[1][1].start()
    tile(1, 0)
    down_line.arrive(1)
    down_line.start(2)
    copies[0][3].wait_recv()
    tile(0, 1)
    copies[0][2].wait_recv()
    copies[1][2].start()
    copies[1][3].start()
    tile(0, 2)
    copies[1][0].wait_recv()
    copies[1][4].start()
    copies[1][1].wait_recv()
    copies[1][5].start()
    copies[0][4].wait_recv()
    copies[0][5].wait_recv()
    tile(0, 3)
    for step in range(3, count):
        down_line.arrive(step - 1)
        down_line.start(step)
    settle(0)
    settle(1)
    for copy in cot_loads(0):
        copy.wait()
    gradient_tiles(hidden_ref.at[0], cot, tiles, sums, down_part_ref, tile_sem, sum_sem)
    for copy in cot_loads(1):
        copy.start()
    copies[1][3].wait_recv()
    tile(1, 1)
    copies[1][2].wait_recv()
    tile(1, 2)
    copies[1][4].wait_recv()
    copies[1][5].wait_recv()
    gathered = pltpu.make_async_copy(rows, all_ref, local.at[0])
    gathered.start()
    tile(1, 3)
    down_line.arrive(count - 1)
    down_line.finish(range(1, count), True)
    whole_down = pltpu.make_async_copy(down, down_all_ref, local.at[1])
    whole_down.start()
    settle(0)
    settle(1)
    for copy in cot_loads(1):
        copy.wait()
    gradient_tiles(
        hidden_ref.at[1], cot, tiles, sums, down_part_ref, tile_sem, sum_sem,
        (down_part_ref, before, before_sem),
    )
    for s in range(2):
        for copy in copies[s]:
            copy.wait_send()
    gathered.wait()
    whole_up.wait()
    whole_down.wait()


def gradient_tiles(
    left_ref, right, tiles, sums, out_ref, tile_sem, sum_sem, before=None, span=None
):
    wide = tiles.shape[-1]
    first, steps = span if span is not None else (0, left_ref.shape[-1] // wide)
    lead = (slice(None),) * (len(left_ref.shape) - 1)
    tall = math.prod(tiles.shape[1:-1])

    def load(at, slot):
        columns = pl.ds(pl.multiple_of(at * wide, wide), wide)
        return pltpu.make_async_copy(
            left_ref.at[lead + (columns,)], tiles.at[slot], tile_sem.at[slot]
        )

    def rows_of(at):
        return pl.ds(pl.multiple_of(at * wide, wide), wide)

    def save(at, slot):
        return pltpu.make_async_copy(sums.at[slot], out_ref.at[rows_of(at), :], sum_sem.at[slot])

    def load_before(at, slot):
        before_ref, buffer, sem = before
        return pltpu.make_async_copy(before_ref.at[rows_of(at), :], buffer.at[slot], sem.at[slot])

    load(first, first % 2).start()
    if before is not None:
        load_before(first, first % 2).start()

    def one(at, carry):
        slot = lax.rem(at, 2)
        load(at, slot).wait()
        if before is not None:
            load_before(at, slot).wait()

        @pl.when(at + 1 < steps)
        def _():
            load(at + 1, 1 - slot).start()
            if before is not None:
                load_before(at + 1, 1 - slot).start()

        @pl.when(at >= first + 2)
        def _():
            save(at - 2, slot).wait()

        result = lax.dot_general(
            tiles[slot].reshape(tall, wide),
            right[...].reshape(tall, right.shape[-1]),
            (((0,), (0,)), ((), ())),
            preferred_element_type=F32,
        )
        if before is not None:
            result = result + before[1][slot].astype(F32)
        sums[slot] = result.astype(LOW)
        save(at, slot).start()
        return carry

    lax.fori_loop(first, steps, one, 0)
    save(steps - 2, (steps - 2) % 2).wait()
    save(steps - 1, (steps - 1) % 2).wait()


def feed_in(second, up_early, down, cot_pieces, up_late):
    rows_here, depth = second.shape[1:]
    units = up_early.shape[0]
    count = lax.axis_size("mp") // 2
    anywhere = pl.BlockSpec(memory_space=pl.ANY)
    dma = pltpu.SemaphoreType.DMA
    return pl.pallas_call(
        partial(feed_in_kernel, tuple(up_late)),
        in_specs=[anywhere] * (10 + len(up_late)),
        out_specs=[anywhere] * 6,
        out_shape=[
            jax.ShapeDtypeStruct((2, 4, rows_here, depth), LOW),
            jax.ShapeDtypeStruct((2, 4, rows_here, units), F32),
            jax.ShapeDtypeStruct((2, 4, rows_here, units), LOW),
            jax.ShapeDtypeStruct((units, depth), LOW),
            jax.ShapeDtypeStruct((units, depth), LOW),
            jax.ShapeDtypeStruct((units, depth), LOW),
        ],
        scratch_shapes=[
            pltpu.VMEM((2, 4, rows_here, depth), LOW),
            pltpu.VMEM((units, depth), LOW),
            pltpu.VMEM((2, rows_here, units), F32),
            pltpu.VMEM((2, rows_here, units), LOW),
            pltpu.VMEM((units, depth), LOW),
            pltpu.VMEM((4, rows_here, depth), LOW),
            pltpu.VMEM((2, 4, rows_here, WIDE), LOW),
            pltpu.VMEM((2, WIDE, depth), LOW),
            pltpu.VMEM((2, WIDE, depth), LOW),
            dma((4,)),
            dma((2, 2)),
            dma((2, 6)),
            dma((2, 6)),
            dma((4, 2)),
            dma((2,)),
            dma((2,)),
            dma((2,)),
        ]
        + [dma((len(up_late),))] * 3
        + line_semaphores(count),
        compiler_params=pltpu.CompilerParams(
            collective_id=1, has_side_effects=True, vmem_limit_bytes=VMEM_LIMIT
        ),
        cost_estimate=pl.CostEstimate(
            flops=2 * 8 * rows_here * depth * units * 3,
            bytes_accessed=60 * 2**20,
            transcendentals=0,
        ),
        name="feed_in",
    )(second, up_early, down, *cot_pieces, *up_late.values())


def piece_copies(pieces, s, m, target, sems):
    half = target.shape[-1] // 2
    if m == 0:
        return [pltpu.make_async_copy(pieces[0].at[s], target, sems.at[0])]
    return [
        pltpu.make_async_copy(
            pieces[2 * m - 1 + side].at[s], target.at[:, pl.ds(side * half, half)], sems.at[side]
        )
        for side in range(2)
    ]


def feed_out_kernel(
    cot_0, cot_1, cot_2, cot_3, cot_4, cot_5, cot_6, relu_ref, second_ref, up_ref, down_ref,
    grad_ref, up_part_ref, back_ref,
    up, shared, cot, relu, grad, part, arrived, tiles, sums, result, local, loads, outs, send, recv,
    tile_sem, sum_sem,
):
    units, depth = up.shape
    down = shared.at[pl.ds(0, units), :]
    second = shared.at[pl.ds(0, 8 * cot.shape[1]), :]
    half = depth // 2
    lanes = (pl.ds(0, half), pl.ds(half, half))
    to_x, to_y = plane_partners()
    weights = [
        pltpu.make_async_copy(down_ref, down, local.at[0]),
        pltpu.make_async_copy(up_ref, up, local.at[1]),
    ]
    order = [(s, m) for s in range(2) for m in (3, 1, 2, 0)]
    pieces = (cot_0, cot_1, cot_2, cot_3, cot_4, cot_5, cot_6)

    def load(at):
        s, m = order[at]
        slot = at % 2
        return piece_copies(pieces, s, m, cot.at[slot], loads.at[slot]) + [
            pltpu.make_async_copy(relu_ref.at[s, m], relu.at[slot], loads.at[slot, 2]),
        ]

    for copy in load(0) + weights:
        copy.start()
    greet([to_x, to_y])
    for copy in weights:
        copy.wait()
    def remote(s, source, number, side, partner):
        return pltpu.make_async_remote_copy(
            src_ref=part.at[s, source, :, lanes[side]],
            dst_ref=arrived.at[s, number],
            send_sem=send.at[s, number],
            recv_sem=recv.at[s, number],
            device_id=partner,
            device_id_type=MESH,
        )

    copies = [
        [
            remote(s, 1, 0, 0, to_x),
            remote(s, 3, 1, 0, to_x),
            remote(s, 2, 2, 1, to_y),
            remote(s, 3, 3, 1, to_y),
            remote(s, 2, 4, 0, to_y),
            remote(s, 1, 5, 1, to_x),
        ]
        for s in range(2)
    ]
    saving = [None, None]
    load_second = pltpu.make_async_copy(second_ref, second, local.at[0])

    def tile(at):
        s, m = order[at]
        slot = at % 2
        for copy in load(at):
            copy.wait()
        if at + 1 < len(order):
            for copy in load(at + 1):
                copy.start()
        if saving[slot] is not None:
            saving[slot].wait()

        def back(step, carry):
            columns = pl.ds(pl.multiple_of(step * CHUNK, CHUNK), CHUNK)
            product = dot_nt(cot[slot], down[columns, :])
            grad[slot, :, columns] = (product * 2.0 * relu[slot, :, columns]).astype(LOW)
            return carry

        lax.fori_loop(0, units // CHUNK, back, 0)
        if at + 1 == len(order):
            load_second.start()
        saving[slot] = pltpu.make_async_copy(grad.at[slot], grad_ref.at[s, m], outs.at[slot])
        saving[slot].start()

        def through(step, carry):
            columns = pl.ds(pl.multiple_of(step * CHUNK, CHUNK), CHUNK)
            part[s, m, :, columns] = dot(grad[slot], up[:, columns]).astype(LOW)
            return carry

        lax.fori_loop(0, depth // CHUNK, through, 0)

    def second_leg(s):
        copies[s][1].wait_recv()
        part[s, 2, :, lanes[0]] = (
            part[s, 2, :, lanes[0]].astype(F32) + arrived[s, 1].astype(F32)
        ).astype(LOW)
        copies[s][4].start()
        copies[s][3].wait_recv()
        part[s, 1, :, lanes[1]] = (
            part[s, 1, :, lanes[1]].astype(F32) + arrived[s, 3].astype(F32)
        ).astype(LOW)
        copies[s][5].start()

    def finish(s):
        for side, near, last in ((0, 0, 4), (1, 2, 5)):
            copies[s][near].wait_recv()
            copies[s][last].wait_recv()
            result[:, lanes[side]] = (
                part[s, 0, :, lanes[side]].astype(F32)
                + arrived[s, near].astype(F32)
                + arrived[s, last].astype(F32)
            )
        done = pltpu.make_async_copy(result, back_ref.at[s], local.at[2])
        done.start()
        return done

    def send_after(at):
        s, m = order[at]
        for number in {3: (1, 3), 1: (0,), 2: (2,), 0: ()}[m]:
            copies[s][number].start()

    for at in range(5):
        tile(at)
        send_after(at)
    second_leg(0)
    for at in range(5, 8):
        tile(at)
        send_after(at)
    done = finish(0)

    for slot in range(2):
        saving[slot].wait()
    load_second.wait()
    halves = units // WIDE // 2

    def some(span):
        gradient_tiles(grad_ref, second, tiles, sums, up_part_ref, tile_sem, sum_sem, span=span)

    some((0, halves))
    second_leg(1)
    some((halves, 2 * halves))
    done.wait()
    finish(1).wait()
    for s in range(2):
        for number in range(6):
            copies[s][number].wait_send()


def feed_out(cot_pieces, relu, second_all, up_all, down_all):
    rows_here, units = relu.shape[2:]
    depth = up_all.shape[1]
    anywhere = pl.BlockSpec(memory_space=pl.ANY)
    dma = pltpu.SemaphoreType.DMA
    return pl.pallas_call(
        feed_out_kernel,
        in_specs=[anywhere] * 11,
        out_specs=[anywhere] * 3,
        out_shape=[
            jax.ShapeDtypeStruct((2, 4, rows_here, units), LOW),
            jax.ShapeDtypeStruct((units, depth), LOW),
            jax.ShapeDtypeStruct((2, rows_here, depth), F32),
        ],
        scratch_shapes=[
            pltpu.VMEM((units, depth), LOW),
            pltpu.VMEM((max(units, 8 * rows_here), depth), LOW),
            pltpu.VMEM((2, rows_here, depth), LOW),
            pltpu.VMEM((2, rows_here, units), F32),
            pltpu.VMEM((2, rows_here, units), LOW),
            pltpu.VMEM((2, 4, rows_here, depth), LOW),
            pltpu.VMEM((2, 6, rows_here, depth // 2), LOW),
            pltpu.VMEM((2, 2, 4, rows_here, WIDE), LOW),
            pltpu.VMEM((2, WIDE, depth), LOW),
            pltpu.VMEM((rows_here, depth), F32),
            dma((3,)),
            dma((2, 3)),
            dma((2,)),
            dma((2, 6)),
            dma((2, 6)),
            dma((2,)),
            dma((2,)),
        ],
        compiler_params=pltpu.CompilerParams(
            collective_id=2, has_side_effects=True, vmem_limit_bytes=VMEM_LIMIT
        ),
        cost_estimate=pl.CostEstimate(
            flops=2 * 8 * rows_here * depth * units * 4,
            bytes_accessed=60 * 2**20,
            transcendentals=0,
        ),
        name="feed_out",
    )(*cot_pieces, relu, second_all.reshape(8 * rows_here, depth), up_all, down_all)


def feed_heads_kernel(
    x_ref, hidden_ref, down_ref,
    o_ref, feed_x0_ref, feed_x1_ref, feed_y0_ref, feed_y1_ref, keep_a_ref, keep_b_ref,
    landed, down, hidden, feed, local, send, recv, loads, outs,
):
    me = lax.axis_index("mp")
    units, depth = down.shape
    half = depth // 2
    lanes = (pl.ds(0, half), pl.ds(half, half))
    feed_x_refs, feed_y_refs = (feed_x0_ref, feed_x1_ref), (feed_y0_ref, feed_y1_ref)

    def source(at):
        return x_ref.at[:, :, head_lanes(at)]

    def target(at):
        return landed.at[:, at]

    weights = pltpu.make_async_copy(down_ref, down, local.at[2])
    weights.start()
    own = pltpu.make_async_copy(source(me), target(me), local.at[0])
    own.start()
    greet_members(())
    copies = member_copies(source, target, send, recv)
    for leaving, _ in copies:
        leaving.start()
    order = [(s, m) for s in range(2) for m in (3, 1, 2, 0)]

    def load(at):
        s, m = order[at]
        return pltpu.make_async_copy(hidden_ref.at[s, m], hidden.at[at % 2], loads.at[at % 2])

    load(0).start()
    weights.wait()
    feeding = [None, None]
    for at, (s, m) in enumerate(order):
        slot = at % 2
        load(at).wait()
        if at + 1 < len(order):
            load(at + 1).start()
        if feeding[slot] is not None:
            for copy in feeding[slot]:
                copy.wait()

        def one(step, carry, slot=slot):
            columns = pl.ds(pl.multiple_of(step * CHUNK, CHUNK), CHUNK)
            feed[slot, :, columns] = dot(hidden[slot], down[:, columns]).astype(LOW)
            return carry

        lax.fori_loop(0, depth // CHUNK, one, 0)
        targets = (
            (keep_a_ref.at[s, 0], feed_x_refs[s].at[0], keep_a_ref.at[s, 1], feed_x_refs[s].at[1])[m],
            (keep_b_ref.at[s, 0], keep_b_ref.at[s, 1], feed_y_refs[s].at[0], feed_y_refs[s].at[1])[m],
        )
        feeding[slot] = [
            pltpu.make_async_copy(feed.at[slot, :, lanes[side]], there, outs.at[slot, side])
            for side, there in enumerate(targets)
        ]
        for copy in feeding[slot]:
            copy.start()
    own.wait()
    for _, landing in copies:
        landing.wait_recv()
    save = pltpu.make_async_copy(landed, o_ref, local.at[1])
    save.start()
    for leaving, _ in copies:
        leaving.wait_send()
    for slot in feeding:
        for copy in slot:
            copy.wait()
    save.wait()


def feed_heads(x, hidden, down_all):
    parts, rows_here, width = x.shape
    mp = lax.axis_size("mp")
    units, depth = down_all.shape
    anywhere = pl.BlockSpec(memory_space=pl.ANY)
    dma = pltpu.SemaphoreType.DMA
    shape = (parts, mp, rows_here, 128)
    out, *terms = pl.pallas_call(
        feed_heads_kernel,
        in_specs=[pl.BlockSpec(memory_space=pltpu.VMEM)] + [anywhere] * 2,
        out_specs=[anywhere] * 7,
        out_shape=[jax.ShapeDtypeStruct(shape, LOW)]
        + [jax.ShapeDtypeStruct((2, rows_here, depth // 2), LOW)] * 4
        + [jax.ShapeDtypeStruct((2, 2, rows_here, depth // 2), LOW)] * 2,
        scratch_shapes=[
            pltpu.VMEM(shape, LOW),
            pltpu.VMEM((units, depth), LOW),
            pltpu.VMEM((2, rows_here, units), LOW),
            pltpu.VMEM((2, rows_here, depth), LOW),
            dma((3,)),
            dma((mp,)),
            dma((mp,)),
            dma((2,)),
            dma((2, 2)),
        ],
        compiler_params=pltpu.CompilerParams(
            collective_id=6, has_side_effects=True, vmem_limit_bytes=48 * 2**20
        ),
        cost_estimate=pl.CostEstimate(flops=2**35, bytes_accessed=2**24, transcendentals=0),
        name="feed_heads",
    )(x, hidden, down_all)
    return [out.reshape(parts, mp * rows_here, 128)] + terms


def finish_kernel(
    ways, qk_ref, v_ref, out_ref, norms_ref, taps_ref, grad_raw_ref, inputs_ref, gain_ref,
    qk_all_ref, v_all_ref, middle_ref, *refs
):
    carried, refs = list(zip(ways, refs[: len(ways)])), refs[len(ways) :]
    joint_ref, norms_sum_ref, taps_sum_ref, input_grad_ref = refs[:4]
    targets, refs = refs[4 : 4 + len(ways)], refs[4 + len(ways) :]
    (
    acc, got, plane_in, line_in, gathered, norms_all, taps_all, norms_dp, taps_dp,
    weights, result, middle, norms, sums, weight_sem,
    local, swap_send, swap_recv, plane_send_sem, plane_recv_sem, line_send_sem, line_recv_sem,
    gather_send, gather_recv, small_send, small_recv, carry_send, carry_recv,
    ) = refs
    mp = lax.axis_size("mp")
    dp = lax.axis_index("dp")
    me = lax.axis_index("mp")
    z, core = mesh_place()
    count = mp // 2
    depth = acc.shape[3]
    half = depth // 2
    lanes = (pl.ds(0, half), pl.ds(half, half))
    to_x, to_y = plane_partners()
    dp_x = dp + 1 - 2 * lax.rem(dp, 2)
    dp_y = dp + 2 - 4 * (dp // 2)
    dp_xy = dp_x + 2 - 4 * (dp_x // 2)
    parts = (qk_ref, v_ref, out_ref)
    spans = (pl.ds(0, HD // 2), pl.ds(HD // 2, HD // 4), pl.ds(3 * HD // 4, HD // 4))
    loads = [
        pltpu.make_async_copy(part.at[:, core], acc.at[:, :, span, :], local.at[at])
        for at, (part, span) in enumerate(zip(parts, spans))
    ]
    for copy in loads:
        copy.start()

    barrier = pltpu.get_barrier_semaphore()
    for step in range(1, mp):
        pl.semaphore_signal(
            barrier, inc=1, device_id={"mp": lax.rem(me + step, mp)}, device_id_type=MESH
        )
    for step in range(1, 4):
        pl.semaphore_signal(
            barrier, inc=1, device_id={"dp": lax.rem(dp + step, 4)}, device_id_type=MESH
        )
    pl.semaphore_wait(barrier, mp + 2)

    swaps = [
        [
            wire(
                part.at[:, 1 - core, quarter], got.at[:, quarter, span, :],
                swap_send.at[at, number], swap_recv.at[at, number], other_core(),
            )
            for at, (part, span) in enumerate(zip(parts, spans))
        ]
        for number, quarter in enumerate((dp_xy, dp_x, dp_y, dp))
    ]
    for group in swaps:
        for copy in group:
            copy.start()

    def small(axis, at, others, source, target, number, first):
        out = []
        for step in range(1, others):
            to = lax.rem(at + step, others)
            frm = lax.rem(at + others - step, others)
            sems = (small_send.at[number, step], small_recv.at[number, step], {axis: to})
            out.append((wire(source(to), target.at[at], *sems), wire(source(to), target.at[frm], *sems)))
        return out

    load_middle = pltpu.make_async_copy(middle_ref, middle, local.at[6])
    load_middle.start()
    own_small = [
        pltpu.make_async_copy(norms, norms_all.at[me], local.at[3]),
        pltpu.make_async_copy(taps_ref.at[me], taps_all.at[me], local.at[4]),
    ]
    over_mp = small("mp", me, mp, lambda to: norms, norms_all, 0, None) + small(
        "mp", me, mp, lambda to: taps_ref.at[to], taps_all, 1, None
    )

    rows_here = inputs_ref.shape[1]
    slots = weights.shape[0]

    def load_weights(at, slot):
        return [
            pltpu.make_async_copy(
                qk_all_ref.at[at], weights.at[slot, pl.ds(0, 4 * HD), :], weight_sem.at[slot, 0]
            )
        ] + [
            pltpu.make_async_copy(
                v_all_ref.at[at, pl.ds(head * HD, HD), :],
                weights.at[slot, pl.ds((4 + 2 * head + copy) * HD, HD), :],
                weight_sem.at[slot, 1 + 2 * head + copy],
            )
            for head in range(2)
            for copy in range(2)
        ]

    def normed_grad():
        if slots == 2:
            for copy in load_weights(0, 0):
                copy.start()
        lane = lax.rem(lax.broadcasted_iota(jnp.int32, (rows_here, 4 * HD), 1), 2 * HD)

        def one(at, carry):
            slot = lax.rem(at, slots)
            if slots == 1:
                for copy in load_weights(at, slot):
                    copy.start()
            for copy in load_weights(at, slot):
                copy.wait()
            if slots == 2:

                @pl.when(at + 1 < count)
                def _():
                    for copy in load_weights(at + 1, 1 - slot):
                        copy.start()

            pair = pl.ds(pl.multiple_of(at * 4 * HD, 4 * HD), 4 * HD)
            side = grad_raw_ref[2, :, pair]
            for s in range(2):
                mine = lane < HD if s == 0 else lane >= HD
                left = jnp.concatenate(
                    [grad_raw_ref[s, :, pair], jnp.where(mine, side, jnp.zeros_like(side))], axis=1
                )
                for first in range(0, depth, CHUNK):
                    columns = pl.ds(first, CHUNK)
                    product = dot(left, weights[slot, :, columns])

                    @pl.when(at == 0)
                    def _(s=s, columns=columns, product=product):
                        result[s, :, columns] = product

                    @pl.when(at > 0)
                    def _(s=s, columns=columns, product=product):
                        result[s, :, columns] += product

            return carry

        lax.fori_loop(0, count, one, 0)

    tall = 16
    tiles = rows_here // tall

    def norm_back(s, first, last):
        def some(at, carry):
            here = pl.ds(pl.multiple_of(at * tall, tall), tall)
            values = inputs_ref[s, here, :].astype(F32)
            centered = values - jnp.mean(values, axis=1, keepdims=True)
            scale = lax.rsqrt(jnp.mean(centered * centered, axis=1, keepdims=True) + 1e-05)
            hat = centered * scale
            grad = result[s, here, :]
            wide = grad * gain_ref[...]
            back = wide - jnp.mean(wide, axis=1, keepdims=True)
            back = scale * (back - hat * jnp.mean(wide * hat, axis=1, keepdims=True))
            result[s, here, :] = middle[s, here, :] + back
            product = grad * hat
            sums[0] += product[:8] + product[8:]
            sums[1] += grad[:8] + grad[8:]
            return carry

        lax.fori_loop(first, last, some, 0)

    def add(quarter, side, number):
        acc[:, quarter, :, lanes[side]] = (
            acc[:, quarter, :, lanes[side]].astype(F32) + plane_in[number].astype(F32)
        ).astype(LOW)

    def add_core(number, quarter):
        for copy in swaps[number]:
            copy.wait_recv()
        acc[:, quarter] = (acc[:, quarter].astype(F32) + got[:, quarter].astype(F32)).astype(LOW)

    def plane(quarter, side, partner, number):
        return wire(
            acc.at[:, quarter, :, lanes[side]], plane_in.at[number],
            plane_send_sem.at[number], plane_recv_sem.at[number], partner,
        )

    sends = [
        plane(dp_x, 0, to_x, 0),
        plane(dp_xy, 0, to_x, 1),
        plane(dp_y, 1, to_y, 2),
        plane(dp_xy, 1, to_y, 3),
        plane(dp_y, 0, to_y, 4),
        plane(dp_x, 1, to_x, 5),
    ]
    for copy in loads:
        copy.wait()
    add_core(0, dp_xy)
    sends[1].start()
    sends[3].start()
    add_core(1, dp_x)
    sends[0].start()
    add_core(2, dp_y)
    sends[2].start()
    add_core(3, dp)
    normed_grad()
    load_middle.wait()
    sums[...] = jnp.zeros(sums.shape, F32)
    saved_rows = [
        pltpu.make_async_copy(result.at[s], input_grad_ref.at[s], local.at[7 + s]) for s in range(2)
    ]
    sends[1].wait_recv()
    add(dp_y, 0, 1)
    sends[4].start()
    sends[3].wait_recv()
    add(dp_x, 1, 3)
    sends[5].start()
    norm_back(0, 0, tiles)
    saved_rows[0].start()
    sends[0].wait_recv()
    add(dp, 0, 0)
    sends[2].wait_recv()
    add(dp, 1, 2)
    sends[4].wait_recv()
    add(dp, 0, 4)
    sends[5].wait_recv()
    add(dp, 1, 5)

    carries = carry_copies(carried, targets, carry_send, carry_recv)
    for copy in carries:
        copy.start()

    def line(step):
        out = []
        for way, turn in enumerate((1, -1)):
            target = z + turn * (count - step)
            far = z + turn
            lands = far - 2 * turn + turn * (count - step)
            sends = (target >= 0) & (target < count)
            receives = (lands >= 0) & (lands < count) & (z - turn >= 0) & (z - turn < count)
            at = jnp.clip(target, 0, count - 1)
            to = jnp.clip(lands, 0, count - 1)
            copy = wire(
                acc.at[at, dp], line_in.at[way, step - 1],
                line_send_sem.at[way, step - 1], line_recv_sem.at[way, step - 1],
                line_partner(z, turn),
            )
            out.append((sends, receives, to, copy))
        return out

    over_dp = []
    for step in range(1, count):
        legs = line(step)
        for sends_now, _, _, copy in legs:
            pl.when(sends_now)(copy.start)
        if step == 1:
            norm_back(1, 0, tiles // 2)
        if step == 2:
            norm_back(1, tiles // 2, tiles)
            saved_rows[1].start()
            norms[...] = norms_ref[...]
            norms[0:1, :] = jnp.sum(sums[0], axis=0, keepdims=True)
            norms[1:2, :] = jnp.sum(sums[1], axis=0, keepdims=True)
            for copy in own_small:
                copy.start()
            for leaving, _ in over_mp:
                leaving.start()
        if step == count - 1:
            for _, landed in over_mp:
                landed.wait_recv()
            for copy in own_small:
                copy.wait()
            norms_dp[dp] = jnp.sum(norms_all[...], axis=0)
            taps_dp[dp] = jnp.sum(taps_all[...], axis=0)
            over_dp = small("dp", dp, 4, lambda to: norms_dp.at[dp], norms_dp, 2, None) + small(
                "dp", dp, 4, lambda to: taps_dp.at[dp], taps_dp, 3, None
            )
            for leaving, _ in over_dp:
                leaving.start()
        for way, (_, receives, to, copy) in enumerate(legs):

            @pl.when(receives)
            def _(to=to, copy=copy, way=way):
                copy.wait_recv()
                acc[to, dp] = (
                    acc[to, dp].astype(F32) + line_in[way, step - 1].astype(F32)
                ).astype(LOW)

    gathered[dp] = acc[z, dp]

    def gather(quarter, side, partner, number):
        block = gathered.at[quarter, :, lanes[side]]
        return wire(block, block, gather_send.at[number], gather_recv.at[number], partner)

    leaving = [
        gather(dp, 0, to_x, 0), gather(dp, 1, to_y, 1), gather(dp, 0, to_y, 2), gather(dp, 1, to_x, 3),
        gather(dp_x, 0, to_y, 4), gather(dp_y, 1, to_x, 5),
    ]
    landing = [
        gather(dp_x, 0, to_x, 0), gather(dp_y, 1, to_y, 1), gather(dp_y, 0, to_y, 2), gather(dp_x, 1, to_x, 3),
        gather(dp_xy, 0, to_y, 4), gather(dp_xy, 1, to_x, 5),
    ]
    for number in range(4):
        leaving[number].start()
    for _, landed in over_dp:
        landed.wait_recv()
    norms_sum_ref[...] = jnp.sum(norms_dp[...], axis=0)
    taps_sum_ref[...] = jnp.sum(taps_dp[...], axis=0)
    landing[0].wait_recv()
    leaving[4].start()
    landing[1].wait_recv()
    leaving[5].start()
    for number in range(2, 6):
        landing[number].wait_recv()
    save = pltpu.make_async_copy(gathered, joint_ref, local.at[5])
    save.start()
    for group in swaps:
        for copy in group:
            copy.wait_send()
    for copy in sends:
        copy.wait_send()
    for step in range(1, count):
        for sends_now, _, _, copy in line(step):
            pl.when(sends_now)(copy.wait_send)
    for copy in leaving:
        copy.wait_send()
    for copy, _ in over_mp + over_dp:
        copy.wait_send()
    for copy in carries + saved_rows:
        copy.wait()
    save.wait()


def finish(qk, v, out, norms, taps, grad_raw, inputs, gain, qk_all, v_all, middle, carried):
    mp = lax.axis_size("mp")
    count = mp // 2
    depth = qk.shape[-1]
    anywhere = pl.BlockSpec(memory_space=pl.ANY)
    vmem = pl.BlockSpec(memory_space=pltpu.VMEM)
    dma = pltpu.SemaphoreType.DMA
    return pl.pallas_call(
        partial(finish_kernel, tuple(way for way, _ in carried)),
        in_specs=[anywhere] * 3 + [vmem] * 5 + [anywhere] * (3 + len(carried)),
        out_specs=[anywhere, vmem, vmem, anywhere] + [anywhere] * len(carried),
        out_shape=[
            jax.ShapeDtypeStruct((4, HD, depth), LOW),
            jax.ShapeDtypeStruct(norms.shape, F32),
            jax.ShapeDtypeStruct(taps.shape[1:], F32),
            jax.ShapeDtypeStruct(middle.shape, F32),
        ]
        + [jax.ShapeDtypeStruct(block.shape, block.dtype) for _, block in carried],
        scratch_shapes=[
            pltpu.VMEM((count, 4, HD, depth), LOW),
            pltpu.VMEM((count, 4, HD, depth), LOW),
            pltpu.VMEM((6, count, HD, depth // 2), LOW),
            pltpu.VMEM((2, count - 1, HD, depth), LOW),
            pltpu.VMEM((4, HD, depth), LOW),
            pltpu.VMEM((mp,) + norms.shape, F32),
            pltpu.VMEM(taps.shape, F32),
            pltpu.VMEM((4,) + norms.shape, F32),
            pltpu.VMEM((4,) + taps.shape[1:], F32),
            pltpu.VMEM((2 if count <= 8 else 1, 8 * HD, depth), LOW),
            pltpu.VMEM(middle.shape, F32),
            pltpu.VMEM(middle.shape, F32),
            pltpu.VMEM(norms.shape, F32),
            pltpu.VMEM((2, 8, depth), F32),
            dma((2, 5)),
            dma((9,)),
            dma((3, 4)),
            dma((3, 4)),
            dma((6,)),
            dma((6,)),
            dma((2, count)),
            dma((2, count)),
            dma((6,)),
            dma((6,)),
            dma((4, mp)),
            dma((4, mp)),
            dma((len(carried),)),
            dma((len(carried),)),
        ],
        compiler_params=pltpu.CompilerParams(
            collective_id=8, has_side_effects=True, vmem_limit_bytes=VMEM_LIMIT + 2**19
        ),
        cost_estimate=pl.CostEstimate(flops=2**36, bytes_accessed=2**26, transcendentals=0),
        name="finish",
    )(
        qk, v, out, norms, taps, grad_raw, inputs, gain.reshape(1, depth), qk_all, v_all, middle, *(block for _, block in carried),
    )


def plane_send(block, mask):
    return lax.ppermute(block, "dp", [(d, d ^ mask) for d in range(lax.axis_size("dp"))])


def placed(own, legs, last, me, turn):
    one_x, two_y, one_y, two_x = legs
    units, width = own.shape
    wide = 256
    steps = width // 2 // wide

    def kernel(me_ref, own_ref, one_x, two_x, one_y, two_y, one_xy, two_xy, o_ref):
        first = pl.program_id(0) < steps
        blocks = [own_ref[...]] + [
            jnp.where(first, one[...], two[...])
            for one, two in ((one_x, two_x), (one_y, two_y), (one_xy, two_xy))
        ]
        odd, high = lax.rem(me_ref[0], 2) == 1, me_ref[0] >= 2
        blocks = [jnp.where(odd, blocks[at ^ 1], blocks[at]) for at in range(4)]
        blocks = [jnp.where(high, blocks[at ^ 2], blocks[at]) for at in range(4)]
        for at, block in enumerate(blocks):
            if turn:
                o_ref[:, at * units : (at + 1) * units] = block.astype(F32).T
            else:
                o_ref[at * units : (at + 1) * units, :] = block.astype(F32)

    def half(side):
        if side == 0:
            return pl.BlockSpec((units, wide), lambda i, me: (0, jnp.minimum(i, steps - 1)))
        return pl.BlockSpec((units, wide), lambda i, me: (0, jnp.maximum(i - steps, 0)))

    if turn:
        shape = (width, 4 * units)
        out_spec = pl.BlockSpec((wide, 4 * units), lambda i, me: (i, 0))
    else:
        shape = (4 * units, width)
        out_spec = pl.BlockSpec((4 * units, wide), lambda i, me: (0, i))
    return pl.pallas_call(
        kernel,
        grid_spec=pltpu.PrefetchScalarGridSpec(
            num_scalar_prefetch=1,
            grid=(2 * steps,),
            in_specs=[pl.BlockSpec((units, wide), lambda i, me: (0, i))] + [half(0), half(1)] * 3,
            out_specs=out_spec,
        ),
        out_shape=jax.ShapeDtypeStruct(shape, F32),
        compiler_params=pltpu.CompilerParams(vmem_limit_bytes=32 * 2**20),
        cost_estimate=pl.CostEstimate(flops=0, bytes_accessed=2**24, transcendentals=0),
        name="placed",
    )(me.reshape(1).astype(jnp.int32), own, one_x, two_x, one_y, two_y, *last)


def plane_gather_begin(block, axis=-1):
    half = block.shape[axis] // 2
    one, two = jnp.split(block, [half], axis=axis)
    return plane_send(one, 1), plane_send(two, 2), plane_send(one, 2), plane_send(two, 1)


def plane_gather_end(legs):
    one_x, two_y, one_y, two_x = legs
    return plane_send(one_x, 2), plane_send(two_y, 1)


def line_step(blocks, step):
    count = lax.axis_size("mp") // 2
    up = [(2 * z + c, 2 * z + 2 + c) for z in range(step - 1, count - 1) for c in range(2)]
    down = [(2 * z + c, 2 * z - 2 + c) for z in range(1, count - step + 1) for c in range(2)]
    return lax.ppermute(blocks[0], "mp", up), lax.ppermute(blocks[1], "mp", down)


def per_device(
    inputs,
    cotangent,
    short_lengths,
    long_lengths,
    norm1_gain,
    norm1_bias,
    query_weight,
    key_weight,
    value_weight,
    query_kernel,
    key_kernel,
    value_kernel,
    out_weight,
    norm2_gain,
    norm2_bias,
    up_weight,
    down_weight,
):
    rows_here = inputs.shape[1]
    width = inputs.shape[2]
    mp = lax.axis_size("mp")
    dp = lax.axis_size("dp")
    me_dp = lax.axis_index("dp")
    me_mp = lax.axis_index("mp")
    group = rows_here * mp
    chips = mp // 2
    hidden_here = up_weight.shape[1]
    share = hidden_here // dp

    starts = jnp.stack(
        [document_starts(short_lengths[0], group), document_starts(long_lengths[0], group)]
    )
    rows = inputs.astype(F32)

    def quarters(weight):
        return weight.reshape(4, weight.shape[0] // 4, width)

    qk_own = jnp.concatenate([query_weight, key_weight], axis=1).T
    up_own = lax.dynamic_slice_in_dim(up_weight, me_dp * share, share, 1).T
    down_own = lax.dynamic_slice_in_dim(down_weight, me_dp * share, share, 0)
    qk_taps = jnp.concatenate([query_kernel, key_kernel], axis=1)
    v_taps = jnp.concatenate([value_kernel, value_kernel], axis=1)
    taps_own = jnp.pad(jnp.stack([qk_taps, qk_taps, v_taps]), ((0, 0), (0, 5), (0, 0)))
    places = jnp.arange(group, dtype=jnp.int32)
    offsets = lax.dynamic_slice_in_dim(
        jnp.pad(places[None, :] - starts, ((0, 0), (0, HALO))), me_mp * rows_here, rows_here + HALO, 1
    )
    masks = jnp.stack(
        [
            offsets[:, :rows_here] >= 1,
            offsets[:, :rows_here] >= 2,
            offsets[:, 1 : rows_here + 1] >= 1,
            offsets[:, 2 : rows_here + 2] >= 2,
        ],
        axis=1,
    ).astype(F32)[..., None]
    wide_masks = jnp.broadcast_to(masks, masks.shape[:3] + (HD,))
    masks = jnp.stack(
        [
            jnp.concatenate([wide_masks[left], wide_masks[right]], axis=2)
            for left, right in ((0, 0), (1, 1), (0, 1))
        ]
    )

    qk_all, v_all, out_all, taps, normed, up_early, raw, mixed, one_x, two_y = front(
        inputs, norm1_gain, norm1_bias, quarters(qk_own), quarters(value_weight.T), quarters(out_weight), taps_own, up_own,
        masks, cotangent,
    )
    qk_all = qk_all.reshape(mp * 2 * HD, width)
    v_all = v_all.reshape(mp * HD, width)
    out_all = out_all.reshape(mp * HD, width)
    mixed = mixed.reshape(3, group, 128)
    cot, mixed, up_early = lax.optimization_barrier((cotangent, mixed, up_early))

    def early_block(at):
        start = (2 * jnp.clip(at, 0, chips - 1) + me_mp % 2) * share
        return lax.dynamic_slice_in_dim(up_early, start, share, 0)

    late = range(early_steps(chips)[-1] + 1, chips)
    up_late = {}
    blocks = (early_block(me_mp // 2 - late[0] + 1), early_block(me_mp // 2 + late[0] - 1))
    for step in late:
        blocks = line_step(blocks, step)
        up_late[step, 1], up_late[step, -1] = blocks
    one_y, two_x = plane_send(cot[:, :, : width // 2], 2), plane_send(cot[:, :, width // 2 :], 1)
    one_xy, two_xy = plane_send(one_x, 2), plane_send(two_y, 1)

    def side_by_side(pair):
        split = pair.reshape(2, rows_here, mp, HD)
        return split.transpose(1, 2, 0, 3).reshape(1, rows_here, mp * 2 * HD)

    def apart(joint):
        split = joint.reshape(joint.shape[1], mp, 2, HD)
        return split.transpose(2, 0, 1, 3).reshape(2, joint.shape[1], mp * HD)

    attended_head, wide, total = attend(mixed, starts)
    attended_head, up_late = lax.optimization_barrier((attended_head, up_late))
    attended = apart(attended_back(attended_head, rows_here))
    middle = rows + dot(attended, out_all)
    second = layer_norm(middle, norm2_gain, norm2_bias).astype(LOW)

    second, one_y, two_x, one_xy, two_xy = lax.optimization_barrier(
        (second, one_y, two_x, one_xy, two_xy)
    )
    cot_pieces = (cot, one_x, two_x, one_y, two_y, one_xy, two_xy)
    second_all, relu, hidden, down_all, up_all, down_part = feed_in(
        second, up_early, down_own, cot_pieces, up_late
    )
    down_mine = lax.psum_scatter(down_part, "mp", scatter_dimension=0, tiled=True)
    grad_pre, up_part, grad_second = feed_out(
        cot_pieces, relu, second_all, up_all, down_all
    )
    up_mine = lax.psum_scatter(up_part, "mp", scatter_dimension=0, tiled=True)
    grad_second, down_mine = lax.optimization_barrier((grad_second, down_mine))
    down_legs = plane_gather_begin(down_mine)

    def norm_back(values, gain, grad):
        flat = values.reshape(-1, width)
        unused, pull = jax.vjp(layer_norm, flat, gain, norm1_bias)
        grad_rows, grad_gain, grad_shift = pull(grad.reshape(-1, width))
        return grad_rows.reshape(values.shape), grad_gain, grad_shift

    grad_middle, gain_two, shift_two = norm_back(middle, norm2_gain, grad_second)
    grad_middle = grad_middle + cotangent.astype(F32)
    branch = grad_middle.astype(LOW)
    grad_attended = jnp.einsum("srd,hd->srh", branch, out_all, preferred_element_type=F32).astype(LOW)
    grad_head, feed_x0, feed_x1, feed_y0, feed_y1, keep_a, keep_b = feed_heads(
        side_by_side(grad_attended), hidden, down_all
    )
    grad_head, down_legs, feed_x0, feed_y0 = lax.optimization_barrier(
        (grad_head, down_legs, feed_x0, feed_y0)
    )
    x_first, y_first = plane_send(feed_x0, 1), plane_send(feed_y0, 2)
    grad_mixed_head = attend_back(mixed, grad_head, wide, total, starts, HALO)
    grad_mixed_head, x_first, y_first, down_legs = lax.optimization_barrier(
        (grad_mixed_head, x_first, y_first, down_legs)
    )
    down_last = plane_gather_end(down_legs)

    def add(left, right):
        return left.astype(F32) + right.astype(F32)

    feed_a0, feed_b0 = add(keep_a[0, 1], x_first[1]).astype(LOW), add(keep_b[0, 1], y_first[1]).astype(LOW)
    grad_raw, tap_sums, qk_part, v_part, out_part, x_second, y_second, feed_a0, feed_b0 = project_back(
        grad_mixed_head, raw, taps, masks, normed, attended, branch,
        ((0, feed_x1), (1, feed_y1), (1, feed_a0), (0, feed_b0)),
    )
    grad_raw, down_last = lax.optimization_barrier((grad_raw, down_last))
    grad_raw, up_mine, down_last = lax.optimization_barrier((grad_raw, up_mine, down_last))
    down_grad = placed(down_mine, down_legs, down_last, me_dp, False)
    up_legs = plane_gather_begin(up_mine)
    feed_a1, feed_b1 = add(keep_a[1, 1], x_second[1]).astype(LOW), add(keep_b[1, 1], y_second[1]).astype(LOW)

    def split_parts(part):
        return part.reshape(mp // 2, 2, 4, part.shape[1] // 8, width)

    norms = jnp.pad(jnp.stack([gain_two, shift_two]), ((2, 4), (0, 0)))
    qk_sums = (tap_sums[0] + tap_sums[1]).reshape(8, mp, 2 * HD)
    v_sums = tap_sums[2].reshape(8, mp, 2, HD).sum(axis=2)
    taps_part = jnp.concatenate([qk_sums, v_sums, jnp.zeros_like(v_sums)], axis=2)
    taps_part = taps_part.transpose(1, 0, 2)
    norms, up_legs = lax.optimization_barrier((norms, up_legs))
    joint_grad, small_sum, taps_sum, input_grads, feed_a1, feed_b1, one_xy, two_xy = finish(
        split_parts(qk_part), split_parts(v_part), split_parts(out_part), norms, taps_part,
        grad_raw, inputs, norm1_gain, qk_all.reshape(chips, 4 * HD, width), v_all.reshape(chips, 2 * HD, width),
        grad_middle,
        ((1, feed_a1), (0, feed_b1), (1, up_legs[0]), (0, up_legs[1])),
    )
    results = jnp.stack(
        [
            middle[s]
            + jnp.concatenate(
                [
                    add(keep_a[s, 0], x_in[0]) + a_in.astype(F32),
                    add(keep_b[s, 0], y_in[0]) + b_in.astype(F32),
                ],
                axis=1,
            )
            for s, (x_in, y_in, a_in, b_in) in enumerate(
                ((x_first, y_first, feed_a0, feed_b0), (x_second, y_second, feed_a1, feed_b1))
            )
        ]
    ).astype(LOW)
    up_grad = placed(up_mine, up_legs, (one_xy, two_xy), me_dp, True)
    joint_grad = joint_grad.astype(F32)
    qk_grad = joint_grad[:, : HD // 2].reshape(2 * HD, width).T
    v_grad = joint_grad[:, HD // 2 : 3 * HD // 4].reshape(HD, width).T
    out_grad = joint_grad[:, 3 * HD // 4 :].reshape(HD, width)
    taps_sum = taps_sum[:3]
    return (
        results,
        input_grads,
        small_sum[0],
        small_sum[1],
        qk_grad[:, :HD],
        qk_grad[:, HD:],
        v_grad,
        taps_sum[:, :HD],
        taps_sum[:, HD : 2 * HD],
        taps_sum[:, 2 * HD : 3 * HD],
        out_grad,
        small_sum[2],
        small_sum[3],
        up_grad,
        down_grad,
    )


def solution(mesh):
    return jax.shard_map(
        per_device,
        mesh=mesh,
        in_specs=(
            P(None, ("dp", "mp"), None),
            P(None, ("dp", "mp"), None),
            P("dp", None),
            P("dp", None),
            P(),
            P(),
            P(None, "mp"),
            P(None, "mp"),
            P(None, "mp"),
            P(None, "mp"),
            P(None, "mp"),
            P(None, "mp"),
            P("mp", None),
            P(),
            P(),
            P(None, "mp"),
            P("mp", None),
        ),
        out_specs=(
            P(None, ("dp", "mp"), None),
            P(None, ("dp", "mp"), None),
            P(),
            P(),
            P(None, "mp"),
            P(None, "mp"),
            P(None, "mp"),
            P(None, "mp"),
            P(None, "mp"),
            P(None, "mp"),
            P("mp", None),
            P(),
            P(),
            P(None, "mp"),
            P("mp", None),
        ),
        check_vma=False,
    )
```
